128 devices in a mesh: ctx: 16 (over z_hi, y, core), exp: 8 (over z_lo, x).
Axes of the slice: x: 4, y: 4, z: 4 (z_hi: 2, z_lo: 2; z = z_hi * 2 + z_lo), core: 2. Of those that a mesh axis runs over, the one named last changes fastest.
Arguments:
- tokens: bfloat16 [8, 3072, 1024], P('exp', 'ctx'), may hold values from -40 to 40
- cotangent: bfloat16 [8, 3072, 1024], P('exp', 'ctx'), may hold values from -6 to 6
- lengths: int32 [8, 4], P('exp'), may hold values from 1 to 2048, 3072 in all within a row
- deal_perm: int32 [8, 16, 16], P('exp'), may hold values from 0 to 15, each once within a row
- routes: int32 [8, 3072, 8], P('exp', 'ctx'), may hold values from 0 to 31, all different within a row; in each aligned block of 192 rows (0 to 191, 192 to 383, ..., all dimensions but the last counted through in order) at most 72 rows name the same one
- gate_logits: float32 [8, 3072, 8], P('exp', 'ctx'), may hold values from -2.5 to 2.5
- norm_attn: bfloat16 [1024], P('exp'), may hold values from 0.25 to 1.75
- norm_query: bfloat16 [1024], P('exp'), may hold values from 0.25 to 1.75
- norm_key: bfloat16 [512], P('exp'), may hold values from 0.25 to 1.75
- norm_ffn: bfloat16 [1024], P('exp'), may hold values from 0.25 to 1.75
- w_query: bfloat16 [1024, 1024], P('exp'), may hold values from -0.1875 to 0.1875
- w_key: bfloat16 [1024, 512], P('exp'), may hold values from -0.1875 to 0.1875
- w_value: bfloat16 [1024, 512], P('exp'), may hold values from -0.1875 to 0.1875
- w_out: bfloat16 [1024, 1024], P('exp'), may hold values from -1.5 to 1.5
- w_gate: bfloat16 [32, 1024, 512], P('exp'), may hold values from -0.1875 to 0.1875
- w_up: bfloat16 [32, 1024, 512], P('exp'), may hold values from -0.1875 to 0.1875
- w_down: bfloat16 [32, 512, 1024], P('exp'), may hold values from -1 to 1
Outputs:
- layer_out: bfloat16 [8, 3072, 1024], P('exp', 'ctx')
- input_grad: float32 [8, 3072, 1024], P('exp', 'ctx')
- w_query_grad: float32 [1024, 1024], P('exp')
- w_key_grad: float32 [1024, 512], P('exp')
- w_value_grad: float32 [1024, 512], P('exp')
- w_out_grad: float32 [1024, 1024], P('exp')
- norm_attn_grad: float32 [1024], P('exp')
- norm_query_grad: float32 [1024], P('exp')
- norm_key_grad: float32 [512], P('exp')
- norm_ffn_grad: float32 [1024], P('exp')
- w_gate_grad: float32 [32, 1024, 512], P('exp', 'ctx')
- w_up_grad: float32 [32, 1024, 512], P('exp', 'ctx')
- w_down_grad: float32 [32, 512, 1024], P('exp', 'ctx')
The draws below stay inside these ranges and needn't reach their ends.
Inputs may be any that keep to these rules, and one draw needn't show every extreme that they name: Each group's 4 lengths sum to 3072; the longest is exactly 2048. Each deal_perm[g, j] is a permutation of the 16 indices. `routes`: A row names 8 different experts; among the 192 rows of one device no expert is named more than 72 times, a bound that some block reaches.
All inputs are finite; a program needn't handle non-finite values.
Results may differ from the reference program's by a relative error of at most 0.029.
Values may be sent and summed in bfloat16 or wider, within the bound.
A program may use at most 320 MiB of HBM per device.

```python
import math
import jax
import jax.numpy as jnp
import numpy as np
from jax import lax

D = 1024
HEADS = 16
KV_HEADS = 8
HD = 64
FF = 512
TOPK = 8
TOK_DEV = 192
NSEQ = 4
GROUPS = 8
GROUP_TOK = 3072
SUB = 12
KVW = 512
EXPERTS = 32
LONGEST = 2048
CAP = 72
N_CTX = 16


def draw_tokens(key, part):
    key = jax.random.fold_in(key, 7)
    base_key, row_key, column_key = jax.random.split(key, 3)
    full_shape = (GROUPS, GROUP_TOK, D)
    row_scale = jnp.exp(jax.random.uniform(row_key, (GROUPS, GROUP_TOK, 1), jnp.float32, -1.15, 1.15))
    column_scale = jnp.exp(jax.random.uniform(column_key, (1, 1, D), jnp.float32, -1.15, 1.15))
    values = jnp.clip(jax.random.normal(base_key, full_shape, jnp.float32), -4.0, 4.0) * row_scale * column_scale
    return values.astype(jnp.bfloat16)


def shard_levels(key, extent, pieces, low, top_value):
    def one(dim, parts):
        draws = jax.random.uniform(jax.random.fold_in(jax.random.fold_in(key, 6), dim), (parts,), jnp.float32, low / len(pieces), top_value / len(pieces))
        return jnp.repeat(jnp.exp(draws), extent[dim] // parts).reshape((-1,) + (1,) * (len(extent) - dim - 1))

    loudness = one(*pieces[0])
    for cut in pieces[1:]:
        loudness = loudness * one(*cut)
    return loudness


def length_profile(amount, total, bound, lean):
    loads = [(1 << 20) // math.isqrt(grade ** lean) + 1 for grade in range(2, amount + 1)]
    rest, counts = total - bound - (amount - 1), [1] * (amount - 1)
    while rest > 0:
        candidates = [i for i in range(amount - 1) if counts[i] < bound]
        pool, budget = sum([loads[i] for i in candidates]), rest
        for i in candidates:
            addition = min(bound - counts[i], max(1, budget * loads[i] // pool), rest)
            counts[i] = counts[i] + addition
            rest = rest - addition
    return np.array([bound] + counts)


def uneven(stream_key, amount, total, reach, slope):
    if amount == 2:
        one = jax.random.randint(stream_key, (), max(1, total - reach), min(reach, total - 1) + 1)
        return jnp.stack([one, total - one])
    sizes = jnp.asarray(length_profile(amount, total, reach, slope), jnp.int32)
    couples = (amount - 1) // 2
    giver, sink = sizes[1:1 + 2 * couples:2], sizes[2:2 + 2 * couples:2]
    margin = jnp.minimum(giver - 1, reach - sink)
    shifted = jax.random.randint(jax.random.fold_in(stream_key, 1), (couples,), 0, 1 << 20) % (margin + 1)
    sizes = sizes.at[1:1 + 2 * couples:2].set(giver - shifted).at[2:2 + 2 * couples:2].set(sink + shifted)
    return sizes[jax.random.permutation(jax.random.fold_in(stream_key, 2), amount)]


def shared_out(key, own, number, rows, count, top, most, lean):
    sequence = jax.random.permutation(key, count)
    packed, usual = shares(count, rows * top, most, lean, True), shares(count, rows * top, most, lean, False)
    places = jnp.arange(count)

    def named(sizes, turn):
        used = int((sizes > 0).sum())
        fixed = max(1, used // 4)
        shifted = fixed + (places - fixed + turn * (used - fixed)) % max(1, count - fixed)
        return jnp.zeros((count,), jnp.int32).at[sequence[jnp.where(places < fixed, places, shifted)]].set(jnp.asarray(sizes, jnp.int32))

    sizes = jnp.where(number % 4 == 0, named(packed, number // 4), named(usual, number - number // 4 - 1))
    mixed = jax.random.permutation(jax.random.fold_in(own, 3), count)
    giver, sink = mixed[0:count // 2 * 2:2], mixed[1:count // 2 * 2:2]
    slack = jnp.minimum(sizes[giver] - 1, most - sizes[sink]) // 2
    slack = jnp.where((giver == sequence[0]) | (sink == sequence[0]) | (sizes[sink] == 0), 0, jnp.maximum(slack, 0))
    shifted = jax.random.randint(jax.random.fold_in(own, 4), (count // 2,), 0, 1 << 20) % (slack + 1)
    sizes = sizes.at[giver].add(-shifted).at[sink].add(shifted)
    labels = jnp.searchsorted(jnp.cumsum(sizes), jnp.arange(rows * top), side="right").astype(jnp.int32)
    grid = labels.reshape(top, rows).T
    grid = grid[jax.random.permutation(jax.random.fold_in(own, 1), rows)]
    turn = jax.random.randint(jax.random.fold_in(own, 2), (rows, 1), 0, top)
    return jnp.take_along_axis(grid, (jnp.arange(top)[None, :] + turn) % top, axis=1)


def shares(count, total, limit, slope, full):
    portions = [(1 << 20) // math.isqrt(standing ** slope) + 1 for standing in range(1, count + 1)]
    largest = limit if full else min(limit, max(-(-total // count), total * portions[0] // sum(portions)))
    least = 1 if total - largest >= count - 1 else 0
    counts, spare = [largest] + [least] * (count - 1), total - largest - least * (count - 1)
    while spare > 0:
        movable = [i for i in range(1, count) if counts[i] < largest] or [i for i in range(1, count) if counts[i] < limit]
        pool, left = sum([portions[i] for i in movable]), spare
        for i in movable:
            extra = min(limit - counts[i], max(1, left * portions[i] // pool), spare)
            counts[i] = counts[i] + extra
            spare = spare - extra
    return np.array(counts)


def noise(own_key, dims, deviation, reach, pieces=(), kind=jnp.bfloat16):
    level = shard_levels(own_key, dims, pieces, -0.22, 0.18) if pieces else 1.0
    values = jax.random.normal(own_key, dims, jnp.float32) * deviation * level
    return jnp.minimum(jnp.maximum(values, -reach), reach).astype(kind)


def setup_inputs(seed: int = 0) -> dict:
    streams_of = jax.random.split(jax.random.key(seed), 18)
    tokens = draw_tokens(jax.random.fold_in(streams_of[17], 71), 0)
    cotangent = noise(streams_of[1], (GROUPS, GROUP_TOK, D), 1.0, 6.0, ((0, 8), (1, 16)))
    lengths = jax.vmap(lambda own: uneven(own, NSEQ, GROUP_TOK, LONGEST, 2))(jax.random.split(streams_of[2], GROUPS)).reshape((GROUPS, NSEQ)).astype(jnp.int32)
    deal_perm = jax.vmap(lambda own: jax.random.permutation(own, N_CTX))(jax.random.split(streams_of[3], GROUPS * N_CTX)).reshape((GROUPS, N_CTX, N_CTX)).astype(jnp.int32)
    routes_keys = jax.random.split(jax.random.fold_in(streams_of[4], 1), GROUPS * GROUP_TOK // TOK_DEV)
    routes_turns = jax.random.permutation(jax.random.fold_in(streams_of[4], 3), GROUPS * GROUP_TOK // TOK_DEV)
    routes = jax.vmap(lambda own, number: shared_out(jax.random.fold_in(streams_of[4], 2), own, number, TOK_DEV, EXPERTS, TOPK, CAP, 1))(routes_keys, routes_turns).reshape((GROUPS, GROUP_TOK, TOPK))
    gate_logits = noise(streams_of[5], (GROUPS, GROUP_TOK, TOPK), 0.5, 2.5, ((0, 8), (1, 16)), jnp.float32)
    norm_attn = jnp.clip(1.0 + 0.15 * jax.random.normal(streams_of[6], (D,), jnp.float32), 0.25, 1.75).astype(jnp.bfloat16)
    norm_query = jnp.clip(1.0 + 0.15 * jax.random.normal(streams_of[7], (D,), jnp.float32), 0.25, 1.75).astype(jnp.bfloat16)
    norm_key = jnp.clip(1.0 + 0.15 * jax.random.normal(streams_of[8], (KVW,), jnp.float32), 0.25, 1.75).astype(jnp.bfloat16)
    norm_ffn = jnp.clip(1.0 + 0.15 * jax.random.normal(streams_of[9], (D,), jnp.float32), 0.25, 1.75).astype(jnp.bfloat16)
    w_query = noise(streams_of[10], (D, D), D ** -0.5, 0.1875, ((0, 8),))
    w_key = noise(streams_of[11], (D, KVW), D ** -0.5, 0.1875, ((0, 8),))
    w_value = noise(streams_of[12], (D, KVW), D ** -0.5, 0.1875, ((0, 8),))
    w_out = noise(streams_of[13], (D, D), (D // 64) ** -0.5, 1.5, ((0, 8),))
    w_gate = noise(streams_of[14], (EXPERTS, D, FF), D ** -0.5, 0.1875, ((0, 8),))
    w_up = noise(streams_of[15], (EXPERTS, D, FF), D ** -0.5, 0.1875, ((0, 8),))
    w_down = noise(streams_of[16], (EXPERTS, FF, D), (FF // 16) ** -0.5, 1.0, ((0, 8),))
    return dict(tokens=tokens, cotangent=cotangent, lengths=lengths, deal_perm=deal_perm, routes=routes, gate_logits=gate_logits, norm_attn=norm_attn, norm_query=norm_query, norm_key=norm_key, norm_ffn=norm_ffn, w_query=w_query, w_key=w_key, w_value=w_value, w_out=w_out, w_gate=w_gate, w_up=w_up, w_down=w_down)


EPSILON = 1e-05
ROPE_BASE = 10000.0
MASKED = -1e+30
HIGHEST = lax.Precision.HIGHEST

@jax.custom_vjp
def low(v):
    return lax.optimization_barrier(v.astype(jnp.bfloat16)).astype(jnp.float32)

@jax.custom_vjp
def low_back(v):
    return v

def low_keep(v):
    return (low(v), None)

def low_pass(kept, grad):
    return (grad,)

def back_keep(v):
    return (v, None)

def back_low(kept, grad):
    return (low(grad),)
low.defvjp(low_keep, low_pass)
low_back.defvjp(back_keep, back_low)

def rms_norm(values, norm_gain):
    return values * lax.rsqrt(lax.optimization_barrier(jnp.mean(values * values, axis=-1, keepdims=True)) + EPSILON) * norm_gain

def rotate(values, offsets, head_count, direction):
    row_total = values.shape[0]
    head_width = values.shape[1] // head_count
    half_width = head_width // 2
    shaped = values.reshape(row_total, head_count, head_width)
    inverse_freq = ROPE_BASE ** (-jnp.arange(half_width).astype(jnp.float32) * 2.0 / head_width)
    angles = offsets.astype(jnp.float32)[:, None] * inverse_freq[None, :]
    cosine = jnp.cos(angles)[:, None, :]
    sine_part = direction * jnp.sin(angles)[:, None, :]
    first_half = shaped[..., :half_width]
    second_half = shaped[..., half_width:]
    turned = jnp.concatenate([first_half * cosine - second_half * sine_part, second_half * cosine + first_half * sine_part], axis=-1)
    return turned.reshape(row_total, head_count * head_width)

def documents(positions, seq_lengths):
    seq_ends = jnp.cumsum(seq_lengths).astype(jnp.int32)
    seq_starts = seq_ends - seq_lengths
    doc_index = lax.optimization_barrier(jnp.sum((positions[:, None] >= seq_ends[None, :]).astype(jnp.int32), axis=1))
    inside = (positions[:, None] >= seq_starts[None, :]) & (positions[:, None] < seq_ends[None, :])
    offsets = positions - lax.optimization_barrier(jnp.sum(jnp.where(inside, seq_starts[None, :], 0), axis=1))
    return (doc_index.astype(jnp.int32), offsets.astype(jnp.int32))

def group_layer(weight_set, inputs):
    gain_attn, gain_query, gain_key, gain_ffn, w_query, w_key, w_value, w_out, w_gate, w_up, w_down = weight_set
    tokens, seq_lengths, deal_perm, routes, gate_logits = inputs
    positions = jnp.arange(GROUP_TOK, dtype=jnp.int32)
    source = positions // TOK_DEV
    piece_index = positions % TOK_DEV // SUB
    causal_pos = (source * N_CTX + deal_perm[source, piece_index]) * SUB + positions % SUB
    doc_index, offsets = documents(positions, seq_lengths)
    normed = low_back(low(rms_norm(tokens, gain_attn)))
    ordered = jnp.zeros_like(normed).at[causal_pos].set(normed)
    query_lin = low_back(jnp.dot(ordered, w_query, precision=HIGHEST))
    key_lin = low_back(jnp.dot(ordered, w_key, precision=HIGHEST))
    value_rows = low(low_back(jnp.dot(ordered, w_value, precision=HIGHEST)))
    query_rows = low(rotate(rms_norm(query_lin, gain_query), offsets, HEADS, 1.0))
    key_rows = low(rotate(rms_norm(key_lin, gain_key), offsets, KV_HEADS, 1.0))
    key_heads = key_rows.reshape(GROUP_TOK, KV_HEADS, HD)
    value_heads = value_rows.reshape(GROUP_TOK, KV_HEADS, HD)
    group_share = HEADS // KV_HEADS

    def attend(block_args):
        query_block, block_pos = block_args
        query_heads = query_block.reshape(TOK_DEV, KV_HEADS, group_share, HD)
        scores = jnp.einsum('qgsd,kgd->gsqk', query_heads, key_heads, precision=HIGHEST) * HD ** (-0.5)
        scores = low_back(scores)
        allowed = (doc_index[block_pos][:, None] == doc_index[None, :]) & (positions[None, :] <= block_pos[:, None])
        scores = jnp.where(allowed[None, None], scores, MASKED)
        log_total = jax.nn.logsumexp(scores, axis=-1, keepdims=True)
        probs = low(jnp.exp(scores - log_total))
        mixed = jnp.einsum('gsqk,kgd->qgsd', probs, value_heads, precision=HIGHEST)
        return mixed.reshape(TOK_DEV, D)
    attended = lax.map(jax.checkpoint(attend), (query_rows.reshape(N_CTX, TOK_DEV, D), positions.reshape(N_CTX, TOK_DEV)))
    attended = low_back(low(attended.reshape(GROUP_TOK, D)))
    branch_rows = low_back(low(jnp.dot(attended, w_out, precision=HIGHEST)))
    resid = tokens + branch_rows[causal_pos]
    ffn_in = low(rms_norm(resid, gain_ffn))
    flat_routes = routes.reshape(-1)
    choice_row = jnp.arange(GROUP_TOK * TOPK, dtype=jnp.int32) // TOPK
    block_id = choice_row // TOK_DEV
    onehot = (flat_routes[:, None] == jnp.arange(EXPERTS, dtype=jnp.int32)[None, :]).astype(jnp.int32)
    onehot = onehot.reshape(N_CTX, TOK_DEV * TOPK, EXPERTS)
    rank_in = lax.optimization_barrier(jnp.sum((jnp.cumsum(onehot, axis=1) - onehot) * onehot, axis=2)).reshape(-1)
    slot_index = flat_routes * (N_CTX * CAP) + block_id * CAP + rank_in
    filled = jnp.zeros((EXPERTS * N_CTX * CAP, D), jnp.float32).at[slot_index].set(ffn_in[choice_row])
    expert_in = low_back(filled).reshape(EXPERTS, N_CTX * CAP, D)
    pre_gate = low_back(jnp.einsum('emd,edf->emf', expert_in, w_gate, precision=HIGHEST))
    pre_up = low_back(jnp.einsum('emd,edf->emf', expert_in, w_up, precision=HIGHEST))
    act_rows = low(jax.nn.silu(pre_gate) * pre_up)
    expert_out = low_back(low(jnp.einsum('emf,efd->emd', act_rows, w_down, precision=HIGHEST)))
    picked = expert_out.reshape(EXPERTS * N_CTX * CAP, D)[slot_index].reshape(GROUP_TOK, TOPK, D)
    gates = jax.nn.softmax(gate_logits, axis=-1)
    return resid + lax.optimization_barrier(jnp.sum(gates[:, :, None] * picked, axis=1))

def reference(tokens, cotangent, lengths, deal_perm, routes, gate_logits, norm_attn, norm_query, norm_key, norm_ffn, w_query, w_key, w_value, w_out, w_gate, w_up, w_down):
    weight_set = tuple((entry_arr.astype(jnp.float32) for entry_arr in (norm_attn, norm_query, norm_key, norm_ffn, w_query, w_key, w_value, w_out, w_gate, w_up, w_down)))
    layer_in = tokens.astype(jnp.float32)

    def forward(weights_now, inputs_now):

        def one_group(group_args):
            return jax.checkpoint(group_layer)(weights_now, group_args)
        return lax.map(one_group, (inputs_now, lengths, deal_perm, routes, gate_logits))
    layer_out, pullback = jax.vjp(forward, weight_set, layer_in)
    weight_grads, input_grad = pullback(cotangent.astype(jnp.float32))
    attn_gain_grad, query_gain_grad, key_gain_grad, ffn_gain_grad, query_grad, key_grad, value_grad, out_grad, gate_grad, up_grad, down_grad = weight_grads
    return (layer_out.astype(jnp.bfloat16), input_grad, query_grad, key_grad, value_grad, out_grad, attn_gain_grad, query_gain_grad, key_gain_grad, ffn_gain_grad, gate_grad, up_grad, down_grad)
```

```python
import jax
import jax.numpy as jnp
from jax import lax
from jax.experimental import pallas as pl
from jax.experimental.pallas import tpu as pltpu
from jax.sharding import PartitionSpec as P

HEADS = 16
KV_HEADS = 8
EPSILON = 1e-05
ROPE_BASE = 10000.0
MASKED = -1e30

MESH = pl.DeviceIdType.MESH
CTX = 16
EXP = 8
CHIPS = 8
ROWS = 192
WIDTH = 1024
FF = 512
LOCAL = 4
CAP = 72
PAIRS = EXP // 2
PAIR_ROWS = 2 * ROWS
PAIR_CAP = 2 * CAP
SLOTS = EXP * CAP
PAIR_SLOTS = LOCAL * PAIR_CAP
KEYS = CTX * ROWS
CHUNK = 2 * ROWS
MIB = 1 << 20

ANY_SPEC = pl.BlockSpec(memory_space=pl.ANY)
F32 = jnp.float32
BF16 = jnp.bfloat16


def dot(a, b, dims=((1,), (0,))):
    return lax.dot_general(a, b, (dims, ((), ())), preferred_element_type=F32)


NT = ((1,), (1,))
TN = ((0,), (0,))


def comm_call(body, name, collective_id, outs, ins, copies):
    return pl.pallas_call(
        body,
        name=name,
        out_shape=outs,
        in_specs=[ANY_SPEC] * len(ins),
        out_specs=[ANY_SPEC] * len(outs),
        scratch_shapes=[
            pltpu.SemaphoreType.DMA((copies,)),
            pltpu.SemaphoreType.DMA((copies,)),
            pltpu.SemaphoreType.DMA((8,)),
        ],
        compiler_params=pltpu.CompilerParams(collective_id=collective_id, has_side_effects=True),
    )(*ins)


class Copier:
    def __init__(self, send_sem, recv_sem, local_sem):
        self.send_sem, self.recv_sem, self.local_sem = send_sem, recv_sem, local_sem
        self.remote, self.local = [], []

    def send(self, src, dst, axis, index):
        at = len(self.remote)
        copy = pltpu.make_async_remote_copy(
            src_ref=src,
            dst_ref=dst,
            send_sem=self.send_sem.at[at],
            recv_sem=self.recv_sem.at[at],
            device_id={axis: index},
            device_id_type=MESH,
        )
        copy.start()
        self.remote.append([copy, False])
        return at

    def keep(self, src, dst):
        copy = pltpu.make_async_copy(src, dst, self.local_sem.at[len(self.local)])
        copy.start()
        self.local.append(copy)

    def arrived(self, at):
        self.remote[at][0].wait_recv()
        self.remote[at][1] = True

    def finish(self):
        for copy, seen in self.remote:
            if not seen:
                copy.wait_recv()
        for copy, _ in self.remote:
            copy.wait_send()
        for copy in self.local:
            copy.wait()


def meet(partners):
    barrier = pltpu.get_barrier_semaphore()
    for axis, index in partners:
        pl.semaphore_signal(barrier, inc=1, device_id={axis: index}, device_id_type=MESH)
    pl.semaphore_wait(barrier, len(partners))


def place():
    ctx = lax.axis_index("ctx")
    core = lax.rem(ctx, 2)
    return ctx, ctx // 2, core, ctx + 1 - 2 * core


def exp_ring():
    me = lax.axis_index("exp")
    half, spot = me // 4, lax.rem(me, 4)
    right = half * 4 + lax.rem(spot + 1, 4)
    left = half * 4 + lax.rem(spot + 3, 4)
    over = (1 - half) * 4
    return (
        me,
        right,
        left,
        half * 4 + lax.rem(spot + 2, 4),
        over + spot,
        over + lax.rem(spot + 1, 4),
        over + lax.rem(spot + 3, 4),
        over + lax.rem(spot + 2, 4),
    )


def relay(copier, own, slot, rows, ring, forward):
    me, right, left, far, over, over_right, over_left, over_far = ring
    half = rows // 2
    low, high = pl.ds(0, half), pl.ds(half, half)
    to_over = copier.send(own, slot(me), "exp", over)
    to_right = copier.send(own, slot(me), "exp", right)
    to_left = copier.send(own, slot(me), "exp", left)
    copier.arrived(to_over)
    over_r = copier.send(slot(over), slot(over), "exp", right)
    over_l = copier.send(slot(over), slot(over), "exp", left)
    copier.arrived(to_right)
    far_r = copier.send(slot(left).at[low], slot(left).at[low], "exp", right)
    copier.arrived(to_left)
    far_l = copier.send(slot(right).at[high], slot(right).at[high], "exp", left)
    for partner in (over, left, right):
        forward(partner)
    copier.arrived(over_r)
    ofar_r = copier.send(slot(over_left).at[low], slot(over_left).at[low], "exp", right)
    copier.arrived(over_l)
    ofar_l = copier.send(slot(over_right).at[high], slot(over_right).at[high], "exp", left)
    forward(over_left)
    forward(over_right)
    copier.arrived(far_r)
    copier.arrived(far_l)
    forward(far)
    copier.arrived(ofar_r)
    copier.arrived(ofar_l)
    forward(over_far)


def gather_weights(shards, gains):
    def body(x_ref, g_ref, w_ref, go_ref, send_sem, recv_sem, local_sem):
        ring = exp_ring()
        me = ring[0]
        _, _, core, sibling = place()
        copier = Copier(send_sem, recv_sem, local_sem)
        meet([("exp", partner) for partner in ring[1:]] + [("ctx", sibling)])
        copier.keep(x_ref.at[0], w_ref.at[0, me])
        copier.keep(x_ref.at[1], w_ref.at[1, me])
        copier.keep(g_ref, go_ref.at[me])
        for partner in ring[1:]:
            copier.send(g_ref, go_ref.at[me], "exp", partner)
        relay(
            copier,
            x_ref.at[core],
            lambda s: w_ref.at[core, s],
            shards.shape[1],
            ring,
            lambda s: copier.send(w_ref.at[core, s], w_ref.at[core, s], "ctx", sibling),
        )
        copier.finish()

    return comm_call(
        body,
        "gather_weights",
        1,
        [
            jax.ShapeDtypeStruct((2, EXP) + shards.shape[1:], shards.dtype),
            jax.ShapeDtypeStruct((EXP,) + gains.shape, gains.dtype),
        ],
        [shards, gains],
        23,
    )


def gather_rows(rows):
    def body(x_ref, o_ref, send_sem, recv_sem, local_sem):
        ring = exp_ring()
        copier = Copier(send_sem, recv_sem, local_sem)
        meet([("exp", ring[1]), ("exp", ring[2]), ("exp", ring[4])])
        copier.keep(x_ref, o_ref.at[ring[0]])
        relay(copier, x_ref, lambda s: o_ref.at[s], rows.shape[0], ring, lambda s: None)
        copier.finish()

    return comm_call(
        body, "gather_rows", 2, [jax.ShapeDtypeStruct((EXP,) + rows.shape, rows.dtype)], [rows], 9
    )[0]


def spread_heads(q_send, kv_send, meta):
    def body(q_ref, kv_ref, m_ref, qo_ref, kvo_ref, mo_ref, send_sem, recv_sem, local_sem):
        _, chip, core, sibling = place()
        me = lax.axis_index("exp")
        chips = [lax.rem(chip + d, CHIPS) for d in range(1, CHIPS)]
        experts = [lax.rem(me + d, EXP) for d in range(1, EXP)]
        copier = Copier(send_sem, recv_sem, local_sem)
        meet([("ctx", 2 * p + core) for p in chips] + [("ctx", sibling)] + [("exp", p) for p in experts])
        own = 2 * chip + core
        first = [copier.send(kv_ref.at[p], kvo_ref.at[own], "ctx", 2 * p + core) for p in chips]
        copier.send(kv_ref.at[chip], kvo_ref.at[own], "ctx", sibling)
        for p in chips:
            copier.send(q_ref.at[p], qo_ref.at[chip], "ctx", 2 * p + core)
        for p in experts:
            copier.send(m_ref.at[p], mo_ref.at[me], "exp", p)
        copier.keep(q_ref.at[chip], qo_ref.at[chip])
        copier.keep(kv_ref.at[chip], kvo_ref.at[own])
        copier.keep(m_ref.at[me], mo_ref.at[me])
        for d, at in enumerate(first, 1):
            copier.arrived(at)
            source = 2 * lax.rem(chip + CHIPS - d, CHIPS) + core
            copier.send(kvo_ref.at[source], kvo_ref.at[source], "ctx", sibling)
        copier.finish()

    return comm_call(
        body,
        "spread_heads",
        3,
        [
            jax.ShapeDtypeStruct((CHIPS, ROWS, 128), BF16),
            jax.ShapeDtypeStruct((CTX, ROWS, 128), BF16),
            jax.ShapeDtypeStruct(meta.shape, F32),
        ],
        [q_send, kv_send, meta],
        29,
    )


def lanes(index):
    return pl.ds(pl.multiple_of(index * 128, 128), 128)


def collect_heads(blocks):
    def body(x_ref, o_ref, send_sem, recv_sem, local_sem):
        _, chip, core, _ = place()
        chips = [lax.rem(chip + d, CHIPS) for d in range(1, CHIPS)]
        copier = Copier(send_sem, recv_sem, local_sem)
        meet([("ctx", 2 * p + core) for p in chips])
        for p in chips:
            copier.send(x_ref.at[p], o_ref.at[:, lanes(chip)], "ctx", 2 * p + core)
        copier.keep(x_ref.at[chip], o_ref.at[:, lanes(chip)])
        copier.finish()

    return comm_call(
        body, "collect_heads", 4, [jax.ShapeDtypeStruct((ROWS, WIDTH), BF16)], [blocks], 7
    )[0]


def spread_grads(rows):
    def body(x_ref, o_ref, send_sem, recv_sem, local_sem):
        _, chip, core, _ = place()
        chips = [lax.rem(chip + d, CHIPS) for d in range(1, CHIPS)]
        copier = Copier(send_sem, recv_sem, local_sem)
        meet([("ctx", 2 * p + core) for p in chips])
        for p in chips:
            copier.send(x_ref.at[:, lanes(p)], o_ref.at[chip], "ctx", 2 * p + core)
        copier.keep(x_ref.at[:, lanes(chip)], o_ref.at[chip])
        copier.finish()

    return comm_call(
        body, "spread_grads", 5, [jax.ShapeDtypeStruct((CHIPS, ROWS, 128), BF16)], [rows], 7
    )[0]


def collect_grads(dq, dkv):
    def body(q_ref, kv_ref, qo_ref, kvo_ref, send_sem, recv_sem, local_sem):
        ctx, chip, core, _ = place()
        chips = [lax.rem(chip + d, CHIPS) for d in range(1, CHIPS)]
        others = [lax.rem(ctx + d, CTX) for d in range(1, CTX)]
        copier = Copier(send_sem, recv_sem, local_sem)
        meet([("ctx", p) for p in others])
        for p in others:
            copier.send(kv_ref.at[p], kvo_ref.at[core, :, lanes(chip)], "ctx", p)
        for p in chips:
            copier.send(q_ref.at[p], qo_ref.at[:, lanes(chip)], "ctx", 2 * p + core)
        copier.keep(q_ref.at[chip], qo_ref.at[:, lanes(chip)])
        copier.keep(kv_ref.at[ctx], kvo_ref.at[core, :, lanes(chip)])
        copier.finish()

    return comm_call(
        body,
        "collect_grads",
        6,
        [
            jax.ShapeDtypeStruct((ROWS, WIDTH), BF16),
            jax.ShapeDtypeStruct((2, ROWS, WIDTH), BF16),
        ],
        [dq, dkv],
        22,
    )


def swap_cores(grads):
    def body(x_ref, o_ref, send_sem, recv_sem, local_sem):
        _, _, core, sibling = place()
        copier = Copier(send_sem, recv_sem, local_sem)
        meet([("ctx", sibling)])
        copier.send(x_ref.at[:, 1 - core], o_ref, "ctx", sibling)
        copier.finish()

    shape = (grads.shape[0],) + grads.shape[2:]
    return comm_call(body, "swap_cores", 7, [jax.ShapeDtypeStruct(shape, BF16)], [grads], 1)[0]


def trade_exp(blocks, collective_id):
    def body(x_ref, o_ref, send_sem, recv_sem, local_sem):
        me = lax.axis_index("exp")
        others = [lax.rem(me + d, EXP) for d in range(1, EXP)]
        copier = Copier(send_sem, recv_sem, local_sem)
        meet([("exp", p) for p in others])
        for p in others:
            copier.send(x_ref.at[p], o_ref.at[me], "exp", p)
        copier.keep(x_ref.at[me], o_ref.at[me])
        copier.finish()

    return comm_call(
        body, "trade_exp", collective_id, [jax.ShapeDtypeStruct(blocks.shape, BF16)], [blocks], 7
    )[0]


def trade_chips(rows):
    def body(x_ref, o_ref, send_sem, recv_sem, local_sem):
        _, chip, core, _ = place()
        chips = [lax.rem(chip + d, CHIPS) for d in range(1, CHIPS)]
        copier = Copier(send_sem, recv_sem, local_sem)
        meet([("ctx", 2 * p + core) for p in chips])
        for p in chips:
            copier.send(x_ref.at[:, lanes(p)], o_ref.at[chip], "ctx", 2 * p + core)
        copier.keep(x_ref.at[:, lanes(chip)], o_ref.at[chip])
        copier.finish()

    return comm_call(
        body, "trade_chips", 9, [jax.ShapeDtypeStruct((CHIPS, rows.shape[0], 128), BF16)], [rows], 7
    )[0]


def share_all(part):
    def body(x_ref, o_ref, send_sem, recv_sem, local_sem):
        _, chip, core, sibling = place()
        chips = [lax.rem(chip + d, CHIPS) for d in range(1, CHIPS)]
        copier = Copier(send_sem, recv_sem, local_sem)
        meet([("ctx", 2 * p + core) for p in chips] + [("ctx", sibling)])
        mine = o_ref.at[core, :, lanes(chip)]
        first = [copier.send(x_ref, mine, "ctx", 2 * p + core) for p in chips]
        copier.send(x_ref, mine, "ctx", sibling)
        copier.keep(x_ref, mine)
        for d, at in enumerate(first, 1):
            copier.arrived(at)
            got = o_ref.at[core, :, lanes(lax.rem(chip + CHIPS - d, CHIPS))]
            copier.send(got, got, "ctx", sibling)
        copier.finish()

    return comm_call(
        body, "share_all", 10, [jax.ShapeDtypeStruct((2, part.shape[0], WIDTH), BF16)], [part], 15
    )[0]


def compute_call(body, name, outs, ins, vmem=48, cost=None, **kw):
    return pl.pallas_call(
        body,
        name=name,
        out_shape=outs,
        compiler_params=pltpu.CompilerParams(vmem_limit_bytes=vmem * MIB),
        **kw,
    )(*ins)


def turn(values, cosine, down, up):
    return values * cosine + pltpu.roll(values, 96, 1) * down + pltpu.roll(values, 32, 1) * up


def row_scale(total, width):
    return lax.rsqrt(total * (1.0 / width) + EPSILON)


def key_lanes():
    return lax.broadcasted_iota(jnp.int32, (1, 128), 1) < 64


def project(tokens, w_q, w_kv, gains, tables, routes_t, logits_t):
    def body(t_ref, wq_ref, wkv_ref, g_ref, tab_ref, r_ref, l_ref, n_ref, q_ref, kv_ref, qs_ref, kvs_ref, m_ref):
        x = t_ref[...].astype(F32)
        scale = row_scale(jnp.sum(x * x, axis=1, keepdims=True), WIDTH)
        normed = (x * scale * g_ref[0:1, :]).astype(BF16)
        n_ref[...] = normed
        q = dot(normed, wq_ref[...])
        kv = dot(normed, wkv_ref[...])
        q_ref[...] = q
        kv_ref[...] = kv
        q_scale = row_scale(jnp.sum(q * q, axis=1, keepdims=True), WIDTH)
        keys = key_lanes()
        total = jnp.zeros((ROWS, 128), F32)
        for c in range(CHIPS):
            piece = kv[:, c * 128 : (c + 1) * 128]
            total = total + jnp.where(keys, piece * piece, 0.0)
        k_scale = row_scale(jnp.sum(total, axis=1, keepdims=True), WIDTH // 2)
        kv_scale = jnp.where(keys, k_scale, 1.0)
        for c in range(CHIPS):
            at = slice(c * 128, (c + 1) * 128)
            qn = q[:, at] * q_scale * g_ref[1:2, at]
            qr = turn(qn, tab_ref[0], tab_ref[1], tab_ref[2])
            qs_ref[c] = (qr.astype(BF16).astype(F32) * 0.125).astype(BF16)
            kn = kv[:, at] * kv_scale * g_ref[2:3, at]
            kvs_ref[c] = turn(kn, tab_ref[3], tab_ref[4], tab_ref[5]).astype(BF16)
        logits = l_ref[...]
        raised = jnp.exp(logits - jnp.max(logits, axis=0, keepdims=True))
        gates = raised / jnp.sum(raised, axis=0, keepdims=True)
        experts = lax.broadcasted_iota(jnp.int32, (32, ROWS), 0)
        member = jnp.zeros((32, ROWS), F32)
        weight = jnp.zeros((32, ROWS), F32)
        for c in range(8):
            hit = r_ref[c : c + 1, :] == experts
            member = member + jnp.where(hit, 1.0, 0.0)
            weight = weight + jnp.where(hit, gates[c : c + 1, :], 0.0)
        before = lax.broadcasted_iota(jnp.int32, (ROWS, ROWS), 0) < lax.broadcasted_iota(
            jnp.int32, (ROWS, ROWS), 1
        )
        rank = dot(member.astype(BF16), jnp.where(before, 1.0, 0.0).astype(BF16))
        spot = jnp.where(member > 0.5, rank, -1.0)
        for e in range(EXP):
            m_ref[e, 0:4, :] = spot[e * 4 : e * 4 + 4, :]
            m_ref[e, 4:8, :] = weight[e * 4 : e * 4 + 4, :]

    return compute_call(
        body,
        "project",
        [
            jax.ShapeDtypeStruct((ROWS, WIDTH), BF16),
            jax.ShapeDtypeStruct((ROWS, WIDTH), F32),
            jax.ShapeDtypeStruct((ROWS, WIDTH), F32),
            jax.ShapeDtypeStruct((CHIPS, ROWS, 128), BF16),
            jax.ShapeDtypeStruct((CHIPS, ROWS, 128), BF16),
            jax.ShapeDtypeStruct((EXP, 8, ROWS), F32),
        ],
        [tokens, w_q, w_kv, gains, tables, routes_t, logits_t],
    )


def split_kv(kv_ref, klo, khi, vlo, vhi):
    low = key_lanes()
    both = kv_ref[...].astype(F32)
    other = pltpu.roll(both, 64, 1)
    if klo is not None:
        klo[...] = jnp.where(low, both, 0.0).astype(BF16)
        khi[...] = jnp.where(low, 0.0, other).astype(BF16)
    vlo[...] = jnp.where(low, other, 0.0).astype(BF16)
    vhi[...] = jnp.where(low, 0.0, both).astype(BF16)


def attend(q, kv, key_pos, query_pos, query_start, first_chunk):
    def body(first_ref, q_ref, kv_ref, kp_ref, qp_ref, qb_ref, o_ref, of_ref, l_ref, klo, khi, vlo, vhi):
        i = pl.program_id(0)

        @pl.when(i == 0)
        def _():
            split_kv(kv_ref, klo, khi, vlo, vhi)

        q_block = q_ref[0]
        at_row, start_row = qp_ref[0], qb_ref[0]
        low = key_lanes()

        def step(p, carry):
            m0, m1, l0, l1, acc = carry
            rows = pl.ds(pl.multiple_of(p * CHUNK, CHUNK), CHUNK)
            at_key = kp_ref[p]
            seen = (at_key >= start_row) & (at_key <= at_row)
            s0 = jnp.where(seen, dot(q_block, klo[rows, :], NT), MASKED)
            s1 = jnp.where(seen, dot(q_block, khi[rows, :], NT), MASKED)
            n0 = jnp.maximum(m0, jnp.max(s0, axis=1, keepdims=True))
            n1 = jnp.maximum(m1, jnp.max(s1, axis=1, keepdims=True))
            p0 = jnp.exp(s0 - n0)
            p1 = jnp.exp(s1 - n1)
            a0 = jnp.exp(m0 - n0)
            a1 = jnp.exp(m1 - n1)
            l0 = l0 * a0 + jnp.sum(p0, axis=1, keepdims=True)
            l1 = l1 * a1 + jnp.sum(p1, axis=1, keepdims=True)
            acc = acc * jnp.where(low, a0, a1)
            acc = acc + dot(p0.astype(BF16), vlo[rows, :]) + dot(p1.astype(BF16), vhi[rows, :])
            return n0, n1, l0, l1, acc

        top = jnp.full((ROWS, 1), MASKED, F32)
        none = jnp.zeros((ROWS, 1), F32)
        m0, m1, l0, l1, acc = lax.fori_loop(
            first_ref[i], i + 1, step, (top, top, none, none, jnp.zeros((ROWS, 128), F32))
        )
        out = acc / jnp.where(low, l0, l1)
        of_ref[0] = out
        o_ref[0] = out.astype(BF16)
        l_ref[0] = jnp.where(low, m0 + jnp.log(l0), m1 + jnp.log(l1))

    def block(*shape):
        return pl.BlockSpec((1,) + shape, lambda i, first: (i, 0, 0))

    return pl.pallas_call(
        body,
        name="attend",
        out_shape=[
            jax.ShapeDtypeStruct((CHIPS, ROWS, 128), BF16),
            jax.ShapeDtypeStruct((CHIPS, ROWS, 128), F32),
            jax.ShapeDtypeStruct((CHIPS, ROWS, 128), F32),
        ],
        grid_spec=pltpu.PrefetchScalarGridSpec(
            num_scalar_prefetch=1,
            grid=(CHIPS,),
            in_specs=[
                block(ROWS, 128),
                pl.BlockSpec((KEYS, 128), lambda i, first: (0, 0)),
                pl.BlockSpec((CHIPS, 1, CHUNK), lambda i, first: (0, 0, 0)),
                block(ROWS, 1),
                block(ROWS, 1),
            ],
            out_specs=[block(ROWS, 128)] * 3,
            scratch_shapes=[pltpu.VMEM((KEYS, 128), BF16)] * 4,
        ),
        compiler_params=pltpu.CompilerParams(vmem_limit_bytes=48 * MIB),
    )(first_chunk, q, kv, key_pos, query_pos, query_start)


def attend_back(q, kv, d_out, out, log_total, key_pos, query_pos, query_start, first_chunk):
    def body(
        first_ref, q_ref, kv_ref, do_ref, o_ref, l_ref, kp_ref, qp_ref, qb_ref, dq_ref, dkv_ref, klo, khi, vlo, vhi, acc
    ):
        i = pl.program_id(0)

        @pl.when(i == 0)
        def _():
            split_kv(kv_ref, klo, khi, vlo, vhi)
            acc[...] = jnp.zeros_like(acc)

        low = key_lanes()
        q_block, do_block = q_ref[0], do_ref[0]
        do_wide, q_wide = do_block.astype(F32), q_block.astype(F32)
        q_turned, do_turned = pltpu.roll(q_wide, 64, 1), pltpu.roll(do_wide, 64, 1)
        right = jnp.concatenate(
            [
                jnp.where(low, q_wide, 0.0).astype(BF16),
                jnp.where(low, q_turned, 0.0).astype(BF16),
                jnp.where(low, 0.0, do_turned).astype(BF16),
                jnp.where(low, 0.0, do_wide).astype(BF16),
            ],
            axis=0,
        )
        row_id = lax.broadcasted_iota(jnp.int32, (8, 128), 0)
        lane_id = lax.broadcasted_iota(jnp.int32, (8, 128), 1)
        halves = jnp.where(lane_id // 64 == row_id, 1.0, 0.0)
        picks = jnp.where(lane_id == 64 * row_id, 1.0, 0.0)

        def across(select, values):
            return lax.dot_general(
                select, values, (NT, ((), ())), precision=lax.Precision.HIGHEST, preferred_element_type=F32
            )

        delta = across(halves, do_wide * o_ref[0])
        total = across(picks, l_ref[0])
        at_row, start_row = qp_ref[0], qb_ref[0]

        def step(p, dq):
            rows = pl.ds(pl.multiple_of(p * CHUNK, CHUNK), CHUNK)
            at_key = kp_ref[p]
            seen = (at_key >= start_row) & (at_key <= at_row)
            k0, k1 = klo[rows, :], khi[rows, :]
            s0 = jnp.where(seen, dot(k0, q_block, NT), MASKED)
            s1 = jnp.where(seen, dot(k1, q_block, NT), MASKED)
            p0 = jnp.exp(s0 - total[0:1, :])
            p1 = jnp.exp(s1 - total[1:2, :])
            d0 = (p0 * (dot(vlo[rows, :], do_block, NT) - delta[0:1, :])).astype(BF16)
            d1 = (p1 * (dot(vhi[rows, :], do_block, NT) - delta[1:2, :])).astype(BF16)
            left = jnp.concatenate([d0, d1, p0.astype(BF16), p1.astype(BF16)], axis=1)
            acc[rows, :] += dot(left, right)
            return dq + dot(d0, k0, TN) + dot(d1, k1, TN)

        dq = lax.fori_loop(first_ref[i], i + 1, step, jnp.zeros((ROWS, 128), F32))
        dq_ref[0] = (dq * 0.125).astype(BF16)

        @pl.when(i == CHIPS - 1)
        def _():
            dkv_ref[...] = acc[...].astype(BF16)

    def block(*shape):
        return pl.BlockSpec((1,) + shape, lambda i, first: (i, 0, 0))

    whole = pl.BlockSpec((KEYS, 128), lambda i, first: (0, 0))
    return pl.pallas_call(
        body,
        name="attend_back",
        out_shape=[
            jax.ShapeDtypeStruct((CHIPS, ROWS, 128), BF16),
            jax.ShapeDtypeStruct((KEYS, 128), BF16),
        ],
        grid_spec=pltpu.PrefetchScalarGridSpec(
            num_scalar_prefetch=1,
            grid=(CHIPS,),
            in_specs=[
                block(ROWS, 128),
                whole,
                block(ROWS, 128),
                block(ROWS, 128),
                block(ROWS, 128),
                pl.BlockSpec((CHIPS, CHUNK, 1), lambda i, first: (0, 0, 0)),
                block(1, ROWS),
                block(1, ROWS),
            ],
            out_specs=[block(ROWS, 128), whole],
            scratch_shapes=[pltpu.VMEM((KEYS, 128), BF16)] * 4 + [pltpu.VMEM((KEYS, 128), F32)],
        ),
        compiler_params=pltpu.CompilerParams(vmem_limit_bytes=48 * MIB),
    )(first_chunk, q, kv, d_out, out, log_total, key_pos, query_pos, query_start)


def finish_attention(attended, w_out, tokens, gains):
    def body(a_ref, w_ref, t_ref, g_ref, r_ref, f_ref):
        branch = dot(a_ref[...], w_ref[...]).astype(BF16).astype(F32)
        resid = t_ref[...].astype(F32) + branch
        r_ref[...] = resid
        scale = row_scale(jnp.sum(resid * resid, axis=1, keepdims=True), WIDTH)
        f_ref[...] = (resid * scale * g_ref[3:4, :]).astype(BF16)

    return compute_call(
        body,
        "finish_attention",
        [jax.ShapeDtypeStruct((ROWS, WIDTH), F32), jax.ShapeDtypeStruct((ROWS, WIDTH), BF16)],
        [attended, w_out, tokens, gains],
    )


def experts(rows, grads, meta, meta_t, w_gate, w_up, w_down):
    half = SLOTS // 2

    def body(
        x_ref, g_ref, m_ref, mt_ref, wg_ref, wu_ref, wd_ref,
        xin_ref, dr_ref, act_ref, dg_ref, du_ref, out_ref, dx_ref,
        made, back, weight,
    ):
        e = pl.program_id(0)

        @pl.when(e == 0)
        def _():
            slot_id = lax.broadcasted_iota(jnp.int32, (PAIR_CAP, PAIR_ROWS), 0).astype(F32)

            def pick(p, _):
                meta_p = m_ref[p]
                parts, gates = [], []
                for k in range(LOCAL):
                    hit = slot_id == meta_p[k : k + 1, :]
                    parts.append(jnp.where(hit, 1.0, 0.0).astype(BF16))
                    gates.append(
                        jnp.sum(jnp.where(hit, meta_p[4 + k : 5 + k, :], 0.0), axis=1, keepdims=True)
                    )
                chosen = jnp.concatenate(parts, axis=0)
                rows_p = dot(chosen, x_ref[p]).astype(BF16)
                grads_p = dot(chosen, g_ref[p])
                at = pl.ds(pl.multiple_of(p * PAIR_CAP, PAIR_CAP), PAIR_CAP)
                for k in range(LOCAL):
                    piece = slice(k * PAIR_CAP, (k + 1) * PAIR_CAP)
                    xin_ref[k, at, :] = rows_p[piece]
                    dr_ref[k, at, :] = (grads_p[piece] * gates[k]).astype(BF16)
                    weight[k, at, :] = gates[k]
                return 0

            lax.fori_loop(0, PAIRS, pick, 0)

        def work(h, _):
            at = pl.ds(pl.multiple_of(h * half, half), half)
            x = xin_ref[e, at, :]
            dr = dr_ref[e, at, :]
            gate = dot(x, wg_ref[0])
            up = dot(x, wu_ref[0])
            sig = jax.nn.sigmoid(gate)
            silu = gate * sig
            act = (silu * up).astype(BF16)
            act_ref[0, at, :] = act
            d_act = dot(dr, wd_ref[0], NT)
            d_gate = (d_act * up * sig * (1.0 + gate * (1.0 - sig))).astype(BF16)
            d_up = (d_act * silu).astype(BF16)
            dg_ref[0, at, :] = d_gate
            du_ref[0, at, :] = d_up
            y = (dot(act, wd_ref[0]) * weight[e, at, :]).astype(BF16)
            dch = (dot(d_gate, wg_ref[0], NT) + dot(d_up, wu_ref[0], NT)).astype(BF16)
            place_at = pl.ds(pl.multiple_of(e * PAIR_CAP, PAIR_CAP), PAIR_CAP)
            for k in range(2):
                piece = slice(k * PAIR_CAP, (k + 1) * PAIR_CAP)
                made[2 * h + k, place_at, :] = y[piece]
                back[2 * h + k, place_at, :] = dch[piece]
            return 0

        lax.fori_loop(0, 2, work, 0)

        @pl.when(e == LOCAL - 1)
        def _():
            lane_id = lax.broadcasted_iota(jnp.int32, (PAIR_ROWS, PAIR_SLOTS), 1).astype(F32)

            def give(p, _):
                meta_p = mt_ref[p]
                chosen = jnp.zeros((PAIR_ROWS, PAIR_SLOTS), F32)
                for k in range(LOCAL):
                    spot = meta_p[:, k : k + 1]
                    lane = jnp.where(spot < 0.0, -1.0, spot + float(k * PAIR_CAP))
                    chosen = chosen + jnp.where(lane_id == lane, 1.0, 0.0)
                chosen = chosen.astype(BF16)
                dx_ref[p] = dot(chosen, back[p]).astype(BF16)
                out_ref[p] = dot(chosen, made[p]).astype(BF16)
                return 0

            lax.fori_loop(0, PAIRS, give, 0)

    def fixed(*shape):
        return pl.BlockSpec(shape, lambda e: (0,) * len(shape), pipeline_mode=pl.Buffered(1))

    def each(*shape):
        return pl.BlockSpec((1,) + shape, lambda e: (e, 0, 0))

    return compute_call(
        body,
        "experts",
        [
            jax.ShapeDtypeStruct((LOCAL, SLOTS, WIDTH), BF16),
            jax.ShapeDtypeStruct((LOCAL, SLOTS, WIDTH), BF16),
            jax.ShapeDtypeStruct((LOCAL, SLOTS, FF), BF16),
            jax.ShapeDtypeStruct((LOCAL, SLOTS, FF), BF16),
            jax.ShapeDtypeStruct((LOCAL, SLOTS, FF), BF16),
            jax.ShapeDtypeStruct((PAIRS, PAIR_ROWS, WIDTH), BF16),
            jax.ShapeDtypeStruct((PAIRS, PAIR_ROWS, WIDTH), BF16),
        ],
        [rows, grads, meta, meta_t, w_gate, w_up, w_down],
        vmem=60,
        grid=(LOCAL,),
        in_specs=[
            fixed(PAIRS, PAIR_ROWS, WIDTH),
            fixed(PAIRS, PAIR_ROWS, WIDTH),
            fixed(PAIRS, 8, PAIR_ROWS),
            fixed(PAIRS, PAIR_ROWS, 8),
            each(WIDTH, FF),
            each(WIDTH, FF),
            each(FF, WIDTH),
        ],
        out_specs=[
            fixed(LOCAL, SLOTS, WIDTH),
            fixed(LOCAL, SLOTS, WIDTH),
            each(SLOTS, FF),
            each(SLOTS, FF),
            each(SLOTS, FF),
            fixed(PAIRS, PAIR_ROWS, WIDTH),
            fixed(PAIRS, PAIR_ROWS, WIDTH),
        ],
        scratch_shapes=[
            pltpu.VMEM((PAIRS, PAIR_SLOTS, WIDTH), BF16),
            pltpu.VMEM((PAIRS, PAIR_SLOTS, WIDTH), BF16),
            pltpu.VMEM((LOCAL, SLOTS, 1), F32),
        ],
    )


def expert_grads(rows, d_rows, act, d_gate, d_up):
    def body(x_ref, dr_ref, a_ref, dg_ref, du_ref, gg_ref, gu_ref, gd_ref):
        def wide(r, _):
            x = x_ref[0, :, pl.ds(pl.multiple_of(r * 256, 256), 256)]
            for d_ref, o_ref in ((dg_ref, gg_ref), (du_ref, gu_ref)):
                grad = dot(x, d_ref[0], TN).astype(BF16)
                for k in range(4):
                    o_ref[k % 2, 2 * r + k // 2, 0] = grad[k * 64 : (k + 1) * 64]
            return 0

        lax.fori_loop(0, 4, wide, 0)

        def tall(r, _):
            a = a_ref[0, :, pl.ds(pl.multiple_of(r * 256, 256), 256)]
            grad = dot(a, dr_ref[0], TN).astype(BF16)
            for k in range(8):
                gd_ref[k % 2, 4 * r + k // 2, 0] = grad[k * 32 : (k + 1) * 32]
            return 0

        lax.fori_loop(0, 2, tall, 0)

    def each(*shape):
        return pl.BlockSpec((1,) + shape, lambda e: (e, 0, 0))

    def cut(*shape):
        return pl.BlockSpec((2, CHIPS, 1) + shape, lambda e: (0, 0, e, 0, 0))

    return compute_call(
        body,
        "expert_grads",
        [
            jax.ShapeDtypeStruct((2, CHIPS, LOCAL, 64, FF), BF16),
            jax.ShapeDtypeStruct((2, CHIPS, LOCAL, 64, FF), BF16),
            jax.ShapeDtypeStruct((2, CHIPS, LOCAL, 32, WIDTH), BF16),
        ],
        [rows, d_rows, act, d_gate, d_up],
        grid=(LOCAL,),
        in_specs=[each(SLOTS, WIDTH), each(SLOTS, WIDTH)] + [each(SLOTS, FF)] * 3,
        out_specs=[cut(64, FF), cut(64, FF), cut(32, WIDTH)],
    )


def norm_back(values, total_squares, width, weighted, mask=None):
    scale = row_scale(total_squares, width)
    inner = jnp.sum(weighted * values, axis=1, keepdims=True) * (1.0 / width)
    return scale * weighted - values * (scale * scale * scale) * inner, scale


def back_to_branch(d_parts, resid, cotangent, gains, w_out):
    def body(p_ref, r_ref, c_ref, g_ref, w_ref, dr_ref, db_ref, da_ref, gg_ref):
        incoming = p_ref[0].astype(F32)
        for s in range(1, EXP):
            incoming = incoming + p_ref[s].astype(F32)
        resid_v = r_ref[...]
        squares = jnp.sum(resid_v * resid_v, axis=1, keepdims=True)
        d_norm, scale = norm_back(resid_v, squares, WIDTH, incoming * g_ref[3:4, :])
        gg_ref[...] = jnp.sum(incoming * resid_v * scale, axis=0, keepdims=True)
        d_resid = c_ref[...].astype(F32) + d_norm
        dr_ref[...] = d_resid
        d_branch = d_resid.astype(BF16)
        db_ref[...] = d_branch
        da_ref[...] = dot(d_branch, w_ref[...], NT).astype(BF16)

    return compute_call(
        body,
        "back_to_branch",
        [
            jax.ShapeDtypeStruct((ROWS, WIDTH), F32),
            jax.ShapeDtypeStruct((ROWS, WIDTH), BF16),
            jax.ShapeDtypeStruct((ROWS, WIDTH), BF16),
            jax.ShapeDtypeStruct((1, WIDTH), F32),
        ],
        [d_parts, resid, cotangent, gains, w_out],
    )


def back_to_input(dq, dkv, q_lin, kv_lin, tokens, d_resid, w_q, w_kv, gains, tables):
    def body(
        dq_ref, dkv_ref, q_ref, kv_ref, t_ref, r_ref, wq_ref, wkv_ref, g_ref, tab_ref,
        dql_ref, dkl_ref, di_ref, gg_ref, e_q, e_kv,
    ):
        keys = key_lanes()
        sums = [jnp.zeros((ROWS, 128), F32) for _ in range(4)]
        for c in range(CHIPS):
            at = slice(c * 128, (c + 1) * 128)
            q = q_ref[:, at]
            e = turn(dq_ref[:, at].astype(F32), tab_ref[0], -tab_ref[1], -tab_ref[2])
            e_q[:, at] = e
            sums[0] = sums[0] + q * q
            sums[1] = sums[1] + e * q * g_ref[1:2, at]
            kv = kv_ref[:, at]
            both = dkv_ref[0, :, at].astype(F32) + dkv_ref[1, :, at].astype(F32)
            e = turn(both, tab_ref[3], -tab_ref[4], -tab_ref[5])
            e_kv[:, at] = e
            sums[2] = sums[2] + jnp.where(keys, kv * kv, 0.0)
            sums[3] = sums[3] + jnp.where(keys, e * kv * g_ref[2:3, at], 0.0)
        qq, qe, kk, ke = [jnp.sum(s, axis=1, keepdims=True) for s in sums]
        q_scale, k_scale = row_scale(qq, WIDTH), row_scale(kk, WIDTH // 2)
        q_cut = q_scale * q_scale * q_scale * qe * (1.0 / WIDTH)
        k_cut = k_scale * k_scale * k_scale * ke * (2.0 / WIDTH)
        k_cut = jnp.where(keys, k_cut, 0.0)
        kv_scale = jnp.where(keys, k_scale, 1.0)
        for c in range(CHIPS):
            at = slice(c * 128, (c + 1) * 128)
            q, e = q_ref[:, at], e_q[:, at]
            gg_ref[1:2, at] = jnp.sum(e * q * q_scale, axis=0, keepdims=True)
            dql_ref[:, at] = (q_scale * (e * g_ref[1:2, at]) - q * q_cut).astype(BF16)
            kv, e = kv_ref[:, at], e_kv[:, at]
            gg_ref[2:3, at] = jnp.sum(e * kv * kv_scale, axis=0, keepdims=True)
            dkl_ref[:, at] = (kv_scale * (e * g_ref[2:3, at]) - kv * k_cut).astype(BF16)
        d_normed = dot(dql_ref[...], wq_ref[...], NT) + dot(dkl_ref[...], wkv_ref[...], NT)
        d_normed = d_normed.astype(BF16).astype(F32)
        x = t_ref[...].astype(F32)
        squares = jnp.sum(x * x, axis=1, keepdims=True)
        d_norm, scale = norm_back(x, squares, WIDTH, d_normed * g_ref[0:1, :])
        gg_ref[0:1, :] = jnp.sum(d_normed * x * scale, axis=0, keepdims=True)
        di_ref[...] = r_ref[...] + d_norm

    return compute_call(
        body,
        "back_to_input",
        [
            jax.ShapeDtypeStruct((ROWS, WIDTH), BF16),
            jax.ShapeDtypeStruct((ROWS, WIDTH), BF16),
            jax.ShapeDtypeStruct((ROWS, WIDTH), F32),
            jax.ShapeDtypeStruct((3, WIDTH), F32),
        ],
        [dq, dkv, q_lin, kv_lin, tokens, d_resid, w_q, w_kv, gains, tables],
        scratch_shapes=[pltpu.VMEM((ROWS, WIDTH), F32)] * 2,
    )


def dense_grads(normed, d_q, d_kv, attended, d_branch, gain_rows):
    def body(n_ref, dq_ref, dkv_ref, a_ref, db_ref, g_ref, o_ref):
        def part(r, _):
            at = pl.ds(pl.multiple_of(r * 256, 256), 256)
            n, a = n_ref[:, at], a_ref[:, at]
            for w, (left, right) in enumerate(((n, dq_ref), (n, dkv_ref), (a, db_ref))):
                grad = dot(left, right[...], TN).astype(BF16)
                for k in range(4):
                    o_ref[2 * r + k // 2, k % 2, w * 64 : (w + 1) * 64, :] = grad[k * 64 : (k + 1) * 64]
            return 0

        lax.fori_loop(0, 4, part, 0)
        for e in range(EXP):
            o_ref[e, 0, 192:208, :] = g_ref[e]
            o_ref[e, 1, 192:208, :] = jnp.zeros((16, WIDTH), BF16)

    return compute_call(
        body,
        "dense_grads",
        [jax.ShapeDtypeStruct((EXP, 2, 208, WIDTH), BF16)],
        [normed, d_q, d_kv, attended, d_branch, gain_rows],
    )[0]


def sum_blocks(blocks):
    return jnp.sum(blocks.astype(F32), axis=0)


def per_device(
    tokens,
    cotangent,
    lengths,
    deal_perm,
    routes,
    gate_logits,
    norm_attn,
    norm_query,
    norm_key,
    norm_ffn,
    w_query,
    w_key,
    w_value,
    w_out,
    w_gate,
    w_up,
    w_down,
):
    ctx_index = lax.axis_index("ctx")
    core = lax.rem(ctx_index, 2)
    tokens, cotangent = tokens[0], cotangent[0]

    pieces = jnp.arange(CTX, dtype=jnp.int32)[:, None] * CTX + deal_perm[0]
    positions = (pieces[:, :, None] * 12 + jnp.arange(12, dtype=jnp.int32)).reshape(CTX, ROWS)
    ends = jnp.cumsum(lengths[0])
    starts = ends - lengths[0]
    inside = positions[:, :, None] >= starts
    row_start = jnp.max(jnp.where(inside, starts, 0), axis=2)
    own = lambda a: lax.dynamic_index_in_dim(a, ctx_index, 0, keepdims=False)
    offsets = own(positions - row_start).astype(F32)
    inverse_freq = ROPE_BASE ** (-jnp.arange(32).astype(F32) * 2.0 / 64)
    angles = offsets[:, None] * inverse_freq[None, :]
    cosine, sine = jnp.cos(angles), jnp.sin(angles)
    zero, one = jnp.zeros_like(cosine), jnp.ones_like(cosine)
    tables = jnp.stack(
        [
            jnp.concatenate(parts, axis=1)
            for parts in (
                [cosine] * 4,
                [-sine, zero, -sine, zero],
                [zero, sine, zero, sine],
                [cosine, cosine, one, one],
                [-sine, zero, zero, zero],
                [zero, sine, zero, zero],
            )
        ]
    )
    paired = lambda a: lax.dynamic_index_in_dim(a.reshape(CHIPS, 2, ROWS), core, 1, keepdims=False)
    query_pos, query_start = paired(positions), paired(row_start)
    key_pos = positions.reshape(CHIPS, CHUNK)
    first_chunk = jnp.min(query_start, axis=1) // CHUNK

    heads_of = lambda w: w.reshape(128, KV_HEADS, 64)
    kv_shard = jnp.concatenate([heads_of(w_key), heads_of(w_value)], axis=2).reshape(128, WIDTH)
    gain_shard = jnp.zeros((8, 128), F32)
    gain_shard = gain_shard.at[0].set(norm_attn.astype(F32)).at[1].set(norm_query.astype(F32))
    gain_shard = gain_shard.at[2].set(jnp.concatenate([norm_key.astype(F32), jnp.ones((64,), F32)]))
    gain_shard = gain_shard.at[3].set(norm_ffn.astype(F32))
    w_both, gain_all = gather_weights(jnp.stack([w_query, kv_shard]), gain_shard)
    w_q, w_kv = w_both[0].reshape(WIDTH, WIDTH), w_both[1].reshape(WIDTH, WIDTH)
    gains = gain_all.transpose(1, 0, 2).reshape(8, WIDTH)

    w_o = lax.all_gather(w_out, "exp", axis=0, tiled=True)
    grads_all = lax.all_gather(cotangent, "exp", axis=0, tiled=True)

    normed, q_lin, kv_lin, q_send, kv_send, meta = project(
        tokens, w_q, w_kv, gains, tables, routes[0].T, gate_logits[0].T
    )
    q_all, kv_all, meta_all = spread_heads(q_send, kv_send, meta)
    kv_all = kv_all.reshape(KEYS, 128)
    out_low, out_wide, log_total = attend(
        q_all, kv_all, key_pos[:, None, :], query_pos[:, :, None], query_start[:, :, None], first_chunk
    )
    attended = collect_heads(out_low)
    resid, ffn_rows = finish_attention(attended, w_o, tokens, gains)
    rows_all = gather_rows(ffn_rows)

    shift = jnp.array([0.0, float(CAP)], F32)[None, None, :, None]
    spots = meta_all[:, :LOCAL].reshape(PAIRS, 2, LOCAL, ROWS).transpose(0, 2, 1, 3)
    spots = jnp.where(spots < 0.0, -1.0, spots + shift).reshape(PAIRS, LOCAL, PAIR_ROWS)
    weights = meta_all[:, LOCAL:].reshape(PAIRS, 2, LOCAL, ROWS).transpose(0, 2, 1, 3)
    pair_meta = jnp.concatenate([spots, weights.reshape(PAIRS, LOCAL, PAIR_ROWS)], axis=1)
    rows_in, d_rows, act, d_gate, d_up, out_parts, d_parts = experts(
        rows_all.reshape(PAIRS, PAIR_ROWS, WIDTH),
        grads_all.reshape(PAIRS, PAIR_ROWS, WIDTH),
        pair_meta,
        pair_meta.transpose(0, 2, 1),
        w_gate,
        w_up,
        w_down,
    )
    d_parts = trade_exp(d_parts.reshape(EXP, ROWS, WIDTH), 8)
    out_parts = lax.all_to_all(
        out_parts.reshape(EXP, ROWS, WIDTH), "exp", split_axis=0, concat_axis=0, tiled=True
    )
    layer_out = (resid + sum_blocks(out_parts)).astype(BF16)

    pieces_w = expert_grads(rows_in, d_rows, act, d_gate, d_up)
    groups = [[2 * c + k for c in range(CHIPS)] for k in range(2)]
    swap = [(k, k ^ 1) for k in range(CTX)]
    summed_w = []
    for piece in pieces_w:
        mine = lax.dynamic_index_in_dim(piece, core, 0, keepdims=False)
        other = lax.ppermute(
            lax.dynamic_index_in_dim(piece, 1 - core, 0, keepdims=False), "ctx", swap
        )
        joint = (mine.astype(F32) + other.astype(F32)).astype(BF16)
        summed_w.append(
            sum_blocks(
                lax.all_to_all(
                    joint, "ctx", split_axis=0, concat_axis=0, tiled=True, axis_index_groups=groups
                )
            )
        )

    d_resid, d_branch, d_attended, ffn_gain_grad = back_to_branch(
        d_parts, resid, cotangent, gains, w_o
    )
    d_out = spread_grads(d_attended)
    dq_all, dkv_all = attend_back(
        q_all,
        kv_all,
        d_out,
        out_wide,
        log_total,
        key_pos[:, :, None],
        query_pos[:, None, :],
        query_start[:, None, :],
        first_chunk,
    )
    dq, dkv = collect_grads(dq_all, dkv_all.reshape(CTX, ROWS, 128))
    d_q_lin, d_kv_lin, input_grad, gain_grads = back_to_input(
        dq, dkv, q_lin, kv_lin, tokens, d_resid, w_q, w_kv, gains, tables
    )
    gain_rows = jnp.concatenate([gain_grads, ffn_gain_grad], axis=0).astype(BF16)
    gain_rows = gain_rows.reshape(4, EXP, 128).transpose(1, 0, 2).reshape(EXP, 1, 512)
    gain_rows = jnp.pad(gain_rows, ((0, 0), (0, 15), (0, 512)))
    parts = dense_grads(normed, d_q_lin, d_kv_lin, attended, d_branch, gain_rows)
    other = swap_cores(parts)
    mine = lax.dynamic_index_in_dim(parts, core, 1, keepdims=False)
    joint = (mine.astype(F32) + other.astype(F32)).astype(BF16)
    joint = sum_blocks(trade_exp(joint, 11)).astype(BF16)
    joint = sum_blocks(trade_chips(joint)).astype(BF16)
    full = share_all(joint).astype(F32)
    dense = full[:, :192].reshape(2, 3, 64, WIDTH).transpose(1, 0, 2, 3).reshape(3, 128, WIDTH)
    kv_grad = dense[1].reshape(128, KV_HEADS, 2, 64)
    gain_out = full[0, 192, :512].reshape(4, 128)
    return (
        layer_out[None],
        input_grad[None],
        dense[0],
        kv_grad[:, :, 0].reshape(128, 512),
        kv_grad[:, :, 1].reshape(128, 512),
        dense[2],
        gain_out[0],
        gain_out[1],
        gain_out[2, :64],
        gain_out[3],
        summed_w[0],
        summed_w[1],
        summed_w[2],
    )


def solution(mesh):
    in_specs = (
        P("exp", "ctx", None),
        P("exp", "ctx", None),
        P("exp", None),
        P("exp", None, None),
        P("exp", "ctx", None),
        P("exp", "ctx", None),
        P("exp"),
        P("exp"),
        P("exp"),
        P("exp"),
        P("exp", None),
        P("exp", None),
        P("exp", None),
        P("exp", None),
        P("exp", None, None),
        P("exp", None, None),
        P("exp", None, None),
    )
    out_specs = (
        P("exp", "ctx", None),
        P("exp", "ctx", None),
        P("exp", None),
        P("exp", None),
        P("exp", None),
        P("exp", None),
        P("exp"),
        P("exp"),
        P("exp"),
        P("exp"),
        P("exp", "ctx", None),
        P("exp", "ctx", None),
        P("exp", "ctx", None),
    )
    return jax.shard_map(
        per_device, mesh=mesh, in_specs=in_specs, out_specs=out_specs, check_vma=False
    )
```

```python
import jax
import jax.numpy as jnp
from jax import lax
from jax.experimental import pallas as pl
from jax.experimental.pallas import tpu as pltpu
from jax.sharding import PartitionSpec as P

HEADS = 16
KV_HEADS = 8
EPSILON = 1e-05
ROPE_BASE = 10000.0
MASKED = -1e30

MESH = pl.DeviceIdType.MESH
CTX = 16
EXP = 8
CHIPS = 8
ROWS = 192
WIDTH = 1024
FF = 512
LOCAL = 4
CAP = 72
PAIRS = EXP // 2
PAIR_ROWS = 2 * ROWS
PAIR_CAP = 2 * CAP
SLOTS = EXP * CAP
PAIR_SLOTS = LOCAL * PAIR_CAP
KEYS = CTX * ROWS
CHUNK = 2 * ROWS
MIB = 1 << 20

ANY_SPEC = pl.BlockSpec(memory_space=pl.ANY)
F32 = jnp.float32
BF16 = jnp.bfloat16


def dot(a, b, dims=((1,), (0,))):
    return lax.dot_general(a, b, (dims, ((), ())), preferred_element_type=F32)


NT = ((1,), (1,))
TN = ((0,), (0,))


def comm_call(body, name, collective_id, outs, ins, copies, in_specs=None):
    return pl.pallas_call(
        body,
        name=name,
        out_shape=outs,
        in_specs=in_specs or [ANY_SPEC] * len(ins),
        out_specs=[ANY_SPEC] * len(outs),
        scratch_shapes=[
            pltpu.SemaphoreType.DMA((copies,)),
            pltpu.SemaphoreType.DMA((copies,)),
            pltpu.SemaphoreType.DMA((8,)),
        ],
        compiler_params=pltpu.CompilerParams(
            collective_id=collective_id, has_side_effects=True, vmem_limit_bytes=60 * MIB
        ),
    )(*ins)


class Copier:
    def __init__(self, send_sem, recv_sem, local_sem):
        self.send_sem, self.recv_sem, self.local_sem = send_sem, recv_sem, local_sem
        self.remote, self.local = [], []

    def send(self, src, dst, axis, index):
        at = len(self.remote)
        copy = pltpu.make_async_remote_copy(
            src_ref=src,
            dst_ref=dst,
            send_sem=self.send_sem.at[at],
            recv_sem=self.recv_sem.at[at],
            device_id={axis: index},
            device_id_type=MESH,
        )
        copy.start()
        self.remote.append([copy, False])
        return at

    def keep(self, src, dst):
        copy = pltpu.make_async_copy(src, dst, self.local_sem.at[len(self.local)])
        copy.start()
        self.local.append([copy, False])
        return len(self.local) - 1

    def arrived(self, at):
        self.remote[at][0].wait_recv()
        self.remote[at][1] = True

    def kept(self, at):
        self.local[at][0].wait()
        self.local[at][1] = True

    def finish(self):
        for copy, seen in self.remote:
            if not seen:
                copy.wait_recv()
        for copy, _ in self.remote:
            copy.wait_send()
        for copy, seen in self.local:
            if not seen:
                copy.wait()


def meet(partners):
    barrier = pltpu.get_barrier_semaphore()
    for axis, index in partners:
        pl.semaphore_signal(barrier, inc=1, device_id={axis: index}, device_id_type=MESH)
    pl.semaphore_wait(barrier, len(partners))


def place():
    ctx = lax.axis_index("ctx")
    core = lax.rem(ctx, 2)
    return ctx, ctx // 2, core, ctx + 1 - 2 * core


def ring_of(me):
    half, spot = me // 4, lax.rem(me, 4)
    over = (1 - half) * 4
    turns = [lax.rem(spot + d, 4) for d in (0, 1, 3, 2)]
    return tuple([half * 4 + t for t in turns] + [over + t for t in turns])


def relay(copier, own, slot, rows, ring, reach, landed=lambda partner: None):
    me, right, left, far, over, over_right, over_left, over_far = ring
    half = rows // 2
    low, high = pl.ds(0, half), pl.ds(half, half)

    def send(src, dst, partner):
        return copier.send(src, dst, *reach(partner))

    to_over = send(own, slot(me), over)
    to_right = send(own, slot(me), right)
    to_left = send(own, slot(me), left)
    yield
    copier.arrived(to_right)
    far_r = send(slot(left).at[low], slot(left).at[low], right)
    landed(left)
    copier.arrived(to_left)
    far_l = send(slot(right).at[high], slot(right).at[high], left)
    landed(right)
    yield
    copier.arrived(to_over)
    over_r = send(slot(over), slot(over), right)
    over_l = send(slot(over), slot(over), left)
    landed(over)
    yield
    copier.arrived(far_r)
    copier.arrived(far_l)
    landed(far)
    yield
    copier.arrived(over_r)
    far_r = send(slot(over_left).at[low], slot(over_left).at[low], right)
    landed(over_left)
    copier.arrived(over_l)
    far_l = send(slot(over_right).at[high], slot(over_right).at[high], left)
    landed(over_right)
    yield
    copier.arrived(far_r)
    copier.arrived(far_l)
    landed(over_far)


def side_by_side(*relays):
    for _ in zip(*relays):
        pass
    for one in relays:
        for _ in one:
            pass


def gather_inputs(tokens, weights, gains):
    half = weights.shape[0] // 2

    def body(t_ref, w_ref, g_ref, to_ref, wo_ref, go_ref, send_sem, recv_sem, local_sem):
        _, chip, core, sibling = place()
        me = lax.axis_index("exp")
        chips, exps = ring_of(chip), ring_of(me)
        to_chip = lambda p: ("ctx", 2 * p + core)
        to_exp = lambda p: ("exp", p)
        copier = Copier(send_sem, recv_sem, local_sem)
        meet([to_chip(chips[k]) for k in (1, 2, 4)] + [to_exp(p) for p in exps[1:]] + [("ctx", sibling)])
        part = pl.ds(pl.multiple_of(core * half, half), half)
        slot = lambda s: wo_ref.at[s, part]
        both = (
            relay(copier, t_ref, lambda s: to_ref.at[s], ROWS, chips, to_chip),
            relay(
                copier,
                w_ref.at[part],
                slot,
                half,
                exps,
                to_exp,
                lambda s: copier.send(slot(s), slot(s), "ctx", sibling),
            ),
        )
        for one in both:
            next(one)
        copier.keep(t_ref, to_ref.at[chip])
        copier.keep(w_ref, wo_ref.at[me])
        copier.keep(g_ref, go_ref.at[me])
        for p in exps[1:]:
            copier.send(g_ref, go_ref.at[me], *to_exp(p))
        side_by_side(*both)
        copier.finish()

    vmem = pl.BlockSpec(memory_space=pltpu.VMEM)
    return comm_call(
        body,
        "gather_inputs",
        1,
        [
            jax.ShapeDtypeStruct((CHIPS, ROWS, WIDTH), BF16),
            jax.ShapeDtypeStruct((EXP,) + weights.shape, BF16),
            jax.ShapeDtypeStruct((EXP, 8, 128), F32),
        ],
        [tokens, weights, gains],
        32,
        in_specs=[vmem] * 3,
    )


def gather_rows(rows, meta):
    def body(x_ref, m_ref, o_ref, mo_ref, send_sem, recv_sem, local_sem):
        ring = ring_of(lax.axis_index("exp"))
        me = ring[0]
        to_exp = lambda p: ("exp", p)
        copier = Copier(send_sem, recv_sem, local_sem)
        meet([to_exp(p) for p in ring[1:]])
        copier.keep(x_ref, o_ref.at[me])
        copier.keep(m_ref.at[me], mo_ref.at[me])
        for p in ring[1:]:
            copier.send(m_ref.at[p], mo_ref.at[me], *to_exp(p))
        side_by_side(relay(copier, x_ref, lambda s: o_ref.at[s], rows.shape[0], ring, to_exp))
        copier.finish()

    return comm_call(
        body,
        "gather_rows",
        2,
        [
            jax.ShapeDtypeStruct((EXP,) + rows.shape, rows.dtype),
            jax.ShapeDtypeStruct(meta.shape, F32),
        ],
        [rows, meta],
        16,
        in_specs=[pl.BlockSpec(memory_space=pltpu.VMEM)] * 2,
    )


def share_totals(totals, collective_id):
    def body(x_ref, o_ref, send_sem, recv_sem, local_sem):
        _, chip, core, _ = place()
        chips = [lax.rem(chip + d, CHIPS) for d in range(1, CHIPS)]
        copier = Copier(send_sem, recv_sem, local_sem)
        meet([("ctx", 2 * p + core) for p in chips])
        for p in chips:
            copier.send(x_ref, o_ref.at[chip], "ctx", 2 * p + core)
        copier.keep(x_ref, o_ref.at[chip])
        copier.finish()

    return comm_call(
        body,
        "share_totals",
        collective_id,
        [jax.ShapeDtypeStruct((CHIPS,) + totals.shape, F32)],
        [totals],
        7,
    )[0]


def pair_keys(kv):
    def body(x_ref, o_ref, send_sem, recv_sem, local_sem):
        _, _, core, sibling = place()
        copier = Copier(send_sem, recv_sem, local_sem)
        meet([("ctx", sibling)])
        copier.send(x_ref, o_ref.at[:, core], "ctx", sibling)
        copier.keep(x_ref, o_ref.at[:, core])
        copier.finish()

    return comm_call(
        body, "pair_keys", 12, [jax.ShapeDtypeStruct((CHIPS, 2, ROWS, 128), BF16)], [kv], 1,
        in_specs=[pl.BlockSpec(memory_space=pltpu.VMEM)],
    )[0]


def pair_grads(dkv):
    def body(x_ref, o_ref, send_sem, recv_sem, local_sem):
        _, _, _, sibling = place()
        copier = Copier(send_sem, recv_sem, local_sem)
        meet([("ctx", sibling)])
        copier.send(x_ref, o_ref, "ctx", sibling)
        copier.finish()

    return comm_call(
        body, "pair_grads", 13, [jax.ShapeDtypeStruct((CHIPS, ROWS, 128), BF16)], [dkv], 1
    )[0]


def lanes(index):
    return pl.ds(pl.multiple_of(index * 128, 128), 128)


def collect_heads(blocks):
    def body(x_ref, o_ref, send_sem, recv_sem, local_sem):
        _, chip, core, _ = place()
        chips = [lax.rem(chip + d, CHIPS) for d in range(1, CHIPS)]
        copier = Copier(send_sem, recv_sem, local_sem)
        meet([("ctx", 2 * p + core) for p in chips])
        for p in chips:
            copier.send(x_ref.at[p], o_ref.at[:, lanes(chip)], "ctx", 2 * p + core)
        copier.keep(x_ref.at[chip], o_ref.at[:, lanes(chip)])
        copier.finish()

    return comm_call(
        body, "collect_heads", 4, [jax.ShapeDtypeStruct((ROWS, WIDTH), BF16)], [blocks], 7
    )[0]


def spread_grads(rows):
    def body(x_ref, o_ref, send_sem, recv_sem, local_sem):
        _, chip, core, _ = place()
        chips = [lax.rem(chip + d, CHIPS) for d in range(1, CHIPS)]
        copier = Copier(send_sem, recv_sem, local_sem)
        meet([("ctx", 2 * p + core) for p in chips])
        for p in chips:
            copier.send(x_ref.at[:, lanes(p)], o_ref.at[chip], "ctx", 2 * p + core)
        copier.keep(x_ref.at[:, lanes(chip)], o_ref.at[chip])
        copier.finish()

    return comm_call(
        body, "spread_grads", 5, [jax.ShapeDtypeStruct((CHIPS, ROWS, 128), BF16)], [rows], 7
    )[0]


def settle_grads(d_q, d_kv, w_parts, out_part, layer_part):
    def body(
        q_ref, kv_ref, w_ref, a_ref, l_ref, qo_ref, kvo_ref, wo_ref, ao_ref, lo_ref,
        got, joint, traded, done, a_got, a_half, a_other, a_done, send_sem, recv_sem, local_sem,
    ):
        ctx, chip, core, sibling = place()
        me = lax.axis_index("exp")
        chips = [lax.rem(chip + d, CHIPS) for d in range(1, CHIPS)]
        exps = [lax.rem(me + d, EXP) for d in range(1, EXP)]
        others = [lax.rem(ctx + d, CTX) for d in range(1, CTX)]
        copier = Copier(send_sem, recv_sem, local_sem)
        meet([("ctx", p) for p in others] + [("exp", p) for p in exps])
        swapped = copier.send(w_ref.at[1 - core], got, "ctx", sibling)
        spread = [copier.send(a_ref.at[:, lanes(p)], a_got.at[chip], "ctx", 2 * p + core) for p in chips]
        for p in chips:
            copier.send(q_ref.at[p], qo_ref.at[:, lanes(chip)], "ctx", 2 * p + core)
            copier.send(kv_ref.at[p], kvo_ref.at[:, lanes(chip)], "ctx", 2 * p + core)
        copier.keep(q_ref.at[chip], qo_ref.at[:, lanes(chip)])
        copier.keep(kv_ref.at[chip], kvo_ref.at[:, lanes(chip)])
        copier.send(l_ref, lo_ref, "exp", lax.rem(me + 4, EXP))
        copier.arrived(swapped)
        both = w_ref[core].astype(F32) + got[...].astype(F32)
        joint[...] = both.astype(BF16).reshape(EXP, 128, 128)
        trades = [copier.send(joint.at[p], traded.at[me], "exp", p) for p in exps]
        traded[me] = joint[me]
        for at in spread:
            copier.arrived(at)
        a_got[chip] = a_ref[:, lanes(chip)]
        total = a_got[0].astype(F32)
        for c in range(1, CHIPS):
            total = total + a_got[c].astype(F32)
        a_half[...] = total.astype(BF16)
        halves = copier.send(a_half, a_other, "ctx", sibling)
        for at in trades:
            copier.arrived(at)
        total = traded[0].astype(F32)
        for e in range(1, EXP):
            total = total + traded[e].astype(F32)
        done[...] = total.astype(BF16)
        for p in others:
            copier.send(done, wo_ref.at[core, :, lanes(chip)], "ctx", p)
        copier.keep(done, wo_ref.at[core, :, lanes(chip)])
        copier.arrived(halves)
        a_done[...] = (a_half[...].astype(F32) + a_other[...].astype(F32)).astype(BF16)
        for p in chips:
            copier.send(a_done, ao_ref.at[:, lanes(chip)], "ctx", 2 * p + core)
        copier.keep(a_done, ao_ref.at[:, lanes(chip)])
        copier.finish()

    vmem = pl.BlockSpec(memory_space=pltpu.VMEM)
    tile = pltpu.VMEM((128, 128), BF16)
    return pl.pallas_call(
        body,
        name="settle_grads",
        out_shape=[
            jax.ShapeDtypeStruct((ROWS, WIDTH), BF16),
            jax.ShapeDtypeStruct((ROWS, WIDTH), BF16),
            jax.ShapeDtypeStruct((2, 128, WIDTH), BF16),
            jax.ShapeDtypeStruct((128, WIDTH), BF16),
            jax.ShapeDtypeStruct((ROWS, WIDTH), BF16),
        ],
        in_specs=[ANY_SPEC, ANY_SPEC, vmem, vmem, ANY_SPEC],
        out_specs=[ANY_SPEC] * 5,
        scratch_shapes=[
            pltpu.VMEM((WIDTH, 128), BF16),
            pltpu.VMEM((EXP, 128, 128), BF16),
            pltpu.VMEM((EXP, 128, 128), BF16),
            tile,
            pltpu.VMEM((CHIPS, 128, 128), BF16),
            tile,
            tile,
            tile,
            pltpu.SemaphoreType.DMA((53,)),
            pltpu.SemaphoreType.DMA((53,)),
            pltpu.SemaphoreType.DMA((8,)),
        ],
        compiler_params=pltpu.CompilerParams(
            collective_id=6, has_side_effects=True, vmem_limit_bytes=60 * MIB
        ),
    )(d_q, d_kv, w_parts, out_part, layer_part)


def sum_gains(parts):
    def body(x_ref, o_ref, traded, mine, shared, send_sem, recv_sem, local_sem):
        ctx, _, _, _ = place()
        me = lax.axis_index("exp")
        exps = [lax.rem(me + d, EXP) for d in range(1, EXP)]
        others = [lax.rem(ctx + d, CTX) for d in range(1, CTX)]
        copier = Copier(send_sem, recv_sem, local_sem)
        meet([("ctx", p) for p in others] + [("exp", p) for p in exps])
        trades = [copier.send(x_ref.at[p], traded.at[me], "exp", p) for p in exps]
        traded[me] = x_ref[me]
        for at in trades:
            copier.arrived(at)
        total = traded[0]
        for e in range(1, EXP):
            total = total + traded[e]
        mine[...] = total
        shares = [copier.send(mine, shared.at[ctx], "ctx", p) for p in others]
        shared[ctx] = total
        for at in shares:
            copier.arrived(at)
        total = shared[0]
        for c in range(1, CTX):
            total = total + shared[c]
        o_ref[...] = total
        copier.finish()

    vmem = pl.BlockSpec(memory_space=pltpu.VMEM)
    return pl.pallas_call(
        body,
        name="sum_gains",
        out_shape=jax.ShapeDtypeStruct((8, 128), F32),
        in_specs=[vmem],
        out_specs=vmem,
        scratch_shapes=[
            pltpu.VMEM((EXP, 8, 128), F32),
            pltpu.VMEM((8, 128), F32),
            pltpu.VMEM((CTX, 8, 128), F32),
            pltpu.SemaphoreType.DMA((22,)),
            pltpu.SemaphoreType.DMA((22,)),
            pltpu.SemaphoreType.DMA((8,)),
        ],
        compiler_params=pltpu.CompilerParams(
            collective_id=7, has_side_effects=True, vmem_limit_bytes=60 * MIB
        ),
    )(parts)


def settle_experts(rows, d_rows, act, d_gate, d_up, d_parts, layer_parts):
    def body(
        x_ref, r_ref, a_ref, g_ref, u_ref, p_ref, l_ref, gate_out, up_out, down_out, dx_out, keep_out, give_out,
        x_v, r_v, a_v, g_v, u_v, gate, up, down, gate_o, up_o, down_o, gate_a, down_a, up_b, down_b,
        gate_c, down_c, up_d, down_d, mine, from_x, to_z, from_z, layer_mine, layer_from, send_sem, recv_sem, local_sem,
    ):
        _, chip, core, sibling = place()
        me = lax.axis_index("exp")
        zl, x = me // 4, lax.rem(me, 4)
        zh, y = chip // 4, lax.rem(chip, 4)
        at_ctx = lambda z, yy: ("ctx", z * 8 + yy * 2 + core)
        over = at_ctx(1 - zh, y)
        columns = [lax.rem(y + d, 4) for d in (1, 3, 2)]
        spots = [lax.rem(x + d, 4) for d in (1, 3, 2)]
        copier = Copier(send_sem, recv_sem, local_sem)
        loads = []
        for e in range(LOCAL):
            pairs = ((x_ref, x_v), (r_ref, r_v), (a_ref, a_v), (g_ref, g_v), (u_ref, u_v))
            loads.append([copier.keep(src.at[e], dst.at[e]) for src, dst in pairs])
        own_part = copier.keep(p_ref.at[:, x], mine)
        own_layer = copier.keep(l_ref.at[:, x], layer_mine)
        meet(
            [("ctx", sibling), over]
            + [at_ctx(zh, c) for c in columns]
            + [("exp", zl * 4 + p) for p in spots]
            + [("exp", (1 - zl) * 4 + x)]
        )
        x_stage = [copier.send(p_ref.at[:, p], from_x.at[x], "exp", zl * 4 + p) for p in spots]

        def work(e):
            for at in loads[e]:
                copier.kept(at)

            def wide(r, _):
                rows_r = x_v[e, :, pl.ds(pl.multiple_of(r * 256, 256), 256)]
                for d_v, o_v in ((g_v, gate), (u_v, up)):
                    grad = dot(rows_r, d_v[e], TN).astype(BF16)
                    for k in range(4):
                        o_v[k % 2, r // 2, 2 * lax.rem(r, 2) + k // 2, e] = grad[k * 64 : (k + 1) * 64]
                return 0

            lax.fori_loop(0, 4, wide, 0)

            def tall(r, _):
                act_r = a_v[e, :, pl.ds(pl.multiple_of(r * 256, 256), 256)]
                grad = dot(act_r, r_v[e], TN).astype(BF16)
                for k in range(8):
                    down[k % 2, r, k // 2, e] = grad[k * 32 : (k + 1) * 32]
                return 0

            lax.fori_loop(0, 2, tall, 0)
            return [
                copier.send(full.at[1 - core, :, :, e], other.at[:, :, e], "ctx", sibling)
                for full, other in ((gate, gate_o), (up, up_o), (down, down_o))
            ]

        first_a, first_b = [], []

        def join(e, swaps):
            for at in swaps:
                copier.arrived(at)

            def add(c, _):
                z, yy = c // 4, lax.rem(c, 4)
                for full, other in ((gate, gate_o), (up, up_o), (down, down_o)):
                    both = full[core, z, yy, e].astype(F32) + other[z, yy, e].astype(F32)
                    full[core, z, yy, e] = both.astype(BF16)
                return 0

            lax.fori_loop(0, CHIPS, add, 0)
            first_a.append(copier.send(gate.at[core, 1 - zh, :, e], gate_a.at[:, e], *over))
            if e < 2:
                first_a.append(copier.send(down.at[core, 1 - zh, :, e], down_a.at[:, e], *over))
            for c in columns:
                to = at_ctx(zh, c)
                first_b.append(copier.send(up.at[core, :, c, e], up_b.at[y, :, e], *to))
                if e >= 2:
                    first_b.append(copier.send(down.at[core, :, c, e], down_b.at[y, :, e - 2], *to))

        swaps = work(0)
        for e in range(1, LOCAL):
            later = work(e)
            join(e - 1, swaps)
            swaps = later
        join(LOCAL - 1, swaps)

        copier.kept(own_part)
        for at in x_stage:
            copier.arrived(at)
        layer_stage = [copier.send(l_ref.at[:, p], layer_from.at[x], "exp", zl * 4 + p) for p in spots]
        sources = [lax.rem(x + d, 4) for d in (1, 2, 3)]

        def gather_x(r, _):
            at = pl.ds(pl.multiple_of(r * 48, 16), 48)
            keep, give = mine[zl, at, :].astype(F32), mine[1 - zl, at, :].astype(F32)
            for p in sources:
                keep = keep + from_x[p, zl, at, :].astype(F32)
                give = give + from_x[p, 1 - zl, at, :].astype(F32)
            dx_out[at, :] = keep
            to_z[at, :] = give.astype(BF16)
            return 0

        lax.fori_loop(0, 4, gather_x, 0)
        z_stage = copier.send(to_z, from_z, "exp", (1 - zl) * 4 + x)

        for at in first_a:
            copier.arrived(at)

        def sum_a(c, _):
            for e in range(LOCAL):
                both = gate[core, zh, c, e].astype(F32) + gate_a[c, e].astype(F32)
                gate[core, zh, c, e] = both.astype(BF16)
            for e in range(2):
                both = down[core, zh, c, e].astype(F32) + down_a[c, e].astype(F32)
                down[core, zh, c, e] = both.astype(BF16)
            return 0

        lax.fori_loop(0, 4, sum_a, 0)
        second_a = []
        for c in columns:
            to = at_ctx(zh, c)
            second_a.append(copier.send(gate.at[core, zh, c], gate_c.at[y], *to))
            second_a.append(copier.send(down.at[core, zh, c, pl.ds(0, 2)], down_c.at[y], *to))

        for at in first_b:
            copier.arrived(at)
        others = [lax.rem(y + d, 4) for d in (1, 2, 3)]

        def sum_b(e, _):
            for z in range(2):
                total = up[core, z, y, e].astype(F32)
                for c in others:
                    total = total + up_b[c, z, e].astype(F32)
                up[core, z, y, e] = total.astype(BF16)
            return 0

        lax.fori_loop(0, LOCAL, sum_b, 0)

        def sum_b_down(e, _):
            for z in range(2):
                total = down[core, z, y, e + 2].astype(F32)
                for c in others:
                    total = total + down_b[c, z, e].astype(F32)
                down[core, z, y, e + 2] = total.astype(BF16)
            return 0

        lax.fori_loop(0, 2, sum_b_down, 0)
        second_b = [
            copier.send(up.at[core, 1 - zh, y], up_d, *over),
            copier.send(down.at[core, 1 - zh, y, pl.ds(2, 2)], down_d, *over),
        ]

        copier.arrived(z_stage)

        def gather_z(r, _):
            at = pl.ds(pl.multiple_of(r * 48, 16), 48)
            dx_out[at, :] += from_z[at, :].astype(F32)
            return 0

        lax.fori_loop(0, 4, gather_z, 0)
        for at in second_a + second_b:
            copier.arrived(at)

        def final(e, _):
            total = gate[core, zh, y, e].astype(F32)
            for c in others:
                total = total + gate_c[c, e].astype(F32)
            gate_out[e] = total
            up_out[e] = up[core, zh, y, e].astype(F32) + up_d[e].astype(F32)
            return 0

        lax.fori_loop(0, LOCAL, final, 0)
        for e in range(2):
            total = down[core, zh, y, e].astype(F32)
            for c in others:
                total = total + down_c[c, e].astype(F32)
            down_out[e] = total
            down_out[e + 2] = down[core, zh, y, e + 2].astype(F32) + down_d[e].astype(F32)
        copier.kept(own_layer)
        for at in layer_stage:
            copier.arrived(at)

        def gather_layer(r, _):
            at = pl.ds(pl.multiple_of(r * 48, 16), 48)
            keep, give = layer_mine[zl, at, :].astype(F32), layer_mine[1 - zl, at, :].astype(F32)
            for p in sources:
                keep = keep + layer_from[p, zl, at, :].astype(F32)
                give = give + layer_from[p, 1 - zl, at, :].astype(F32)
            keep_out[at, :] = keep
            give_out[at, :] = give.astype(BF16)
            return 0

        lax.fori_loop(0, 4, gather_layer, 0)
        copier.finish()

    vmem = pl.BlockSpec(memory_space=pltpu.VMEM)
    buf = lambda *shape: pltpu.VMEM(shape, BF16)
    wide, tall = (64, FF), (32, WIDTH)
    return pl.pallas_call(
        body,
        name="settle_experts",
        out_shape=[
            jax.ShapeDtypeStruct((LOCAL,) + wide, F32),
            jax.ShapeDtypeStruct((LOCAL,) + wide, F32),
            jax.ShapeDtypeStruct((LOCAL,) + tall, F32),
            jax.ShapeDtypeStruct((ROWS, WIDTH), F32),
            jax.ShapeDtypeStruct((ROWS, WIDTH), F32),
            jax.ShapeDtypeStruct((ROWS, WIDTH), BF16),
        ],
        in_specs=[ANY_SPEC] * 7,
        out_specs=[vmem] * 6,
        scratch_shapes=[
            buf(LOCAL, SLOTS, WIDTH),
            buf(LOCAL, SLOTS, WIDTH),
            buf(LOCAL, SLOTS, FF),
            buf(LOCAL, SLOTS, FF),
            buf(LOCAL, SLOTS, FF),
            buf(2, 2, 4, LOCAL, *wide),
            buf(2, 2, 4, LOCAL, *wide),
            buf(2, 2, 4, LOCAL, *tall),
            buf(2, 4, LOCAL, *wide),
            buf(2, 4, LOCAL, *wide),
            buf(2, 4, LOCAL, *tall),
            buf(4, LOCAL, *wide),
            buf(4, 2, *tall),
            buf(4, 2, LOCAL, *wide),
            buf(4, 2, 2, *tall),
            buf(4, LOCAL, *wide),
            buf(4, 2, *tall),
            buf(LOCAL, *wide),
            buf(2, *tall),
            buf(2, ROWS, WIDTH),
            buf(4, 2, ROWS, WIDTH),
            buf(ROWS, WIDTH),
            buf(ROWS, WIDTH),
            buf(2, ROWS, WIDTH),
            buf(4, 2, ROWS, WIDTH),
            pltpu.SemaphoreType.DMA((51,)),
            pltpu.SemaphoreType.DMA((51,)),
            pltpu.SemaphoreType.DMA((24,)),
        ],
        compiler_params=pltpu.CompilerParams(
            collective_id=8, has_side_effects=True, vmem_limit_bytes=62 * MIB
        ),
    )(rows, d_rows, act, d_gate, d_up, d_parts, layer_parts)


def compute_call(body, name, outs, ins, vmem=60, **kw):
    return pl.pallas_call(
        body,
        name=name,
        out_shape=outs,
        compiler_params=pltpu.CompilerParams(vmem_limit_bytes=vmem * MIB),
        **kw,
    )(*ins)


def row_scale(total, width):
    return lax.rsqrt(total * (1.0 / width) + EPSILON)


def key_lanes():
    return lax.broadcasted_iota(jnp.int32, (1, 128), 1) < 64


def turn(values, cosine, sine):
    first = lax.rem(lax.broadcasted_iota(jnp.int32, (1, 128), 1), 64) < 32
    return values * cosine + jnp.where(first, -pltpu.roll(values, 96, 1), pltpu.roll(values, 32, 1)) * sine


def across(select, values):
    return lax.dot_general(
        select, values, (NT, ((), ())), precision=lax.Precision.HIGHEST, preferred_element_type=F32
    )


def both_totals(left, right):
    row_id = lax.broadcasted_iota(jnp.int32, (8, 128), 0)
    ones = jnp.where(row_id == 0, 1.0, 0.0)
    keys = jnp.where((row_id == 1) & key_lanes(), 1.0, 0.0)
    return (across(ones, left) + across(keys, right))[0:2, :]


def down_rows(values, row, width=128):
    chosen = lax.broadcasted_iota(jnp.int32, (2, width), 0) == row
    return lax.dot_general(
        values,
        jnp.where(chosen, 1.0, 0.0),
        (TN, ((), ())),
        precision=lax.Precision.HIGHEST,
        preferred_element_type=F32,
    )


def own_chip():
    return lax.axis_index("ctx") // 2


def project(rows, weights, gains, chip):
    step = 2 * ROWS

    def body(c_ref, x_ref, wq_ref, wk_ref, wv_ref, g_ref, n_ref, q_ref, kv_ref, s_ref, w_own):
        @pl.when(pl.program_id(0) == 0)
        def _():
            odd = lax.rem(c_ref[0], 2) == 1
            wk, wv = wk_ref[...].astype(F32), wv_ref[...].astype(F32)
            wk = jnp.where(odd, pltpu.roll(wk, 64, 1), wk)
            wv = jnp.where(odd, wv, pltpu.roll(wv, 64, 1))
            w_own[:, 0:128] = wq_ref[...]
            w_own[:, 128:256] = jnp.where(key_lanes(), wk, wv).astype(BF16)

        x = x_ref[...].astype(F32)
        scale = row_scale(jnp.sum(x * x, axis=1, keepdims=True), WIDTH)
        normed = (x * scale * g_ref[0:1, :]).astype(BF16)
        n_ref[...] = normed
        both = dot(normed, w_own[...])
        q, kv = both[:, 0:128], both[:, 128:256]
        q_ref[...] = q
        kv_ref[...] = kv
        for k in range(2):
            at = slice(k * ROWS, (k + 1) * ROWS)
            s_ref[k] = both_totals(q[at] * q[at], kv[at] * kv[at])

    def each(*shape):
        return pl.BlockSpec((step,) + shape, lambda i, c: (i, 0))

    return pl.pallas_call(
        body,
        name="project",
        out_shape=[
            jax.ShapeDtypeStruct((CHIPS * ROWS, WIDTH), BF16),
            jax.ShapeDtypeStruct((CHIPS * ROWS, 128), F32),
            jax.ShapeDtypeStruct((CHIPS * ROWS, 128), F32),
            jax.ShapeDtypeStruct((CHIPS, 2, ROWS), F32),
        ],
        grid_spec=pltpu.PrefetchScalarGridSpec(
            num_scalar_prefetch=1,
            grid=(CHIPS // 2,),
            in_specs=[
                each(WIDTH),
                pl.BlockSpec((WIDTH, 128), lambda i, c: (0, c[0])),
                pl.BlockSpec((WIDTH, 128), lambda i, c: (0, 8 + c[0] // 2)),
                pl.BlockSpec((WIDTH, 128), lambda i, c: (0, 12 + c[0] // 2)),
                pl.BlockSpec((8, WIDTH), lambda i, c: (0, 0)),
            ],
            out_specs=[
                each(WIDTH),
                each(128),
                each(128),
                pl.BlockSpec((2, 2, ROWS), lambda i, c: (i, 0, 0)),
            ],
            scratch_shapes=[pltpu.VMEM((WIDTH, 256), BF16)],
        ),
        compiler_params=pltpu.CompilerParams(vmem_limit_bytes=60 * MIB),
    )(chip, rows, weights, weights, weights, gains)


def turn_heads(q_lin, kv_lin, totals, places, gains):
    def body(q_ref, kv_ref, t_ref, p_ref, g_ref, qo_ref, kvo_ref, s_ref, c_ref, n_ref):
        gain = g_ref[own_chip()]
        keys = key_lanes()
        lane = lax.broadcasted_iota(jnp.int32, (1, 128), 1)
        freq = jnp.exp(lax.rem(lane, 32).astype(F32) * (-2.0 / 64 * 9.210340371976184))
        shift = jnp.where(keys, 0.0, 1.5707963267948966)

        def one(i, _):
            place_i = p_ref[i]
            offset = down_rows(place_i, 0) - down_rows(place_i, 1)
            mixed = jnp.cos(offset * freq - shift)
            other = pltpu.roll(mixed, 64, 1)
            cos, sin = jnp.where(keys, mixed, other), jnp.where(keys, other, mixed)
            c_ref[i] = cos
            n_ref[i] = sin
            squares = t_ref[0, i]
            for c in range(1, CHIPS):
                squares = squares + t_ref[c, i]
            s_ref[i] = squares
            q = q_ref[i] * row_scale(down_rows(squares, 0), WIDTH) * gain[1:2, :]
            q = turn(q, cos, sin).astype(BF16).astype(F32)
            qo_ref[i] = (q * 0.125).astype(BF16)
            scale = jnp.where(keys, row_scale(down_rows(squares, 1), WIDTH // 2), 1.0)
            kv = kv_ref[i] * scale * gain[2:3, :]
            kvo_ref[i] = turn(kv, jnp.where(keys, cos, 1.0), jnp.where(keys, sin, 0.0)).astype(BF16)
            return 0

        lax.fori_loop(0, CHIPS, one, 0)

    return compute_call(
        body,
        "turn_heads",
        [jax.ShapeDtypeStruct((CHIPS, ROWS, 128), BF16)] * 2
        + [jax.ShapeDtypeStruct((CHIPS, 2, ROWS), F32)]
        + [jax.ShapeDtypeStruct((CHIPS, ROWS, 128), F32)] * 2,
        [q_lin, kv_lin, totals, places, gains],
    )


def route(routes_t, logits_t):
    def body(r_ref, l_ref, m_ref):
        logits = l_ref[...]
        raised = jnp.exp(logits - jnp.max(logits, axis=0, keepdims=True))
        gates = raised / jnp.sum(raised, axis=0, keepdims=True)
        experts = lax.broadcasted_iota(jnp.int32, (32, ROWS), 0)
        member = jnp.zeros((32, ROWS), F32)
        weight = jnp.zeros((32, ROWS), F32)
        for c in range(8):
            hit = r_ref[c : c + 1, :] == experts
            member = member + jnp.where(hit, 1.0, 0.0)
            weight = weight + jnp.where(hit, gates[c : c + 1, :], 0.0)
        before = lax.broadcasted_iota(jnp.int32, (ROWS, ROWS), 0) < lax.broadcasted_iota(
            jnp.int32, (ROWS, ROWS), 1
        )
        rank = dot(member.astype(BF16), jnp.where(before, 1.0, 0.0).astype(BF16))
        spot = jnp.where(member > 0.5, rank, -1.0)
        for e in range(EXP):
            m_ref[e, 0:4, :] = spot[e * 4 : e * 4 + 4, :]
            m_ref[e, 4:8, :] = weight[e * 4 : e * 4 + 4, :]

    return compute_call(
        body, "route", [jax.ShapeDtypeStruct((EXP, 8, ROWS), F32)], [routes_t, logits_t]
    )[0]


def split_kv(kv_ref, klo, khi, vlo, vhi):
    low = key_lanes()
    both = kv_ref[...].astype(F32)
    other = pltpu.roll(both, 64, 1)
    if klo is not None:
        klo[...] = jnp.where(low, both, 0.0).astype(BF16)
        khi[...] = jnp.where(low, 0.0, other).astype(BF16)
    vlo[...] = jnp.where(low, other, 0.0).astype(BF16)
    vhi[...] = jnp.where(low, 0.0, both).astype(BF16)


def attend(q, kv, key_pos, places, first_chunk):
    def body(first_ref, q_ref, kv_ref, kp_ref, p_ref, o_ref, of_ref, l_ref, klo, khi, vlo, vhi):
        i = pl.program_id(0)

        @pl.when(i == 0)
        def _():
            split_kv(kv_ref, klo, khi, vlo, vhi)

        q_block = q_ref[0]
        at_row, start_row = [
            jnp.concatenate([down_rows(p_ref[0], k)] * (CHUNK // 128), axis=1) for k in range(2)
        ]
        low = key_lanes()

        def step(p, carry):
            m0, m1, l0, l1, acc = carry
            rows = pl.ds(pl.multiple_of(p * CHUNK, CHUNK), CHUNK)
            at_key = kp_ref[p]
            seen = (at_key >= start_row) & (at_key <= at_row)
            s0 = jnp.where(seen, dot(q_block, klo[rows, :], NT), MASKED)
            s1 = jnp.where(seen, dot(q_block, khi[rows, :], NT), MASKED)
            n0 = jnp.maximum(m0, jnp.max(s0, axis=1, keepdims=True))
            n1 = jnp.maximum(m1, jnp.max(s1, axis=1, keepdims=True))
            p0 = jnp.exp(s0 - n0)
            p1 = jnp.exp(s1 - n1)
            a0 = jnp.exp(m0 - n0)
            a1 = jnp.exp(m1 - n1)
            l0 = l0 * a0 + jnp.sum(p0, axis=1, keepdims=True)
            l1 = l1 * a1 + jnp.sum(p1, axis=1, keepdims=True)
            acc = acc * jnp.where(low, a0, a1)
            acc = acc + dot(p0.astype(BF16), vlo[rows, :]) + dot(p1.astype(BF16), vhi[rows, :])
            return n0, n1, l0, l1, acc

        top = jnp.full((ROWS, 1), MASKED, F32)
        none = jnp.zeros((ROWS, 1), F32)
        m0, m1, l0, l1, acc = lax.fori_loop(
            first_ref[i], i + 1, step, (top, top, none, none, jnp.zeros((ROWS, 128), F32))
        )
        out = acc / jnp.where(low, l0, l1)
        of_ref[0] = out
        o_ref[0] = out.astype(BF16)
        l_ref[0] = jnp.where(low, m0 + jnp.log(l0), m1 + jnp.log(l1))

    def block(*shape):
        return pl.BlockSpec((1,) + shape, lambda i, first: (i, 0, 0))

    return pl.pallas_call(
        body,
        name="attend",
        out_shape=[
            jax.ShapeDtypeStruct((CHIPS, ROWS, 128), BF16),
            jax.ShapeDtypeStruct((CHIPS, ROWS, 128), F32),
            jax.ShapeDtypeStruct((CHIPS, ROWS, 128), F32),
        ],
        grid_spec=pltpu.PrefetchScalarGridSpec(
            num_scalar_prefetch=1,
            grid=(CHIPS,),
            in_specs=[
                block(ROWS, 128),
                pl.BlockSpec((KEYS, 128), lambda i, first: (0, 0)),
                pl.BlockSpec((CHIPS, 1, CHUNK), lambda i, first: (0, 0, 0)),
                block(2, ROWS),
            ],
            out_specs=[block(ROWS, 128)] * 3,
            scratch_shapes=[pltpu.VMEM((KEYS, 128), BF16)] * 4,
        ),
        compiler_params=pltpu.CompilerParams(vmem_limit_bytes=60 * MIB),
    )(first_chunk, q, kv, key_pos, places)


def attend_back(q, kv, d_out, out, log_total, key_pos, places, first_chunk):
    def body(
        first_ref, q_ref, kv_ref, do_ref, o_ref, l_ref, kp_ref, p_ref,
        dq_ref, mine_ref, other_ref, klo, khi, vlo, vhi, acc, key_at,
    ):
        i = pl.program_id(0)

        @pl.when(i == 0)
        def _():
            split_kv(kv_ref, klo, khi, vlo, vhi)
            acc[...] = jnp.zeros_like(acc)

            def place_keys(p, _):
                both = jnp.concatenate([kp_ref[p], kp_ref[p]], axis=0)
                key_at[pl.ds(pl.multiple_of(p * CHUNK, CHUNK), CHUNK), :] = down_rows(both, 0, ROWS)
                return 0

            lax.fori_loop(0, CHIPS, place_keys, 0)

        low = key_lanes()
        q_block, do_block = q_ref[0], do_ref[0]
        do_wide, q_wide = do_block.astype(F32), q_block.astype(F32)
        q_turned, do_turned = pltpu.roll(q_wide, 64, 1), pltpu.roll(do_wide, 64, 1)
        right = jnp.concatenate(
            [
                jnp.where(low, q_wide, 0.0).astype(BF16),
                jnp.where(low, q_turned, 0.0).astype(BF16),
                jnp.where(low, 0.0, do_turned).astype(BF16),
                jnp.where(low, 0.0, do_wide).astype(BF16),
            ],
            axis=0,
        )
        row_id = lax.broadcasted_iota(jnp.int32, (8, 128), 0)
        lane_id = lax.broadcasted_iota(jnp.int32, (8, 128), 1)
        halves = jnp.where(lane_id // 64 == row_id, 1.0, 0.0)
        picks = jnp.where(lane_id == 64 * row_id, 1.0, 0.0)

        delta = across(halves, do_wide * o_ref[0])
        total = across(picks, l_ref[0])
        at_row, start_row = p_ref[0, 0:1, :], p_ref[0, 1:2, :]

        def step(p, dq):
            rows = pl.ds(pl.multiple_of(p * CHUNK, CHUNK), CHUNK)
            at_key = key_at[rows, :]
            seen = (at_key >= start_row) & (at_key <= at_row)
            k0, k1 = klo[rows, :], khi[rows, :]
            s0 = jnp.where(seen, dot(k0, q_block, NT), MASKED)
            s1 = jnp.where(seen, dot(k1, q_block, NT), MASKED)
            p0 = jnp.exp(s0 - total[0:1, :])
            p1 = jnp.exp(s1 - total[1:2, :])
            d0 = (p0 * (dot(vlo[rows, :], do_block, NT) - delta[0:1, :])).astype(BF16)
            d1 = (p1 * (dot(vhi[rows, :], do_block, NT) - delta[1:2, :])).astype(BF16)
            left = jnp.concatenate([d0, d1, p0.astype(BF16), p1.astype(BF16)], axis=1)
            acc[rows, :] += dot(left, right)
            return dq + dot(d0, k0, TN) + dot(d1, k1, TN)

        dq = lax.fori_loop(first_ref[i], i + 1, step, jnp.zeros((ROWS, 128), F32))
        dq_ref[0] = dq * 0.125

        @pl.when(i == CHIPS - 1)
        def _():
            core = lax.rem(lax.axis_index("ctx"), 2)

            def part(s, _):
                mine = pl.ds(pl.multiple_of((2 * s + core) * ROWS, ROWS), ROWS)
                other = pl.ds(pl.multiple_of((2 * s + 1 - core) * ROWS, ROWS), ROWS)
                mine_ref[s] = acc[mine, :]
                other_ref[s] = acc[other, :].astype(BF16)
                return 0

            lax.fori_loop(0, CHIPS, part, 0)

    def block(*shape):
        return pl.BlockSpec((1,) + shape, lambda i, first: (i, 0, 0))

    whole = pl.BlockSpec((KEYS, 128), lambda i, first: (0, 0))
    return pl.pallas_call(
        body,
        name="attend_back",
        out_shape=[
            jax.ShapeDtypeStruct((CHIPS, ROWS, 128), F32),
            jax.ShapeDtypeStruct((CHIPS, ROWS, 128), F32),
            jax.ShapeDtypeStruct((CHIPS, ROWS, 128), BF16),
        ],
        grid_spec=pltpu.PrefetchScalarGridSpec(
            num_scalar_prefetch=1,
            grid=(CHIPS,),
            in_specs=[
                block(ROWS, 128),
                whole,
                block(ROWS, 128),
                block(ROWS, 128),
                block(ROWS, 128),
                pl.BlockSpec((CHIPS, 1, CHUNK), lambda i, first: (0, 0, 0)),
                block(2, ROWS),
            ],
            out_specs=[block(ROWS, 128)] + [pl.BlockSpec((CHIPS, ROWS, 128), lambda i, first: (0, 0, 0))] * 2,
            scratch_shapes=[pltpu.VMEM((KEYS, 128), BF16)] * 4
            + [pltpu.VMEM((KEYS, 128), F32), pltpu.VMEM((KEYS, ROWS), F32)],
        ),
        compiler_params=pltpu.CompilerParams(vmem_limit_bytes=60 * MIB),
    )(first_chunk, q, kv, d_out, out, log_total, key_pos, places)


def whole(*shape):
    return pl.BlockSpec(shape, lambda i: (0,) * len(shape))


def columns(block, width=WIDTH):
    return pl.BlockSpec((WIDTH, width), lambda i: (0, block))


def finish_attention(attended, w_out, tokens, gains):
    def body(a_ref, w_ref, t_ref, g_ref, r_ref, f_ref):
        branch = dot(a_ref[...], w_ref[...]).astype(BF16).astype(F32)
        resid = t_ref[...].astype(F32) + branch
        r_ref[...] = resid
        scale = row_scale(jnp.sum(resid * resid, axis=1, keepdims=True), WIDTH)
        f_ref[...] = (resid * scale * g_ref[3:4, :]).astype(BF16)

    return compute_call(
        body,
        "finish_attention",
        [jax.ShapeDtypeStruct((ROWS, WIDTH), F32), jax.ShapeDtypeStruct((ROWS, WIDTH), BF16)],
        [attended, w_out, tokens, gains],
        grid=(1,),
        in_specs=[whole(ROWS, WIDTH), columns(2), whole(ROWS, WIDTH), whole(8, WIDTH)],
        out_specs=[whole(ROWS, WIDTH)] * 2,
    )


def experts(rows, grads, meta, meta_t, w_gate, w_up, w_down):
    half = SLOTS // 2

    def body(
        x_ref, g_ref, m_ref, mt_ref, wg_ref, wu_ref, wd_ref,
        xin_ref, dr_ref, act_ref, dg_ref, du_ref, out_ref, dx_ref,
        made, back, weight,
    ):
        e = pl.program_id(0)

        @pl.when(e == 0)
        def _():
            slot_id = lax.broadcasted_iota(jnp.int32, (PAIR_CAP, PAIR_ROWS), 0).astype(F32)

            def pick(p, _):
                meta_p = m_ref[p]
                parts, gates = [], []
                for k in range(LOCAL):
                    hit = slot_id == meta_p[k : k + 1, :]
                    parts.append(jnp.where(hit, 1.0, 0.0).astype(BF16))
                    gates.append(
                        jnp.sum(jnp.where(hit, meta_p[4 + k : 5 + k, :], 0.0), axis=1, keepdims=True)
                    )
                chosen = jnp.concatenate(parts, axis=0)
                rows_p = dot(chosen, x_ref[p]).astype(BF16)
                grads_p = dot(chosen, g_ref[p])
                at = pl.ds(pl.multiple_of(p * PAIR_CAP, PAIR_CAP), PAIR_CAP)
                for k in range(LOCAL):
                    piece = slice(k * PAIR_CAP, (k + 1) * PAIR_CAP)
                    xin_ref[k, at, :] = rows_p[piece]
                    dr_ref[k, at, :] = (grads_p[piece] * gates[k]).astype(BF16)
                    weight[k, at, :] = gates[k]
                return 0

            lax.fori_loop(0, PAIRS, pick, 0)

        def work(h, _):
            at = pl.ds(pl.multiple_of(h * half, half), half)
            x = xin_ref[e, at, :]
            dr = dr_ref[e, at, :]
            gate = dot(x, wg_ref[0])
            up = dot(x, wu_ref[0])
            sig = jax.nn.sigmoid(gate)
            silu = gate * sig
            act = (silu * up).astype(BF16)
            act_ref[0, at, :] = act
            d_act = dot(dr, wd_ref[0], NT)
            d_gate = (d_act * up * sig * (1.0 + gate * (1.0 - sig))).astype(BF16)
            d_up = (d_act * silu).astype(BF16)
            dg_ref[0, at, :] = d_gate
            du_ref[0, at, :] = d_up
            y = (dot(act, wd_ref[0]) * weight[e, at, :]).astype(BF16)
            dch = (dot(d_gate, wg_ref[0], NT) + dot(d_up, wu_ref[0], NT)).astype(BF16)
            place_at = pl.ds(pl.multiple_of(e * PAIR_CAP, PAIR_CAP), PAIR_CAP)
            for k in range(2):
                piece = slice(k * PAIR_CAP, (k + 1) * PAIR_CAP)
                made[2 * h + k, place_at, :] = y[piece]
                back[2 * h + k, place_at, :] = dch[piece]
            return 0

        lax.fori_loop(0, 2, work, 0)

        @pl.when(e == LOCAL - 1)
        def _():
            lane_id = lax.broadcasted_iota(jnp.int32, (PAIR_ROWS, PAIR_SLOTS), 1).astype(F32)

            def give(p, _):
                meta_p = mt_ref[p]
                chosen = jnp.zeros((PAIR_ROWS, PAIR_SLOTS), F32)
                for k in range(LOCAL):
                    spot = meta_p[:, k : k + 1]
                    lane = jnp.where(spot < 0.0, -1.0, spot + float(k * PAIR_CAP))
                    chosen = chosen + jnp.where(lane_id == lane, 1.0, 0.0)
                chosen = chosen.astype(BF16)
                dx_ref[p] = dot(chosen, back[p]).astype(BF16)
                out_ref[p] = dot(chosen, made[p]).astype(BF16)
                return 0

            lax.fori_loop(0, PAIRS, give, 0)

    def fixed(*shape):
        return pl.BlockSpec(shape, lambda e: (0,) * len(shape), pipeline_mode=pl.Buffered(1))

    def each(*shape):
        return pl.BlockSpec((1,) + shape, lambda e: (e, 0, 0))

    return compute_call(
        body,
        "experts",
        [
            jax.ShapeDtypeStruct((LOCAL, SLOTS, WIDTH), BF16),
            jax.ShapeDtypeStruct((LOCAL, SLOTS, WIDTH), BF16),
            jax.ShapeDtypeStruct((LOCAL, SLOTS, FF), BF16),
            jax.ShapeDtypeStruct((LOCAL, SLOTS, FF), BF16),
            jax.ShapeDtypeStruct((LOCAL, SLOTS, FF), BF16),
            jax.ShapeDtypeStruct((PAIRS, PAIR_ROWS, WIDTH), BF16),
            jax.ShapeDtypeStruct((PAIRS, PAIR_ROWS, WIDTH), BF16),
        ],
        [rows, grads, meta, meta_t, w_gate, w_up, w_down],
        vmem=60,
        grid=(LOCAL,),
        in_specs=[
            fixed(PAIRS, PAIR_ROWS, WIDTH),
            fixed(PAIRS, PAIR_ROWS, WIDTH),
            fixed(PAIRS, 8, PAIR_ROWS),
            fixed(PAIRS, PAIR_ROWS, 8),
            each(WIDTH, FF),
            each(WIDTH, FF),
            each(FF, WIDTH),
        ],
        out_specs=[
            fixed(LOCAL, SLOTS, WIDTH),
            fixed(LOCAL, SLOTS, WIDTH),
            each(SLOTS, FF),
            each(SLOTS, FF),
            each(SLOTS, FF),
            fixed(PAIRS, PAIR_ROWS, WIDTH),
            fixed(PAIRS, PAIR_ROWS, WIDTH),
        ],
        scratch_shapes=[
            pltpu.VMEM((PAIRS, PAIR_SLOTS, WIDTH), BF16),
            pltpu.VMEM((PAIRS, PAIR_SLOTS, WIDTH), BF16),
            pltpu.VMEM((LOCAL, SLOTS, 1), F32),
        ],
    )


def norm_back(values, total_squares, width, weighted, mask=None):
    scale = row_scale(total_squares, width)
    inner = jnp.sum(weighted * values, axis=1, keepdims=True) * (1.0 / width)
    return scale * weighted - values * (scale * scale * scale) * inner, scale


def back_to_branch(d_ffn, resid, cotangent, gains, w_out):
    def body(p_ref, r_ref, c_ref, g_ref, w_ref, dr_ref, db_ref, da_ref, gg_ref):
        incoming = p_ref[...]
        resid_v = r_ref[...]
        squares = jnp.sum(resid_v * resid_v, axis=1, keepdims=True)
        d_norm, scale = norm_back(resid_v, squares, WIDTH, incoming * g_ref[3:4, :])
        gg_ref[...] = jnp.sum(incoming * resid_v * scale, axis=0, keepdims=True)
        d_resid = c_ref[...].astype(F32) + d_norm
        dr_ref[...] = d_resid
        d_branch = d_resid.astype(BF16)
        db_ref[...] = d_branch
        da_ref[...] = dot(d_branch, w_ref[...], NT).astype(BF16)

    return compute_call(
        body,
        "back_to_branch",
        [
            jax.ShapeDtypeStruct((ROWS, WIDTH), F32),
            jax.ShapeDtypeStruct((ROWS, WIDTH), BF16),
            jax.ShapeDtypeStruct((ROWS, WIDTH), BF16),
            jax.ShapeDtypeStruct((1, WIDTH), F32),
        ],
        [d_ffn, resid, cotangent, gains, w_out],
        grid=(1,),
        in_specs=[whole(ROWS, WIDTH)] * 3 + [whole(8, WIDTH), columns(2)],
        out_specs=[whole(ROWS, WIDTH)] * 3 + [whole(1, WIDTH)],
    )


def out_grads(attended, d_branch):
    def body(a_ref, d_ref, o_ref):
        def part(r, _):
            at = pl.ds(pl.multiple_of(r * 256, 256), 256)
            o_ref[at, :] = dot(a_ref[:, at], d_ref[...], TN).astype(BF16)
            return 0

        lax.fori_loop(0, 4, part, 0)

    return compute_call(
        body, "out_grads", [jax.ShapeDtypeStruct((WIDTH, WIDTH), BF16)], [attended, d_branch]
    )[0]


def unturn_heads(dq, dkv, dkv_other, q_lin, kv_lin, gains, cosine, sine):
    def body(dq_ref, dk_ref, do_ref, q_ref, kv_ref, g_ref, c_ref, n_ref, eq_ref, ek_ref, s_ref):
        gain = g_ref[own_chip()]
        keys = key_lanes()

        def one(i, _):
            cos, sin = c_ref[i], -n_ref[i]
            e_q = turn(dq_ref[i], cos, sin)
            eq_ref[i] = e_q
            both = dk_ref[i] + do_ref[i].astype(F32)
            e_kv = turn(both, jnp.where(keys, cos, 1.0), jnp.where(keys, sin, 0.0))
            ek_ref[i] = e_kv
            s_ref[i] = both_totals(e_q * gain[1:2, :] * q_ref[i], e_kv * gain[2:3, :] * kv_ref[i])
            return 0

        lax.fori_loop(0, CHIPS, one, 0)

    return compute_call(
        body,
        "unturn_heads",
        [jax.ShapeDtypeStruct((CHIPS, ROWS, 128), F32)] * 2 + [jax.ShapeDtypeStruct((CHIPS, 2, ROWS), F32)],
        [dq, dkv, dkv_other, q_lin, kv_lin, gains, cosine, sine],
    )


def head_grads(e_q, e_kv, inner, squares, q_lin, kv_lin, normed, gains):
    def body(eq_ref, ek_ref, i_ref, s_ref, q_ref, kv_ref, n_ref, g_ref, dq_ref, dk_ref, w_ref, gg_ref):
        gain = g_ref[own_chip()]
        keys = key_lanes()

        def one(i, carry):
            q_sum, kv_sum = carry
            inner = i_ref[0, i]
            for c in range(1, CHIPS):
                inner = inner + i_ref[c, i]
            q_scale = row_scale(down_rows(s_ref[i], 0), WIDTH)
            k_scale = row_scale(down_rows(s_ref[i], 1), WIDTH // 2)
            q_cut = q_scale * q_scale * q_scale * down_rows(inner, 0) * (1.0 / WIDTH)
            k_cut = k_scale * k_scale * k_scale * down_rows(inner, 1) * (2.0 / WIDTH)
            kv_scale = jnp.where(keys, k_scale, 1.0)
            k_cut = jnp.where(keys, k_cut, 0.0)
            q, e = q_ref[i], eq_ref[i]
            dq_ref[i] = (q_scale * (e * gain[1:2, :]) - q * q_cut).astype(BF16)
            q_sum = q_sum + jnp.sum(e * q * q_scale, axis=0, keepdims=True)
            kv, e = kv_ref[i], ek_ref[i]
            dk_ref[i] = (kv_scale * (e * gain[2:3, :]) - kv * k_cut).astype(BF16)
            kv_sum = kv_sum + jnp.sum(e * kv * kv_scale, axis=0, keepdims=True)
            return q_sum, kv_sum

        none = jnp.zeros((1, 128), F32)
        q_sum, kv_sum = lax.fori_loop(0, CHIPS, one, (none, none))
        gg_ref[...] = jnp.concatenate([q_sum, kv_sum], axis=0)
        d_q = dq_ref[...].reshape(CHIPS * ROWS, 128)
        d_kv = dk_ref[...].reshape(CHIPS * ROWS, 128)

        def part(r, _):
            at = pl.ds(pl.multiple_of(r * 256, 256), 256)
            n = n_ref[:, at]
            w_ref[0, at, :] = dot(n, d_q, TN).astype(BF16)
            w_ref[1, at, :] = dot(n, d_kv, TN).astype(BF16)
            return 0

        lax.fori_loop(0, 4, part, 0)

    return compute_call(
        body,
        "head_grads",
        [jax.ShapeDtypeStruct((CHIPS, ROWS, 128), BF16)] * 2
        + [jax.ShapeDtypeStruct((2, WIDTH, 128), BF16), jax.ShapeDtypeStruct((2, 128), F32)],
        [e_q, e_kv, inner, squares, q_lin, kv_lin, normed, gains],
    )


def apart(pieces):
    first, second = pieces
    keys = key_lanes()
    return (
        jnp.where(keys, first, pltpu.roll(second, 64, 1)),
        jnp.where(keys, pltpu.roll(first, 64, 1), second),
    )


def back_to_input(d_q, d_kv, tokens, d_resid, weights, gains):
    def body(dq_ref, dkv_ref, t_ref, r_ref, w_ref, g_ref, di_ref, gg_ref):
        keys, values = [], []
        for c in range(4):
            k, v = apart([dkv_ref[:, (2 * c + j) * 128 : (2 * c + j + 1) * 128].astype(F32) for j in range(2)])
            keys.append(k.astype(BF16))
            values.append(v.astype(BF16))
        left = jnp.concatenate([dq_ref[...]] + keys + values, axis=1)
        d_normed = dot(left, w_ref[...], NT)
        d_normed = d_normed.astype(BF16).astype(F32)
        x = t_ref[...].astype(F32)
        squares = jnp.sum(x * x, axis=1, keepdims=True)
        d_norm, scale = norm_back(x, squares, WIDTH, d_normed * g_ref[0:1, :])
        gg_ref[...] = jnp.sum(d_normed * x * scale, axis=0, keepdims=True)
        di_ref[...] = r_ref[...] + d_norm

    return compute_call(
        body,
        "back_to_input",
        [jax.ShapeDtypeStruct((ROWS, WIDTH), F32), jax.ShapeDtypeStruct((1, WIDTH), F32)],
        [d_q, d_kv, tokens, d_resid, weights, gains],
        grid=(1,),
        in_specs=[whole(ROWS, WIDTH)] * 4 + [columns(0, 2 * WIDTH), whole(8, WIDTH)],
        out_specs=[whole(ROWS, WIDTH), whole(1, WIDTH)],
    )


def deliver(resid, layer_keep, layer_got, dense, out_grad, gain_sums, expert_sums):
    def body(r_ref, k_ref, g_ref, d_ref, o_ref, s_ref, eg_ref, eu_ref, ed_ref, lo, wq, wk, wv, wo, ga, gq, gk, gf, eg, eu, ed):
        lo[...] = (r_ref[...] + k_ref[...] + g_ref[...].astype(F32)).astype(BF16)
        wq[...] = d_ref[0].astype(F32)
        for c in range(4):
            k, v = apart([d_ref[1, :, (2 * c + j) * 128 : (2 * c + j + 1) * 128].astype(F32) for j in range(2)])
            wk[:, c * 128 : (c + 1) * 128] = k
            wv[:, c * 128 : (c + 1) * 128] = v
        wo[...] = o_ref[...].astype(F32)
        ga[...] = s_ref[0:1, :]
        gq[...] = s_ref[1:2, :]
        gk[...] = s_ref[2:3, 0:64]
        gf[...] = s_ref[3:4, :]
        eg[...] = eg_ref[...]
        eu[...] = eu_ref[...]
        ed[...] = ed_ref[...]

    return compute_call(
        body,
        "deliver",
        [
            jax.ShapeDtypeStruct((ROWS, WIDTH), BF16),
            jax.ShapeDtypeStruct((128, WIDTH), F32),
            jax.ShapeDtypeStruct((128, 512), F32),
            jax.ShapeDtypeStruct((128, 512), F32),
            jax.ShapeDtypeStruct((128, WIDTH), F32),
            jax.ShapeDtypeStruct((1, 128), F32),
            jax.ShapeDtypeStruct((1, 128), F32),
            jax.ShapeDtypeStruct((1, 64), F32),
            jax.ShapeDtypeStruct((1, 128), F32),
        ]
        + [jax.ShapeDtypeStruct(a.shape, F32) for a in expert_sums],
        [resid, layer_keep, layer_got, dense, out_grad, gain_sums, *expert_sums],
    )


def sum_blocks(blocks):
    return jnp.sum(blocks.astype(F32), axis=0)


def per_device(
    tokens,
    cotangent,
    lengths,
    deal_perm,
    routes,
    gate_logits,
    norm_attn,
    norm_query,
    norm_key,
    norm_ffn,
    w_query,
    w_key,
    w_value,
    w_out,
    w_gate,
    w_up,
    w_down,
):
    ctx_index = lax.axis_index("ctx")
    core, chip = lax.rem(ctx_index, 2), ctx_index // 2
    tokens, cotangent = tokens[0], cotangent[0]

    weights = jnp.concatenate([w_query, w_key, w_value, w_out], axis=1)
    gain_shard = jnp.stack(
        [
            norm_attn.astype(F32),
            norm_query.astype(F32),
            jnp.concatenate([norm_key.astype(F32), jnp.ones((64,), F32)]),
            norm_ffn.astype(F32),
        ]
        + [jnp.zeros((128,), F32)] * 4
    )
    rows_group, weights, gain_all = gather_inputs(tokens, weights, gain_shard)
    weights = weights.reshape(WIDTH, 3 * WIDTH)
    gains = gain_all.transpose(1, 0, 2).reshape(8, WIDTH)

    pieces = jnp.arange(CTX, dtype=jnp.int32)[:, None] * CTX + deal_perm[0]
    positions = (pieces[:, :, None] * 12 + jnp.arange(12, dtype=jnp.int32)).reshape(CTX, ROWS)
    ends = jnp.cumsum(lengths[0])
    starts = ends - lengths[0]
    row_start = jnp.zeros_like(positions)
    for k in range(1, starts.shape[0]):
        row_start = jnp.where(positions >= starts[k], starts[k], row_start)
    paired = lambda a: lax.dynamic_index_in_dim(a.reshape(CHIPS, 2, ROWS), core, 1, keepdims=False)
    query_pos, query_start = paired(positions), paired(row_start)
    places = jnp.stack([query_pos, query_start], axis=1).astype(F32)
    key_pos = positions.reshape(CHIPS, 1, CHUNK).astype(F32)
    first_chunk = jnp.min(query_start, axis=1) // CHUNK

    normed, q_lin, kv_lin, totals = project(
        rows_group.reshape(CHIPS * ROWS, WIDTH), weights, gains, chip.reshape(1)
    )
    q_lin, kv_lin = q_lin.reshape(CHIPS, ROWS, 128), kv_lin.reshape(CHIPS, ROWS, 128)
    totals, cotangent_late = lax.optimization_barrier((share_totals(totals, 3), cotangent))
    grads_all = lax.all_gather(cotangent_late, "exp", axis=0, tiled=True)
    q_all, kv_half, squares, cosine, sine = turn_heads(q_lin, kv_lin, totals, places, gain_all)
    kv_all = pair_keys(kv_half).reshape(KEYS, 128)
    out_low, out_wide, log_total = attend(q_all, kv_all, key_pos, places, first_chunk)
    attended = collect_heads(out_low)
    resid, ffn_rows = finish_attention(attended, weights, tokens, gains)
    rows_all, meta_all = gather_rows(ffn_rows, route(routes[0].T, gate_logits[0].T))

    shift = jnp.array([0.0, float(CAP)], F32)[None, None, :, None]
    spots = meta_all[:, :LOCAL].reshape(PAIRS, 2, LOCAL, ROWS).transpose(0, 2, 1, 3)
    spots = jnp.where(spots < 0.0, -1.0, spots + shift).reshape(PAIRS, LOCAL, PAIR_ROWS)
    gates = meta_all[:, LOCAL:].reshape(PAIRS, 2, LOCAL, ROWS).transpose(0, 2, 1, 3)
    pair_meta = jnp.concatenate([spots, gates.reshape(PAIRS, LOCAL, PAIR_ROWS)], axis=1)
    rows_in, d_rows, act, d_gate, d_up, out_parts, d_parts = experts(
        rows_all.reshape(PAIRS, PAIR_ROWS, WIDTH),
        grads_all.reshape(PAIRS, PAIR_ROWS, WIDTH),
        pair_meta,
        pair_meta.transpose(0, 2, 1),
        w_gate,
        w_up,
        w_down,
    )
    gate_grad, up_grad, down_grad, d_ffn, layer_keep, layer_give = settle_experts(
        rows_in,
        d_rows,
        act,
        d_gate,
        d_up,
        d_parts.reshape(2, 4, ROWS, WIDTH),
        out_parts.reshape(2, 4, ROWS, WIDTH),
    )
    d_resid, d_branch, d_attended, ffn_gain_grad = back_to_branch(
        d_ffn, resid, cotangent, gains, weights
    )
    d_out = spread_grads(d_attended)
    out_part = lax.psum_scatter(
        out_grads(attended, d_branch), "exp", scatter_dimension=0, tiled=True
    )
    dq, dkv_mine, dkv_other = attend_back(
        q_all, kv_all, d_out, out_wide, log_total, key_pos, places, first_chunk
    )
    e_q, e_kv, inner = unturn_heads(
        dq, dkv_mine, pair_grads(dkv_other), q_lin, kv_lin, gain_all, cosine, sine
    )
    inner = share_totals(inner, 9)
    d_q_heads, d_kv_heads, w_parts, head_gains = head_grads(
        e_q, e_kv, inner, squares, q_lin, kv_lin, normed, gain_all
    )
    d_q, d_kv, dense, out_grad, layer_got = settle_grads(
        d_q_heads, d_kv_heads, w_parts, out_part, layer_give
    )
    input_grad, attn_gain_grad = back_to_input(d_q, d_kv, tokens, d_resid, weights, gains)
    here = (jnp.arange(EXP) == chip)[:, None, None]
    gain_sums = sum_gains(
        jnp.concatenate(
            [
                attn_gain_grad.reshape(EXP, 1, 128),
                jnp.where(here, head_gains[None], 0.0),
                ffn_gain_grad.reshape(EXP, 1, 128),
                jnp.zeros((EXP, 4, 128), F32),
            ],
            axis=1,
        )
    )
    outs = deliver(
        resid, layer_keep, layer_got, dense, out_grad, gain_sums, (gate_grad, up_grad, down_grad)
    )
    return (
        outs[0][None],
        input_grad[None],
        *outs[1:5],
        *[g.reshape(-1) for g in outs[5:9]],
        *outs[9:],
    )


def solution(mesh):
    in_specs = (
        P("exp", "ctx", None),
        P("exp", "ctx", None),
        P("exp", None),
        P("exp", None, None),
        P("exp", "ctx", None),
        P("exp", "ctx", None),
        P("exp"),
        P("exp"),
        P("exp"),
        P("exp"),
        P("exp", None),
        P("exp", None),
        P("exp", None),
        P("exp", None),
        P("exp", None, None),
        P("exp", None, None),
        P("exp", None, None),
    )
    out_specs = (
        P("exp", "ctx", None),
        P("exp", "ctx", None),
        P("exp", None),
        P("exp", None),
        P("exp", None),
        P("exp", None),
        P("exp"),
        P("exp"),
        P("exp"),
        P("exp"),
        P("exp", "ctx", None),
        P("exp", "ctx", None),
        P("exp", "ctx", None),
    )
    return jax.shard_map(
        per_device, mesh=mesh, in_specs=in_specs, out_specs=out_specs, check_vma=False
    )
```

```python
import jax
import jax.numpy as jnp
from jax import lax
from jax.experimental import pallas as pl
from jax.experimental.pallas import tpu as pltpu
from jax.sharding import PartitionSpec as P

HEADS = 16
KV_HEADS = 8
EPSILON = 1e-05
ROPE_BASE = 10000.0
MASKED = -1e30

MESH = pl.DeviceIdType.MESH
CTX = 16
EXP = 8
CHIPS = 8
ROWS = 192
WIDTH = 1024
FF = 512
LOCAL = 4
CAP = 72
PAIRS = EXP // 2
PAIR_ROWS = 2 * ROWS
PAIR_CAP = 2 * CAP
SLOTS = EXP * CAP
PAIR_SLOTS = LOCAL * PAIR_CAP
KEYS = CTX * ROWS
CHUNK = 2 * ROWS
MIB = 1 << 20
FAR_FIRST = (6, 2, 5, 7, 4, 1, 3)

ANY_SPEC = pl.BlockSpec(memory_space=pl.ANY)
F32 = jnp.float32
BF16 = jnp.bfloat16


def dot(a, b, dims=((1,), (0,))):
    return lax.dot_general(a, b, (dims, ((), ())), preferred_element_type=F32)


NT = ((1,), (1,))
TN = ((0,), (0,))


def comm_call(body, name, collective_id, outs, ins, copies, in_specs=None):
    return pl.pallas_call(
        body,
        name=name,
        out_shape=outs,
        in_specs=in_specs or [ANY_SPEC] * len(ins),
        out_specs=[ANY_SPEC] * len(outs),
        scratch_shapes=[
            pltpu.SemaphoreType.DMA((copies,)),
            pltpu.SemaphoreType.DMA((copies,)),
            pltpu.SemaphoreType.DMA((8,)),
        ],
        compiler_params=pltpu.CompilerParams(
            collective_id=collective_id, has_side_effects=True, vmem_limit_bytes=60 * MIB
        ),
    )(*ins)


class Copier:
    def __init__(self, send_sem, recv_sem, local_sem):
        self.send_sem, self.recv_sem, self.local_sem = send_sem, recv_sem, local_sem
        self.remote, self.local = [], []

    def send(self, src, dst, axis, index):
        at = len(self.remote)
        copy = pltpu.make_async_remote_copy(
            src_ref=src,
            dst_ref=dst,
            send_sem=self.send_sem.at[at],
            recv_sem=self.recv_sem.at[at],
            device_id={axis: index},
            device_id_type=MESH,
        )
        copy.start()
        self.remote.append([copy, False])
        return at

    def keep(self, src, dst):
        copy = pltpu.make_async_copy(src, dst, self.local_sem.at[len(self.local)])
        copy.start()
        self.local.append([copy, False])
        return len(self.local) - 1

    def arrived(self, at):
        self.remote[at][0].wait_recv()
        self.remote[at][1] = True

    def kept(self, at):
        self.local[at][0].wait()
        self.local[at][1] = True

    def finish(self):
        for copy, seen in self.remote:
            if not seen:
                copy.wait_recv()
        for copy, _ in self.remote:
            copy.wait_send()
        for copy, seen in self.local:
            if not seen:
                copy.wait()


def meet(partners):
    barrier = pltpu.get_barrier_semaphore()
    for axis, index in partners:
        pl.semaphore_signal(barrier, inc=1, device_id={axis: index}, device_id_type=MESH)
    pl.semaphore_wait(barrier, len(partners))


def place():
    ctx = lax.axis_index("ctx")
    core = lax.rem(ctx, 2)
    return ctx, ctx // 2, core, ctx + 1 - 2 * core


def ring_of(me):
    half, spot = me // 4, lax.rem(me, 4)
    over = (1 - half) * 4
    turns = [lax.rem(spot + d, 4) for d in (0, 1, 3, 2)]
    return tuple([half * 4 + t for t in turns] + [over + t for t in turns])


def relay(copier, own, slot, rows, ring, reach, landed=lambda partner: None):
    me, right, left, far, over, over_right, over_left, over_far = ring
    half = rows // 2
    low, high = pl.ds(0, half), pl.ds(half, half)

    def send(block, to, part, partner):
        return copier.send(block.at[part], slot(to).at[part], *reach(partner))

    def on(of, part, partner):
        return send(slot(of), of, part, partner)

    over_low = send(own, me, low, over)
    over_high = send(own, me, high, over)
    yield
    right_low = send(own, me, low, right)
    left_high = send(own, me, high, left)
    right_high = send(own, me, high, right)
    left_low = send(own, me, low, left)
    yield
    copier.arrived(right_low)
    far_right = on(left, low, right)
    copier.arrived(left_high)
    far_left = on(right, high, left)
    yield
    copier.arrived(over_low)
    next_right_low = on(over, low, right)
    next_left_low = on(over, low, left)
    copier.arrived(over_high)
    next_left_high = on(over, high, left)
    next_right_high = on(over, high, right)
    landed(over)
    yield
    copier.arrived(right_high)
    landed(left)
    copier.arrived(left_low)
    landed(right)
    yield
    copier.arrived(far_right)
    copier.arrived(far_left)
    landed(far)
    yield
    copier.arrived(next_right_low)
    far_right = on(over_left, low, right)
    copier.arrived(next_left_high)
    far_left = on(over_right, high, left)
    copier.arrived(next_right_high)
    landed(over_left)
    copier.arrived(next_left_low)
    landed(over_right)
    yield
    copier.arrived(far_right)
    copier.arrived(far_left)
    landed(over_far)


def side_by_side(*relays):
    for _ in zip(*relays):
        pass
    for one in relays:
        for _ in one:
            pass


def gather_rows(rows, meta):
    def body(x_ref, m_ref, o_ref, mo_ref, send_sem, recv_sem, local_sem):
        ring = ring_of(lax.axis_index("exp"))
        me = ring[0]
        to_exp = lambda p: ("exp", p)
        copier = Copier(send_sem, recv_sem, local_sem)
        meet([to_exp(p) for p in ring[1:]])
        copier.keep(x_ref, o_ref.at[me])
        copier.keep(m_ref.at[me], mo_ref.at[me])
        for p in ring[1:]:
            copier.send(m_ref.at[p], mo_ref.at[me], *to_exp(p))
        side_by_side(relay(copier, x_ref, lambda s: o_ref.at[s], rows.shape[0], ring, to_exp))
        copier.finish()

    return comm_call(
        body,
        "gather_rows",
        2,
        [
            jax.ShapeDtypeStruct((EXP,) + rows.shape, rows.dtype),
            jax.ShapeDtypeStruct(meta.shape, F32),
        ],
        [rows, meta],
        21,
        in_specs=[pl.BlockSpec(memory_space=pltpu.VMEM)] * 2,
    )


def lanes(index):
    return pl.ds(pl.multiple_of(index * 128, 128), 128)


def collect_heads(blocks):
    def body(x_ref, o_ref, send_sem, recv_sem, local_sem):
        _, chip, core, _ = place()
        chips = [lax.rem(chip + d, CHIPS) for d in FAR_FIRST]
        copier = Copier(send_sem, recv_sem, local_sem)
        meet([("ctx", 2 * p + core) for p in chips])
        for p in chips:
            copier.send(x_ref.at[p], o_ref.at[:, lanes(chip)], "ctx", 2 * p + core)
        copier.keep(x_ref.at[chip], o_ref.at[:, lanes(chip)])
        copier.finish()

    return comm_call(
        body, "collect_heads", 4, [jax.ShapeDtypeStruct((ROWS, WIDTH), BF16)], [blocks], 7
    )[0]


def spread_grads(rows):
    def body(x_ref, o_ref, send_sem, recv_sem, local_sem):
        _, chip, core, _ = place()
        chips = [lax.rem(chip + d, CHIPS) for d in FAR_FIRST]
        copier = Copier(send_sem, recv_sem, local_sem)
        meet([("ctx", 2 * p + core) for p in chips])
        for p in chips:
            copier.send(x_ref.at[:, lanes(p)], o_ref.at[chip], "ctx", 2 * p + core)
        copier.keep(x_ref.at[:, lanes(chip)], o_ref.at[chip])
        copier.finish()

    return comm_call(
        body, "spread_grads", 5, [jax.ShapeDtypeStruct((CHIPS, ROWS, 128), BF16)], [rows], 7
    )[0]


def settle_experts(rows, d_rows, act, d_gate, d_up, d_parts, layer_parts):
    def body(
        x_ref, r_ref, a_ref, g_ref, u_ref, p_ref, l_ref, gate_out, up_out, down_a_out, down_b_out, dx_out, keep_out, give_out,
        x_v, r_v, a_v, g_v, u_v, gate, up, down, gate_o, up_o, down_o, gate_a, down_a, up_b, down_b,
        to_z, from_z, d_own, d_right, d_left, d_low, d_high, d_from, l_own, l_right, l_left, l_low, l_high, l_from, send_sem, recv_sem, local_sem,
    ):
        _, chip, core, sibling = place()
        me = lax.axis_index("exp")
        zl, x = me // 4, lax.rem(me, 4)
        zh, y = chip // 4, lax.rem(chip, 4)
        at_ctx = lambda z, yy: ("ctx", z * 8 + yy * 2 + core)
        over = at_ctx(1 - zh, y)
        columns = [lax.rem(y + d, 4) for d in (1, 3, 2)]
        right, left, far = [lax.rem(x + d, 4) for d in (1, 3, 2)]
        at_exp = lambda p: ("exp", zl * 4 + p)
        low, high = pl.ds(0, ROWS // 2), pl.ds(ROWS // 2, ROWS // 2)
        copier = Copier(send_sem, recv_sem, local_sem)
        loads = []
        for e in range(LOCAL):
            pairs = ((x_ref, x_v), (r_ref, r_v), (a_ref, a_v), (g_ref, g_v), (u_ref, u_v))
            loads.append([copier.keep(src.at[e], dst.at[e]) for src, dst in pairs])
        parts = (p_ref, d_own, d_right, d_left, d_low, d_high, d_from)
        layers = (l_ref, l_own, l_right, l_left, l_low, l_high, l_from)

        def fetch(src, own, to_right, to_left, *_):
            return [
                copier.keep(src.at[:, x], own),
                copier.keep(src.at[:, right, low], to_right),
                copier.keep(src.at[:, left, high], to_left),
            ]

        part_loads, layer_loads = fetch(*parts), fetch(*layers)
        meet(
            [("ctx", sibling), over]
            + [at_ctx(zh, c) for c in columns]
            + [at_exp(right), at_exp(left)]
            + [("exp", (1 - zl) * 4 + x)]
        )

        def set_out(src, own, to_right, to_left, in_low, in_high, arrived):
            return [
                copier.send(src.at[:, far, low], in_low, *at_exp(right)),
                copier.send(src.at[:, far, high], in_high, *at_exp(left)),
                copier.send(src.at[:, right, high], arrived.at[0, :, high], *at_exp(right)),
                copier.send(src.at[:, left, low], arrived.at[1, :, low], *at_exp(left)),
            ]

        def pass_on(stage, loads_of, src, own, to_right, to_left, in_low, in_high, arrived):
            for at in loads_of:
                copier.kept(at)
            for at in stage[:2]:
                copier.arrived(at)

            def add(r, _):
                at = pl.ds(pl.multiple_of(r * 48, 16), 48)
                for z in range(2):
                    for mine, other in ((to_right, in_low), (to_left, in_high)):
                        mine[z, at, :] = (mine[z, at, :].astype(F32) + other[z, at, :].astype(F32)).astype(BF16)
                return 0

            lax.fori_loop(0, 2, add, 0)
            return stage[2:] + [
                copier.send(to_right, arrived.at[0, :, low], *at_exp(right)),
                copier.send(to_left, arrived.at[1, :, high], *at_exp(left)),
            ]

        part_stage = set_out(*parts)

        def work(e):
            for at in loads[e]:
                copier.kept(at)

            def wide(r, _):
                rows_r = x_v[e, :, pl.ds(pl.multiple_of(r * 256, 256), 256)]
                for d_v, o_v in ((g_v, gate), (u_v, up)):
                    grad = dot(rows_r, d_v[e], TN).astype(BF16)
                    for k in range(4):
                        o_v[k % 2, r // 2, 2 * lax.rem(r, 2) + k // 2, e] = grad[k * 64 : (k + 1) * 64]
                return 0

            lax.fori_loop(0, 4, wide, 0)

            def tall(r, _):
                act_r = a_v[e, :, pl.ds(pl.multiple_of(r * 256, 256), 256)]
                grad = dot(act_r, r_v[e], TN).astype(BF16)
                for k in range(8):
                    down[k % 2, r, k // 2, e] = grad[k * 32 : (k + 1) * 32]
                return 0

            lax.fori_loop(0, 2, tall, 0)
            return [
                copier.send(full.at[1 - core, :, :, e], other.at[:, :, e], "ctx", sibling)
                for full, other in ((gate, gate_o), (up, up_o), (down, down_o))
            ]

        first_a, first_b = [], []

        def join(e, swaps):
            for at in swaps:
                copier.arrived(at)

            def add(c, _):
                z, yy = c // 4, lax.rem(c, 4)
                for full, other in ((gate, gate_o), (up, up_o), (down, down_o)):
                    both = full[core, z, yy, e].astype(F32) + other[z, yy, e].astype(F32)
                    full[core, z, yy, e] = both.astype(BF16)
                return 0

            lax.fori_loop(0, CHIPS, add, 0)
            first_a.append(copier.send(gate.at[core, 1 - zh, :, e], gate_a.at[:, e], *over))
            if e < 2:
                first_a.append(copier.send(down.at[core, 1 - zh, :, e], down_a.at[:, e], *over))
            for c in columns:
                to = at_ctx(zh, c)
                first_b.append(copier.send(up.at[core, :, c, e], up_b.at[y, :, e], *to))
                if e >= 2:
                    first_b.append(copier.send(down.at[core, :, c, e], down_b.at[y, :, e - 2], *to))

        swaps = work(0)
        later = work(1)
        join(0, swaps)
        part_stage = pass_on(part_stage, part_loads, *parts)
        layer_stage = set_out(*layers)
        swaps = later
        later = work(2)
        join(1, swaps)
        swaps = later
        later = work(3)
        join(2, swaps)
        join(3, later)

        def sum_up(stage, own, arrived, keep_ref, give_ref):
            for at in stage:
                copier.arrived(at)

            def add(r, _):
                at = pl.ds(pl.multiple_of(r * 48, 16), 48)
                keep, give = [
                    own[z, at, :].astype(F32) + arrived[0, z, at, :].astype(F32) + arrived[1, z, at, :].astype(F32)
                    for z in (zl, 1 - zl)
                ]
                keep_ref[at, :] = keep
                give_ref[at, :] = give.astype(BF16)
                return 0

            lax.fori_loop(0, 4, add, 0)

        sum_up(part_stage, d_own, d_from, dx_out, to_z)
        z_stage = copier.send(to_z, from_z, "exp", (1 - zl) * 4 + x)
        layer_stage = pass_on(layer_stage, layer_loads, *layers)

        for at in first_a:
            copier.arrived(at)

        def sum_a(c, _):
            for e in range(LOCAL):
                both = gate[core, zh, c, e].astype(F32) + gate_a[c, e].astype(F32)
                gate_out[c, e] = both.astype(BF16)
            for e in range(2):
                both = down[core, zh, c, e].astype(F32) + down_a[c, e].astype(F32)
                down_a_out[c, e] = both.astype(BF16)
            return 0

        lax.fori_loop(0, 4, sum_a, 0)

        for at in first_b:
            copier.arrived(at)
        others = [lax.rem(y + d, 4) for d in (1, 2, 3)]

        def sum_b(e, _):
            for z in range(2):
                total = up[core, z, y, e].astype(F32)
                for c in others:
                    total = total + up_b[c, z, e].astype(F32)
                up_out[z, e] = total.astype(BF16)
            return 0

        lax.fori_loop(0, LOCAL, sum_b, 0)

        def sum_b_down(e, _):
            for z in range(2):
                total = down[core, z, y, e + 2].astype(F32)
                for c in others:
                    total = total + down_b[c, z, e].astype(F32)
                down_b_out[z, e] = total.astype(BF16)
            return 0

        lax.fori_loop(0, 2, sum_b_down, 0)
        copier.arrived(z_stage)

        def gather_z(r, _):
            at = pl.ds(pl.multiple_of(r * 48, 16), 48)
            dx_out[at, :] += from_z[at, :].astype(F32)
            return 0

        lax.fori_loop(0, 4, gather_z, 0)
        sum_up(layer_stage, l_own, l_from, keep_out, give_out)
        copier.finish()

    vmem = pl.BlockSpec(memory_space=pltpu.VMEM)
    buf = lambda *shape: pltpu.VMEM(shape, BF16)
    wide, tall = (64, FF), (32, WIDTH)
    return pl.pallas_call(
        body,
        name="settle_experts",
        out_shape=[
            jax.ShapeDtypeStruct((4, LOCAL) + wide, BF16),
            jax.ShapeDtypeStruct((2, LOCAL) + wide, BF16),
            jax.ShapeDtypeStruct((4, 2) + tall, BF16),
            jax.ShapeDtypeStruct((2, 2) + tall, BF16),
            jax.ShapeDtypeStruct((ROWS, WIDTH), F32),
            jax.ShapeDtypeStruct((ROWS, WIDTH), F32),
            jax.ShapeDtypeStruct((ROWS, WIDTH), BF16),
        ],
        in_specs=[ANY_SPEC] * 7,
        out_specs=[vmem] * 7,
        scratch_shapes=[
            buf(LOCAL, SLOTS, WIDTH),
            buf(LOCAL, SLOTS, WIDTH),
            buf(LOCAL, SLOTS, FF),
            buf(LOCAL, SLOTS, FF),
            buf(LOCAL, SLOTS, FF),
            buf(2, 2, 4, LOCAL, *wide),
            buf(2, 2, 4, LOCAL, *wide),
            buf(2, 2, 4, LOCAL, *tall),
            buf(2, 4, LOCAL, *wide),
            buf(2, 4, LOCAL, *wide),
            buf(2, 4, LOCAL, *tall),
            buf(4, LOCAL, *wide),
            buf(4, 2, *tall),
            buf(4, 2, LOCAL, *wide),
            buf(4, 2, 2, *tall),
            buf(ROWS, WIDTH),
            buf(ROWS, WIDTH),
        ]
        + [
            buf(2, ROWS, WIDTH),
            buf(2, ROWS // 2, WIDTH),
            buf(2, ROWS // 2, WIDTH),
            buf(2, ROWS // 2, WIDTH),
            buf(2, ROWS // 2, WIDTH),
            buf(2, 2, ROWS, WIDTH),
        ]
        * 2
        + [
            pltpu.SemaphoreType.DMA((49,)),
            pltpu.SemaphoreType.DMA((49,)),
            pltpu.SemaphoreType.DMA((28,)),
        ],
        compiler_params=pltpu.CompilerParams(
            collective_id=8, has_side_effects=True, vmem_limit_bytes=62 * MIB
        ),
    )(rows, d_rows, act, d_gate, d_up, d_parts, layer_parts)


def compute_call(body, name, outs, ins, vmem=60, **kw):
    return pl.pallas_call(
        body,
        name=name,
        out_shape=outs,
        compiler_params=pltpu.CompilerParams(vmem_limit_bytes=vmem * MIB),
        **kw,
    )(*ins)


def row_scale(total, width):
    return lax.rsqrt(total * (1.0 / width) + EPSILON)


def key_lanes():
    return lax.broadcasted_iota(jnp.int32, (1, 128), 1) < 64


def turn(values, cosine, sine):
    first = lax.rem(lax.broadcasted_iota(jnp.int32, (1, 128), 1), 64) < 32
    return values * cosine + jnp.where(first, -pltpu.roll(values, 96, 1), pltpu.roll(values, 32, 1)) * sine


def across(select, values):
    return lax.dot_general(
        select, values, (NT, ((), ())), precision=lax.Precision.HIGHEST, preferred_element_type=F32
    )


def both_totals(left, right):
    row_id = lax.broadcasted_iota(jnp.int32, (8, 128), 0)
    ones = jnp.where(row_id == 0, 1.0, 0.0)
    keys = jnp.where((row_id == 1) & key_lanes(), 1.0, 0.0)
    return (across(ones, left) + across(keys, right))[0:2, :]


def down_rows(values, row, width=128):
    chosen = lax.broadcasted_iota(jnp.int32, (2, width), 0) == row
    return lax.dot_general(
        values,
        jnp.where(chosen, 1.0, 0.0),
        (TN, ((), ())),
        precision=lax.Precision.HIGHEST,
        preferred_element_type=F32,
    )


def own_chip():
    return lax.axis_index("ctx") // 2


def route(routes_t, logits_t):
    def body(r_ref, l_ref, m_ref):
        logits = l_ref[...]
        raised = jnp.exp(logits - jnp.max(logits, axis=0, keepdims=True))
        gates = raised / jnp.sum(raised, axis=0, keepdims=True)
        experts = lax.broadcasted_iota(jnp.int32, (32, ROWS), 0)
        member = jnp.zeros((32, ROWS), F32)
        weight = jnp.zeros((32, ROWS), F32)
        for c in range(8):
            hit = r_ref[c : c + 1, :] == experts
            member = member + jnp.where(hit, 1.0, 0.0)
            weight = weight + jnp.where(hit, gates[c : c + 1, :], 0.0)
        before = lax.broadcasted_iota(jnp.int32, (ROWS, ROWS), 0) < lax.broadcasted_iota(
            jnp.int32, (ROWS, ROWS), 1
        )
        rank = dot(member.astype(BF16), jnp.where(before, 1.0, 0.0).astype(BF16))
        spot = jnp.where(member > 0.5, rank, -1.0)
        for e in range(EXP):
            m_ref[e, 0:4, :] = spot[e * 4 : e * 4 + 4, :]
            m_ref[e, 4:8, :] = weight[e * 4 : e * 4 + 4, :]

    return compute_call(
        body, "route", [jax.ShapeDtypeStruct((EXP, 8, ROWS), F32)], [routes_t, logits_t]
    )[0]


def split_kv(kv_ref, klo, khi, vlo, vhi):
    low = key_lanes()
    both = kv_ref[...].astype(F32)
    other = pltpu.roll(both, 64, 1)
    if klo is not None:
        klo[...] = jnp.where(low, both, 0.0).astype(BF16)
        khi[...] = jnp.where(low, 0.0, other).astype(BF16)
    vlo[...] = jnp.where(low, other, 0.0).astype(BF16)
    vhi[...] = jnp.where(low, 0.0, both).astype(BF16)


def attend(q, kv, key_pos, places, first_chunk):
    def body(first_ref, q_ref, kv_ref, kp_ref, p_ref, o_ref, of_ref, l_ref, klo, khi, vlo, vhi):
        i = pl.program_id(0)

        @pl.when(i == 0)
        def _():
            split_kv(kv_ref, klo, khi, vlo, vhi)

        q_block = q_ref[0]
        at_row, start_row = [
            jnp.concatenate([down_rows(p_ref[0], k)] * (CHUNK // 128), axis=1) for k in range(2)
        ]
        low = key_lanes()

        def step(p, carry):
            m0, m1, l0, l1, acc = carry
            rows = pl.ds(pl.multiple_of(p * CHUNK, CHUNK), CHUNK)
            at_key = kp_ref[p]
            seen = (at_key >= start_row) & (at_key <= at_row)
            s0 = jnp.where(seen, dot(q_block, klo[rows, :], NT), MASKED)
            s1 = jnp.where(seen, dot(q_block, khi[rows, :], NT), MASKED)
            n0 = jnp.maximum(m0, jnp.max(s0, axis=1, keepdims=True))
            n1 = jnp.maximum(m1, jnp.max(s1, axis=1, keepdims=True))
            p0 = jnp.exp(s0 - n0)
            p1 = jnp.exp(s1 - n1)
            a0 = jnp.exp(m0 - n0)
            a1 = jnp.exp(m1 - n1)
            l0 = l0 * a0 + jnp.sum(p0, axis=1, keepdims=True)
            l1 = l1 * a1 + jnp.sum(p1, axis=1, keepdims=True)
            acc = acc * jnp.where(low, a0, a1)
            acc = acc + dot(p0.astype(BF16), vlo[rows, :]) + dot(p1.astype(BF16), vhi[rows, :])
            return n0, n1, l0, l1, acc

        top = jnp.full((ROWS, 1), MASKED, F32)
        none = jnp.zeros((ROWS, 1), F32)
        m0, m1, l0, l1, acc = lax.fori_loop(
            first_ref[i], i + 1, step, (top, top, none, none, jnp.zeros((ROWS, 128), F32))
        )
        out = acc / jnp.where(low, l0, l1)
        of_ref[0] = out
        o_ref[0] = out.astype(BF16)
        l_ref[0] = jnp.where(low, m0 + jnp.log(l0), m1 + jnp.log(l1))

    def block(*shape):
        return pl.BlockSpec((1,) + shape, lambda i, first: (i, 0, 0))

    return pl.pallas_call(
        body,
        name="attend",
        out_shape=[
            jax.ShapeDtypeStruct((CHIPS, ROWS, 128), BF16),
            jax.ShapeDtypeStruct((CHIPS, ROWS, 128), F32),
            jax.ShapeDtypeStruct((CHIPS, ROWS, 128), F32),
        ],
        grid_spec=pltpu.PrefetchScalarGridSpec(
            num_scalar_prefetch=1,
            grid=(CHIPS,),
            in_specs=[
                block(ROWS, 128),
                pl.BlockSpec((KEYS, 128), lambda i, first: (0, 0)),
                pl.BlockSpec((CHIPS, 1, CHUNK), lambda i, first: (0, 0, 0)),
                block(2, ROWS),
            ],
            out_specs=[block(ROWS, 128)] * 3,
            scratch_shapes=[pltpu.VMEM((KEYS, 128), BF16)] * 4,
        ),
        compiler_params=pltpu.CompilerParams(vmem_limit_bytes=60 * MIB),
    )(first_chunk, q, kv, key_pos, places)


def attend_back(q, kv, d_out, out, log_total, key_pos, places, first_chunk):
    def body(
        first_ref, q_ref, kv_ref, do_ref, o_ref, l_ref, kp_ref, p_ref,
        dq_ref, mine_ref, other_ref, klo, khi, vlo, vhi, acc, key_at,
    ):
        i = pl.program_id(0)

        @pl.when(i == 0)
        def _():
            split_kv(kv_ref, klo, khi, vlo, vhi)
            acc[...] = jnp.zeros_like(acc)

            def place_keys(p, _):
                both = jnp.concatenate([kp_ref[p], kp_ref[p]], axis=0)
                key_at[pl.ds(pl.multiple_of(p * CHUNK, CHUNK), CHUNK), :] = down_rows(both, 0, ROWS)
                return 0

            lax.fori_loop(0, CHIPS, place_keys, 0)

        low = key_lanes()
        q_block, do_block = q_ref[0], do_ref[0]
        do_wide, q_wide = do_block.astype(F32), q_block.astype(F32)
        q_turned, do_turned = pltpu.roll(q_wide, 64, 1), pltpu.roll(do_wide, 64, 1)
        right = jnp.concatenate(
            [
                jnp.where(low, q_wide, 0.0).astype(BF16),
                jnp.where(low, q_turned, 0.0).astype(BF16),
                jnp.where(low, 0.0, do_turned).astype(BF16),
                jnp.where(low, 0.0, do_wide).astype(BF16),
            ],
            axis=0,
        )
        row_id = lax.broadcasted_iota(jnp.int32, (8, 128), 0)
        lane_id = lax.broadcasted_iota(jnp.int32, (8, 128), 1)
        halves = jnp.where(lane_id // 64 == row_id, 1.0, 0.0)
        picks = jnp.where(lane_id == 64 * row_id, 1.0, 0.0)

        delta = across(halves, do_wide * o_ref[0])
        total = across(picks, l_ref[0])
        at_row, start_row = p_ref[0, 0:1, :], p_ref[0, 1:2, :]

        def step(p, dq):
            rows = pl.ds(pl.multiple_of(p * CHUNK, CHUNK), CHUNK)
            at_key = key_at[rows, :]
            seen = (at_key >= start_row) & (at_key <= at_row)
            k0, k1 = klo[rows, :], khi[rows, :]
            s0 = jnp.where(seen, dot(k0, q_block, NT), MASKED)
            s1 = jnp.where(seen, dot(k1, q_block, NT), MASKED)
            p0 = jnp.exp(s0 - total[0:1, :])
            p1 = jnp.exp(s1 - total[1:2, :])
            d0 = (p0 * (dot(vlo[rows, :], do_block, NT) - delta[0:1, :])).astype(BF16)
            d1 = (p1 * (dot(vhi[rows, :], do_block, NT) - delta[1:2, :])).astype(BF16)
            left = jnp.concatenate([d0, d1, p0.astype(BF16), p1.astype(BF16)], axis=1)
            acc[rows, :] += dot(left, right)
            return dq + dot(d0, k0, TN) + dot(d1, k1, TN)

        dq = lax.fori_loop(first_ref[i], i + 1, step, jnp.zeros((ROWS, 128), F32))
        dq_ref[0] = dq * 0.125

        @pl.when(i == CHIPS - 1)
        def _():
            core = lax.rem(lax.axis_index("ctx"), 2)

            def part(s, _):
                mine = pl.ds(pl.multiple_of((2 * s + core) * ROWS, ROWS), ROWS)
                other = pl.ds(pl.multiple_of((2 * s + 1 - core) * ROWS, ROWS), ROWS)
                mine_ref[s] = acc[mine, :]
                other_ref[s] = acc[other, :].astype(BF16)
                return 0

            lax.fori_loop(0, CHIPS, part, 0)

    def block(*shape):
        return pl.BlockSpec((1,) + shape, lambda i, first: (i, 0, 0))

    whole = pl.BlockSpec((KEYS, 128), lambda i, first: (0, 0))
    return pl.pallas_call(
        body,
        name="attend_back",
        out_shape=[
            jax.ShapeDtypeStruct((CHIPS, ROWS, 128), F32),
            jax.ShapeDtypeStruct((CHIPS, ROWS, 128), F32),
            jax.ShapeDtypeStruct((CHIPS, ROWS, 128), BF16),
        ],
        grid_spec=pltpu.PrefetchScalarGridSpec(
            num_scalar_prefetch=1,
            grid=(CHIPS,),
            in_specs=[
                block(ROWS, 128),
                whole,
                block(ROWS, 128),
                block(ROWS, 128),
                block(ROWS, 128),
                pl.BlockSpec((CHIPS, 1, CHUNK), lambda i, first: (0, 0, 0)),
                block(2, ROWS),
            ],
            out_specs=[block(ROWS, 128)] + [pl.BlockSpec((CHIPS, ROWS, 128), lambda i, first: (0, 0, 0))] * 2,
            scratch_shapes=[pltpu.VMEM((KEYS, 128), BF16)] * 4
            + [pltpu.VMEM((KEYS, 128), F32), pltpu.VMEM((KEYS, ROWS), F32)],
        ),
        compiler_params=pltpu.CompilerParams(vmem_limit_bytes=60 * MIB),
    )(first_chunk, q, kv, d_out, out, log_total, key_pos, places)


def whole(*shape):
    return pl.BlockSpec(shape, lambda i: (0,) * len(shape))


def columns(block, width=WIDTH):
    return pl.BlockSpec((WIDTH, width), lambda i: (0, block))


def finish_attention(attended, w_out, tokens, gains):
    def body(a_ref, w_ref, t_ref, g_ref, r_ref, f_ref):
        branch = dot(a_ref[...], w_ref[...]).astype(BF16).astype(F32)
        resid = t_ref[...].astype(F32) + branch
        r_ref[...] = resid
        scale = row_scale(jnp.sum(resid * resid, axis=1, keepdims=True), WIDTH)
        f_ref[...] = (resid * scale * g_ref[3:4, :]).astype(BF16)

    return compute_call(
        body,
        "finish_attention",
        [jax.ShapeDtypeStruct((ROWS, WIDTH), F32), jax.ShapeDtypeStruct((ROWS, WIDTH), BF16)],
        [attended, w_out, tokens, gains],
        grid=(1,),
        in_specs=[whole(ROWS, WIDTH), whole(WIDTH, WIDTH), whole(ROWS, WIDTH), whole(8, WIDTH)],
        out_specs=[whole(ROWS, WIDTH)] * 2,
    )


def experts(rows, grads, meta, meta_t, w_gate, w_up, w_down):
    half = SLOTS // 2

    def body(
        x_ref, g_ref, m_ref, mt_ref, wg_ref, wu_ref, wd_ref,
        xin_ref, dr_ref, act_ref, dg_ref, du_ref, out_ref, dx_ref,
        made, back, weight,
    ):
        e = pl.program_id(0)

        @pl.when(e == 0)
        def _():
            slot_id = lax.broadcasted_iota(jnp.int32, (PAIR_CAP, PAIR_ROWS), 0).astype(F32)

            def pick(p, _):
                meta_p = m_ref[p]
                parts, gates = [], []
                for k in range(LOCAL):
                    hit = slot_id == meta_p[k : k + 1, :]
                    parts.append(jnp.where(hit, 1.0, 0.0).astype(BF16))
                    gates.append(
                        jnp.sum(jnp.where(hit, meta_p[4 + k : 5 + k, :], 0.0), axis=1, keepdims=True)
                    )
                chosen = jnp.concatenate(parts, axis=0)
                rows_p = dot(chosen, x_ref[p]).astype(BF16)
                grads_p = dot(chosen, g_ref[p])
                at = pl.ds(pl.multiple_of(p * PAIR_CAP, PAIR_CAP), PAIR_CAP)
                for k in range(LOCAL):
                    piece = slice(k * PAIR_CAP, (k + 1) * PAIR_CAP)
                    xin_ref[k, at, :] = rows_p[piece]
                    dr_ref[k, at, :] = (grads_p[piece] * gates[k]).astype(BF16)
                    weight[k, at, :] = gates[k]
                return 0

            lax.fori_loop(0, PAIRS, pick, 0)

        def work(h, _):
            at = pl.ds(pl.multiple_of(h * half, half), half)
            x = xin_ref[e, at, :]
            dr = dr_ref[e, at, :]
            gate = dot(x, wg_ref[0])
            up = dot(x, wu_ref[0])
            sig = jax.nn.sigmoid(gate)
            silu = gate * sig
            act = (silu * up).astype(BF16)
            act_ref[0, at, :] = act
            d_act = dot(dr, wd_ref[0], NT)
            d_gate = (d_act * up * sig * (1.0 + gate * (1.0 - sig))).astype(BF16)
            d_up = (d_act * silu).astype(BF16)
            dg_ref[0, at, :] = d_gate
            du_ref[0, at, :] = d_up
            y = (dot(act, wd_ref[0]) * weight[e, at, :]).astype(BF16)
            dch = (dot(d_gate, wg_ref[0], NT) + dot(d_up, wu_ref[0], NT)).astype(BF16)
            place_at = pl.ds(pl.multiple_of(e * PAIR_CAP, PAIR_CAP), PAIR_CAP)
            for k in range(2):
                piece = slice(k * PAIR_CAP, (k + 1) * PAIR_CAP)
                made[2 * h + k, place_at, :] = y[piece]
                back[2 * h + k, place_at, :] = dch[piece]
            return 0

        lax.fori_loop(0, 2, work, 0)

        @pl.when(e == LOCAL - 1)
        def _():
            lane_id = lax.broadcasted_iota(jnp.int32, (PAIR_ROWS, PAIR_SLOTS), 1).astype(F32)

            def give(p, _):
                meta_p = mt_ref[p]
                chosen = jnp.zeros((PAIR_ROWS, PAIR_SLOTS), F32)
                for k in range(LOCAL):
                    spot = meta_p[:, k : k + 1]
                    lane = jnp.where(spot < 0.0, -1.0, spot + float(k * PAIR_CAP))
                    chosen = chosen + jnp.where(lane_id == lane, 1.0, 0.0)
                chosen = chosen.astype(BF16)
                dx_ref[p] = dot(chosen, back[p]).astype(BF16)
                out_ref[p] = dot(chosen, made[p]).astype(BF16)
                return 0

            lax.fori_loop(0, PAIRS, give, 0)

    def fixed(*shape):
        return pl.BlockSpec(shape, lambda e: (0,) * len(shape), pipeline_mode=pl.Buffered(1))

    def each(*shape):
        return pl.BlockSpec((1,) + shape, lambda e: (e, 0, 0))

    return compute_call(
        body,
        "experts",
        [
            jax.ShapeDtypeStruct((LOCAL, SLOTS, WIDTH), BF16),
            jax.ShapeDtypeStruct((LOCAL, SLOTS, WIDTH), BF16),
            jax.ShapeDtypeStruct((LOCAL, SLOTS, FF), BF16),
            jax.ShapeDtypeStruct((LOCAL, SLOTS, FF), BF16),
            jax.ShapeDtypeStruct((LOCAL, SLOTS, FF), BF16),
            jax.ShapeDtypeStruct((PAIRS, PAIR_ROWS, WIDTH), BF16),
            jax.ShapeDtypeStruct((PAIRS, PAIR_ROWS, WIDTH), BF16),
        ],
        [rows, grads, meta, meta_t, w_gate, w_up, w_down],
        vmem=60,
        grid=(LOCAL,),
        in_specs=[
            fixed(PAIRS, PAIR_ROWS, WIDTH),
            fixed(PAIRS, PAIR_ROWS, WIDTH),
            fixed(PAIRS, 8, PAIR_ROWS),
            fixed(PAIRS, PAIR_ROWS, 8),
            each(WIDTH, FF),
            each(WIDTH, FF),
            each(FF, WIDTH),
        ],
        out_specs=[
            fixed(LOCAL, SLOTS, WIDTH),
            fixed(LOCAL, SLOTS, WIDTH),
            each(SLOTS, FF),
            each(SLOTS, FF),
            each(SLOTS, FF),
            fixed(PAIRS, PAIR_ROWS, WIDTH),
            fixed(PAIRS, PAIR_ROWS, WIDTH),
        ],
        scratch_shapes=[
            pltpu.VMEM((PAIRS, PAIR_SLOTS, WIDTH), BF16),
            pltpu.VMEM((PAIRS, PAIR_SLOTS, WIDTH), BF16),
            pltpu.VMEM((LOCAL, SLOTS, 1), F32),
        ],
    )


def norm_back(values, total_squares, width, weighted, mask=None):
    scale = row_scale(total_squares, width)
    inner = jnp.sum(weighted * values, axis=1, keepdims=True) * (1.0 / width)
    return scale * weighted - values * (scale * scale * scale) * inner, scale


def back_to_branch(d_ffn, resid, cotangent, gains, w_out):
    def body(p_ref, r_ref, c_ref, g_ref, w_ref, dr_ref, db_ref, da_ref, gg_ref):
        incoming = p_ref[...]
        resid_v = r_ref[...]
        squares = jnp.sum(resid_v * resid_v, axis=1, keepdims=True)
        d_norm, scale = norm_back(resid_v, squares, WIDTH, incoming * g_ref[3:4, :])
        gg_ref[...] = jnp.sum(incoming * resid_v * scale, axis=0, keepdims=True)
        d_resid = c_ref[...].astype(F32) + d_norm
        dr_ref[...] = d_resid
        d_branch = d_resid.astype(BF16)
        db_ref[...] = d_branch
        da_ref[...] = dot(d_branch, w_ref[...], NT).astype(BF16)

    return compute_call(
        body,
        "back_to_branch",
        [
            jax.ShapeDtypeStruct((ROWS, WIDTH), F32),
            jax.ShapeDtypeStruct((ROWS, WIDTH), BF16),
            jax.ShapeDtypeStruct((ROWS, WIDTH), BF16),
            jax.ShapeDtypeStruct((1, WIDTH), F32),
        ],
        [d_ffn, resid, cotangent, gains, w_out],
        grid=(1,),
        in_specs=[whole(ROWS, WIDTH)] * 3 + [whole(8, WIDTH), whole(WIDTH, WIDTH)],
        out_specs=[whole(ROWS, WIDTH)] * 3 + [whole(1, WIDTH)],
    )


def out_grads(attended, d_branch):
    def body(a_ref, d_ref, o_ref):
        def part(r, _):
            at = pl.ds(pl.multiple_of(r * 256, 256), 256)
            o_ref[at, :] = dot(a_ref[:, at], d_ref[...], TN).astype(BF16)
            return 0

        lax.fori_loop(0, 4, part, 0)

    return compute_call(
        body, "out_grads", [jax.ShapeDtypeStruct((WIDTH, WIDTH), BF16)], [attended, d_branch]
    )[0]


def deliver(resid, layer_keep, layer_got, dense, out_grad, gain_sums, input_grad, expert_sums):
    def body(
        r_ref, k_ref, g_ref, d_ref, o_ref, s_ref, i_ref, eg_ref, eu_ref, ed_ref,
        lo, wq, wk, wv, wo, ga, gq, gk, gf, di, eg, eu, ed,
    ):
        lo[...] = (r_ref[...] + k_ref[...] + g_ref[...].astype(F32)).astype(BF16)
        wq[...] = d_ref[0].astype(F32)
        for c in range(4):
            k, v = apart([d_ref[1, :, (2 * c + j) * 128 : (2 * c + j + 1) * 128].astype(F32) for j in range(2)])
            wk[:, c * 128 : (c + 1) * 128] = k
            wv[:, c * 128 : (c + 1) * 128] = v
        wo[...] = o_ref[...].astype(F32)
        ga[...] = s_ref[0:1, :]
        gq[...] = s_ref[1:2, :]
        gk[...] = s_ref[2:3, 0:64]
        gf[...] = s_ref[3:4, :]
        di[...] = i_ref[...]
        eg[...] = eg_ref[...]
        eu[...] = eu_ref[...]
        ed[...] = ed_ref[...]

    return compute_call(
        body,
        "deliver",
        [
            jax.ShapeDtypeStruct((ROWS, WIDTH), BF16),
            jax.ShapeDtypeStruct((128, WIDTH), F32),
            jax.ShapeDtypeStruct((128, 512), F32),
            jax.ShapeDtypeStruct((128, 512), F32),
            jax.ShapeDtypeStruct((128, WIDTH), F32),
            jax.ShapeDtypeStruct((1, 128), F32),
            jax.ShapeDtypeStruct((1, 128), F32),
            jax.ShapeDtypeStruct((1, 64), F32),
            jax.ShapeDtypeStruct((1, 128), F32),
            jax.ShapeDtypeStruct((ROWS, WIDTH), F32),
        ]
        + [jax.ShapeDtypeStruct(a.shape, F32) for a in expert_sums],
        [resid, layer_keep, layer_got, dense, out_grad, gain_sums, input_grad, *expert_sums],
    )


def cosine_of_turns(turns):
    part = turns - jnp.floor(turns + 0.5)
    square = part * part * 39.47841760435743
    total = jnp.full_like(square, -1.0 / 6402373705728000.0)
    for n in (20922789888000.0, -87178291200.0, 479001600.0, -3628800.0, 40320.0, -720.0, 24.0, -2.0, 1.0):
        total = total * square + 1.0 / n
    return total


def front(tokens, cotangent, dense, norms, perm, lengths):
    half = 64

    def body(
        t_ref, cot_ref, wq_ref, wk_ref, wv_ref, wd_ref, na_ref, nq_ref, nk_ref, nf_ref, perm_ref, len_ref,
        wo_ref, go_ref, n_ref, ql_ref, kl_ref, s_ref, c_ref, sn_ref, p_ref, q_ref, kv_ref, co_ref,
        g_ref, w_mine, rows, normed, gains_v, w_own, totals, totals_all, kv_half, send_sem, recv_sem, local_sem,
    ):
        _, chip, core, sibling = place()
        me = lax.axis_index("exp")
        chips, exps = ring_of(chip), ring_of(me)
        twins = [lax.rem(chip + d, CHIPS) for d in (2, 6, 4, 1, 3, 5, 7)]
        to_chip = lambda p: ("ctx", 2 * p + core)
        to_exp = lambda p: ("exp", p)
        copier = Copier(send_sem, recv_sem, local_sem)
        keys = key_lanes()
        odd = lax.rem(chip, 2) == 1
        wk, wv = wk_ref[:, lanes(chip // 2)].astype(F32), wv_ref[:, lanes(chip // 2)].astype(F32)
        wk = jnp.where(odd, pltpu.roll(wk, 64, 1), wk)
        wv = jnp.where(odd, wv, pltpu.roll(wv, 64, 1))
        w_mine[:, 0:128] = wq_ref[:, lanes(chip)]
        w_mine[:, 128:256] = jnp.where(keys, wk, wv).astype(BF16)
        g_ref[...] = jnp.ones((8, 128), F32)
        g_ref[0:1, :] = na_ref[...].astype(F32)
        g_ref[1:2, :] = nq_ref[...].astype(F32)
        g_ref[2:3, 0:64] = nk_ref[...].astype(F32)
        g_ref[3:4, :] = nf_ref[...].astype(F32)
        meet([to_chip(p) for p in twins] + [to_exp(p) for p in exps[1:]] + [("ctx", sibling)])
        gain_sends = [copier.send(g_ref, gains_v.at[me], *to_exp(p)) for p in exps[1:]]
        part = pl.ds(pl.multiple_of(core * half, half), half)
        slot = lambda s: wo_ref.at[s, part]
        handed = []

        def norm(block, s):
            x = block.astype(F32)
            scale = row_scale(jnp.sum(x * x, axis=1, keepdims=True), WIDTH)
            for e in range(EXP):
                at = slice(e * 128, (e + 1) * 128)
                normed[s, :, at] = (x[:, at] * scale * gains_v[e, 0:1, :]).astype(BF16)

        projected = []

        def project(s):
            both = dot(normed[s], w_own[...].reshape(WIDTH, 256))
            q, kv = both[:, 0:128], both[:, 128:256]
            ql_ref[s] = q
            kl_ref[s] = kv
            totals[s] = both_totals(q * q, kv * kv)

        def landed(s):
            norm(rows[s], s)
            projected.append(s)

        main = relay(copier, t_ref, lambda s: rows.at[s], ROWS, chips, to_chip, landed)
        extra = relay(copier, cot_ref, lambda s: co_ref.at[s], ROWS, exps, to_exp)
        dense = relay(
            copier,
            wd_ref.at[part],
            slot,
            half,
            exps,
            to_exp,
            lambda s: handed.append(copier.send(slot(s), slot(s), "ctx", sibling)),
        )
        next(main)
        next(main)
        next(dense)
        next(dense)
        copier.keep(wd_ref, wo_ref.at[me])
        copier.keep(cot_ref, co_ref.at[me])
        w_own[me] = w_mine[...]
        gains_v[me] = g_ref[...]

        row = lax.broadcasted_iota(jnp.int32, (CTX, ROWS), 1)
        piece = jnp.where(row // 12 == lax.broadcasted_iota(jnp.int32, (CTX, ROWS), 0), 1.0, 0.0)
        dealt = dot(perm_ref[...].astype(F32).astype(BF16), piece.astype(BF16))
        source = lax.broadcasted_iota(jnp.int32, (CTX, ROWS), 0)
        position = (source * CTX).astype(F32) + dealt
        position = position * 12.0 + lax.rem(row, 12).astype(F32)
        begin = jnp.zeros((CTX, ROWS), F32)
        ends = jnp.zeros((1, 1), F32)
        for k in range(3):
            ends = ends + len_ref[0:1, k : k + 1].astype(F32)
            begin = jnp.where(position >= ends, ends, begin)
        for i in range(CHIPS):
            mine = [jnp.where(core == 0, v[2 * i : 2 * i + 1], v[2 * i + 1 : 2 * i + 2]) for v in (position, begin)]
            p_ref[i] = jnp.concatenate(mine, axis=0)

        def angles(i, _):
            keys = key_lanes()
            lane = lax.broadcasted_iota(jnp.int32, (1, 128), 1)
            freq = jnp.exp(lax.rem(lane, 32).astype(F32) * (-2.0 / 64 * 9.210340371976184))
            place_i = p_ref[i]
            offset = down_rows(place_i, 0) - down_rows(place_i, 1)
            mixed = cosine_of_turns(offset * (freq * 0.15915494309189535) - jnp.where(keys, 0.0, 0.25))
            other = pltpu.roll(mixed, 64, 1)
            c_ref[i] = jnp.where(keys, mixed, other)
            sn_ref[i] = jnp.where(keys, other, mixed)
            return 0

        lax.fori_loop(0, CHIPS, angles, 0)
        for at in gain_sends:
            copier.arrived(at)
        go_ref[...] = gains_v[...]
        norm(t_ref[...], chip)
        projected.append(chip)
        next(main)
        next(dense)
        next(main)
        own_sends = [copier.send(w_mine, w_own.at[me], *to_exp(p)) for p in exps[1:]]
        next(extra)
        next(extra)
        next(dense)
        next(main)
        next(main)
        next(dense)
        for at in own_sends:
            copier.arrived(at)
        for s in projected:
            project(s)
        projected.clear()
        next(extra)
        next(extra)
        next(main)
        next(dense)
        for s in projected:
            project(s)
        projected.clear()
        side_by_side(main)
        for s in projected:
            project(s)
        shares = [copier.send(totals, totals_all.at[chip], *to_chip(p)) for p in twins]
        totals_all[chip] = totals[...]
        side_by_side(dense)
        copier.keep(normed, n_ref)
        for _ in range(3):
            next(extra)
        for at in shares:
            copier.arrived(at)

        def turn_one(i, _):
            squares = totals_all[0, i]
            for c in range(1, CHIPS):
                squares = squares + totals_all[c, i]
            s_ref[i] = squares
            cos, sin = c_ref[i], sn_ref[i]
            gain = gains_v[chip]
            q = ql_ref[i] * row_scale(down_rows(squares, 0), WIDTH) * gain[1:2, :]
            q = turn(q, cos, sin).astype(BF16).astype(F32)
            q_ref[i] = (q * 0.125).astype(BF16)
            scale = jnp.where(keys, row_scale(down_rows(squares, 1), WIDTH // 2), 1.0)
            kv = kl_ref[i] * scale * gain[2:3, :]
            kv_half[i] = turn(kv, jnp.where(keys, cos, 1.0), jnp.where(keys, sin, 0.0)).astype(BF16)
            return 0

        lax.fori_loop(0, CHIPS, turn_one, 0)
        copier.send(kv_half, kv_ref.at[:, core], "ctx", sibling)
        copier.keep(kv_half, kv_ref.at[:, core])
        side_by_side(extra)
        copier.finish()

    vmem = pl.BlockSpec(memory_space=pltpu.VMEM)
    wide = jax.ShapeDtypeStruct((CHIPS, ROWS, 128), F32)
    return pl.pallas_call(
        body,
        name="front",
        out_shape=[
            jax.ShapeDtypeStruct((EXP, 128, WIDTH), BF16),
            jax.ShapeDtypeStruct((EXP, 8, 128), F32),
            jax.ShapeDtypeStruct((CHIPS, ROWS, WIDTH), BF16),
            wide,
            wide,
            jax.ShapeDtypeStruct((CHIPS, 2, ROWS), F32),
            wide,
            wide,
            jax.ShapeDtypeStruct((CHIPS, 2, ROWS), F32),
            jax.ShapeDtypeStruct((CHIPS, ROWS, 128), BF16),
            jax.ShapeDtypeStruct((CHIPS, 2, ROWS, 128), BF16),
            jax.ShapeDtypeStruct((EXP, ROWS, WIDTH), BF16),
        ],
        in_specs=[vmem] * 12,
        out_specs=[ANY_SPEC, vmem, ANY_SPEC] + [vmem] * 7 + [ANY_SPEC] * 2,
        scratch_shapes=[
            pltpu.VMEM((8, 128), F32),
            pltpu.VMEM((128, 256), BF16),
            pltpu.VMEM((CHIPS, ROWS, WIDTH), BF16),
            pltpu.VMEM((CHIPS, ROWS, WIDTH), BF16),
            pltpu.VMEM((EXP, 8, 128), F32),
            pltpu.VMEM((EXP, 128, 256), BF16),
            pltpu.VMEM((CHIPS, 2, ROWS), F32),
            pltpu.VMEM((CHIPS, CHIPS, 2, ROWS), F32),
            pltpu.VMEM((CHIPS, ROWS, 128), BF16),
            pltpu.SemaphoreType.DMA((71,)),
            pltpu.SemaphoreType.DMA((71,)),
            pltpu.SemaphoreType.DMA((8,)),
        ],
        compiler_params=pltpu.CompilerParams(
            collective_id=1, has_side_effects=True, vmem_limit_bytes=60 * MIB
        ),
    )(tokens, cotangent, *dense, *norms, perm, lengths)


def apart(pieces):
    first, second = pieces
    keys = key_lanes()
    return (
        jnp.where(keys, first, pltpu.roll(second, 64, 1)),
        jnp.where(keys, pltpu.roll(first, 64, 1), second),
    )


def tail(
    dq, dkv_mine, dkv_other, q_lin, kv_lin, cosine, sine, squares, gains, normed, out_part, layer_part,
    weights, tokens, d_resid, ffn_gain, gate_part, up_part, down_a, down_b,
):
    def body(
        dq_ref, dm_ref, do_ref, ql_ref, kl_ref, c_ref, sn_ref, s_ref, g_ref, n_ref, op_ref, lp_ref,
        w_ref, t_ref, r_ref, fg_ref, gp_ref, up_ref, da_ref, db_ref,
        eg_ref, eu_ref, ed_ref, di_ref, dense_ref, og_ref, lo_ref, gs_ref,
        dq_v, dm_v, ql_v, kl_v, c_v, sn_v, n_v, w_v, t_v, r_v,
        got, e_q, e_kv, totals, totals_all, d_lin, home, w_give, w_keep, w_got, joint, traded, done,
        o_keep, o_got, o_traded, o_half, a_got, a_done, packet, packets, mine, shared, gate_c, down_c, up_d, down_d, send_sem, recv_sem, local_sem,
    ):
        ctx, chip, core, sibling = place()
        me = lax.axis_index("exp")
        twins = [lax.rem(chip + d, CHIPS) for d in (2, 6, 4, 1, 3, 5, 7)]
        exps = [lax.rem(me + d, EXP) for d in range(1, EXP)]
        others = [lax.rem(ctx + d, CTX) for d in range(1, CTX)]
        to_chip = lambda p: ("ctx", 2 * p + core)
        copier = Copier(send_sem, recv_sem, local_sem)
        heads = [
            copier.keep(src, dst)
            for src, dst in ((dq_ref, dq_v), (c_ref, c_v), (sn_ref, sn_v), (ql_ref, ql_v), (kl_ref, kl_v), (dm_ref, dm_v))
        ]
        late = [
            copier.keep(src, dst)
            for src, dst in ((n_ref, n_v), (w_ref, w_v), (t_ref, t_v), (r_ref, r_v))
        ]
        o_load = copier.keep(op_ref.at[:, core], o_keep)
        meet([("ctx", p) for p in others] + [("exp", p) for p in exps])
        swapped = copier.send(do_ref, got, "ctx", sibling)
        o_swap = copier.send(op_ref.at[:, 1 - core], o_got, "ctx", sibling)
        keys = key_lanes()
        gain = g_ref[chip]
        for at in heads:
            copier.kept(at)

        def unturn_q(i, _):
            e_q[i] = turn(dq_v[i], c_v[i], -sn_v[i])
            return 0

        lax.fori_loop(0, CHIPS, unturn_q, 0)
        copier.arrived(swapped)

        def unturn_kv(i, carry):
            q_sum, kv_sum = carry
            cos, sin = jnp.where(keys, c_v[i], 1.0), jnp.where(keys, -sn_v[i], 0.0)
            e = turn(dm_v[i] + got[i].astype(F32), cos, sin)
            e_kv[i] = e
            q_part, kv_part = e_q[i] * ql_v[i], e * kl_v[i]
            totals[i] = both_totals(q_part * gain[1:2, :], kv_part * gain[2:3, :])
            q_scale = row_scale(down_rows(s_ref[i], 0), WIDTH)
            k_scale = row_scale(down_rows(s_ref[i], 1), WIDTH // 2)
            q_sum = q_sum + jnp.sum(q_part * q_scale, axis=0, keepdims=True)
            kv_sum = kv_sum + jnp.sum(kv_part * jnp.where(keys, k_scale, 1.0), axis=0, keepdims=True)
            return q_sum, kv_sum

        none = jnp.zeros((1, 128), F32)
        q_sum, kv_sum = lax.fori_loop(0, CHIPS, unturn_kv, (none, none))
        shares = [copier.send(totals, totals_all.at[chip], *to_chip(p)) for p in twins]
        totals_all[chip] = totals[...]
        copier.kept(o_load)
        copier.arrived(o_swap)

        def add_cores(e, _):
            o_keep[e] = (o_keep[e].astype(F32) + o_got[e].astype(F32)).astype(BF16)
            return 0

        lax.fori_loop(0, EXP, add_cores, 0)
        o_trades = [copier.send(o_keep.at[p], o_traded.at[me], "exp", p) for p in exps]
        for at in shares:
            copier.arrived(at)

        def gradient(i):
            inner = totals_all[0, i]
            for c in range(1, CHIPS):
                inner = inner + totals_all[c, i]
            squares_i = s_ref[i]
            q_scale = row_scale(down_rows(squares_i, 0), WIDTH)
            k_scale = row_scale(down_rows(squares_i, 1), WIDTH // 2)
            q_cut = q_scale * q_scale * q_scale * down_rows(inner, 0) * (1.0 / WIDTH)
            k_cut = k_scale * k_scale * k_scale * down_rows(inner, 1) * (2.0 / WIDTH)
            d_lin[0, i] = (q_scale * (e_q[i] * gain[1:2, :]) - ql_v[i] * q_cut).astype(BF16)
            kv_scale = jnp.where(keys, k_scale, 1.0)
            k_cut = jnp.where(keys, k_cut, 0.0)
            d_lin[1, i] = (kv_scale * (e_kv[i] * gain[2:3, :]) - kl_v[i] * k_cut).astype(BF16)

        homeward = []
        for p in twins:
            gradient(p)
            for k in range(2):
                homeward.append(copier.send(d_lin.at[k, p], home.at[k, :, lanes(chip)], *to_chip(p)))
        zh, y = chip // 4, lax.rem(chip, 4)
        second = []
        for d in (1, 3, 2):
            c = lax.rem(y + d, 4)
            second.append(copier.send(gp_ref.at[c], gate_c.at[y], *to_chip(zh * 4 + c)))
            second.append(copier.send(da_ref.at[c], down_c.at[y], *to_chip(zh * 4 + c)))
        second.append(copier.send(up_ref.at[1 - zh], up_d, *to_chip((1 - zh) * 4 + y)))
        second.append(copier.send(db_ref.at[1 - zh], down_d, *to_chip((1 - zh) * 4 + y)))
        gradient(chip)
        for k in range(2):
            home[k, :, lanes(chip)] = d_lin[k, chip]
        for at in late:
            copier.kept(at)

        def columns_grad(half, out):
            d = d_lin[half].reshape(CHIPS * ROWS, 128)

            def part(r, _):
                n = n_v[:, :, pl.ds(pl.multiple_of(r * 256, 256), 256)].reshape(CHIPS * ROWS, 256)
                out[pl.ds(pl.multiple_of(r * 256, 256), 256), :] = dot(n, d, TN).astype(BF16)
                return 0

            lax.fori_loop(0, 4, part, 0)

        for at in o_trades:
            copier.arrived(at)
        o_traded[me] = o_keep[me]
        total = o_traded[0].astype(F32)
        for e in range(1, EXP):
            total = total + o_traded[e].astype(F32)
        o_half[...] = total.astype(BF16)
        spread = [copier.send(o_half.at[:, lanes(p)], a_got.at[chip], *to_chip(p)) for p in twins]
        a_got[chip] = o_half[:, lanes(chip)]
        columns_grad(1 - core, w_give)
        w_swap = copier.send(w_give, w_got, "ctx", sibling)
        columns_grad(core, w_keep)
        copier.arrived(w_swap)
        both = w_keep[...].astype(F32) + w_got[...].astype(F32)
        joint[...] = both.astype(BF16).reshape(EXP, 128, 128)
        trades = [copier.send(joint.at[p], traded.at[me], "exp", p) for p in exps]
        traded[me] = joint[me]
        for at in spread:
            copier.arrived(at)
        total = a_got[0].astype(F32)
        for c in range(1, CHIPS):
            total = total + a_got[c].astype(F32)
        a_done[...] = total.astype(BF16)

        for at in homeward:
            copier.arrived(at)
        k_parts, v_parts = [], []
        for c in range(4):
            k, v = apart([home[1, :, (2 * c + j) * 128 : (2 * c + j + 1) * 128].astype(F32) for j in range(2)])
            k_parts.append(k.astype(BF16))
            v_parts.append(v.astype(BF16))
        left = jnp.concatenate([home[0]] + k_parts + v_parts, axis=1)
        x = t_v[...].astype(F32)
        scale = row_scale(jnp.sum(x * x, axis=1, keepdims=True), WIDTH)
        inner = jnp.zeros((ROWS, 1), F32)
        pieces = []
        for e in range(EXP):
            at = slice(e * 128, (e + 1) * 128)
            d_normed = dot(left, w_v[e], NT).astype(BF16).astype(F32)
            packet[e] = jnp.zeros((8, 128), F32)
            packet[e, 0:1, :] = jnp.sum(d_normed * x[:, at] * scale, axis=0, keepdims=True)
            packet[e, 3:4, :] = fg_ref[:, at]
            weighted = d_normed * g_ref[e, 0:1, :]
            inner = inner + jnp.sum(weighted * x[:, at], axis=1, keepdims=True)
            pieces.append(weighted)
        packet[chip, 1:2, :] = q_sum
        packet[chip, 2:3, :] = kv_sum
        gain_trades = [copier.send(packet.at[p], packets.at[me], "exp", p) for p in exps]
        packets[me] = packet[me]

        for at in trades:
            copier.arrived(at)
        total = traded[0].astype(F32)
        for e in range(1, EXP):
            total = total + traded[e].astype(F32)
        done[...] = total.astype(BF16)
        spot = dense_ref.at[core, :, lanes(chip)]
        w_shares = [copier.send(done, spot, *to_chip(p)) for p in twins]
        copier.send(done, spot, "ctx", sibling)
        copier.keep(done, spot)
        half = pl.ds(pl.multiple_of(core * 64, 64), 64)
        a_shares = [copier.send(a_done, og_ref.at[half, lanes(chip)], *to_chip(p)) for p in twins]
        copier.send(a_done, og_ref.at[half, lanes(chip)], "ctx", sibling)
        copier.keep(a_done, og_ref.at[half, lanes(chip)])
        copier.send(lp_ref, lo_ref, "exp", lax.rem(me + 4, EXP))

        for at in gain_trades:
            copier.arrived(at)
        total = packets[0]
        for e in range(1, EXP):
            total = total + packets[e]
        mine[...] = total
        gain_shares = [copier.send(mine, shared.at[ctx], "ctx", p) for p in others]
        shared[ctx] = total

        inner = inner * (1.0 / WIDTH)
        cut = scale * scale * scale * inner
        for e in range(EXP):
            at = slice(e * 128, (e + 1) * 128)
            di_ref[:, at] = r_v[:, at] + scale * pieces[e] - x[:, at] * cut
        for at in second:
            copier.arrived(at)
        columns = [lax.rem(y + d, 4) for d in (1, 2, 3)]

        def add_experts(e, _):
            total = gp_ref[y, e].astype(F32)
            for c in columns:
                total = total + gate_c[c, e].astype(F32)
            eg_ref[e] = total
            eu_ref[e] = up_ref[zh, e].astype(F32) + up_d[e].astype(F32)
            return 0

        lax.fori_loop(0, LOCAL, add_experts, 0)
        for e in range(2):
            total = da_ref[y, e].astype(F32)
            for c in columns:
                total = total + down_c[c, e].astype(F32)
            ed_ref[e] = total
            ed_ref[e + 2] = db_ref[zh, e].astype(F32) + down_d[e].astype(F32)
        for d, at in zip((2, 6, 4, 1, 3, 5, 7), w_shares):
            copier.arrived(at)
            got_at = dense_ref.at[core, :, lanes(lax.rem(chip + CHIPS - d, CHIPS))]
            copier.send(got_at, got_at, "ctx", sibling)
        for d, at in zip((2, 6, 4, 1, 3, 5, 7), a_shares):
            copier.arrived(at)
            got_at = og_ref.at[half, lanes(lax.rem(chip + CHIPS - d, CHIPS))]
            copier.send(got_at, got_at, "ctx", sibling)
        for at in gain_shares:
            copier.arrived(at)
        total = shared[0]
        for c in range(1, CTX):
            total = total + shared[c]
        gs_ref[...] = total
        copier.finish()

    vmem = pl.BlockSpec(memory_space=pltpu.VMEM)
    block = (CHIPS, ROWS, 128)
    tile = pltpu.VMEM((128, 128), BF16)
    return pl.pallas_call(
        body,
        name="tail",
        out_shape=[
            jax.ShapeDtypeStruct((LOCAL, 64, FF), F32),
            jax.ShapeDtypeStruct((LOCAL, 64, FF), F32),
            jax.ShapeDtypeStruct((LOCAL, 32, WIDTH), F32),
            jax.ShapeDtypeStruct((ROWS, WIDTH), F32),
            jax.ShapeDtypeStruct((2, 128, WIDTH), BF16),
            jax.ShapeDtypeStruct((128, WIDTH), BF16),
            jax.ShapeDtypeStruct((ROWS, WIDTH), BF16),
            jax.ShapeDtypeStruct((8, 128), F32),
        ],
        in_specs=[ANY_SPEC] * 7 + [vmem] * 2 + [ANY_SPEC] * 6 + [vmem] * 5,
        out_specs=[vmem] * 4 + [ANY_SPEC] * 3 + [vmem],
        scratch_shapes=[
            pltpu.VMEM(block, F32),
            pltpu.VMEM(block, F32),
            pltpu.VMEM(block, F32),
            pltpu.VMEM(block, F32),
            pltpu.VMEM(block, F32),
            pltpu.VMEM(block, F32),
            pltpu.VMEM((CHIPS, ROWS, WIDTH), BF16),
            pltpu.VMEM((EXP, 128, 2 * WIDTH), BF16),
            pltpu.VMEM((ROWS, WIDTH), BF16),
            pltpu.VMEM((ROWS, WIDTH), F32),
            pltpu.VMEM(block, BF16),
            pltpu.VMEM(block, F32),
            pltpu.VMEM(block, F32),
            pltpu.VMEM((CHIPS, 2, ROWS), F32),
            pltpu.VMEM((CHIPS, CHIPS, 2, ROWS), F32),
            pltpu.VMEM((2,) + block, BF16),
            pltpu.VMEM((2, ROWS, WIDTH), BF16),
            pltpu.VMEM((WIDTH, 128), BF16),
            pltpu.VMEM((WIDTH, 128), BF16),
            pltpu.VMEM((WIDTH, 128), BF16),
            pltpu.VMEM((EXP, 128, 128), BF16),
            pltpu.VMEM((EXP, 128, 128), BF16),
            tile,
            pltpu.VMEM((EXP, 64, WIDTH), BF16),
            pltpu.VMEM((EXP, 64, WIDTH), BF16),
            pltpu.VMEM((EXP, 64, WIDTH), BF16),
            pltpu.VMEM((64, WIDTH), BF16),
            pltpu.VMEM((CHIPS, 64, 128), BF16),
            pltpu.VMEM((64, 128), BF16),
            pltpu.VMEM((EXP, 8, 128), F32),
            pltpu.VMEM((EXP, 8, 128), F32),
            pltpu.VMEM((8, 128), F32),
            pltpu.VMEM((CTX, 8, 128), F32),
            pltpu.VMEM((4, LOCAL, 64, FF), BF16),
            pltpu.VMEM((4, 2, 32, WIDTH), BF16),
            pltpu.VMEM((LOCAL, 64, FF), BF16),
            pltpu.VMEM((2, 32, WIDTH), BF16),
            pltpu.SemaphoreType.DMA((106,)),
            pltpu.SemaphoreType.DMA((106,)),
            pltpu.SemaphoreType.DMA((14,)),
        ],
        compiler_params=pltpu.CompilerParams(
            collective_id=6, has_side_effects=True, vmem_limit_bytes=60 * MIB
        ),
    )(
        dq, dkv_mine, dkv_other, q_lin, kv_lin, cosine, sine, squares, gains, normed, out_part, layer_part,
        weights, tokens, d_resid, ffn_gain, gate_part, up_part, down_a, down_b,
    )


def sum_blocks(blocks):
    return jnp.sum(blocks.astype(F32), axis=0)


def per_device(
    tokens,
    cotangent,
    lengths,
    deal_perm,
    routes,
    gate_logits,
    norm_attn,
    norm_query,
    norm_key,
    norm_ffn,
    w_query,
    w_key,
    w_value,
    w_out,
    w_gate,
    w_up,
    w_down,
):
    tokens, cotangent = tokens[0], cotangent[0]

    row = lambda v: v.reshape(1, -1)
    (
        w_o, gain_all, normed, q_lin, kv_lin, squares, cosine, sine, places, q_all, kv_all, grads_all,
    ) = front(
        tokens,
        cotangent,
        (w_query, w_key, w_value, w_out),
        (row(norm_attn), row(norm_query), row(norm_key), row(norm_ffn)),
        deal_perm[0],
        lengths,
    )

    pieces = jnp.arange(CTX, dtype=jnp.int32)[:, None] * CTX + deal_perm[0]
    positions = (pieces[:, :, None] * 12 + jnp.arange(12, dtype=jnp.int32)).reshape(CTX, ROWS)
    key_pos = positions.reshape(CHIPS, 1, CHUNK).astype(F32)
    first_chunk = jnp.min(places[:, 1], axis=1).astype(jnp.int32) // CHUNK
    gains = gain_all.transpose(1, 0, 2).reshape(8, WIDTH)
    w_o = w_o.reshape(WIDTH, WIDTH)
    kv_all = kv_all.reshape(KEYS, 128)
    out_low, out_wide, log_total = attend(q_all, kv_all, key_pos, places, first_chunk)
    attended = collect_heads(out_low)
    resid, ffn_rows = finish_attention(attended, w_o, tokens, gains)
    rows_all, meta_all = gather_rows(ffn_rows, route(routes[0].T, gate_logits[0].T))

    rows_all, dense_late = lax.optimization_barrier(
        (rows_all, jnp.concatenate([w_query, w_key, w_value], axis=1))
    )
    dense_late = lax.all_gather(dense_late, "exp", axis=0, tiled=True)

    shift = jnp.array([0.0, float(CAP)], F32)[None, None, :, None]
    spots = meta_all[:, :LOCAL].reshape(PAIRS, 2, LOCAL, ROWS).transpose(0, 2, 1, 3)
    spots = jnp.where(spots < 0.0, -1.0, spots + shift).reshape(PAIRS, LOCAL, PAIR_ROWS)
    gates = meta_all[:, LOCAL:].reshape(PAIRS, 2, LOCAL, ROWS).transpose(0, 2, 1, 3)
    pair_meta = jnp.concatenate([spots, gates.reshape(PAIRS, LOCAL, PAIR_ROWS)], axis=1)
    rows_in, d_rows, act, d_gate, d_up, out_parts, d_parts = experts(
        rows_all.reshape(PAIRS, PAIR_ROWS, WIDTH),
        grads_all.reshape(PAIRS, PAIR_ROWS, WIDTH),
        pair_meta,
        pair_meta.transpose(0, 2, 1),
        w_gate,
        w_up,
        w_down,
    )
    gate_part, up_part, down_a, down_b, d_ffn, layer_keep, layer_give = settle_experts(
        rows_in,
        d_rows,
        act,
        d_gate,
        d_up,
        d_parts.reshape(2, 4, ROWS, WIDTH),
        out_parts.reshape(2, 4, ROWS, WIDTH),
    )
    d_resid, d_branch, d_attended, ffn_gain_grad = back_to_branch(
        d_ffn, resid, cotangent, gains, w_o
    )
    d_out = spread_grads(d_attended)
    out_part = out_grads(attended, d_branch).reshape(EXP, 2, 64, WIDTH)
    dq, dkv_mine, dkv_other = attend_back(
        q_all, kv_all, d_out, out_wide, log_total, key_pos, places, first_chunk
    )
    gate_grad, up_grad, down_grad, input_grad, dense, out_grad, layer_got, gain_sums = tail(
        dq,
        dkv_mine,
        dkv_other,
        q_lin,
        kv_lin,
        cosine,
        sine,
        squares,
        gain_all,
        normed,
        out_part,
        layer_give,
        dense_late.reshape(EXP, 128, 2 * WIDTH),
        tokens,
        d_resid,
        ffn_gain_grad,
        gate_part,
        up_part,
        down_a,
        down_b,
    )
    outs = deliver(
        resid,
        layer_keep,
        layer_got,
        dense,
        out_grad,
        gain_sums,
        input_grad,
        (gate_grad, up_grad, down_grad),
    )
    return (
        outs[0][None],
        outs[9][None],
        *outs[1:5],
        *[g.reshape(-1) for g in outs[5:9]],
        *outs[10:],
    )


def solution(mesh):
    in_specs = (
        P("exp", "ctx", None),
        P("exp", "ctx", None),
        P("exp", None),
        P("exp", None, None),
        P("exp", "ctx", None),
        P("exp", "ctx", None),
        P("exp"),
        P("exp"),
        P("exp"),
        P("exp"),
        P("exp", None),
        P("exp", None),
        P("exp", None),
        P("exp", None),
        P("exp", None, None),
        P("exp", None, None),
        P("exp", None, None),
    )
    out_specs = (
        P("exp", "ctx", None),
        P("exp", "ctx", None),
        P("exp", None),
        P("exp", None),
        P("exp", None),
        P("exp", None),
        P("exp"),
        P("exp"),
        P("exp"),
        P("exp"),
        P("exp", "ctx", None),
        P("exp", "ctx", None),
        P("exp", "ctx", None),
    )
    return jax.shard_map(
        per_device, mesh=mesh, in_specs=in_specs, out_specs=out_specs, check_vma=False
    )
```

```python
import jax
import jax.numpy as jnp
from jax import lax
from jax.experimental import pallas as pl
from jax.experimental.pallas import tpu as pltpu
from jax.sharding import PartitionSpec as P

HEADS = 16
KV_HEADS = 8
EPSILON = 1e-05
ROPE_BASE = 10000.0
MASKED = -1e30

MESH = pl.DeviceIdType.MESH
CTX = 16
EXP = 8
CHIPS = 8
ROWS = 192
WIDTH = 1024
FF = 512
LOCAL = 4
CAP = 72
PAIRS = EXP // 2
PAIR_ROWS = 2 * ROWS
PAIR_CAP = 2 * CAP
SLOTS = EXP * CAP
PAIR_SLOTS = LOCAL * PAIR_CAP
KEYS = CTX * ROWS
CHUNK = 2 * ROWS
MIB = 1 << 20
FAR_FIRST = (6, 2, 5, 7, 4, 1, 3)

ANY_SPEC = pl.BlockSpec(memory_space=pl.ANY)
F32 = jnp.float32
BF16 = jnp.bfloat16


def dot(a, b, dims=((1,), (0,))):
    return lax.dot_general(a, b, (dims, ((), ())), preferred_element_type=F32)


NT = ((1,), (1,))
TN = ((0,), (0,))


def comm_call(body, name, collective_id, outs, ins, copies, in_specs=None):
    return pl.pallas_call(
        body,
        name=name,
        out_shape=outs,
        in_specs=in_specs or [ANY_SPEC] * len(ins),
        out_specs=[ANY_SPEC] * len(outs),
        scratch_shapes=[
            pltpu.SemaphoreType.DMA((copies,)),
            pltpu.SemaphoreType.DMA((copies,)),
            pltpu.SemaphoreType.DMA((8,)),
        ],
        compiler_params=pltpu.CompilerParams(
            collective_id=collective_id, has_side_effects=True, vmem_limit_bytes=60 * MIB
        ),
    )(*ins)


class Copier:
    def __init__(self, send_sem, recv_sem, local_sem):
        self.send_sem, self.recv_sem, self.local_sem = send_sem, recv_sem, local_sem
        self.remote, self.local = [], []

    def send(self, src, dst, axis, index):
        at = len(self.remote)
        copy = pltpu.make_async_remote_copy(
            src_ref=src,
            dst_ref=dst,
            send_sem=self.send_sem.at[at],
            recv_sem=self.recv_sem.at[at],
            device_id={axis: index},
            device_id_type=MESH,
        )
        copy.start()
        self.remote.append([copy, False])
        return at

    def keep(self, src, dst):
        copy = pltpu.make_async_copy(src, dst, self.local_sem.at[len(self.local)])
        copy.start()
        self.local.append([copy, False])
        return len(self.local) - 1

    def arrived(self, at):
        self.remote[at][0].wait_recv()
        self.remote[at][1] = True

    def kept(self, at):
        self.local[at][0].wait()
        self.local[at][1] = True

    def finish(self):
        for copy, seen in self.remote:
            if not seen:
                copy.wait_recv()
        for copy, _ in self.remote:
            copy.wait_send()
        for copy, seen in self.local:
            if not seen:
                copy.wait()


def meet(partners):
    barrier = pltpu.get_barrier_semaphore()
    for axis, index in partners:
        pl.semaphore_signal(barrier, inc=1, device_id={axis: index}, device_id_type=MESH)
    pl.semaphore_wait(barrier, len(partners))


def place():
    ctx = lax.axis_index("ctx")
    core = lax.rem(ctx, 2)
    return ctx, ctx // 2, core, ctx + 1 - 2 * core


def ring_of(me):
    half, spot = me // 4, lax.rem(me, 4)
    over = (1 - half) * 4
    turns = [lax.rem(spot + d, 4) for d in (0, 1, 3, 2)]
    return tuple([half * 4 + t for t in turns] + [over + t for t in turns])


def relay(copier, own, slot, rows, ring, reach, landed=lambda partner: None):
    me, right, left, far, over, over_right, over_left, over_far = ring
    half = rows // 2
    low, high = pl.ds(0, half), pl.ds(half, half)

    def send(block, to, part, partner):
        return copier.send(block.at[part], slot(to).at[part], *reach(partner))

    def on(of, part, partner):
        return send(slot(of), of, part, partner)

    over_low = send(own, me, low, over)
    over_high = send(own, me, high, over)
    yield
    right_low = send(own, me, low, right)
    left_high = send(own, me, high, left)
    right_high = send(own, me, high, right)
    left_low = send(own, me, low, left)
    yield
    copier.arrived(right_low)
    far_right = on(left, low, right)
    copier.arrived(left_high)
    far_left = on(right, high, left)
    yield
    copier.arrived(over_low)
    next_right_low = on(over, low, right)
    next_left_low = on(over, low, left)
    copier.arrived(over_high)
    next_left_high = on(over, high, left)
    next_right_high = on(over, high, right)
    landed(over)
    yield
    copier.arrived(right_high)
    landed(left)
    copier.arrived(left_low)
    landed(right)
    yield
    copier.arrived(far_right)
    copier.arrived(far_left)
    landed(far)
    yield
    copier.arrived(next_right_low)
    far_right = on(over_left, low, right)
    copier.arrived(next_left_high)
    far_left = on(over_right, high, left)
    copier.arrived(next_right_high)
    landed(over_left)
    copier.arrived(next_left_low)
    landed(over_right)
    yield
    copier.arrived(far_right)
    copier.arrived(far_left)
    landed(over_far)


def side_by_side(*relays):
    for _ in zip(*relays):
        pass
    for one in relays:
        for _ in one:
            pass


def lanes(index):
    return pl.ds(pl.multiple_of(index * 128, 128), 128)


def join_heads(blocks, w_out, tokens, gains, routes_t, logits_t):
    def body(
        x_ref, w_ref, t_ref, g_ref, r_ref, l_ref,
        a_ref, res_ref, o_ref, mo_ref, w_v, ffn, m_v, send_sem, recv_sem, local_sem,
    ):
        _, chip, core, _ = place()
        ring = ring_of(lax.axis_index("exp"))
        me = ring[0]
        twins = [lax.rem(chip + d, CHIPS) for d in FAR_FIRST]
        to_chip = lambda p: ("ctx", 2 * p + core)
        to_exp = lambda p: ("exp", p)
        copier = Copier(send_sem, recv_sem, local_sem)
        load = copier.keep(w_ref, w_v)
        meet([to_chip(p) for p in twins] + [to_exp(p) for p in ring[1:]])
        arrivals = [copier.send(x_ref.at[p], a_ref.at[:, lanes(chip)], *to_chip(p)) for p in twins]
        own = copier.keep(x_ref.at[chip], a_ref.at[:, lanes(chip)])

        logits = l_ref[...]
        raised = jnp.exp(logits - jnp.max(logits, axis=0, keepdims=True))
        gates = raised / jnp.sum(raised, axis=0, keepdims=True)
        experts = lax.broadcasted_iota(jnp.int32, (32, ROWS), 0)
        member = jnp.zeros((32, ROWS), F32)
        weight = jnp.zeros((32, ROWS), F32)
        for c in range(8):
            hit = r_ref[c : c + 1, :] == experts
            member = member + jnp.where(hit, 1.0, 0.0)
            weight = weight + jnp.where(hit, gates[c : c + 1, :], 0.0)
        before = lax.broadcasted_iota(jnp.int32, (ROWS, ROWS), 0) < lax.broadcasted_iota(
            jnp.int32, (ROWS, ROWS), 1
        )
        rank = dot(member.astype(BF16), jnp.where(before, 1.0, 0.0).astype(BF16))
        spot = jnp.where(member > 0.5, rank, -1.0)
        for e in range(EXP):
            m_v[e, 0:4, :] = spot[e * 4 : e * 4 + 4, :]
            m_v[e, 4:8, :] = weight[e * 4 : e * 4 + 4, :]
        for p in ring[1:]:
            copier.send(m_v.at[p], mo_ref.at[me], *to_exp(p))
        copier.keep(m_v.at[me], mo_ref.at[me])

        copier.kept(load)
        copier.kept(own)
        for at in arrivals:
            copier.arrived(at)
        branch = dot(a_ref[...], w_v[...]).astype(BF16).astype(F32)
        resid = t_ref[...].astype(F32) + branch
        res_ref[...] = resid
        scale = row_scale(jnp.sum(resid * resid, axis=1, keepdims=True), WIDTH)
        for e in range(EXP):
            at = slice(e * 128, (e + 1) * 128)
            ffn[:, at] = (resid[:, at] * scale * g_ref[e, 3:4, :]).astype(BF16)
        rows_out = relay(copier, ffn, lambda s: o_ref.at[s], ROWS, ring, to_exp)
        next(rows_out)
        next(rows_out)
        copier.keep(ffn, o_ref.at[me])
        side_by_side(rows_out)
        copier.finish()

    vmem = pl.BlockSpec(memory_space=pltpu.VMEM)
    return pl.pallas_call(
        body,
        name="join_heads",
        out_shape=[
            jax.ShapeDtypeStruct((ROWS, WIDTH), BF16),
            jax.ShapeDtypeStruct((ROWS, WIDTH), F32),
            jax.ShapeDtypeStruct((EXP, ROWS, WIDTH), BF16),
            jax.ShapeDtypeStruct((EXP, 8, ROWS), F32),
        ],
        in_specs=[ANY_SPEC] * 2 + [vmem] * 4,
        out_specs=[vmem, vmem, ANY_SPEC, ANY_SPEC],
        scratch_shapes=[
            pltpu.VMEM((WIDTH, WIDTH), BF16),
            pltpu.VMEM((ROWS, WIDTH), BF16),
            pltpu.VMEM((EXP, 8, ROWS), F32),
            pltpu.SemaphoreType.DMA((28,)),
            pltpu.SemaphoreType.DMA((28,)),
            pltpu.SemaphoreType.DMA((8,)),
        ],
        compiler_params=pltpu.CompilerParams(
            collective_id=2, has_side_effects=True, vmem_limit_bytes=60 * MIB
        ),
    )(blocks, w_out, tokens, gains, routes_t, logits_t)


def settle_experts(
    rows, d_rows, act, d_gate, d_up, d_parts, layer_parts, resid, cotangent, gains, w_out
):
    def body(
        x_ref, r_ref, a_ref, g_ref, u_ref, p_ref, l_ref, res_ref, cot_ref, gain_ref, w_ref,
        gate_out, up_out, down_a_out, down_b_out, dr_out, db_out, gg_out, do_out, keep_out, give_out, dx_out, d_att,
        x_v, r_v, a_v, g_v, u_v, gate, up, down, gate_o, up_o, down_o, gate_a, down_a, up_b, down_b,
        to_z, from_z, d_own, d_right, d_left, d_low, d_high, d_from, l_own, l_right, l_left, l_low, l_high, l_from, send_sem, recv_sem, local_sem,
    ):
        _, chip, core, sibling = place()
        me = lax.axis_index("exp")
        zl, x = me // 4, lax.rem(me, 4)
        zh, y = chip // 4, lax.rem(chip, 4)
        at_ctx = lambda z, yy: ("ctx", z * 8 + yy * 2 + core)
        over = at_ctx(1 - zh, y)
        columns = [lax.rem(y + d, 4) for d in (1, 3, 2)]
        twins = [lax.rem(chip + d, CHIPS) for d in FAR_FIRST]
        right, left, far = [lax.rem(x + d, 4) for d in (1, 3, 2)]
        at_exp = lambda p: ("exp", zl * 4 + p)
        low, high = pl.ds(0, ROWS // 2), pl.ds(ROWS // 2, ROWS // 2)
        copier = Copier(send_sem, recv_sem, local_sem)
        loads = []
        for e in range(LOCAL):
            pairs = ((x_ref, x_v), (r_ref, r_v), (a_ref, a_v), (g_ref, g_v), (u_ref, u_v))
            loads.append([copier.keep(src.at[e], dst.at[e]) for src, dst in pairs])
        parts = (p_ref, d_own, d_right, d_left, d_low, d_high, d_from)
        layers = (l_ref, l_own, l_right, l_left, l_low, l_high, l_from)

        def fetch(src, own, to_right, to_left, *_):
            return [
                copier.keep(src.at[:, x], own),
                copier.keep(src.at[:, right, low], to_right),
                copier.keep(src.at[:, left, high], to_left),
            ]

        part_loads, layer_loads = fetch(*parts), fetch(*layers)
        meet(
            [("ctx", sibling)]
            + [("ctx", 2 * p + core) for p in twins]
            + [at_exp(right), at_exp(left)]
            + [("exp", (1 - zl) * 4 + x)]
        )

        def set_out(src, own, to_right, to_left, in_low, in_high, arrived):
            return [
                copier.send(src.at[:, far, low], in_low, *at_exp(right)),
                copier.send(src.at[:, far, high], in_high, *at_exp(left)),
                copier.send(src.at[:, right, high], arrived.at[0, :, high], *at_exp(right)),
                copier.send(src.at[:, left, low], arrived.at[1, :, low], *at_exp(left)),
            ]

        def pass_on(stage, loads_of, src, own, to_right, to_left, in_low, in_high, arrived):
            for at in loads_of:
                copier.kept(at)
            for at in stage[:2]:
                copier.arrived(at)

            def add(r, _):
                at = pl.ds(pl.multiple_of(r * 48, 16), 48)
                for z in range(2):
                    for mine, other in ((to_right, in_low), (to_left, in_high)):
                        mine[z, at, :] = (mine[z, at, :].astype(F32) + other[z, at, :].astype(F32)).astype(BF16)
                return 0

            lax.fori_loop(0, 2, add, 0)
            return stage[2:] + [
                copier.send(to_right, arrived.at[0, :, low], *at_exp(right)),
                copier.send(to_left, arrived.at[1, :, high], *at_exp(left)),
            ]

        part_stage = set_out(*parts)

        def work(e):
            for at in loads[e]:
                copier.kept(at)

            def wide(r, _):
                rows_r = x_v[e, :, pl.ds(pl.multiple_of(r * 256, 256), 256)]
                for d_v, o_v in ((g_v, gate), (u_v, up)):
                    grad = dot(rows_r, d_v[e], TN).astype(BF16)
                    for k in range(4):
                        o_v[k % 2, r // 2, 2 * lax.rem(r, 2) + k // 2, e] = grad[k * 64 : (k + 1) * 64]
                return 0

            lax.fori_loop(0, 4, wide, 0)

            def tall(r, _):
                act_r = a_v[e, :, pl.ds(pl.multiple_of(r * 256, 256), 256)]
                grad = dot(act_r, r_v[e], TN).astype(BF16)
                for k in range(8):
                    down[k % 2, r, k // 2, e] = grad[k * 32 : (k + 1) * 32]
                return 0

            lax.fori_loop(0, 2, tall, 0)
            return [
                copier.send(full.at[1 - core, :, :, e], other.at[:, :, e], "ctx", sibling)
                for full, other in ((gate, gate_o), (up, up_o), (down, down_o))
            ]

        first_a, first_b = [], []

        def join(e, swaps):
            for at in swaps:
                copier.arrived(at)

            def add(c, _):
                z, yy = c // 4, lax.rem(c, 4)
                for full, other in ((gate, gate_o), (up, up_o), (down, down_o)):
                    both = full[core, z, yy, e].astype(F32) + other[z, yy, e].astype(F32)
                    full[core, z, yy, e] = both.astype(BF16)
                return 0

            lax.fori_loop(0, CHIPS, add, 0)
            first_a.append(copier.send(gate.at[core, 1 - zh, :, e], gate_a.at[:, e], *over))
            if e < 2:
                first_a.append(copier.send(down.at[core, 1 - zh, :, e], down_a.at[:, e], *over))
            for c in columns:
                to = at_ctx(zh, c)
                first_b.append(copier.send(up.at[core, :, c, e], up_b.at[y, :, e], *to))
                if e >= 2:
                    first_b.append(copier.send(down.at[core, :, c, e], down_b.at[y, :, e - 2], *to))

        swaps = work(0)
        later = work(1)
        join(0, swaps)
        part_stage = pass_on(part_stage, part_loads, *parts)
        layer_stage = set_out(*layers)
        swaps = later
        later = work(2)
        join(1, swaps)
        swaps = later
        later = work(3)
        w_loads = [copier.keep(w_ref.at[pl.ds(k * FF, FF)], r_v.at[k, pl.ds(0, FF)]) for k in range(2)]
        join(2, swaps)
        join(3, later)

        def sum_up(stage, own, arrived, keep_ref, give_ref):
            for at in stage:
                copier.arrived(at)

            def add(r, _):
                at = pl.ds(pl.multiple_of(r * 48, 16), 48)
                keep, give = [
                    own[z, at, :].astype(F32) + arrived[0, z, at, :].astype(F32) + arrived[1, z, at, :].astype(F32)
                    for z in (zl, 1 - zl)
                ]
                keep_ref[at, :] = keep
                give_ref[at, :] = give.astype(BF16)
                return 0

            lax.fori_loop(0, 4, add, 0)

        sum_up(part_stage, d_own, d_from, dx_out, to_z)
        z_stage = copier.send(to_z, from_z, "exp", (1 - zl) * 4 + x)
        layer_stage = pass_on(layer_stage, layer_loads, *layers)

        copier.arrived(z_stage)
        incoming = dx_out[...] + from_z[...].astype(F32)
        resid_v = res_ref[...]
        scale = row_scale(jnp.sum(resid_v * resid_v, axis=1, keepdims=True), WIDTH)
        inner = jnp.zeros((ROWS, 1), F32)
        for e in range(EXP):
            at = slice(e * 128, (e + 1) * 128)
            product = incoming[:, at] * resid_v[:, at]
            gg_out[:, at] = jnp.sum(product * scale, axis=0, keepdims=True)
            inner = inner + jnp.sum(product * gain_ref[e, 3:4, :], axis=1, keepdims=True)
        cut = scale * scale * scale * inner * (1.0 / WIDTH)
        for e in range(EXP):
            at = slice(e * 128, (e + 1) * 128)
            d_norm = scale * (incoming[:, at] * gain_ref[e, 3:4, :]) - resid_v[:, at] * cut
            d_resid = cot_ref[:, at].astype(F32) + d_norm
            dr_out[:, at] = d_resid
            db_out[:, at] = d_resid.astype(BF16)
        for at in w_loads:
            copier.kept(at)
        for k in range(2):
            d_att[:, k * FF : (k + 1) * FF] = dot(db_out[...], r_v[k, 0:FF, :], NT).astype(BF16)
        for p in twins:
            copier.send(d_att.at[:, lanes(p)], do_out.at[chip], "ctx", 2 * p + core)
        copier.keep(d_att.at[:, lanes(chip)], do_out.at[chip])
        for at in first_a:
            copier.arrived(at)

        def sum_a(c, _):
            for e in range(LOCAL):
                both = gate[core, zh, c, e].astype(F32) + gate_a[c, e].astype(F32)
                gate_out[c, e] = both.astype(BF16)
            for e in range(2):
                both = down[core, zh, c, e].astype(F32) + down_a[c, e].astype(F32)
                down_a_out[c, e] = both.astype(BF16)
            return 0

        lax.fori_loop(0, 4, sum_a, 0)

        for at in first_b:
            copier.arrived(at)
        others = [lax.rem(y + d, 4) for d in (1, 2, 3)]

        def sum_b(e, _):
            for z in range(2):
                total = up[core, z, y, e].astype(F32)
                for c in others:
                    total = total + up_b[c, z, e].astype(F32)
                up_out[z, e] = total.astype(BF16)
            return 0

        lax.fori_loop(0, LOCAL, sum_b, 0)

        def sum_b_down(e, _):
            for z in range(2):
                total = down[core, z, y, e + 2].astype(F32)
                for c in others:
                    total = total + down_b[c, z, e].astype(F32)
                down_b_out[z, e] = total.astype(BF16)
            return 0

        lax.fori_loop(0, 2, sum_b_down, 0)
        sum_up(layer_stage, l_own, l_from, keep_out, give_out)
        copier.finish()

    vmem = pl.BlockSpec(memory_space=pltpu.VMEM)
    buf = lambda *shape: pltpu.VMEM(shape, BF16)
    wide, tall = (64, FF), (32, WIDTH)
    return pl.pallas_call(
        body,
        name="settle_experts",
        out_shape=[
            jax.ShapeDtypeStruct((4, LOCAL) + wide, BF16),
            jax.ShapeDtypeStruct((2, LOCAL) + wide, BF16),
            jax.ShapeDtypeStruct((4, 2) + tall, BF16),
            jax.ShapeDtypeStruct((2, 2) + tall, BF16),
            jax.ShapeDtypeStruct((ROWS, WIDTH), F32),
            jax.ShapeDtypeStruct((ROWS, WIDTH), BF16),
            jax.ShapeDtypeStruct((1, WIDTH), F32),
            jax.ShapeDtypeStruct((CHIPS, ROWS, 128), BF16),
            jax.ShapeDtypeStruct((ROWS, WIDTH), F32),
            jax.ShapeDtypeStruct((ROWS, WIDTH), BF16),
        ],
        in_specs=[ANY_SPEC] * 7 + [vmem] * 3 + [ANY_SPEC],
        out_specs=[vmem] * 7 + [ANY_SPEC] + [vmem] * 2,
        scratch_shapes=[
            pltpu.VMEM((ROWS, WIDTH), F32),
            buf(ROWS, WIDTH),
            buf(LOCAL, SLOTS, WIDTH),
            buf(LOCAL, SLOTS, WIDTH),
            buf(LOCAL, SLOTS, FF),
            buf(LOCAL, SLOTS, FF),
            buf(LOCAL, SLOTS, FF),
            buf(2, 2, 4, LOCAL, *wide),
            buf(2, 2, 4, LOCAL, *wide),
            buf(2, 2, 4, LOCAL, *tall),
            buf(2, 4, LOCAL, *wide),
            buf(2, 4, LOCAL, *wide),
            buf(2, 4, LOCAL, *tall),
            buf(4, LOCAL, *wide),
            buf(4, 2, *tall),
            buf(4, 2, LOCAL, *wide),
            buf(4, 2, 2, *tall),
            buf(ROWS, WIDTH),
            buf(ROWS, WIDTH),
        ]
        + [
            buf(2, ROWS, WIDTH),
            buf(2, ROWS // 2, WIDTH),
            buf(2, ROWS // 2, WIDTH),
            buf(2, ROWS // 2, WIDTH),
            buf(2, ROWS // 2, WIDTH),
            buf(2, 2, ROWS, WIDTH),
        ]
        * 2
        + [
            pltpu.SemaphoreType.DMA((56,)),
            pltpu.SemaphoreType.DMA((56,)),
            pltpu.SemaphoreType.DMA((32,)),
        ],
        compiler_params=pltpu.CompilerParams(
            collective_id=8, has_side_effects=True, vmem_limit_bytes=63 * MIB
        ),
    )(rows, d_rows, act, d_gate, d_up, d_parts, layer_parts, resid, cotangent, gains, w_out)


def compute_call(body, name, outs, ins, vmem=60, **kw):
    return pl.pallas_call(
        body,
        name=name,
        out_shape=outs,
        compiler_params=pltpu.CompilerParams(vmem_limit_bytes=vmem * MIB),
        **kw,
    )(*ins)


def row_scale(total, width):
    return lax.rsqrt(total * (1.0 / width) + EPSILON)


def key_lanes():
    return lax.broadcasted_iota(jnp.int32, (1, 128), 1) < 64


def turn(values, cosine, sine):
    first = lax.rem(lax.broadcasted_iota(jnp.int32, (1, 128), 1), 64) < 32
    return values * cosine + jnp.where(first, -pltpu.roll(values, 96, 1), pltpu.roll(values, 32, 1)) * sine


def across(select, values):
    return lax.dot_general(
        select, values, (NT, ((), ())), precision=lax.Precision.HIGHEST, preferred_element_type=F32
    )


def both_totals(left, right):
    row_id = lax.broadcasted_iota(jnp.int32, (8, 128), 0)
    ones = jnp.where(row_id == 0, 1.0, 0.0)
    keys = jnp.where((row_id == 1) & key_lanes(), 1.0, 0.0)
    return (across(ones, left) + across(keys, right))[0:2, :]


def down_rows(values, row, width=128):
    chosen = lax.broadcasted_iota(jnp.int32, (2, width), 0) == row
    return lax.dot_general(
        values,
        jnp.where(chosen, 1.0, 0.0),
        (TN, ((), ())),
        precision=lax.Precision.HIGHEST,
        preferred_element_type=F32,
    )


def own_chip():
    return lax.axis_index("ctx") // 2


def key_columns(row):
    upper = jnp.floor(row * (1.0 / 64.0))
    parts = jnp.concatenate([upper, row - 64.0 * upper], axis=0).astype(BF16)
    scale = jnp.where(lax.broadcasted_iota(jnp.int32, (2, 128), 0) == 0, 64.0, 1.0).astype(BF16)
    return dot(parts, scale, TN)


def pair_rows(places_i):
    return [jnp.concatenate([places_i[k : k + 1, :]] * 2, axis=1) for k in range(2)]


def attend(q, kv, key_pos, places, chunks):
    def body(at_ref, q_ref, kv_ref, kp_ref, p_ref, o_ref, ot_ref, l_ref, keys, values, key_at):
        low = key_lanes()

        def place_keys(p, _):
            rows = pl.ds(pl.multiple_of(p * CHUNK, CHUNK), CHUNK)
            both = kv_ref[rows, :].astype(F32)
            keys[rows, :] = jnp.where(low, both, 0.0).astype(BF16)
            values[:, rows] = jnp.where(low, pltpu.roll(both, 64, 1), 0.0).T.astype(BF16)
            key_at[rows, :] = key_columns(kp_ref[p])
            return 0

        lax.fori_loop(0, CHIPS, place_keys, 0)

        def block(i, _):
            wide = q_ref[i].astype(F32)
            stacked = jnp.concatenate([wide, pltpu.roll(wide, 64, 1)], axis=0).astype(BF16)
            at_row, start_row = pair_rows(p_ref[i])

            def step(masked, diagonal, p, carry):
                top, total, acc = carry
                rows = pl.ds(pl.multiple_of(p * CHUNK, CHUNK), CHUNK)
                scores = dot(keys[rows, :], stacked, NT)
                if masked:
                    at_key = jnp.concatenate([key_at[rows, :]] * (CHUNK // 128), axis=1)
                    seen = at_key >= start_row
                    if diagonal:
                        seen = seen & (at_key <= at_row)
                    scores = jnp.where(seen, scores, MASKED)
                new_top = jnp.maximum(top, jnp.max(scores, axis=0, keepdims=True))
                probs = jnp.exp(scores - new_top)
                scale = jnp.exp(top - new_top)
                total = total * scale + jnp.sum(probs, axis=0, keepdims=True)
                acc = acc * scale + dot(values[:, rows], probs.astype(BF16))
                return new_top, total, acc

            def masked_step(p, carry):
                return step(True, False, p, carry)

            def plain_step(p, carry):
                return step(False, False, p, carry)

            none = jnp.zeros((1, 2 * ROWS), F32)
            carry = (none + MASKED, none, jnp.zeros((128, 2 * ROWS), F32))
            carry = lax.fori_loop(at_ref[0, i], at_ref[1, i], masked_step, carry)
            carry = lax.fori_loop(at_ref[1, i], i, plain_step, carry)
            top, total, acc = step(True, True, i, carry)
            turned = acc[0:64, :] / total
            ot_ref[i] = turned
            l_ref[i] = top + jnp.log(total)
            out = jnp.concatenate([turned, turned], axis=0).T
            o_ref[i] = jnp.where(low, out[:ROWS], out[ROWS:]).astype(BF16)
            return 0

        lax.fori_loop(0, CHIPS, block, 0)

    vmem = pl.BlockSpec(memory_space=pltpu.VMEM)
    return pl.pallas_call(
        body,
        name="attend",
        out_shape=[
            jax.ShapeDtypeStruct((CHIPS, ROWS, 128), BF16),
            jax.ShapeDtypeStruct((CHIPS, 64, 2 * ROWS), F32),
            jax.ShapeDtypeStruct((CHIPS, 1, 2 * ROWS), F32),
        ],
        in_specs=[pl.BlockSpec(memory_space=pltpu.SMEM)] + [vmem] * 4,
        out_specs=[vmem] * 3,
        scratch_shapes=[
            pltpu.VMEM((KEYS, 128), BF16),
            pltpu.VMEM((128, KEYS), BF16),
            pltpu.VMEM((KEYS, 128), F32),
        ],
        compiler_params=pltpu.CompilerParams(vmem_limit_bytes=60 * MIB),
    )(chunks, q, kv, key_pos, places)


def attend_back(q, kv, d_out, out_turned, log_total, key_pos, places, chunks):
    def body(
        at_ref, q_ref, kv_ref, do_ref, ot_ref, l_ref, kp_ref, p_ref,
        dq_ref, mine_ref, other_ref, keys, values, acc, key_at, keys_t,
    ):
        low = key_lanes()

        def place_keys(p, _):
            rows = pl.ds(pl.multiple_of(p * CHUNK, CHUNK), CHUNK)
            both = kv_ref[rows, :].astype(F32)
            own_keys = jnp.where(low, both, 0.0)
            keys[rows, :] = own_keys.astype(BF16)
            keys_t[:, rows] = own_keys.T.astype(BF16)
            values[rows, :] = jnp.where(low, pltpu.roll(both, 64, 1), 0.0).astype(BF16)
            key_at[rows, :] = key_columns(kp_ref[p])
            acc[rows, :] = jnp.zeros((CHUNK, 128), F32)
            return 0

        lax.fori_loop(0, CHIPS, place_keys, 0)

        def block(i, _):
            q_wide, do_wide = q_ref[i].astype(F32), do_ref[i].astype(F32)
            q_turned, do_turned = pltpu.roll(q_wide, 64, 1), pltpu.roll(do_wide, 64, 1)
            q_rows = jnp.concatenate([q_wide, q_turned], axis=0)
            do_rows = jnp.concatenate([do_wide, do_turned], axis=0)
            do_high = jnp.concatenate([do_turned, do_wide], axis=0)
            right = [jnp.where(low, q_rows, 0.0), jnp.where(low, 0.0, do_high)]
            right = jnp.concatenate(right, axis=0).astype(BF16)
            q_rows = q_rows.astype(BF16)
            delta = jnp.sum(do_rows.T[0:64, :] * ot_ref[i], axis=0, keepdims=True)
            do_rows = do_rows.astype(BF16)
            total = l_ref[i]
            at_row, start_row = pair_rows(p_ref[i])

            def step(masked, diagonal, p, dq):
                rows = pl.ds(pl.multiple_of(p * CHUNK, CHUNK), CHUNK)
                scores = dot(keys[rows, :], q_rows, NT)
                if masked:
                    at_key = jnp.concatenate([key_at[rows, :]] * (CHUNK // 128), axis=1)
                    seen = at_key >= start_row
                    if diagonal:
                        seen = seen & (at_key <= at_row)
                    scores = jnp.where(seen, scores, MASKED)
                probs = jnp.exp(scores - total)
                d_scores = (probs * (dot(values[rows, :], do_rows, NT) - delta)).astype(BF16)
                acc[rows, :] += dot(jnp.concatenate([d_scores, probs.astype(BF16)], axis=1), right)
                return dq + dot(keys_t[:, rows], d_scores)

            def masked_step(p, dq):
                return step(True, False, p, dq)

            def plain_step(p, dq):
                return step(False, False, p, dq)

            dq = jnp.zeros((128, 2 * ROWS), F32)
            dq = lax.fori_loop(at_ref[0, i], at_ref[1, i], masked_step, dq)
            dq = lax.fori_loop(at_ref[1, i], i, plain_step, dq)
            dq = step(True, True, i, dq).T * 0.125
            dq_ref[i] = jnp.where(low, dq[:ROWS], pltpu.roll(dq[ROWS:], 64, 1))
            return 0

        lax.fori_loop(0, CHIPS, block, 0)
        core = lax.rem(lax.axis_index("ctx"), 2)

        def part(s, _):
            mine = pl.ds(pl.multiple_of((2 * s + core) * ROWS, ROWS), ROWS)
            other = pl.ds(pl.multiple_of((2 * s + 1 - core) * ROWS, ROWS), ROWS)
            mine_ref[s] = acc[mine, :]
            other_ref[s] = acc[other, :].astype(BF16)
            return 0

        lax.fori_loop(0, CHIPS, part, 0)

    vmem = pl.BlockSpec(memory_space=pltpu.VMEM)
    return pl.pallas_call(
        body,
        name="attend_back",
        out_shape=[
            jax.ShapeDtypeStruct((CHIPS, ROWS, 128), F32),
            jax.ShapeDtypeStruct((CHIPS, ROWS, 128), F32),
            jax.ShapeDtypeStruct((CHIPS, ROWS, 128), BF16),
        ],
        in_specs=[pl.BlockSpec(memory_space=pltpu.SMEM)] + [vmem] * 7,
        out_specs=[vmem] * 3,
        scratch_shapes=[
            pltpu.VMEM((KEYS, 128), BF16),
            pltpu.VMEM((KEYS, 128), BF16),
            pltpu.VMEM((KEYS, 128), F32),
            pltpu.VMEM((KEYS, 128), F32),
            pltpu.VMEM((128, KEYS), BF16),
        ],
        compiler_params=pltpu.CompilerParams(vmem_limit_bytes=60 * MIB),
    )(chunks, q, kv, d_out, out_turned, log_total, key_pos, places)


def experts(rows, grads, meta, meta_t, w_gate, w_up, w_down):
    half = SLOTS // 2

    def body(
        x_ref, g_ref, m_ref, mt_ref, wg_ref, wu_ref, wd_ref,
        xin_ref, dr_ref, act_ref, dg_ref, du_ref, out_ref, dx_ref,
        made, back, weight,
    ):
        e = pl.program_id(0)

        @pl.when(e == 0)
        def _():
            slot_id = lax.broadcasted_iota(jnp.int32, (PAIR_CAP, PAIR_ROWS), 0).astype(F32)

            def pick(p, _):
                meta_p = m_ref[p]
                parts, gates = [], []
                for k in range(LOCAL):
                    hit = slot_id == meta_p[k : k + 1, :]
                    parts.append(jnp.where(hit, 1.0, 0.0).astype(BF16))
                    gates.append(
                        jnp.sum(jnp.where(hit, meta_p[4 + k : 5 + k, :], 0.0), axis=1, keepdims=True)
                    )
                chosen = jnp.concatenate(parts, axis=0)
                rows_p = dot(chosen, x_ref[p]).astype(BF16)
                grads_p = dot(chosen, g_ref[p])
                at = pl.ds(pl.multiple_of(p * PAIR_CAP, PAIR_CAP), PAIR_CAP)
                for k in range(LOCAL):
                    piece = slice(k * PAIR_CAP, (k + 1) * PAIR_CAP)
                    xin_ref[k, at, :] = rows_p[piece]
                    dr_ref[k, at, :] = (grads_p[piece] * gates[k]).astype(BF16)
                    weight[k, at, :] = gates[k]
                return 0

            lax.fori_loop(0, PAIRS, pick, 0)

        def work(h, _):
            at = pl.ds(pl.multiple_of(h * half, half), half)
            x = xin_ref[e, at, :]
            dr = dr_ref[e, at, :]
            gate = dot(x, wg_ref[0])
            up = dot(x, wu_ref[0])
            sig = jax.nn.sigmoid(gate)
            silu = gate * sig
            act = (silu * up).astype(BF16)
            act_ref[0, at, :] = act
            d_act = dot(dr, wd_ref[0], NT)
            d_gate = (d_act * up * sig * (1.0 + gate * (1.0 - sig))).astype(BF16)
            d_up = (d_act * silu).astype(BF16)
            dg_ref[0, at, :] = d_gate
            du_ref[0, at, :] = d_up
            y = (dot(act, wd_ref[0]) * weight[e, at, :]).astype(BF16)
            dch = (dot(d_gate, wg_ref[0], NT) + dot(d_up, wu_ref[0], NT)).astype(BF16)
            place_at = pl.ds(pl.multiple_of(e * PAIR_CAP, PAIR_CAP), PAIR_CAP)
            for k in range(2):
                piece = slice(k * PAIR_CAP, (k + 1) * PAIR_CAP)
                made[2 * h + k, place_at, :] = y[piece]
                back[2 * h + k, place_at, :] = dch[piece]
            return 0

        lax.fori_loop(0, 2, work, 0)

        @pl.when(e == LOCAL - 1)
        def _():
            lane_id = lax.broadcasted_iota(jnp.int32, (PAIR_ROWS, PAIR_SLOTS), 1).astype(F32)

            def give(p, _):
                meta_p = mt_ref[p]
                chosen = jnp.zeros((PAIR_ROWS, PAIR_SLOTS), F32)
                for k in range(LOCAL):
                    spot = meta_p[:, k : k + 1]
                    lane = jnp.where(spot < 0.0, -1.0, spot + float(k * PAIR_CAP))
                    chosen = chosen + jnp.where(lane_id == lane, 1.0, 0.0)
                chosen = chosen.astype(BF16)
                dx_ref[p] = dot(chosen, back[p]).astype(BF16)
                out_ref[p] = dot(chosen, made[p]).astype(BF16)
                return 0

            lax.fori_loop(0, PAIRS, give, 0)

    def fixed(*shape):
        return pl.BlockSpec(shape, lambda e: (0,) * len(shape), pipeline_mode=pl.Buffered(1))

    def each(*shape):
        return pl.BlockSpec((1,) + shape, lambda e: (e, 0, 0))

    return compute_call(
        body,
        "experts",
        [
            jax.ShapeDtypeStruct((LOCAL, SLOTS, WIDTH), BF16),
            jax.ShapeDtypeStruct((LOCAL, SLOTS, WIDTH), BF16),
            jax.ShapeDtypeStruct((LOCAL, SLOTS, FF), BF16),
            jax.ShapeDtypeStruct((LOCAL, SLOTS, FF), BF16),
            jax.ShapeDtypeStruct((LOCAL, SLOTS, FF), BF16),
            jax.ShapeDtypeStruct((PAIRS, PAIR_ROWS, WIDTH), BF16),
            jax.ShapeDtypeStruct((PAIRS, PAIR_ROWS, WIDTH), BF16),
        ],
        [rows, grads, meta, meta_t, w_gate, w_up, w_down],
        vmem=60,
        grid=(LOCAL,),
        in_specs=[
            fixed(PAIRS, PAIR_ROWS, WIDTH),
            fixed(PAIRS, PAIR_ROWS, WIDTH),
            fixed(PAIRS, 8, PAIR_ROWS),
            fixed(PAIRS, PAIR_ROWS, 8),
            each(WIDTH, FF),
            each(WIDTH, FF),
            each(FF, WIDTH),
        ],
        out_specs=[
            fixed(LOCAL, SLOTS, WIDTH),
            fixed(LOCAL, SLOTS, WIDTH),
            each(SLOTS, FF),
            each(SLOTS, FF),
            each(SLOTS, FF),
            fixed(PAIRS, PAIR_ROWS, WIDTH),
            fixed(PAIRS, PAIR_ROWS, WIDTH),
        ],
        scratch_shapes=[
            pltpu.VMEM((PAIRS, PAIR_SLOTS, WIDTH), BF16),
            pltpu.VMEM((PAIRS, PAIR_SLOTS, WIDTH), BF16),
            pltpu.VMEM((LOCAL, SLOTS, 1), F32),
        ],
    )


def norm_back(values, total_squares, width, weighted, mask=None):
    scale = row_scale(total_squares, width)
    inner = jnp.sum(weighted * values, axis=1, keepdims=True) * (1.0 / width)
    return scale * weighted - values * (scale * scale * scale) * inner, scale


def out_grads(attended, d_branch):
    def body(a_ref, d_ref, o_ref):
        def part(r, _):
            at = pl.ds(pl.multiple_of(r * 256, 256), 256)
            o_ref[at, :] = dot(a_ref[:, at], d_ref[...], TN).astype(BF16)
            return 0

        lax.fori_loop(0, 4, part, 0)

    return compute_call(
        body, "out_grads", [jax.ShapeDtypeStruct((WIDTH, WIDTH), BF16)], [attended, d_branch]
    )[0]


def deliver(resid, layer_keep, layer_got, dense, out_grad, gain_sums, input_grad, expert_sums):
    def body(
        r_ref, k_ref, g_ref, d_ref, o_ref, s_ref, i_ref, eg_ref, eu_ref, ed_ref,
        lo, wq, wk, wv, wo, ga, gq, gk, gf, di, eg, eu, ed,
    ):
        lo[...] = (r_ref[...] + k_ref[...] + g_ref[...].astype(F32)).astype(BF16)
        wq[...] = d_ref[0].astype(F32)
        for c in range(4):
            k, v = apart([d_ref[1, :, (2 * c + j) * 128 : (2 * c + j + 1) * 128].astype(F32) for j in range(2)])
            wk[:, c * 128 : (c + 1) * 128] = k
            wv[:, c * 128 : (c + 1) * 128] = v
        wo[...] = o_ref[...].astype(F32)
        ga[...] = s_ref[0:1, :]
        gq[...] = s_ref[1:2, :]
        gk[...] = s_ref[2:3, 0:64]
        gf[...] = s_ref[3:4, :]
        di[...] = i_ref[...]
        eg[...] = eg_ref[...]
        eu[...] = eu_ref[...]
        ed[...] = ed_ref[...]

    return compute_call(
        body,
        "deliver",
        [
            jax.ShapeDtypeStruct((ROWS, WIDTH), BF16),
            jax.ShapeDtypeStruct((128, WIDTH), F32),
            jax.ShapeDtypeStruct((128, 512), F32),
            jax.ShapeDtypeStruct((128, 512), F32),
            jax.ShapeDtypeStruct((128, WIDTH), F32),
            jax.ShapeDtypeStruct((1, 128), F32),
            jax.ShapeDtypeStruct((1, 128), F32),
            jax.ShapeDtypeStruct((1, 64), F32),
            jax.ShapeDtypeStruct((1, 128), F32),
            jax.ShapeDtypeStruct((ROWS, WIDTH), F32),
        ]
        + [jax.ShapeDtypeStruct(a.shape, F32) for a in expert_sums],
        [resid, layer_keep, layer_got, dense, out_grad, gain_sums, input_grad, *expert_sums],
    )


def cosine_of_turns(turns):
    part = turns - jnp.floor(turns + 0.5)
    square = part * part * 39.47841760435743
    total = jnp.full_like(square, -1.0 / 6402373705728000.0)
    for n in (20922789888000.0, -87178291200.0, 479001600.0, -3628800.0, 40320.0, -720.0, 24.0, -2.0, 1.0):
        total = total * square + 1.0 / n
    return total


def front(tokens, cotangent, dense, norms, perm, lengths):
    half = 64

    def body(
        t_ref, cot_ref, wq_ref, wk_ref, wv_ref, wd_ref, na_ref, nq_ref, nk_ref, nf_ref, perm_ref, len_ref,
        wo_ref, go_ref, n_ref, ql_ref, kl_ref, s_ref, c_ref, sn_ref, p_ref, q_ref, kv_ref, co_ref,
        g_ref, w_mine, rows, normed, gains_v, w_own, totals, totals_all, kv_half, send_sem, recv_sem, local_sem,
    ):
        _, chip, core, sibling = place()
        me = lax.axis_index("exp")
        chips, exps = ring_of(chip), ring_of(me)
        twins = [lax.rem(chip + d, CHIPS) for d in (2, 6, 4, 1, 3, 5, 7)]
        to_chip = lambda p: ("ctx", 2 * p + core)
        to_exp = lambda p: ("exp", p)
        copier = Copier(send_sem, recv_sem, local_sem)
        keys = key_lanes()
        odd = lax.rem(chip, 2) == 1
        wk, wv = wk_ref[:, lanes(chip // 2)].astype(F32), wv_ref[:, lanes(chip // 2)].astype(F32)
        wk = jnp.where(odd, pltpu.roll(wk, 64, 1), wk)
        wv = jnp.where(odd, wv, pltpu.roll(wv, 64, 1))
        w_mine[:, 0:128] = wq_ref[:, lanes(chip)]
        w_mine[:, 128:256] = jnp.where(keys, wk, wv).astype(BF16)
        g_ref[...] = jnp.ones((8, 128), F32)
        g_ref[0:1, :] = na_ref[...].astype(F32)
        g_ref[1:2, :] = nq_ref[...].astype(F32)
        g_ref[2:3, 0:64] = nk_ref[...].astype(F32)
        g_ref[3:4, :] = nf_ref[...].astype(F32)
        meet([to_chip(p) for p in twins] + [to_exp(p) for p in exps[1:]] + [("ctx", sibling)])
        gain_sends = [copier.send(g_ref, gains_v.at[me], *to_exp(p)) for p in exps[1:]]
        part = pl.ds(pl.multiple_of(core * half, half), half)
        slot = lambda s: wo_ref.at[s, part]
        handed = []

        def norm(block, s):
            x = block.astype(F32)
            scale = row_scale(jnp.sum(x * x, axis=1, keepdims=True), WIDTH)
            for e in range(EXP):
                at = slice(e * 128, (e + 1) * 128)
                normed[s, :, at] = (x[:, at] * scale * gains_v[e, 0:1, :]).astype(BF16)

        projected = []

        def project(s):
            both = dot(normed[s], w_own[...].reshape(WIDTH, 256))
            q, kv = both[:, 0:128], both[:, 128:256]
            ql_ref[s] = q
            kl_ref[s] = kv
            totals[s] = both_totals(q * q, kv * kv)

        def landed(s):
            norm(rows[s], s)
            projected.append(s)

        main = relay(copier, t_ref, lambda s: rows.at[s], ROWS, chips, to_chip, landed)
        extra = relay(copier, cot_ref, lambda s: co_ref.at[s], ROWS, exps, to_exp)
        dense = relay(
            copier,
            wd_ref.at[part],
            slot,
            half,
            exps,
            to_exp,
            lambda s: handed.append(copier.send(slot(s), slot(s), "ctx", sibling)),
        )
        next(main)
        next(main)
        next(dense)
        next(dense)
        copier.keep(wd_ref, wo_ref.at[me])
        copier.keep(cot_ref, co_ref.at[me])
        w_own[me] = w_mine[...]
        gains_v[me] = g_ref[...]

        row = lax.broadcasted_iota(jnp.int32, (CTX, ROWS), 1)
        piece = jnp.where(row // 12 == lax.broadcasted_iota(jnp.int32, (CTX, ROWS), 0), 1.0, 0.0)
        dealt = dot(perm_ref[...].astype(F32).astype(BF16), piece.astype(BF16))
        source = lax.broadcasted_iota(jnp.int32, (CTX, ROWS), 0)
        position = (source * CTX).astype(F32) + dealt
        position = position * 12.0 + lax.rem(row, 12).astype(F32)
        begin = jnp.zeros((CTX, ROWS), F32)
        ends = jnp.zeros((1, 1), F32)
        for k in range(3):
            ends = ends + len_ref[0:1, k : k + 1].astype(F32)
            begin = jnp.where(position >= ends, ends, begin)
        for i in range(CHIPS):
            mine = [jnp.where(core == 0, v[2 * i : 2 * i + 1], v[2 * i + 1 : 2 * i + 2]) for v in (position, begin)]
            p_ref[i] = jnp.concatenate(mine, axis=0)

        def angles(i, _):
            keys = key_lanes()
            lane = lax.broadcasted_iota(jnp.int32, (1, 128), 1)
            freq = jnp.exp(lax.rem(lane, 32).astype(F32) * (-2.0 / 64 * 9.210340371976184))
            place_i = p_ref[i]
            offset = down_rows(place_i, 0) - down_rows(place_i, 1)
            mixed = cosine_of_turns(offset * (freq * 0.15915494309189535) - jnp.where(keys, 0.0, 0.25))
            other = pltpu.roll(mixed, 64, 1)
            c_ref[i] = jnp.where(keys, mixed, other)
            sn_ref[i] = jnp.where(keys, other, mixed)
            return 0

        lax.fori_loop(0, CHIPS, angles, 0)
        for at in gain_sends:
            copier.arrived(at)
        go_ref[...] = gains_v[...]
        norm(t_ref[...], chip)
        projected.append(chip)
        next(main)
        next(dense)
        next(main)
        own_sends = [copier.send(w_mine, w_own.at[me], *to_exp(p)) for p in exps[1:]]
        next(extra)
        next(extra)
        next(dense)
        next(main)
        next(main)
        next(dense)
        for at in own_sends:
            copier.arrived(at)
        for s in projected:
            project(s)
        projected.clear()
        next(extra)
        next(extra)
        next(main)
        next(dense)
        for s in projected:
            project(s)
        projected.clear()
        side_by_side(main)
        for s in projected:
            project(s)
        shares = [copier.send(totals, totals_all.at[chip], *to_chip(p)) for p in twins]
        totals_all[chip] = totals[...]
        side_by_side(dense)
        copier.keep(normed, n_ref)
        for _ in range(3):
            next(extra)
        for at in shares:
            copier.arrived(at)

        def turn_one(i, _):
            squares = totals_all[0, i]
            for c in range(1, CHIPS):
                squares = squares + totals_all[c, i]
            s_ref[i] = squares
            cos, sin = c_ref[i], sn_ref[i]
            gain = gains_v[chip]
            q = ql_ref[i] * row_scale(down_rows(squares, 0), WIDTH) * gain[1:2, :]
            q = turn(q, cos, sin).astype(BF16).astype(F32)
            q_ref[i] = (q * 0.125).astype(BF16)
            scale = jnp.where(keys, row_scale(down_rows(squares, 1), WIDTH // 2), 1.0)
            kv = kl_ref[i] * scale * gain[2:3, :]
            kv_half[i] = turn(kv, jnp.where(keys, cos, 1.0), jnp.where(keys, sin, 0.0)).astype(BF16)
            return 0

        lax.fori_loop(0, CHIPS, turn_one, 0)
        copier.send(kv_half, kv_ref.at[:, core], "ctx", sibling)
        copier.keep(kv_half, kv_ref.at[:, core])
        side_by_side(extra)
        copier.finish()

    vmem = pl.BlockSpec(memory_space=pltpu.VMEM)
    wide = jax.ShapeDtypeStruct((CHIPS, ROWS, 128), F32)
    return pl.pallas_call(
        body,
        name="front",
        out_shape=[
            jax.ShapeDtypeStruct((EXP, 128, WIDTH), BF16),
            jax.ShapeDtypeStruct((EXP, 8, 128), F32),
            jax.ShapeDtypeStruct((CHIPS, ROWS, WIDTH), BF16),
            wide,
            wide,
            jax.ShapeDtypeStruct((CHIPS, 2, ROWS), F32),
            wide,
            wide,
            jax.ShapeDtypeStruct((CHIPS, 2, ROWS), F32),
            jax.ShapeDtypeStruct((CHIPS, ROWS, 128), BF16),
            jax.ShapeDtypeStruct((CHIPS, 2, ROWS, 128), BF16),
            jax.ShapeDtypeStruct((EXP, ROWS, WIDTH), BF16),
        ],
        in_specs=[vmem] * 12,
        out_specs=[ANY_SPEC, vmem, ANY_SPEC] + [vmem] * 7 + [ANY_SPEC] * 2,
        scratch_shapes=[
            pltpu.VMEM((8, 128), F32),
            pltpu.VMEM((128, 256), BF16),
            pltpu.VMEM((CHIPS, ROWS, WIDTH), BF16),
            pltpu.VMEM((CHIPS, ROWS, WIDTH), BF16),
            pltpu.VMEM((EXP, 8, 128), F32),
            pltpu.VMEM((EXP, 128, 256), BF16),
            pltpu.VMEM((CHIPS, 2, ROWS), F32),
            pltpu.VMEM((CHIPS, CHIPS, 2, ROWS), F32),
            pltpu.VMEM((CHIPS, ROWS, 128), BF16),
            pltpu.SemaphoreType.DMA((71,)),
            pltpu.SemaphoreType.DMA((71,)),
            pltpu.SemaphoreType.DMA((8,)),
        ],
        compiler_params=pltpu.CompilerParams(
            collective_id=1, has_side_effects=True, vmem_limit_bytes=60 * MIB
        ),
    )(tokens, cotangent, *dense, *norms, perm, lengths)


def apart(pieces):
    first, second = pieces
    keys = key_lanes()
    return (
        jnp.where(keys, first, pltpu.roll(second, 64, 1)),
        jnp.where(keys, pltpu.roll(first, 64, 1), second),
    )


def tail(
    dq, dkv_mine, dkv_other, q_lin, kv_lin, cosine, sine, squares, gains, normed, out_part, layer_part,
    weights, tokens, d_resid, ffn_gain, gate_part, up_part, down_a, down_b,
):
    def body(
        dq_ref, dm_ref, do_ref, ql_ref, kl_ref, c_ref, sn_ref, s_ref, g_ref, n_ref, op_ref, lp_ref,
        w_ref, t_ref, r_ref, fg_ref, gp_ref, up_ref, da_ref, db_ref,
        eg_ref, eu_ref, ed_ref, di_ref, dense_ref, og_ref, lo_ref, gs_ref,
        dq_v, dm_v, ql_v, kl_v, c_v, sn_v, n_v, w_v, t_v, r_v,
        got, e_q, e_kv, totals, totals_all, d_lin, home, w_give, w_keep, w_got, joint, traded, done,
        o_keep, o_got, o_traded, o_pair, o_half, o_full, a_got, a_done, packet, packets, mine, shared, gate_c, down_c, up_d, down_d, send_sem, recv_sem, local_sem,
    ):
        ctx, chip, core, sibling = place()
        me = lax.axis_index("exp")
        twins = [lax.rem(chip + d, CHIPS) for d in (2, 6, 4, 1, 3, 5, 7)]
        exps = [lax.rem(me + d, EXP) for d in range(1, EXP)]
        others = [lax.rem(ctx + d, CTX) for d in range(1, CTX)]
        to_chip = lambda p: ("ctx", 2 * p + core)
        copier = Copier(send_sem, recv_sem, local_sem)
        heads = [
            copier.keep(src, dst)
            for src, dst in ((dq_ref, dq_v), (c_ref, c_v), (sn_ref, sn_v), (ql_ref, ql_v), (kl_ref, kl_v), (dm_ref, dm_v))
        ]
        late = [
            copier.keep(src, dst)
            for src, dst in ((n_ref, n_v), (w_ref, w_v), (t_ref, t_v), (r_ref, r_v))
        ]
        o_load = copier.keep(op_ref.at[:, core], o_keep)
        meet([("ctx", p) for p in others] + [("exp", p) for p in exps])
        swapped = copier.send(do_ref, got, "ctx", sibling)
        o_swap = copier.send(op_ref.at[:, 1 - core], o_got, "ctx", sibling)
        copier.send(lp_ref, lo_ref, "exp", lax.rem(me + 4, EXP))
        keys = key_lanes()
        gain = g_ref[chip]
        for at in heads:
            copier.kept(at)

        def unturn_q(i, _):
            e_q[i] = turn(dq_v[i], c_v[i], -sn_v[i])
            return 0

        lax.fori_loop(0, CHIPS, unturn_q, 0)
        copier.arrived(swapped)

        def unturn_kv(i, carry):
            q_sum, kv_sum = carry
            cos, sin = jnp.where(keys, c_v[i], 1.0), jnp.where(keys, -sn_v[i], 0.0)
            e = turn(dm_v[i] + got[i].astype(F32), cos, sin)
            e_kv[i] = e
            q_part, kv_part = e_q[i] * ql_v[i], e * kl_v[i]
            totals[i] = both_totals(q_part * gain[1:2, :], kv_part * gain[2:3, :])
            q_scale = row_scale(down_rows(s_ref[i], 0), WIDTH)
            k_scale = row_scale(down_rows(s_ref[i], 1), WIDTH // 2)
            q_sum = q_sum + jnp.sum(q_part * q_scale, axis=0, keepdims=True)
            kv_sum = kv_sum + jnp.sum(kv_part * jnp.where(keys, k_scale, 1.0), axis=0, keepdims=True)
            return q_sum, kv_sum

        none = jnp.zeros((1, 128), F32)
        q_sum, kv_sum = lax.fori_loop(0, CHIPS, unturn_kv, (none, none))
        shares = [copier.send(totals, totals_all.at[chip], *to_chip(p)) for p in twins]
        totals_all[chip] = totals[...]
        copier.kept(o_load)
        copier.arrived(o_swap)

        def add_cores(e, _):
            o_keep[e] = (o_keep[e].astype(F32) + o_got[e].astype(F32)).astype(BF16)
            return 0

        lax.fori_loop(0, EXP, add_cores, 0)
        zl, x = me // 4, lax.rem(me, 4)
        o_trades = []
        for d in (2, 1, 3):
            p = lax.rem(x + d, 4)
            for z in range(2):
                o_trades.append(copier.send(o_keep.at[z * 4 + p], o_traded.at[x, z], "exp", zl * 4 + p))
        for at in shares:
            copier.arrived(at)

        def gradient(i):
            inner = totals_all[0, i]
            for c in range(1, CHIPS):
                inner = inner + totals_all[c, i]
            squares_i = s_ref[i]
            q_scale = row_scale(down_rows(squares_i, 0), WIDTH)
            k_scale = row_scale(down_rows(squares_i, 1), WIDTH // 2)
            q_cut = q_scale * q_scale * q_scale * down_rows(inner, 0) * (1.0 / WIDTH)
            k_cut = k_scale * k_scale * k_scale * down_rows(inner, 1) * (2.0 / WIDTH)
            d_lin[0, i] = (q_scale * (e_q[i] * gain[1:2, :]) - ql_v[i] * q_cut).astype(BF16)
            kv_scale = jnp.where(keys, k_scale, 1.0)
            k_cut = jnp.where(keys, k_cut, 0.0)
            d_lin[1, i] = (kv_scale * (e_kv[i] * gain[2:3, :]) - kl_v[i] * k_cut).astype(BF16)

        homeward = []
        for p in twins:
            gradient(p)
            for k in range(2):
                homeward.append(copier.send(d_lin.at[k, p], home.at[k, :, lanes(chip)], *to_chip(p)))
        zh, y = chip // 4, lax.rem(chip, 4)
        second = []
        for d in (1, 3, 2):
            c = lax.rem(y + d, 4)
            second.append(copier.send(gp_ref.at[c], gate_c.at[y], *to_chip(zh * 4 + c)))
            second.append(copier.send(da_ref.at[c], down_c.at[y], *to_chip(zh * 4 + c)))
        second.append(copier.send(up_ref.at[1 - zh], up_d, *to_chip((1 - zh) * 4 + y)))
        second.append(copier.send(db_ref.at[1 - zh], down_d, *to_chip((1 - zh) * 4 + y)))
        gradient(chip)
        for k in range(2):
            home[k, :, lanes(chip)] = d_lin[k, chip]
        for at in late:
            copier.kept(at)

        def columns_grad(half, out):
            d = d_lin[half].reshape(CHIPS * ROWS, 128)

            def part(r, _):
                n = n_v[:, :, pl.ds(pl.multiple_of(r * 256, 256), 256)].reshape(CHIPS * ROWS, 256)
                out[pl.ds(pl.multiple_of(r * 256, 256), 256), :] = dot(n, d, TN).astype(BF16)
                return 0

            lax.fori_loop(0, 4, part, 0)

        columns_grad(1 - core, w_give)
        w_swap = copier.send(w_give, w_got, "ctx", sibling)
        columns_grad(core, w_keep)
        copier.arrived(w_swap)
        both = w_keep[...].astype(F32) + w_got[...].astype(F32)
        joint[...] = both.astype(BF16).reshape(EXP, 128, 128)
        trades = [copier.send(joint.at[p], traded.at[me], "exp", p) for p in exps]
        traded[me] = joint[me]
        for at in o_trades:
            copier.arrived(at)
        keep, give = o_keep[zl * 4 + x].astype(F32), o_keep[(1 - zl) * 4 + x].astype(F32)
        for d in (1, 2, 3):
            p = lax.rem(x + d, 4)
            keep = keep + o_traded[p, zl].astype(F32)
            give = give + o_traded[p, 1 - zl].astype(F32)
        o_half[...] = give.astype(BF16)
        o_pairs = copier.send(o_half, o_pair, "exp", (1 - zl) * 4 + x)

        for at in homeward:
            copier.arrived(at)
        k_parts, v_parts = [], []
        for c in range(4):
            k, v = apart([home[1, :, (2 * c + j) * 128 : (2 * c + j + 1) * 128].astype(F32) for j in range(2)])
            k_parts.append(k.astype(BF16))
            v_parts.append(v.astype(BF16))
        left = jnp.concatenate([home[0]] + k_parts + v_parts, axis=1)
        x = t_v[...].astype(F32)
        scale = row_scale(jnp.sum(x * x, axis=1, keepdims=True), WIDTH)
        inner = jnp.zeros((ROWS, 1), F32)
        pieces = []
        for e in range(EXP):
            at = slice(e * 128, (e + 1) * 128)
            d_normed = dot(left, w_v[e], NT).astype(BF16).astype(F32)
            packet[e] = jnp.zeros((8, 128), F32)
            packet[e, 0:1, :] = jnp.sum(d_normed * x[:, at] * scale, axis=0, keepdims=True)
            packet[e, 3:4, :] = fg_ref[:, at]
            weighted = d_normed * g_ref[e, 0:1, :]
            inner = inner + jnp.sum(weighted * x[:, at], axis=1, keepdims=True)
            pieces.append(weighted)
        copier.arrived(o_pairs)
        o_full[...] = (keep + o_pair[...].astype(F32)).astype(BF16)
        spread = [copier.send(o_full.at[:, lanes(p)], a_got.at[chip], *to_chip(p)) for p in twins]
        a_got[chip] = o_full[:, lanes(chip)]
        packet[chip, 1:2, :] = q_sum
        packet[chip, 2:3, :] = kv_sum
        gain_trades = [copier.send(packet.at[p], packets.at[me], "exp", p) for p in exps]
        packets[me] = packet[me]

        for at in trades:
            copier.arrived(at)
        total = traded[0].astype(F32)
        for e in range(1, EXP):
            total = total + traded[e].astype(F32)
        done[...] = total.astype(BF16)
        spot = dense_ref.at[core, :, lanes(chip)]
        w_shares = [copier.send(done, spot, *to_chip(p)) for p in twins]
        copier.send(done, spot, "ctx", sibling)
        copier.keep(done, spot)

        for at in gain_trades:
            copier.arrived(at)
        total = packets[0]
        for e in range(1, EXP):
            total = total + packets[e]
        mine[...] = total
        gain_shares = [copier.send(mine, shared.at[ctx], "ctx", p) for p in others]
        shared[ctx] = total

        for at in spread:
            copier.arrived(at)
        total = a_got[0].astype(F32)
        for c in range(1, CHIPS):
            total = total + a_got[c].astype(F32)
        a_done[...] = total.astype(BF16)
        half = pl.ds(pl.multiple_of(core * 64, 64), 64)
        a_shares = [copier.send(a_done, og_ref.at[half, lanes(chip)], *to_chip(p)) for p in twins]
        copier.send(a_done, og_ref.at[half, lanes(chip)], "ctx", sibling)
        copier.keep(a_done, og_ref.at[half, lanes(chip)])
        inner = inner * (1.0 / WIDTH)
        cut = scale * scale * scale * inner
        for e in range(EXP):
            at = slice(e * 128, (e + 1) * 128)
            di_ref[:, at] = r_v[:, at] + scale * pieces[e] - x[:, at] * cut
        for at in second:
            copier.arrived(at)
        columns = [lax.rem(y + d, 4) for d in (1, 2, 3)]

        def add_experts(e, _):
            total = gp_ref[y, e].astype(F32)
            for c in columns:
                total = total + gate_c[c, e].astype(F32)
            eg_ref[e] = total
            eu_ref[e] = up_ref[zh, e].astype(F32) + up_d[e].astype(F32)
            return 0

        lax.fori_loop(0, LOCAL, add_experts, 0)
        for e in range(2):
            total = da_ref[y, e].astype(F32)
            for c in columns:
                total = total + down_c[c, e].astype(F32)
            ed_ref[e] = total
            ed_ref[e + 2] = db_ref[zh, e].astype(F32) + down_d[e].astype(F32)
        for d, at in zip((2, 6, 4, 1, 3, 5, 7), w_shares):
            copier.arrived(at)
            got_at = dense_ref.at[core, :, lanes(lax.rem(chip + CHIPS - d, CHIPS))]
            copier.send(got_at, got_at, "ctx", sibling)
        for d, at in zip((2, 6, 4, 1, 3, 5, 7), a_shares):
            copier.arrived(at)
            got_at = og_ref.at[half, lanes(lax.rem(chip + CHIPS - d, CHIPS))]
            copier.send(got_at, got_at, "ctx", sibling)
        for at in gain_shares:
            copier.arrived(at)
        total = shared[0]
        for c in range(1, CTX):
            total = total + shared[c]
        gs_ref[...] = total
        copier.finish()

    vmem = pl.BlockSpec(memory_space=pltpu.VMEM)
    block = (CHIPS, ROWS, 128)
    tile = pltpu.VMEM((128, 128), BF16)
    return pl.pallas_call(
        body,
        name="tail",
        out_shape=[
            jax.ShapeDtypeStruct((LOCAL, 64, FF), F32),
            jax.ShapeDtypeStruct((LOCAL, 64, FF), F32),
            jax.ShapeDtypeStruct((LOCAL, 32, WIDTH), F32),
            jax.ShapeDtypeStruct((ROWS, WIDTH), F32),
            jax.ShapeDtypeStruct((2, 128, WIDTH), BF16),
            jax.ShapeDtypeStruct((128, WIDTH), BF16),
            jax.ShapeDtypeStruct((ROWS, WIDTH), BF16),
            jax.ShapeDtypeStruct((8, 128), F32),
        ],
        in_specs=[ANY_SPEC] * 7 + [vmem] * 2 + [ANY_SPEC] * 6 + [vmem] * 5,
        out_specs=[vmem] * 4 + [ANY_SPEC] * 3 + [vmem],
        scratch_shapes=[
            pltpu.VMEM(block, F32),
            pltpu.VMEM(block, F32),
            pltpu.VMEM(block, F32),
            pltpu.VMEM(block, F32),
            pltpu.VMEM(block, F32),
            pltpu.VMEM(block, F32),
            pltpu.VMEM((CHIPS, ROWS, WIDTH), BF16),
            pltpu.VMEM((EXP, 128, 2 * WIDTH), BF16),
            pltpu.VMEM((ROWS, WIDTH), BF16),
            pltpu.VMEM((ROWS, WIDTH), F32),
            pltpu.VMEM(block, BF16),
            pltpu.VMEM(block, F32),
            pltpu.VMEM(block, F32),
            pltpu.VMEM((CHIPS, 2, ROWS), F32),
            pltpu.VMEM((CHIPS, CHIPS, 2, ROWS), F32),
            pltpu.VMEM((2,) + block, BF16),
            pltpu.VMEM((2, ROWS, WIDTH), BF16),
            pltpu.VMEM((WIDTH, 128), BF16),
            pltpu.VMEM((WIDTH, 128), BF16),
            pltpu.VMEM((WIDTH, 128), BF16),
            pltpu.VMEM((EXP, 128, 128), BF16),
            pltpu.VMEM((EXP, 128, 128), BF16),
            tile,
            pltpu.VMEM((EXP, 64, WIDTH), BF16),
            pltpu.VMEM((EXP, 64, WIDTH), BF16),
            pltpu.VMEM((4, 2, 64, WIDTH), BF16),
            pltpu.VMEM((64, WIDTH), BF16),
            pltpu.VMEM((64, WIDTH), BF16),
            pltpu.VMEM((64, WIDTH), BF16),
            pltpu.VMEM((CHIPS, 64, 128), BF16),
            pltpu.VMEM((64, 128), BF16),
            pltpu.VMEM((EXP, 8, 128), F32),
            pltpu.VMEM((EXP, 8, 128), F32),
            pltpu.VMEM((8, 128), F32),
            pltpu.VMEM((CTX, 8, 128), F32),
            pltpu.VMEM((4, LOCAL, 64, FF), BF16),
            pltpu.VMEM((4, 2, 32, WIDTH), BF16),
            pltpu.VMEM((LOCAL, 64, FF), BF16),
            pltpu.VMEM((2, 32, WIDTH), BF16),
            pltpu.SemaphoreType.DMA((106,)),
            pltpu.SemaphoreType.DMA((106,)),
            pltpu.SemaphoreType.DMA((14,)),
        ],
        compiler_params=pltpu.CompilerParams(
            collective_id=6, has_side_effects=True, vmem_limit_bytes=60 * MIB
        ),
    )(
        dq, dkv_mine, dkv_other, q_lin, kv_lin, cosine, sine, squares, gains, normed, out_part, layer_part,
        weights, tokens, d_resid, ffn_gain, gate_part, up_part, down_a, down_b,
    )


def sum_blocks(blocks):
    return jnp.sum(blocks.astype(F32), axis=0)


def per_device(
    tokens,
    cotangent,
    lengths,
    deal_perm,
    routes,
    gate_logits,
    norm_attn,
    norm_query,
    norm_key,
    norm_ffn,
    w_query,
    w_key,
    w_value,
    w_out,
    w_gate,
    w_up,
    w_down,
):
    tokens, cotangent = tokens[0], cotangent[0]

    row = lambda v: v.reshape(1, -1)
    (
        w_o, gain_all, normed, q_lin, kv_lin, squares, cosine, sine, places, q_all, kv_all, grads_all,
    ) = front(
        tokens,
        cotangent,
        (w_query, w_key, w_value, w_out),
        (row(norm_attn), row(norm_query), row(norm_key), row(norm_ffn)),
        deal_perm[0],
        lengths,
    )

    pieces = jnp.arange(CTX, dtype=jnp.int32)[:, None] * CTX + deal_perm[0]
    positions = (pieces[:, :, None] * 12 + jnp.arange(12, dtype=jnp.int32)).reshape(CTX, ROWS)
    key_pos = positions.reshape(CHIPS, 1, CHUNK).astype(F32)
    starts = places[:, 1].astype(jnp.int32)
    whole_from = (jnp.max(starts, axis=1) + CHUNK - 1) // CHUNK
    chunks = jnp.stack(
        [jnp.min(starts, axis=1) // CHUNK, jnp.minimum(whole_from, jnp.arange(CHIPS, dtype=jnp.int32))]
    )
    w_o = w_o.reshape(WIDTH, WIDTH)
    kv_all = kv_all.reshape(KEYS, 128)
    out_low, out_wide, log_total = attend(q_all, kv_all, key_pos, places, chunks)
    attended, resid, rows_all, meta_all = join_heads(
        out_low, w_o, tokens, gain_all, routes[0].T, gate_logits[0].T
    )

    rows_all, dense_late = lax.optimization_barrier(
        (rows_all, jnp.concatenate([w_query, w_key, w_value], axis=1))
    )
    dense_late = lax.all_gather(dense_late, "exp", axis=0, tiled=True)

    shift = jnp.array([0.0, float(CAP)], F32)[None, None, :, None]
    spots = meta_all[:, :LOCAL].reshape(PAIRS, 2, LOCAL, ROWS).transpose(0, 2, 1, 3)
    spots = jnp.where(spots < 0.0, -1.0, spots + shift).reshape(PAIRS, LOCAL, PAIR_ROWS)
    gates = meta_all[:, LOCAL:].reshape(PAIRS, 2, LOCAL, ROWS).transpose(0, 2, 1, 3)
    pair_meta = jnp.concatenate([spots, gates.reshape(PAIRS, LOCAL, PAIR_ROWS)], axis=1)
    rows_in, d_rows, act, d_gate, d_up, out_parts, d_parts = experts(
        rows_all.reshape(PAIRS, PAIR_ROWS, WIDTH),
        grads_all.reshape(PAIRS, PAIR_ROWS, WIDTH),
        pair_meta,
        pair_meta.transpose(0, 2, 1),
        w_gate,
        w_up,
        w_down,
    )
    (
        gate_part, up_part, down_a, down_b, d_resid, d_branch, ffn_gain_grad, d_out, layer_keep, layer_give,
    ) = settle_experts(
        rows_in,
        d_rows,
        act,
        d_gate,
        d_up,
        d_parts.reshape(2, 4, ROWS, WIDTH),
        out_parts.reshape(2, 4, ROWS, WIDTH),
        resid,
        cotangent,
        gain_all,
        w_o,
    )
    out_part = out_grads(attended, d_branch).reshape(EXP, 2, 64, WIDTH)
    dq, dkv_mine, dkv_other = attend_back(
        q_all, kv_all, d_out, out_wide, log_total, key_pos, places, chunks
    )
    gate_grad, up_grad, down_grad, input_grad, dense, out_grad, layer_got, gain_sums = tail(
        dq,
        dkv_mine,
        dkv_other,
        q_lin,
        kv_lin,
        cosine,
        sine,
        squares,
        gain_all,
        normed,
        out_part,
        layer_give,
        dense_late.reshape(EXP, 128, 2 * WIDTH),
        tokens,
        d_resid,
        ffn_gain_grad,
        gate_part,
        up_part,
        down_a,
        down_b,
    )
    outs = deliver(
        resid,
        layer_keep,
        layer_got,
        dense,
        out_grad,
        gain_sums,
        input_grad,
        (gate_grad, up_grad, down_grad),
    )
    return (
        outs[0][None],
        outs[9][None],
        *outs[1:5],
        *[g.reshape(-1) for g in outs[5:9]],
        *outs[10:],
    )


def solution(mesh):
    in_specs = (
        P("exp", "ctx", None),
        P("exp", "ctx", None),
        P("exp", None),
        P("exp", None, None),
        P("exp", "ctx", None),
        P("exp", "ctx", None),
        P("exp"),
        P("exp"),
        P("exp"),
        P("exp"),
        P("exp", None),
        P("exp", None),
        P("exp", None),
        P("exp", None),
        P("exp", None, None),
        P("exp", None, None),
        P("exp", None, None),
    )
    out_specs = (
        P("exp", "ctx", None),
        P("exp", "ctx", None),
        P("exp", None),
        P("exp", None),
        P("exp", None),
        P("exp", None),
        P("exp"),
        P("exp"),
        P("exp"),
        P("exp"),
        P("exp", "ctx", None),
        P("exp", "ctx", None),
        P("exp", "ctx", None),
    )
    return jax.shard_map(
        per_device, mesh=mesh, in_specs=in_specs, out_specs=out_specs, check_vma=False
    )
```

```python
import jax
import jax.numpy as jnp
from jax import lax
from jax.experimental import pallas as pl
from jax.experimental.pallas import tpu as pltpu
from jax.sharding import PartitionSpec as P

HEADS = 16
KV_HEADS = 8
EPSILON = 1e-05
ROPE_BASE = 10000.0
MASKED = -1e30

MESH = pl.DeviceIdType.MESH
CTX = 16
EXP = 8
CHIPS = 8
ROWS = 192
WIDTH = 1024
FF = 512
LOCAL = 4
CAP = 72
PAIRS = EXP // 2
PAIR_ROWS = 2 * ROWS
PAIR_CAP = 2 * CAP
SLOTS = EXP * CAP
PAIR_SLOTS = LOCAL * PAIR_CAP
KEYS = CTX * ROWS
CHUNK = 2 * ROWS
MIB = 1 << 20
FAR_FIRST = (6, 2, 5, 7, 4, 1, 3)

ANY_SPEC = pl.BlockSpec(memory_space=pl.ANY)
F32 = jnp.float32
BF16 = jnp.bfloat16


def dot(a, b, dims=((1,), (0,))):
    return lax.dot_general(a, b, (dims, ((), ())), preferred_element_type=F32)


NT = ((1,), (1,))
TN = ((0,), (0,))


def comm_call(body, name, collective_id, outs, ins, copies, in_specs=None):
    return pl.pallas_call(
        body,
        name=name,
        out_shape=outs,
        in_specs=in_specs or [ANY_SPEC] * len(ins),
        out_specs=[ANY_SPEC] * len(outs),
        scratch_shapes=[
            pltpu.SemaphoreType.DMA((copies,)),
            pltpu.SemaphoreType.DMA((copies,)),
            pltpu.SemaphoreType.DMA((8,)),
        ],
        compiler_params=pltpu.CompilerParams(
            collective_id=collective_id, has_side_effects=True, vmem_limit_bytes=60 * MIB
        ),
    )(*ins)


class Copier:
    def __init__(self, send_sem, recv_sem, local_sem):
        self.send_sem, self.recv_sem, self.local_sem = send_sem, recv_sem, local_sem
        self.remote, self.local = [], []

    def send(self, src, dst, axis, index):
        at = len(self.remote)
        copy = pltpu.make_async_remote_copy(
            src_ref=src,
            dst_ref=dst,
            send_sem=self.send_sem.at[at],
            recv_sem=self.recv_sem.at[at],
            device_id={axis: index},
            device_id_type=MESH,
        )
        copy.start()
        self.remote.append([copy, False])
        return at

    def keep(self, src, dst):
        copy = pltpu.make_async_copy(src, dst, self.local_sem.at[len(self.local)])
        copy.start()
        self.local.append([copy, False])
        return len(self.local) - 1

    def arrived(self, at):
        self.remote[at][0].wait_recv()
        self.remote[at][1] = True

    def kept(self, at):
        self.local[at][0].wait()
        self.local[at][1] = True

    def finish(self):
        for copy, seen in self.remote:
            if not seen:
                copy.wait_recv()
        for copy, _ in self.remote:
            copy.wait_send()
        for copy, seen in self.local:
            if not seen:
                copy.wait()


def meet(partners):
    barrier = pltpu.get_barrier_semaphore()
    for axis, index in partners:
        pl.semaphore_signal(barrier, inc=1, device_id={axis: index}, device_id_type=MESH)
    pl.semaphore_wait(barrier, len(partners))


def place():
    ctx = lax.axis_index("ctx")
    core = lax.rem(ctx, 2)
    return ctx, ctx // 2, core, ctx + 1 - 2 * core


def ring_of(me):
    half, spot = me // 4, lax.rem(me, 4)
    over = (1 - half) * 4
    turns = [lax.rem(spot + d, 4) for d in (0, 1, 3, 2)]
    return tuple([half * 4 + t for t in turns] + [over + t for t in turns])


def relay(copier, own, slot, rows, ring, reach, landed=lambda partner: None):
    me, right, left, far, over, over_right, over_left, over_far = ring
    half = rows // 2
    low, high = pl.ds(0, half), pl.ds(half, half)

    def send(block, to, part, partner):
        return copier.send(block.at[part], slot(to).at[part], *reach(partner))

    def on(of, part, partner):
        return send(slot(of), of, part, partner)

    over_low = send(own, me, low, over)
    over_high = send(own, me, high, over)
    yield
    right_low = send(own, me, low, right)
    left_high = send(own, me, high, left)
    right_high = send(own, me, high, right)
    left_low = send(own, me, low, left)
    yield
    copier.arrived(right_low)
    far_right = on(left, low, right)
    copier.arrived(left_high)
    far_left = on(right, high, left)
    yield
    copier.arrived(over_low)
    next_right_low = on(over, low, right)
    next_left_low = on(over, low, left)
    copier.arrived(over_high)
    next_left_high = on(over, high, left)
    next_right_high = on(over, high, right)
    landed(over)
    yield
    copier.arrived(right_high)
    landed(left)
    copier.arrived(left_low)
    landed(right)
    yield
    copier.arrived(far_right)
    copier.arrived(far_left)
    landed(far)
    yield
    copier.arrived(next_right_low)
    far_right = on(over_left, low, right)
    copier.arrived(next_left_high)
    far_left = on(over_right, high, left)
    copier.arrived(next_right_high)
    landed(over_left)
    copier.arrived(next_left_low)
    landed(over_right)
    yield
    copier.arrived(far_right)
    copier.arrived(far_left)
    landed(over_far)


def side_by_side(*relays):
    for _ in zip(*relays):
        pass
    for one in relays:
        for _ in one:
            pass


def lanes(index):
    return pl.ds(pl.multiple_of(index * 128, 128), 128)


def join_heads(blocks, w_out, tokens, gains, routes_t, logits_t):
    def body(
        x_ref, w_ref, t_ref, g_ref, r_ref, l_ref,
        a_ref, res_ref, o_ref, mo_ref, w_v, ffn, m_v, send_sem, recv_sem, local_sem,
    ):
        _, chip, core, _ = place()
        ring = ring_of(lax.axis_index("exp"))
        me = ring[0]
        twins = [lax.rem(chip + d, CHIPS) for d in FAR_FIRST]
        to_chip = lambda p: ("ctx", 2 * p + core)
        to_exp = lambda p: ("exp", p)
        copier = Copier(send_sem, recv_sem, local_sem)
        load = copier.keep(w_ref, w_v)
        meet([to_chip(p) for p in twins] + [to_exp(p) for p in ring[1:]])
        arrivals = [copier.send(x_ref.at[p], a_ref.at[:, lanes(chip)], *to_chip(p)) for p in twins]
        own = copier.keep(x_ref.at[chip], a_ref.at[:, lanes(chip)])

        logits = l_ref[...]
        raised = jnp.exp(logits - jnp.max(logits, axis=0, keepdims=True))
        gates = raised / jnp.sum(raised, axis=0, keepdims=True)
        experts = lax.broadcasted_iota(jnp.int32, (32, ROWS), 0)
        member = jnp.zeros((32, ROWS), F32)
        weight = jnp.zeros((32, ROWS), F32)
        for c in range(8):
            hit = r_ref[c : c + 1, :] == experts
            member = member + jnp.where(hit, 1.0, 0.0)
            weight = weight + jnp.where(hit, gates[c : c + 1, :], 0.0)
        before = lax.broadcasted_iota(jnp.int32, (ROWS, ROWS), 0) < lax.broadcasted_iota(
            jnp.int32, (ROWS, ROWS), 1
        )
        rank = dot(member.astype(BF16), jnp.where(before, 1.0, 0.0).astype(BF16))
        spot = jnp.where(member > 0.5, rank, -1.0)
        for e in range(EXP):
            m_v[e, 0:4, :] = spot[e * 4 : e * 4 + 4, :]
            m_v[e, 4:8, :] = weight[e * 4 : e * 4 + 4, :]
        for p in ring[1:]:
            copier.send(m_v.at[p], mo_ref.at[me], *to_exp(p))
        copier.keep(m_v.at[me], mo_ref.at[me])

        copier.kept(load)
        copier.kept(own)
        for at in arrivals:
            copier.arrived(at)
        branch = dot(a_ref[...], w_v[...]).astype(BF16).astype(F32)
        resid = t_ref[...].astype(F32) + branch
        res_ref[...] = resid
        scale = row_scale(jnp.sum(resid * resid, axis=1, keepdims=True), WIDTH)
        for e in range(EXP):
            at = slice(e * 128, (e + 1) * 128)
            ffn[:, at] = (resid[:, at] * scale * g_ref[e, 3:4, :]).astype(BF16)
        rows_out = relay(copier, ffn, lambda s: o_ref.at[s], ROWS, ring, to_exp)
        next(rows_out)
        next(rows_out)
        copier.keep(ffn, o_ref.at[me])
        side_by_side(rows_out)
        copier.finish()

    vmem = pl.BlockSpec(memory_space=pltpu.VMEM)
    return pl.pallas_call(
        body,
        name="join_heads",
        out_shape=[
            jax.ShapeDtypeStruct((ROWS, WIDTH), BF16),
            jax.ShapeDtypeStruct((ROWS, WIDTH), F32),
            jax.ShapeDtypeStruct((EXP, ROWS, WIDTH), BF16),
            jax.ShapeDtypeStruct((EXP, 8, ROWS), F32),
        ],
        in_specs=[ANY_SPEC] * 2 + [vmem] * 4,
        out_specs=[vmem, vmem, ANY_SPEC, ANY_SPEC],
        scratch_shapes=[
            pltpu.VMEM((WIDTH, WIDTH), BF16),
            pltpu.VMEM((ROWS, WIDTH), BF16),
            pltpu.VMEM((EXP, 8, ROWS), F32),
            pltpu.SemaphoreType.DMA((28,)),
            pltpu.SemaphoreType.DMA((28,)),
            pltpu.SemaphoreType.DMA((8,)),
        ],
        compiler_params=pltpu.CompilerParams(
            collective_id=2, has_side_effects=True, vmem_limit_bytes=60 * MIB
        ),
    )(blocks, w_out, tokens, gains, routes_t, logits_t)


def settle_experts(
    rows, d_rows, act, d_gate, d_up, d_parts, layer_parts, resid, cotangent, gains, w_out
):
    def body(
        x_ref, r_ref, a_ref, g_ref, u_ref, p_ref, l_ref, res_ref, cot_ref, gain_ref, w_ref,
        gate_out, up_out, down_a_out, down_b_out, dr_out, db_out, gg_out, do_out, keep_out, give_out, dx_out, d_att,
        x_v, r_v, a_v, g_v, u_v, gate, up, down, gate_o, up_o, down_o, gate_a, down_a, up_b, down_b,
        to_z, from_z, d_own, d_right, d_left, d_low, d_high, d_from, l_own, l_right, l_left, l_low, l_high, l_from, send_sem, recv_sem, local_sem,
    ):
        _, chip, core, sibling = place()
        me = lax.axis_index("exp")
        zl, x = me // 4, lax.rem(me, 4)
        zh, y = chip // 4, lax.rem(chip, 4)
        at_ctx = lambda z, yy: ("ctx", z * 8 + yy * 2 + core)
        over = at_ctx(1 - zh, y)
        columns = [lax.rem(y + d, 4) for d in (1, 3, 2)]
        twins = [lax.rem(chip + d, CHIPS) for d in FAR_FIRST]
        right, left, far = [lax.rem(x + d, 4) for d in (1, 3, 2)]
        at_exp = lambda p: ("exp", zl * 4 + p)
        low, high = pl.ds(0, ROWS // 2), pl.ds(ROWS // 2, ROWS // 2)
        copier = Copier(send_sem, recv_sem, local_sem)
        loads = []
        for e in range(LOCAL):
            pairs = ((x_ref, x_v), (r_ref, r_v), (a_ref, a_v), (g_ref, g_v), (u_ref, u_v))
            loads.append([copier.keep(src.at[e], dst.at[e]) for src, dst in pairs])
        parts = (p_ref, d_own, d_right, d_left, d_low, d_high, d_from)
        layers = (l_ref, l_own, l_right, l_left, l_low, l_high, l_from)

        def fetch(src, own, to_right, to_left, *_):
            return [
                copier.keep(src.at[:, x], own),
                copier.keep(src.at[:, right, low], to_right),
                copier.keep(src.at[:, left, high], to_left),
            ]

        part_loads, layer_loads = fetch(*parts), fetch(*layers)
        meet(
            [("ctx", sibling)]
            + [("ctx", 2 * p + core) for p in twins]
            + [at_exp(right), at_exp(left)]
            + [("exp", (1 - zl) * 4 + x)]
        )

        def set_out(src, own, to_right, to_left, in_low, in_high, arrived):
            return [
                copier.send(src.at[:, far, low], in_low, *at_exp(right)),
                copier.send(src.at[:, far, high], in_high, *at_exp(left)),
                copier.send(src.at[:, right, high], arrived.at[0, :, high], *at_exp(right)),
                copier.send(src.at[:, left, low], arrived.at[1, :, low], *at_exp(left)),
            ]

        def pass_on(stage, loads_of, src, own, to_right, to_left, in_low, in_high, arrived):
            for at in loads_of:
                copier.kept(at)
            for at in stage[:2]:
                copier.arrived(at)

            def add(r, _):
                at = pl.ds(pl.multiple_of(r * 48, 16), 48)
                for z in range(2):
                    for mine, other in ((to_right, in_low), (to_left, in_high)):
                        mine[z, at, :] = (mine[z, at, :].astype(F32) + other[z, at, :].astype(F32)).astype(BF16)
                return 0

            lax.fori_loop(0, 2, add, 0)
            return stage[2:] + [
                copier.send(to_right, arrived.at[0, :, low], *at_exp(right)),
                copier.send(to_left, arrived.at[1, :, high], *at_exp(left)),
            ]

        part_stage = set_out(*parts)

        def work(e):
            for at in loads[e]:
                copier.kept(at)

            def wide(r, _):
                rows_r = x_v[e, :, pl.ds(pl.multiple_of(r * 256, 256), 256)]
                for d_v, o_v in ((g_v, gate), (u_v, up)):
                    grad = dot(rows_r, d_v[e], TN).astype(BF16)
                    for k in range(4):
                        o_v[k % 2, r // 2, 2 * lax.rem(r, 2) + k // 2, e] = grad[k * 64 : (k + 1) * 64]
                return 0

            lax.fori_loop(0, 4, wide, 0)

            def tall(r, _):
                act_r = a_v[e, :, pl.ds(pl.multiple_of(r * 256, 256), 256)]
                grad = dot(act_r, r_v[e], TN).astype(BF16)
                for k in range(8):
                    down[k % 2, r, k // 2, e] = grad[k * 32 : (k + 1) * 32]
                return 0

            lax.fori_loop(0, 2, tall, 0)
            return [
                copier.send(full.at[1 - core, :, :, e], other.at[:, :, e], "ctx", sibling)
                for full, other in ((gate, gate_o), (up, up_o), (down, down_o))
            ]

        first_a, first_b = [], []

        def join(e, swaps):
            for at in swaps:
                copier.arrived(at)

            def add(c, _):
                z, yy = c // 4, lax.rem(c, 4)
                for full, other in ((gate, gate_o), (up, up_o), (down, down_o)):
                    both = full[core, z, yy, e].astype(F32) + other[z, yy, e].astype(F32)
                    full[core, z, yy, e] = both.astype(BF16)
                return 0

            lax.fori_loop(0, CHIPS, add, 0)
            first_a.append(copier.send(gate.at[core, 1 - zh, :, e], gate_a.at[:, e], *over))
            if e < 2:
                first_a.append(copier.send(down.at[core, 1 - zh, :, e], down_a.at[:, e], *over))
            for c in columns:
                to = at_ctx(zh, c)
                first_b.append(copier.send(up.at[core, :, c, e], up_b.at[y, :, e], *to))
                if e >= 2:
                    first_b.append(copier.send(down.at[core, :, c, e], down_b.at[y, :, e - 2], *to))

        swaps = work(0)
        later = work(1)
        join(0, swaps)
        part_stage = pass_on(part_stage, part_loads, *parts)
        layer_stage = set_out(*layers)
        swaps = later
        later = work(2)
        join(1, swaps)
        swaps = later
        later = work(3)
        w_loads = [copier.keep(w_ref.at[pl.ds(k * FF, FF)], r_v.at[k, pl.ds(0, FF)]) for k in range(2)]
        join(2, swaps)
        join(3, later)

        def sum_up(stage, own, arrived, keep_ref, give_ref):
            for at in stage:
                copier.arrived(at)

            def add(r, _):
                at = pl.ds(pl.multiple_of(r * 48, 16), 48)
                keep, give = [
                    own[z, at, :].astype(F32) + arrived[0, z, at, :].astype(F32) + arrived[1, z, at, :].astype(F32)
                    for z in (zl, 1 - zl)
                ]
                keep_ref[at, :] = keep
                give_ref[at, :] = give.astype(BF16)
                return 0

            lax.fori_loop(0, 4, add, 0)

        sum_up(part_stage, d_own, d_from, dx_out, to_z)
        z_stage = copier.send(to_z, from_z, "exp", (1 - zl) * 4 + x)
        layer_stage = pass_on(layer_stage, layer_loads, *layers)

        copier.arrived(z_stage)
        incoming = dx_out[...] + from_z[...].astype(F32)
        resid_v = res_ref[...]
        scale = row_scale(jnp.sum(resid_v * resid_v, axis=1, keepdims=True), WIDTH)
        inner = jnp.zeros((ROWS, 1), F32)
        for e in range(EXP):
            at = slice(e * 128, (e + 1) * 128)
            product = incoming[:, at] * resid_v[:, at]
            gg_out[:, at] = jnp.sum(product * scale, axis=0, keepdims=True)
            inner = inner + jnp.sum(product * gain_ref[e, 3:4, :], axis=1, keepdims=True)
        cut = scale * scale * scale * inner * (1.0 / WIDTH)
        for e in range(EXP):
            at = slice(e * 128, (e + 1) * 128)
            d_norm = scale * (incoming[:, at] * gain_ref[e, 3:4, :]) - resid_v[:, at] * cut
            d_resid = cot_ref[:, at].astype(F32) + d_norm
            dr_out[:, at] = d_resid
            db_out[:, at] = d_resid.astype(BF16)
        for at in w_loads:
            copier.kept(at)
        for k in range(2):
            d_att[:, k * FF : (k + 1) * FF] = dot(db_out[...], r_v[k, 0:FF, :], NT).astype(BF16)
        for p in twins:
            copier.send(d_att.at[:, lanes(p)], do_out.at[chip], "ctx", 2 * p + core)
        copier.keep(d_att.at[:, lanes(chip)], do_out.at[chip])
        for at in first_a:
            copier.arrived(at)

        def sum_a(c, _):
            for e in range(LOCAL):
                both = gate[core, zh, c, e].astype(F32) + gate_a[c, e].astype(F32)
                gate_out[c, e] = both.astype(BF16)
            for e in range(2):
                both = down[core, zh, c, e].astype(F32) + down_a[c, e].astype(F32)
                down_a_out[c, e] = both.astype(BF16)
            return 0

        lax.fori_loop(0, 4, sum_a, 0)

        for at in first_b:
            copier.arrived(at)
        others = [lax.rem(y + d, 4) for d in (1, 2, 3)]

        def sum_b(e, _):
            for z in range(2):
                total = up[core, z, y, e].astype(F32)
                for c in others:
                    total = total + up_b[c, z, e].astype(F32)
                up_out[z, e] = total.astype(BF16)
            return 0

        lax.fori_loop(0, LOCAL, sum_b, 0)

        def sum_b_down(e, _):
            for z in range(2):
                total = down[core, z, y, e + 2].astype(F32)
                for c in others:
                    total = total + down_b[c, z, e].astype(F32)
                down_b_out[z, e] = total.astype(BF16)
            return 0

        lax.fori_loop(0, 2, sum_b_down, 0)
        sum_up(layer_stage, l_own, l_from, keep_out, give_out)
        copier.finish()

    vmem = pl.BlockSpec(memory_space=pltpu.VMEM)
    buf = lambda *shape: pltpu.VMEM(shape, BF16)
    wide, tall = (64, FF), (32, WIDTH)
    return pl.pallas_call(
        body,
        name="settle_experts",
        out_shape=[
            jax.ShapeDtypeStruct((4, LOCAL) + wide, BF16),
            jax.ShapeDtypeStruct((2, LOCAL) + wide, BF16),
            jax.ShapeDtypeStruct((4, 2) + tall, BF16),
            jax.ShapeDtypeStruct((2, 2) + tall, BF16),
            jax.ShapeDtypeStruct((ROWS, WIDTH), F32),
            jax.ShapeDtypeStruct((ROWS, WIDTH), BF16),
            jax.ShapeDtypeStruct((1, WIDTH), F32),
            jax.ShapeDtypeStruct((CHIPS, ROWS, 128), BF16),
            jax.ShapeDtypeStruct((ROWS, WIDTH), F32),
            jax.ShapeDtypeStruct((ROWS, WIDTH), BF16),
        ],
        in_specs=[ANY_SPEC] * 7 + [vmem] * 3 + [ANY_SPEC],
        out_specs=[vmem] * 7 + [ANY_SPEC] + [vmem] * 2,
        scratch_shapes=[
            pltpu.VMEM((ROWS, WIDTH), F32),
            buf(ROWS, WIDTH),
            buf(LOCAL, SLOTS, WIDTH),
            buf(LOCAL, SLOTS, WIDTH),
            buf(LOCAL, SLOTS, FF),
            buf(LOCAL, SLOTS, FF),
            buf(LOCAL, SLOTS, FF),
            buf(2, 2, 4, LOCAL, *wide),
            buf(2, 2, 4, LOCAL, *wide),
            buf(2, 2, 4, LOCAL, *tall),
            buf(2, 4, LOCAL, *wide),
            buf(2, 4, LOCAL, *wide),
            buf(2, 4, LOCAL, *tall),
            buf(4, LOCAL, *wide),
            buf(4, 2, *tall),
            buf(4, 2, LOCAL, *wide),
            buf(4, 2, 2, *tall),
            buf(ROWS, WIDTH),
            buf(ROWS, WIDTH),
        ]
        + [
            buf(2, ROWS, WIDTH),
            buf(2, ROWS // 2, WIDTH),
            buf(2, ROWS // 2, WIDTH),
            buf(2, ROWS // 2, WIDTH),
            buf(2, ROWS // 2, WIDTH),
            buf(2, 2, ROWS, WIDTH),
        ]
        * 2
        + [
            pltpu.SemaphoreType.DMA((56,)),
            pltpu.SemaphoreType.DMA((56,)),
            pltpu.SemaphoreType.DMA((32,)),
        ],
        compiler_params=pltpu.CompilerParams(
            collective_id=8, has_side_effects=True, vmem_limit_bytes=63 * MIB
        ),
    )(rows, d_rows, act, d_gate, d_up, d_parts, layer_parts, resid, cotangent, gains, w_out)


def compute_call(body, name, outs, ins, vmem=60, **kw):
    return pl.pallas_call(
        body,
        name=name,
        out_shape=outs,
        compiler_params=pltpu.CompilerParams(vmem_limit_bytes=vmem * MIB),
        **kw,
    )(*ins)


def row_scale(total, width):
    return lax.rsqrt(total * (1.0 / width) + EPSILON)


def key_lanes():
    return lax.broadcasted_iota(jnp.int32, (1, 128), 1) < 64


def turn(values, cosine, sine):
    first = lax.rem(lax.broadcasted_iota(jnp.int32, (1, 128), 1), 64) < 32
    return values * cosine + jnp.where(first, -pltpu.roll(values, 96, 1), pltpu.roll(values, 32, 1)) * sine


def across(select, values):
    return lax.dot_general(
        select, values, (NT, ((), ())), precision=lax.Precision.HIGHEST, preferred_element_type=F32
    )


def both_totals(left, right):
    row_id = lax.broadcasted_iota(jnp.int32, (8, 128), 0)
    ones = jnp.where(row_id == 0, 1.0, 0.0)
    keys = jnp.where((row_id == 1) & key_lanes(), 1.0, 0.0)
    return (across(ones, left) + across(keys, right))[0:2, :]


def down_rows(values, row, width=128):
    chosen = lax.broadcasted_iota(jnp.int32, (2, width), 0) == row
    return lax.dot_general(
        values,
        jnp.where(chosen, 1.0, 0.0),
        (TN, ((), ())),
        precision=lax.Precision.HIGHEST,
        preferred_element_type=F32,
    )


def own_chip():
    return lax.axis_index("ctx") // 2


def key_columns(row):
    upper = jnp.floor(row * (1.0 / 64.0))
    parts = jnp.concatenate([upper, row - 64.0 * upper], axis=0).astype(BF16)
    scale = jnp.where(lax.broadcasted_iota(jnp.int32, (2, 128), 0) == 0, 64.0, 1.0).astype(BF16)
    return dot(parts, scale, TN)


def pair_rows(places_i):
    return [jnp.concatenate([places_i[k : k + 1, :]] * 2, axis=1) for k in range(2)]


def block_chunks(len_ref, i):
    first_row = (2 * i + lax.rem(lax.axis_index("ctx"), 2)) * ROWS
    first, last, end = 0, 0, 0
    for k in range(3):
        end = end + len_ref[0, k]
        first = jnp.where(first_row >= end, end, first)
        last = jnp.where(first_row + ROWS - 1 >= end, end, last)
    return first // CHUNK, jnp.minimum((last + CHUNK - 1) // CHUNK, i)


def attend(q, kv, key_pos, places, lengths):
    def body(at_ref, q_ref, kv_ref, kp_ref, p_ref, o_ref, ot_ref, l_ref, keys, values, key_at):
        low = key_lanes()

        def place_keys(p, _):
            rows = pl.ds(pl.multiple_of(p * CHUNK, CHUNK), CHUNK)
            both = kv_ref[rows, :].astype(F32)
            keys[rows, :] = jnp.where(low, both, 0.0).astype(BF16)
            values[:, rows] = jnp.where(low, pltpu.roll(both, 64, 1), 0.0).T.astype(BF16)
            key_at[rows, :] = key_columns(kp_ref[p])
            return 0

        lax.fori_loop(0, CHIPS, place_keys, 0)

        def block(i, _):
            wide = q_ref[i].astype(F32)
            stacked = jnp.concatenate([wide, pltpu.roll(wide, 64, 1)], axis=0).astype(BF16)
            at_row, start_row = pair_rows(p_ref[i])

            def step(masked, diagonal, p, carry):
                top, total, acc = carry
                rows = pl.ds(pl.multiple_of(p * CHUNK, CHUNK), CHUNK)
                scores = dot(keys[rows, :], stacked, NT)
                if masked:
                    at_key = jnp.concatenate([key_at[rows, :]] * (CHUNK // 128), axis=1)
                    seen = at_key >= start_row
                    if diagonal:
                        seen = seen & (at_key <= at_row)
                    scores = jnp.where(seen, scores, MASKED)
                new_top = jnp.maximum(top, jnp.max(scores, axis=0, keepdims=True))
                probs = jnp.exp(scores - new_top)
                scale = jnp.exp(top - new_top)
                total = total * scale + jnp.sum(probs, axis=0, keepdims=True)
                acc = acc * scale + dot(values[:, rows], probs.astype(BF16))
                return new_top, total, acc

            def masked_step(p, carry):
                return step(True, False, p, carry)

            def plain_step(p, carry):
                return step(False, False, p, carry)

            none = jnp.zeros((1, 2 * ROWS), F32)
            carry = (none + MASKED, none, jnp.zeros((128, 2 * ROWS), F32))
            first, plain = block_chunks(at_ref, i)
            carry = lax.fori_loop(first, plain, masked_step, carry)
            carry = lax.fori_loop(plain, i, plain_step, carry)
            top, total, acc = step(True, True, i, carry)
            turned = acc[0:64, :] / total
            ot_ref[i] = turned
            l_ref[i] = top + jnp.log(total)
            out = jnp.concatenate([turned, turned], axis=0).T
            o_ref[i] = jnp.where(low, out[:ROWS], out[ROWS:]).astype(BF16)
            return 0

        lax.fori_loop(0, CHIPS, block, 0)

    vmem = pl.BlockSpec(memory_space=pltpu.VMEM)
    return pl.pallas_call(
        body,
        name="attend",
        out_shape=[
            jax.ShapeDtypeStruct((CHIPS, ROWS, 128), BF16),
            jax.ShapeDtypeStruct((CHIPS, 64, 2 * ROWS), F32),
            jax.ShapeDtypeStruct((CHIPS, 1, 2 * ROWS), F32),
        ],
        in_specs=[pl.BlockSpec(memory_space=pltpu.SMEM)] + [vmem] * 4,
        out_specs=[vmem] * 3,
        scratch_shapes=[
            pltpu.VMEM((KEYS, 128), BF16),
            pltpu.VMEM((128, KEYS), BF16),
            pltpu.VMEM((KEYS, 128), F32),
        ],
        compiler_params=pltpu.CompilerParams(vmem_limit_bytes=60 * MIB),
    )(lengths, q, kv, key_pos, places)


def experts(rows, grads, meta, w_gate, w_up, w_down):
    half = SLOTS // 2

    def body(
        x_ref, g_ref, m_ref, wg_ref, wu_ref, wd_ref,
        xin_ref, dr_ref, act_ref, dg_ref, du_ref, out_ref, dx_ref,
        x, g, wg, wu, wd, xin, dr, act, dg, du, out, dx, made, back, weight, sems,
    ):
        def pair_in(p):
            at = pl.ds(2 * p, 2)
            return [pltpu.make_async_copy(a.at[at], b.at[at], sems.at[0, p]) for a, b in ((x_ref, x), (g_ref, g))]

        def weights_in(e):
            pairs = ((wg_ref, wg), (wu_ref, wu), (wd_ref, wd))
            return [pltpu.make_async_copy(a.at[e], b.at[e], sems.at[1, e]) for a, b in pairs]

        def rows_out(e):
            return [pltpu.make_async_copy(a.at[e], b.at[e], sems.at[2, e]) for a, b in ((xin, xin_ref), (dr, dr_ref))]

        def acts_out(e):
            pairs = ((act, act_ref), (dg, dg_ref), (du, du_ref))
            return [pltpu.make_async_copy(a.at[e], b.at[e], sems.at[3, e]) for a, b in pairs]

        def pair_out(p):
            at = pl.ds(2 * p, 2)
            return [pltpu.make_async_copy(a.at[at], b.at[at], sems.at[4, p]) for a, b in ((dx, dx_ref), (out, out_ref))]

        def start(copies):
            for copy in copies:
                copy.start()

        def wait(copies):
            for copy in copies:
                copy.wait()

        for p in range(PAIRS):
            start(pair_in(p))
        for e in range(LOCAL):
            start(weights_in(e))

        def pair_meta(p):
            first, second = m_ref[2 * p], m_ref[2 * p + 1]
            slots = jnp.where(second[:LOCAL] < 0.0, -1.0, second[:LOCAL] + float(CAP))
            return jnp.concatenate([first, jnp.concatenate([slots, second[LOCAL:]], axis=0)], axis=1)

        slot_id = lax.broadcasted_iota(jnp.int32, (PAIR_CAP, PAIR_ROWS), 0).astype(F32)

        def pick(p, _):
            wait(pair_in(p))
            meta_p = pair_meta(p)
            parts, gates = [], []
            for k in range(LOCAL):
                hit = slot_id == meta_p[k : k + 1, :]
                parts.append(jnp.where(hit, 1.0, 0.0).astype(BF16))
                gates.append(jnp.sum(jnp.where(hit, meta_p[4 + k : 5 + k, :], 0.0), axis=1, keepdims=True))
            chosen = jnp.concatenate(parts, axis=0)
            at_pair = pl.ds(2 * p, 2)
            rows_p = dot(chosen, x[at_pair].reshape(PAIR_ROWS, WIDTH)).astype(BF16)
            grads_p = dot(chosen, g[at_pair].reshape(PAIR_ROWS, WIDTH))
            at = pl.ds(pl.multiple_of(p * PAIR_CAP, PAIR_CAP), PAIR_CAP)
            for k in range(LOCAL):
                piece = slice(k * PAIR_CAP, (k + 1) * PAIR_CAP)
                xin[k, at, :] = rows_p[piece]
                dr[k, at, :] = (grads_p[piece] * gates[k]).astype(BF16)
                weight[k, at, :] = gates[k]
            return 0

        lax.fori_loop(0, PAIRS, pick, 0)
        for e in range(LOCAL):
            start(rows_out(e))

        def expert(e, _):
            wait(weights_in(e))

            def work(h, _):
                at = pl.ds(pl.multiple_of(h * half, half), half)
                x_h, dr_h = xin[e, at, :], dr[e, at, :]
                gate = dot(x_h, wg[e])
                up = dot(x_h, wu[e])
                sig = jax.nn.sigmoid(gate)
                silu = gate * sig
                act_h = (silu * up).astype(BF16)
                act[e, at, :] = act_h
                d_act = dot(dr_h, wd[e], NT)
                d_gate = (d_act * up * sig * (1.0 + gate * (1.0 - sig))).astype(BF16)
                d_up = (d_act * silu).astype(BF16)
                dg[e, at, :] = d_gate
                du[e, at, :] = d_up
                y = (dot(act_h, wd[e]) * weight[e, at, :]).astype(BF16)
                dch = (dot(d_gate, wg[e], NT) + dot(d_up, wu[e], NT)).astype(BF16)
                place_at = pl.ds(pl.multiple_of(e * PAIR_CAP, PAIR_CAP), PAIR_CAP)
                for k in range(2):
                    piece = slice(k * PAIR_CAP, (k + 1) * PAIR_CAP)
                    made[2 * h + k, place_at, :] = y[piece]
                    back[2 * h + k, place_at, :] = dch[piece]
                return 0

            lax.fori_loop(0, 2, work, 0)
            start(acts_out(e))
            return 0

        lax.fori_loop(0, LOCAL, expert, 0)
        lane_id = lax.broadcasted_iota(jnp.int32, (PAIR_ROWS, PAIR_SLOTS), 1).astype(F32)

        def give(p, _):
            turned = jnp.concatenate([pair_meta(p), jnp.zeros((120, PAIR_ROWS), F32)], axis=0).T
            chosen = jnp.zeros((PAIR_ROWS, PAIR_SLOTS), F32)
            for k in range(LOCAL):
                spot = turned[:, k : k + 1]
                lane = jnp.where(spot < 0.0, -1.0, spot + float(k * PAIR_CAP))
                chosen = chosen + jnp.where(lane_id == lane, 1.0, 0.0)
            chosen = chosen.astype(BF16)
            at_pair = pl.ds(2 * p, 2)
            dx[at_pair] = dot(chosen, back[p]).astype(BF16).reshape(2, ROWS, WIDTH)
            out[at_pair] = dot(chosen, made[p]).astype(BF16).reshape(2, ROWS, WIDTH)
            start(pair_out(p))
            return 0

        lax.fori_loop(0, PAIRS, give, 0)
        for e in range(LOCAL):
            wait(rows_out(e))
            wait(acts_out(e))
        for p in range(PAIRS):
            wait(pair_out(p))

    vmem = pl.BlockSpec(memory_space=pltpu.VMEM)
    buf = lambda *shape: pltpu.VMEM(shape, BF16)
    wide, narrow, source = (LOCAL, SLOTS, WIDTH), (LOCAL, SLOTS, FF), (EXP, ROWS, WIDTH)
    return compute_call(
        body,
        "experts",
        [jax.ShapeDtypeStruct(shape, BF16) for shape in (wide, wide, narrow, narrow, narrow, source, source)],
        [rows, grads, meta, w_gate, w_up, w_down],
        vmem=63,
        in_specs=[ANY_SPEC, ANY_SPEC, vmem] + [ANY_SPEC] * 3,
        out_specs=[ANY_SPEC] * 7,
        scratch_shapes=[
            buf(*source),
            buf(*source),
            buf(LOCAL, WIDTH, FF),
            buf(LOCAL, WIDTH, FF),
            buf(LOCAL, FF, WIDTH),
            buf(*wide),
            buf(*wide),
            buf(*narrow),
            buf(*narrow),
            buf(*narrow),
            buf(*source),
            buf(*source),
            buf(PAIRS, PAIR_SLOTS, WIDTH),
            buf(PAIRS, PAIR_SLOTS, WIDTH),
            pltpu.VMEM((LOCAL, SLOTS, 1), F32),
            pltpu.SemaphoreType.DMA((5, 4)),
        ],
    )


def norm_back(values, total_squares, width, weighted, mask=None):
    scale = row_scale(total_squares, width)
    inner = jnp.sum(weighted * values, axis=1, keepdims=True) * (1.0 / width)
    return scale * weighted - values * (scale * scale * scale) * inner, scale


def deliver(resid, layer_keep, layer_got, dense, out_grad, gain_sums, input_grad, expert_sums):
    def body(
        r_ref, k_ref, g_ref, d_ref, o_ref, s_ref, i_ref, eg_ref, eu_ref, ed_ref,
        lo, wq, wk, wv, wo, ga, gq, gk, gf, di, eg, eu, ed,
    ):
        lo[...] = (r_ref[...] + k_ref[...] + g_ref[...].astype(F32)).astype(BF16)
        wq[...] = d_ref[0].astype(F32)
        for c in range(4):
            k, v = apart([d_ref[1, :, (2 * c + j) * 128 : (2 * c + j + 1) * 128].astype(F32) for j in range(2)])
            wk[:, c * 128 : (c + 1) * 128] = k
            wv[:, c * 128 : (c + 1) * 128] = v
        wo[...] = o_ref[...].astype(F32)
        ga[...] = s_ref[0:1, :]
        gq[...] = s_ref[1:2, :]
        gk[...] = s_ref[2:3, 0:64]
        gf[...] = s_ref[3:4, :]
        di[...] = i_ref[...]
        eg[...] = eg_ref[...]
        eu[...] = eu_ref[...]
        ed[...] = ed_ref[...]

    return compute_call(
        body,
        "deliver",
        [
            jax.ShapeDtypeStruct((ROWS, WIDTH), BF16),
            jax.ShapeDtypeStruct((128, WIDTH), F32),
            jax.ShapeDtypeStruct((128, 512), F32),
            jax.ShapeDtypeStruct((128, 512), F32),
            jax.ShapeDtypeStruct((128, WIDTH), F32),
            jax.ShapeDtypeStruct((1, 128), F32),
            jax.ShapeDtypeStruct((1, 128), F32),
            jax.ShapeDtypeStruct((1, 64), F32),
            jax.ShapeDtypeStruct((1, 128), F32),
            jax.ShapeDtypeStruct((ROWS, WIDTH), F32),
        ]
        + [jax.ShapeDtypeStruct(a.shape, F32) for a in expert_sums],
        [resid, layer_keep, layer_got, dense, out_grad, gain_sums, input_grad, *expert_sums],
    )


def cosine_of_turns(turns):
    part = turns - jnp.floor(turns + 0.5)
    square = part * part * 39.47841760435743
    total = jnp.full_like(square, -1.0 / 6402373705728000.0)
    for n in (20922789888000.0, -87178291200.0, 479001600.0, -3628800.0, 40320.0, -720.0, 24.0, -2.0, 1.0):
        total = total * square + 1.0 / n
    return total


def front(tokens, cotangent, dense, norms, perm, lengths):
    half = 64

    def body(
        t_ref, cot_ref, wq_ref, wk_ref, wv_ref, wd_ref, na_ref, nq_ref, nk_ref, nf_ref, perm_ref, len_ref,
        wo_ref, go_ref, n_ref, ql_ref, kl_ref, s_ref, c_ref, sn_ref, p_ref, kp_ref, q_ref, kv_ref, co_ref,
        g_ref, w_mine, rows, normed, gains_v, w_own, totals, totals_all, kv_half, send_sem, recv_sem, local_sem,
    ):
        _, chip, core, sibling = place()
        me = lax.axis_index("exp")
        chips, exps = ring_of(chip), ring_of(me)
        twins = [lax.rem(chip + d, CHIPS) for d in (2, 6, 4, 1, 3, 5, 7)]
        to_chip = lambda p: ("ctx", 2 * p + core)
        to_exp = lambda p: ("exp", p)
        copier = Copier(send_sem, recv_sem, local_sem)
        keys = key_lanes()
        odd = lax.rem(chip, 2) == 1
        wk, wv = wk_ref[:, lanes(chip // 2)].astype(F32), wv_ref[:, lanes(chip // 2)].astype(F32)
        wk = jnp.where(odd, pltpu.roll(wk, 64, 1), wk)
        wv = jnp.where(odd, wv, pltpu.roll(wv, 64, 1))
        w_mine[:, 0:128] = wq_ref[:, lanes(chip)]
        w_mine[:, 128:256] = jnp.where(keys, wk, wv).astype(BF16)
        g_ref[...] = jnp.ones((8, 128), F32)
        g_ref[0:1, :] = na_ref[...].astype(F32)
        g_ref[1:2, :] = nq_ref[...].astype(F32)
        g_ref[2:3, 0:64] = nk_ref[...].astype(F32)
        g_ref[3:4, :] = nf_ref[...].astype(F32)
        meet([to_chip(p) for p in twins] + [to_exp(p) for p in exps[1:]] + [("ctx", sibling)])
        gain_sends = [copier.send(g_ref, gains_v.at[me], *to_exp(p)) for p in exps[1:]]
        part = pl.ds(pl.multiple_of(core * half, half), half)
        slot = lambda s: wo_ref.at[s, part]
        handed = []

        def norm(block, s):
            x = block.astype(F32)
            scale = row_scale(jnp.sum(x * x, axis=1, keepdims=True), WIDTH)
            for e in range(EXP):
                at = slice(e * 128, (e + 1) * 128)
                normed[s, :, at] = (x[:, at] * scale * gains_v[e, 0:1, :]).astype(BF16)

        projected = []

        def project(s):
            both = dot(normed[s], w_own[...].reshape(WIDTH, 256))
            q, kv = both[:, 0:128], both[:, 128:256]
            ql_ref[s] = q
            kl_ref[s] = kv
            totals[s] = both_totals(q * q, kv * kv)

        def landed(s):
            norm(rows[s], s)
            projected.append(s)

        main = relay(copier, t_ref, lambda s: rows.at[s], ROWS, chips, to_chip, landed)
        extra = relay(copier, cot_ref, lambda s: co_ref.at[s], ROWS, exps, to_exp)
        dense = relay(
            copier,
            wd_ref.at[part],
            slot,
            half,
            exps,
            to_exp,
            lambda s: handed.append(copier.send(slot(s), slot(s), "ctx", sibling)),
        )
        next(main)
        next(main)
        next(dense)
        next(dense)
        copier.keep(wd_ref, wo_ref.at[me])
        copier.keep(cot_ref, co_ref.at[me])
        w_own[me] = w_mine[...]
        gains_v[me] = g_ref[...]

        row = lax.broadcasted_iota(jnp.int32, (CTX, ROWS), 1)
        piece = jnp.where(row // 12 == lax.broadcasted_iota(jnp.int32, (CTX, ROWS), 0), 1.0, 0.0)
        dealt = dot(perm_ref[...].astype(F32).astype(BF16), piece.astype(BF16))
        source = lax.broadcasted_iota(jnp.int32, (CTX, ROWS), 0)
        position = (source * CTX).astype(F32) + dealt
        position = position * 12.0 + lax.rem(row, 12).astype(F32)
        begin = jnp.zeros((CTX, ROWS), F32)
        ends = jnp.zeros((1, 1), F32)
        for k in range(3):
            ends = ends + len_ref[0:1, k : k + 1].astype(F32)
            begin = jnp.where(position >= ends, ends, begin)
        for i in range(CHIPS):
            mine = [jnp.where(core == 0, v[2 * i : 2 * i + 1], v[2 * i + 1 : 2 * i + 2]) for v in (position, begin)]
            p_ref[i] = jnp.concatenate(mine, axis=0)
            kp_ref[i] = jnp.concatenate([position[2 * i : 2 * i + 1], position[2 * i + 1 : 2 * i + 2]], axis=1)

        def angles(i, _):
            keys = key_lanes()
            lane = lax.broadcasted_iota(jnp.int32, (1, 128), 1)
            freq = jnp.exp(lax.rem(lane, 32).astype(F32) * (-2.0 / 64 * 9.210340371976184))
            place_i = p_ref[i]
            offset = down_rows(place_i, 0) - down_rows(place_i, 1)
            mixed = cosine_of_turns(offset * (freq * 0.15915494309189535) - jnp.where(keys, 0.0, 0.25))
            other = pltpu.roll(mixed, 64, 1)
            c_ref[i] = jnp.where(keys, mixed, other)
            sn_ref[i] = jnp.where(keys, other, mixed)
            return 0

        lax.fori_loop(0, CHIPS, angles, 0)
        for at in gain_sends:
            copier.arrived(at)
        go_ref[...] = gains_v[...]
        norm(t_ref[...], chip)
        projected.append(chip)
        next(main)
        next(dense)
        next(main)
        own_sends = [copier.send(w_mine, w_own.at[me], *to_exp(p)) for p in exps[1:]]
        next(extra)
        next(extra)
        next(dense)
        next(main)
        next(main)
        next(dense)
        for at in own_sends:
            copier.arrived(at)
        for s in projected:
            project(s)
        projected.clear()
        next(extra)
        next(extra)
        next(main)
        next(dense)
        for s in projected:
            project(s)
        projected.clear()
        side_by_side(main)
        for s in projected:
            project(s)
        shares = [copier.send(totals, totals_all.at[chip], *to_chip(p)) for p in twins]
        totals_all[chip] = totals[...]
        side_by_side(dense)
        copier.keep(normed, n_ref)
        for _ in range(3):
            next(extra)
        for at in shares:
            copier.arrived(at)

        def turn_one(i, _):
            squares = totals_all[0, i]
            for c in range(1, CHIPS):
                squares = squares + totals_all[c, i]
            s_ref[i] = squares
            cos, sin = c_ref[i], sn_ref[i]
            gain = gains_v[chip]
            q = ql_ref[i] * row_scale(down_rows(squares, 0), WIDTH) * gain[1:2, :]
            q = turn(q, cos, sin).astype(BF16).astype(F32)
            q_ref[i] = (q * 0.125).astype(BF16)
            scale = jnp.where(keys, row_scale(down_rows(squares, 1), WIDTH // 2), 1.0)
            kv = kl_ref[i] * scale * gain[2:3, :]
            kv_half[i] = turn(kv, jnp.where(keys, cos, 1.0), jnp.where(keys, sin, 0.0)).astype(BF16)
            return 0

        lax.fori_loop(0, CHIPS, turn_one, 0)
        copier.send(kv_half, kv_ref.at[:, core], "ctx", sibling)
        copier.keep(kv_half, kv_ref.at[:, core])
        side_by_side(extra)
        copier.finish()

    vmem = pl.BlockSpec(memory_space=pltpu.VMEM)
    wide = jax.ShapeDtypeStruct((CHIPS, ROWS, 128), F32)
    return pl.pallas_call(
        body,
        name="front",
        out_shape=[
            jax.ShapeDtypeStruct((EXP, 128, WIDTH), BF16),
            jax.ShapeDtypeStruct((EXP, 8, 128), F32),
            jax.ShapeDtypeStruct((CHIPS, ROWS, WIDTH), BF16),
            wide,
            wide,
            jax.ShapeDtypeStruct((CHIPS, 2, ROWS), F32),
            wide,
            wide,
            jax.ShapeDtypeStruct((CHIPS, 2, ROWS), F32),
            jax.ShapeDtypeStruct((CHIPS, 1, CHUNK), F32),
            jax.ShapeDtypeStruct((CHIPS, ROWS, 128), BF16),
            jax.ShapeDtypeStruct((CHIPS, 2, ROWS, 128), BF16),
            jax.ShapeDtypeStruct((EXP, ROWS, WIDTH), BF16),
        ],
        in_specs=[vmem] * 12,
        out_specs=[ANY_SPEC, vmem, ANY_SPEC] + [vmem] * 8 + [ANY_SPEC] * 2,
        scratch_shapes=[
            pltpu.VMEM((8, 128), F32),
            pltpu.VMEM((128, 256), BF16),
            pltpu.VMEM((CHIPS, ROWS, WIDTH), BF16),
            pltpu.VMEM((CHIPS, ROWS, WIDTH), BF16),
            pltpu.VMEM((EXP, 8, 128), F32),
            pltpu.VMEM((EXP, 128, 256), BF16),
            pltpu.VMEM((CHIPS, 2, ROWS), F32),
            pltpu.VMEM((CHIPS, CHIPS, 2, ROWS), F32),
            pltpu.VMEM((CHIPS, ROWS, 128), BF16),
            pltpu.SemaphoreType.DMA((71,)),
            pltpu.SemaphoreType.DMA((71,)),
            pltpu.SemaphoreType.DMA((8,)),
        ],
        compiler_params=pltpu.CompilerParams(
            collective_id=1, has_side_effects=True, vmem_limit_bytes=60 * MIB
        ),
    )(tokens, cotangent, *dense, *norms, perm, lengths)


def apart(pieces):
    first, second = pieces
    keys = key_lanes()
    return (
        jnp.where(keys, first, pltpu.roll(second, 64, 1)),
        jnp.where(keys, pltpu.roll(first, 64, 1), second),
    )


def tail(
    q, kv, d_out, out_turned, log_total, key_pos, places, q_lin, kv_lin, cosine, sine, squares, gains, normed, attended, d_branch, layer_part,
    w_query, w_key, w_value, tokens, d_resid, ffn_gain, gate_part, up_part, down_a, down_b,
):
    def body(
        q_ref, kv_ref, do_ref, ot_ref, l_ref, kp_ref, p_ref, ql_ref, kl_ref, c_ref, sn_ref, s_ref, g_ref, n_ref, at_ref, br_ref, lp_ref,
        wq_ref, wk_ref, wv_ref, t_ref, r_ref, fg_ref, gp_ref, up_ref, da_ref, db_ref,
        eg_ref, eu_ref, ed_ref, di_ref, dense_ref, og_ref, lo_ref, gs_ref,
        keys_v, values, acc, key_at, keys_t, dq_v, other_v, w_mine, ql_v, kl_v, c_v, sn_v, n_v, w_v, t_v, r_v,
        got, e_q, e_kv, totals, totals_all, d_lin, home, w_give, w_keep, w_got, joint, traded, done,
        o_both, o_keep, o_got, o_traded, o_pair, o_half, o_full, a_got, a_done, packet, packets, mine, shared, gate_c, down_c, up_d, down_d, send_sem, recv_sem, local_sem,
    ):
        ctx, chip, core, sibling = place()
        me = lax.axis_index("exp")
        twins = [lax.rem(chip + d, CHIPS) for d in (2, 6, 4, 1, 3, 5, 7)]
        exps = [lax.rem(me + d, EXP) for d in range(1, EXP)]
        others = [lax.rem(ctx + d, CTX) for d in range(1, CTX)]
        to_chip = lambda p: ("ctx", 2 * p + core)
        copier = Copier(send_sem, recv_sem, local_sem)
        heads = [
            copier.keep(src, dst)
            for src, dst in ((c_ref, c_v), (sn_ref, sn_v), (ql_ref, ql_v), (kl_ref, kl_v))
        ]
        late = [
            copier.keep(src, dst)
            for src, dst in ((n_ref, n_v),  (t_ref, t_v), (r_ref, r_v))
        ]
        w_mine[:, 0:1024] = wq_ref[...]
        w_mine[:, 1024:1536] = wk_ref[...]
        w_mine[:, 1536:2048] = wv_ref[...]
        w_v[me] = w_mine[...]
        w_part = pl.ds(pl.multiple_of(core * 64, 64), 64)
        w_slot = lambda s: w_v.at[s, w_part]
        handed = []
        weights = relay(
            copier,
            w_mine.at[w_part],
            w_slot,
            64,
            ring_of(me),
            lambda p: ("exp", p),
            lambda s: handed.append(copier.send(w_slot(s), w_slot(s), "ctx", sibling)),
        )
        meet([("ctx", p) for p in others] + [("exp", p) for p in exps])
        next(weights)
        next(weights)
        copier.send(lp_ref, lo_ref, "exp", lax.rem(me + 4, EXP))
        zh, y = chip // 4, lax.rem(chip, 4)
        second = []
        for d in (1, 3, 2):
            c = lax.rem(y + d, 4)
            second.append(copier.send(gp_ref.at[c], gate_c.at[y], *to_chip(zh * 4 + c)))
            second.append(copier.send(da_ref.at[c], down_c.at[y], *to_chip(zh * 4 + c)))
        second.append(copier.send(up_ref.at[1 - zh], up_d, *to_chip((1 - zh) * 4 + y)))
        second.append(copier.send(db_ref.at[1 - zh], down_d, *to_chip((1 - zh) * 4 + y)))

        def out_grad(r, _):
            grad = dot(at_ref[:, pl.ds(pl.multiple_of(r * 256, 256), 256)], br_ref[...], TN).astype(BF16)
            for k in range(2):
                for c in range(2):
                    o_both[c, 2 * r + k] = grad[(2 * k + c) * 64 : (2 * k + c + 1) * 64]
            return 0

        lax.fori_loop(0, 4, out_grad, 0)
        o_swap = copier.send(o_both.at[1 - core], o_got, "ctx", sibling)
        low = key_lanes()

        def place_keys(p, _):
            rows = pl.ds(pl.multiple_of(p * CHUNK, CHUNK), CHUNK)
            both = kv_ref[rows, :].astype(F32)
            own_keys = jnp.where(low, both, 0.0)
            keys_v[rows, :] = own_keys.astype(BF16)
            keys_t[:, rows] = own_keys.T.astype(BF16)
            values[rows, :] = jnp.where(low, pltpu.roll(both, 64, 1), 0.0).astype(BF16)
            key_at[rows, :] = key_columns(kp_ref[p])
            acc[rows, :] = jnp.zeros((CHUNK, 128), F32)
            return 0

        lax.fori_loop(0, CHIPS, place_keys, 0)

        def attend_block(i, _):
            q_wide, do_wide = q_ref[i].astype(F32), do_ref[i].astype(F32)
            q_turned, do_turned = pltpu.roll(q_wide, 64, 1), pltpu.roll(do_wide, 64, 1)
            q_rows = jnp.concatenate([q_wide, q_turned], axis=0)
            do_rows = jnp.concatenate([do_wide, do_turned], axis=0)
            do_high = jnp.concatenate([do_turned, do_wide], axis=0)
            right = [jnp.where(low, q_rows, 0.0), jnp.where(low, 0.0, do_high)]
            right = jnp.concatenate(right, axis=0).astype(BF16)
            q_rows = q_rows.astype(BF16)
            delta = jnp.sum(do_rows.T[0:64, :] * ot_ref[i], axis=0, keepdims=True)
            do_rows = do_rows.astype(BF16)
            total = l_ref[i]
            at_row, start_row = pair_rows(p_ref[i])

            def step(diagonal, p, dq):
                rows = pl.ds(pl.multiple_of(p * CHUNK, CHUNK), CHUNK)
                scores = dot(keys_v[rows, :], q_rows, NT)
                at_key = jnp.concatenate([key_at[rows, :]] * (CHUNK // 128), axis=1)
                seen = at_key >= start_row
                if diagonal:
                    seen = seen & (at_key <= at_row)
                probs = jnp.exp(jnp.where(seen, scores, MASKED) - total)
                d_scores = (probs * (dot(values[rows, :], do_rows, NT) - delta)).astype(BF16)
                acc[rows, :] += dot(jnp.concatenate([d_scores, probs.astype(BF16)], axis=1), right)
                return dq + dot(keys_t[:, rows], d_scores)

            dq = lax.fori_loop(0, i, lambda p, dq: step(False, p, dq), jnp.zeros((128, 2 * ROWS), F32))
            dq = step(True, i, dq).T * 0.125
            dq_v[i] = jnp.where(low, dq[:ROWS], pltpu.roll(dq[ROWS:], 64, 1))
            return 0

        lax.fori_loop(0, 4, attend_block, 0)
        next(weights)
        next(weights)
        copier.arrived(o_swap)

        def add_cores(e, _):
            o_keep[e] = (o_both[core, e].astype(F32) + o_got[e].astype(F32)).astype(BF16)
            return 0

        lax.fori_loop(0, EXP, add_cores, 0)
        zl, x = me // 4, lax.rem(me, 4)
        o_trades = []
        for d in (2, 1, 3):
            p = lax.rem(x + d, 4)
            for z in range(2):
                o_trades.append(copier.send(o_keep.at[z * 4 + p], o_traded.at[x, z], "exp", zl * 4 + p))
        lax.fori_loop(4, 6, attend_block, 0)
        next(weights)
        next(weights)
        lax.fori_loop(6, 7, attend_block, 0)
        next(weights)
        for at in o_trades:
            copier.arrived(at)
        keep, give = o_keep[zl * 4 + x].astype(F32), o_keep[(1 - zl) * 4 + x].astype(F32)
        for d in (1, 2, 3):
            p = lax.rem(x + d, 4)
            keep = keep + o_traded[p, zl].astype(F32)
            give = give + o_traded[p, 1 - zl].astype(F32)
        o_half[...] = give.astype(BF16)
        o_full[...] = keep.astype(BF16)
        o_pairs = copier.send(o_half, o_pair, "exp", (1 - zl) * 4 + x)
        lax.fori_loop(7, CHIPS, attend_block, 0)

        side_by_side(weights)

        def give_other(s, _):
            other = pl.ds(pl.multiple_of((2 * s + 1 - core) * ROWS, ROWS), ROWS)
            other_v[s] = acc[other, :].astype(BF16)
            return 0

        lax.fori_loop(0, CHIPS, give_other, 0)
        swapped = copier.send(other_v, got, "ctx", sibling)
        copier.arrived(o_pairs)
        o_full[...] = (o_full[...].astype(F32) + o_pair[...].astype(F32)).astype(BF16)
        spread = [copier.send(o_full.at[:, lanes(p)], a_got.at[chip], *to_chip(p)) for p in twins]
        a_got[chip] = o_full[:, lanes(chip)]
        keys = key_lanes()
        gain = g_ref[chip]
        for at in heads:
            copier.kept(at)

        def unturn_q(i, _):
            e_q[i] = turn(dq_v[i], c_v[i], -sn_v[i])
            return 0

        lax.fori_loop(0, CHIPS, unturn_q, 0)
        copier.arrived(swapped)

        def unturn_kv(i, carry):
            q_sum, kv_sum = carry
            cos, sin = jnp.where(keys, c_v[i], 1.0), jnp.where(keys, -sn_v[i], 0.0)
            mine_rows = pl.ds(pl.multiple_of((2 * i + core) * ROWS, ROWS), ROWS)
            e = turn(acc[mine_rows, :] + got[i].astype(F32), cos, sin)
            e_kv[i] = e
            q_part, kv_part = e_q[i] * ql_v[i], e * kl_v[i]
            totals[i] = both_totals(q_part * gain[1:2, :], kv_part * gain[2:3, :])
            q_scale = row_scale(down_rows(s_ref[i], 0), WIDTH)
            k_scale = row_scale(down_rows(s_ref[i], 1), WIDTH // 2)
            q_sum = q_sum + jnp.sum(q_part * q_scale, axis=0, keepdims=True)
            kv_sum = kv_sum + jnp.sum(kv_part * jnp.where(keys, k_scale, 1.0), axis=0, keepdims=True)
            return q_sum, kv_sum

        none = jnp.zeros((1, 128), F32)
        q_sum, kv_sum = lax.fori_loop(0, CHIPS, unturn_kv, (none, none))
        shares = [copier.send(totals, totals_all.at[chip], *to_chip(p)) for p in twins]
        totals_all[chip] = totals[...]
        for at in spread:
            copier.arrived(at)
        total = a_got[0].astype(F32)
        for c in range(1, CHIPS):
            total = total + a_got[c].astype(F32)
        a_done[...] = total.astype(BF16)
        half = pl.ds(pl.multiple_of(core * 64, 64), 64)
        a_shares = [copier.send(a_done, og_ref.at[half, lanes(chip)], *to_chip(p)) for p in twins]
        copier.send(a_done, og_ref.at[half, lanes(chip)], "ctx", sibling)
        copier.keep(a_done, og_ref.at[half, lanes(chip)])
        for at in shares:
            copier.arrived(at)

        def gradient(i):
            inner = totals_all[0, i]
            for c in range(1, CHIPS):
                inner = inner + totals_all[c, i]
            squares_i = s_ref[i]
            q_scale = row_scale(down_rows(squares_i, 0), WIDTH)
            k_scale = row_scale(down_rows(squares_i, 1), WIDTH // 2)
            q_cut = q_scale * q_scale * q_scale * down_rows(inner, 0) * (1.0 / WIDTH)
            k_cut = k_scale * k_scale * k_scale * down_rows(inner, 1) * (2.0 / WIDTH)
            d_lin[0, i] = (q_scale * (e_q[i] * gain[1:2, :]) - ql_v[i] * q_cut).astype(BF16)
            kv_scale = jnp.where(keys, k_scale, 1.0)
            k_cut = jnp.where(keys, k_cut, 0.0)
            d_lin[1, i] = (kv_scale * (e_kv[i] * gain[2:3, :]) - kl_v[i] * k_cut).astype(BF16)

        homeward = []
        for p in twins:
            gradient(p)
            for k in range(2):
                homeward.append(copier.send(d_lin.at[k, p], home.at[k, :, lanes(chip)], *to_chip(p)))
        gradient(chip)
        for k in range(2):
            home[k, :, lanes(chip)] = d_lin[k, chip]
        for at in late:
            copier.kept(at)

        def columns_grad(half, out):
            d = d_lin[half].reshape(CHIPS * ROWS, 128)

            def part(r, _):
                n = n_v[:, :, pl.ds(pl.multiple_of(r * 256, 256), 256)].reshape(CHIPS * ROWS, 256)
                out[pl.ds(pl.multiple_of(r * 256, 256), 256), :] = dot(n, d, TN).astype(BF16)
                return 0

            lax.fori_loop(0, 4, part, 0)

        columns_grad(1 - core, w_give)
        w_swap = copier.send(w_give, w_got, "ctx", sibling)
        columns_grad(core, w_keep)
        copier.arrived(w_swap)
        both = w_keep[...].astype(F32) + w_got[...].astype(F32)
        joint[...] = both.astype(BF16).reshape(EXP, 128, 128)
        trades = [copier.send(joint.at[p], traded.at[me], "exp", p) for p in exps]
        traded[me] = joint[me]

        for at in homeward + handed:
            copier.arrived(at)
        k_parts, v_parts = [], []
        for c in range(4):
            k, v = apart([home[1, :, (2 * c + j) * 128 : (2 * c + j + 1) * 128].astype(F32) for j in range(2)])
            k_parts.append(k.astype(BF16))
            v_parts.append(v.astype(BF16))
        left = jnp.concatenate([home[0]] + k_parts + v_parts, axis=1)
        x = t_v[...].astype(F32)
        scale = row_scale(jnp.sum(x * x, axis=1, keepdims=True), WIDTH)
        inner = jnp.zeros((ROWS, 1), F32)
        pieces = []
        for e in range(EXP):
            at = slice(e * 128, (e + 1) * 128)
            d_normed = dot(left, w_v[e], NT).astype(BF16).astype(F32)
            packet[e] = jnp.zeros((8, 128), F32)
            packet[e, 0:1, :] = jnp.sum(d_normed * x[:, at] * scale, axis=0, keepdims=True)
            packet[e, 3:4, :] = fg_ref[:, at]
            weighted = d_normed * g_ref[e, 0:1, :]
            inner = inner + jnp.sum(weighted * x[:, at], axis=1, keepdims=True)
            pieces.append(weighted)
        packet[chip, 1:2, :] = q_sum
        packet[chip, 2:3, :] = kv_sum
        gain_trades = [copier.send(packet.at[p], packets.at[me], "exp", p) for p in exps]
        packets[me] = packet[me]

        for at in trades:
            copier.arrived(at)
        total = traded[0].astype(F32)
        for e in range(1, EXP):
            total = total + traded[e].astype(F32)
        done[...] = total.astype(BF16)
        spot = dense_ref.at[core, :, lanes(chip)]
        w_shares = [copier.send(done, spot, *to_chip(p)) for p in twins]
        copier.send(done, spot, "ctx", sibling)
        copier.keep(done, spot)

        for at in gain_trades:
            copier.arrived(at)
        total = packets[0]
        for e in range(1, EXP):
            total = total + packets[e]
        mine[...] = total
        gain_shares = [copier.send(mine, shared.at[ctx], "ctx", p) for p in others]
        shared[ctx] = total

        inner = inner * (1.0 / WIDTH)
        cut = scale * scale * scale * inner
        for e in range(EXP):
            at = slice(e * 128, (e + 1) * 128)
            di_ref[:, at] = r_v[:, at] + scale * pieces[e] - x[:, at] * cut
        for at in second:
            copier.arrived(at)
        columns = [lax.rem(y + d, 4) for d in (1, 2, 3)]

        def add_experts(e, _):
            total = gp_ref[y, e].astype(F32)
            for c in columns:
                total = total + gate_c[c, e].astype(F32)
            eg_ref[e] = total
            eu_ref[e] = up_ref[zh, e].astype(F32) + up_d[e].astype(F32)
            return 0

        lax.fori_loop(0, LOCAL, add_experts, 0)
        for e in range(2):
            total = da_ref[y, e].astype(F32)
            for c in columns:
                total = total + down_c[c, e].astype(F32)
            ed_ref[e] = total
            ed_ref[e + 2] = db_ref[zh, e].astype(F32) + down_d[e].astype(F32)
        for d, at in zip((2, 6, 4, 1, 3, 5, 7), w_shares):
            copier.arrived(at)
            got_at = dense_ref.at[core, :, lanes(lax.rem(chip + CHIPS - d, CHIPS))]
            copier.send(got_at, got_at, "ctx", sibling)
        for d, at in zip((2, 6, 4, 1, 3, 5, 7), a_shares):
            copier.arrived(at)
            got_at = og_ref.at[half, lanes(lax.rem(chip + CHIPS - d, CHIPS))]
            copier.send(got_at, got_at, "ctx", sibling)
        for at in gain_shares:
            copier.arrived(at)
        total = shared[0]
        for c in range(1, CTX):
            total = total + shared[c]
        gs_ref[...] = total
        copier.finish()

    vmem = pl.BlockSpec(memory_space=pltpu.VMEM)
    block = (CHIPS, ROWS, 128)
    tile = pltpu.VMEM((128, 128), BF16)
    return pl.pallas_call(
        body,
        name="tail",
        out_shape=[
            jax.ShapeDtypeStruct((LOCAL, 64, FF), F32),
            jax.ShapeDtypeStruct((LOCAL, 64, FF), F32),
            jax.ShapeDtypeStruct((LOCAL, 32, WIDTH), F32),
            jax.ShapeDtypeStruct((ROWS, WIDTH), F32),
            jax.ShapeDtypeStruct((2, 128, WIDTH), BF16),
            jax.ShapeDtypeStruct((128, WIDTH), BF16),
            jax.ShapeDtypeStruct((ROWS, WIDTH), BF16),
            jax.ShapeDtypeStruct((8, 128), F32),
        ],
        in_specs=[vmem] * 7 + [ANY_SPEC] * 4 + [vmem] * 2 + [ANY_SPEC] + [vmem] * 2 + [ANY_SPEC] + [vmem] * 3 + [ANY_SPEC] * 2 + [vmem] * 5,
        out_specs=[vmem] * 4 + [ANY_SPEC] * 3 + [vmem],
        scratch_shapes=[
            pltpu.VMEM((KEYS, 128), BF16),
            pltpu.VMEM((KEYS, 128), BF16),
            pltpu.VMEM((KEYS, 128), F32),
            pltpu.VMEM((KEYS, 128), F32),
            pltpu.VMEM((128, KEYS), BF16),
            pltpu.VMEM(block, F32),
            pltpu.VMEM(block, BF16),
            pltpu.VMEM((128, 2 * WIDTH), BF16),
            pltpu.VMEM(block, F32),
            pltpu.VMEM(block, F32),
            pltpu.VMEM(block, F32),
            pltpu.VMEM(block, F32),
            pltpu.VMEM((CHIPS, ROWS, WIDTH), BF16),
            pltpu.VMEM((EXP, 128, 2 * WIDTH), BF16),
            pltpu.VMEM((ROWS, WIDTH), BF16),
            pltpu.VMEM((ROWS, WIDTH), F32),
            pltpu.VMEM(block, BF16),
            pltpu.VMEM(block, F32),
            pltpu.VMEM(block, F32),
            pltpu.VMEM((CHIPS, 2, ROWS), F32),
            pltpu.VMEM((CHIPS, CHIPS, 2, ROWS), F32),
            pltpu.VMEM((2,) + block, BF16),
            pltpu.VMEM((2, ROWS, WIDTH), BF16),
            pltpu.VMEM((WIDTH, 128), BF16),
            pltpu.VMEM((WIDTH, 128), BF16),
            pltpu.VMEM((WIDTH, 128), BF16),
            pltpu.VMEM((EXP, 128, 128), BF16),
            pltpu.VMEM((EXP, 128, 128), BF16),
            tile,
            pltpu.VMEM((2, EXP, 64, WIDTH), BF16),
            pltpu.VMEM((EXP, 64, WIDTH), BF16),
            pltpu.VMEM((EXP, 64, WIDTH), BF16),
            pltpu.VMEM((4, 2, 64, WIDTH), BF16),
            pltpu.VMEM((64, WIDTH), BF16),
            pltpu.VMEM((64, WIDTH), BF16),
            pltpu.VMEM((64, WIDTH), BF16),
            pltpu.VMEM((CHIPS, 64, 128), BF16),
            pltpu.VMEM((64, 128), BF16),
            pltpu.VMEM((EXP, 8, 128), F32),
            pltpu.VMEM((EXP, 8, 128), F32),
            pltpu.VMEM((8, 128), F32),
            pltpu.VMEM((CTX, 8, 128), F32),
            pltpu.VMEM((4, LOCAL, 64, FF), BF16),
            pltpu.VMEM((4, 2, 32, WIDTH), BF16),
            pltpu.VMEM((LOCAL, 64, FF), BF16),
            pltpu.VMEM((2, 32, WIDTH), BF16),
            pltpu.SemaphoreType.DMA((127,)),
            pltpu.SemaphoreType.DMA((127,)),
            pltpu.SemaphoreType.DMA((15,)),
        ],
        compiler_params=pltpu.CompilerParams(
            collective_id=6, has_side_effects=True, vmem_limit_bytes=60 * MIB
        ),
    )(
        q, kv, d_out, out_turned, log_total, key_pos, places, q_lin, kv_lin, cosine, sine, squares, gains, normed, attended, d_branch, layer_part,
        w_query, w_key, w_value, tokens, d_resid, ffn_gain, gate_part, up_part, down_a, down_b,
    )


def sum_blocks(blocks):
    return jnp.sum(blocks.astype(F32), axis=0)


def per_device(
    tokens,
    cotangent,
    lengths,
    deal_perm,
    routes,
    gate_logits,
    norm_attn,
    norm_query,
    norm_key,
    norm_ffn,
    w_query,
    w_key,
    w_value,
    w_out,
    w_gate,
    w_up,
    w_down,
):
    tokens, cotangent = tokens[0], cotangent[0]

    row = lambda v: v.reshape(1, -1)
    (
        w_o, gain_all, normed, q_lin, kv_lin, squares, cosine, sine, places, key_pos, q_all, kv_all, grads_all,
    ) = front(
        tokens,
        cotangent,
        (w_query, w_key, w_value, w_out),
        (row(norm_attn), row(norm_query), row(norm_key), row(norm_ffn)),
        deal_perm[0],
        lengths,
    )

    w_o = w_o.reshape(WIDTH, WIDTH)
    kv_all = kv_all.reshape(KEYS, 128)
    out_low, out_wide, log_total = attend(q_all, kv_all, key_pos, places, lengths)
    attended, resid, rows_all, meta_all = join_heads(
        out_low, w_o, tokens, gain_all, routes[0].T, gate_logits[0].T
    )

    rows_in, d_rows, act, d_gate, d_up, out_parts, d_parts = experts(
        rows_all, grads_all, meta_all, w_gate, w_up, w_down
    )
    (
        gate_part, up_part, down_a, down_b, d_resid, d_branch, ffn_gain_grad, d_out, layer_keep, layer_give,
    ) = settle_experts(
        rows_in,
        d_rows,
        act,
        d_gate,
        d_up,
        d_parts.reshape(2, 4, ROWS, WIDTH),
        out_parts.reshape(2, 4, ROWS, WIDTH),
        resid,
        cotangent,
        gain_all,
        w_o,
    )
    gate_grad, up_grad, down_grad, input_grad, dense, out_grad, layer_got, gain_sums = tail(
        q_all,
        kv_all,
        d_out,
        out_wide,
        log_total,
        key_pos,
        places,
        q_lin,
        kv_lin,
        cosine,
        sine,
        squares,
        gain_all,
        normed,
        attended,
        d_branch,
        layer_give,
        w_query,
        w_key,
        w_value,
        tokens,
        d_resid,
        ffn_gain_grad,
        gate_part,
        up_part,
        down_a,
        down_b,
    )
    outs = deliver(
        resid,
        layer_keep,
        layer_got,
        dense,
        out_grad,
        gain_sums,
        input_grad,
        (gate_grad, up_grad, down_grad),
    )
    return (
        outs[0][None],
        outs[9][None],
        *outs[1:5],
        *[g.reshape(-1) for g in outs[5:9]],
        *outs[10:],
    )


def solution(mesh):
    in_specs = (
        P("exp", "ctx", None),
        P("exp", "ctx", None),
        P("exp", None),
        P("exp", None, None),
        P("exp", "ctx", None),
        P("exp", "ctx", None),
        P("exp"),
        P("exp"),
        P("exp"),
        P("exp"),
        P("exp", None),
        P("exp", None),
        P("exp", None),
        P("exp", None),
        P("exp", None, None),
        P("exp", None, None),
        P("exp", None, None),
    )
    out_specs = (
        P("exp", "ctx", None),
        P("exp", "ctx", None),
        P("exp", None),
        P("exp", None),
        P("exp", None),
        P("exp", None),
        P("exp"),
        P("exp"),
        P("exp"),
        P("exp"),
        P("exp", "ctx", None),
        P("exp", "ctx", None),
        P("exp", "ctx", None),
    )
    return jax.shard_map(
        per_device, mesh=mesh, in_specs=in_specs, out_specs=out_specs, check_vma=False
    )
```

```python
import jax
import jax.numpy as jnp
from jax import lax
from jax.experimental import pallas as pl
from jax.experimental.pallas import tpu as pltpu
from jax.sharding import PartitionSpec as P

HEADS = 16
KV_HEADS = 8
EPSILON = 1e-05
ROPE_BASE = 10000.0
MASKED = -1e30

MESH = pl.DeviceIdType.MESH
CTX = 16
EXP = 8
CHIPS = 8
ROWS = 192
WIDTH = 1024
FF = 512
LOCAL = 4
CAP = 72
PAIRS = EXP // 2
LONGEST = 2048
PAIR_ROWS = 2 * ROWS
PAIR_CAP = 2 * CAP
SLOTS = EXP * CAP
PAIR_SLOTS = LOCAL * PAIR_CAP
KEYS = CTX * ROWS
CHUNK = 2 * ROWS
MIB = 1 << 20
FAR_FIRST = (6, 2, 5, 7, 4, 1, 3)

ANY_SPEC = pl.BlockSpec(memory_space=pl.ANY)
F32 = jnp.float32
BF16 = jnp.bfloat16


def dot(a, b, dims=((1,), (0,))):
    return lax.dot_general(a, b, (dims, ((), ())), preferred_element_type=F32)


NT = ((1,), (1,))
TN = ((0,), (0,))


def comm_call(body, name, collective_id, outs, ins, copies, in_specs=None):
    return pl.pallas_call(
        body,
        name=name,
        out_shape=outs,
        in_specs=in_specs or [ANY_SPEC] * len(ins),
        out_specs=[ANY_SPEC] * len(outs),
        scratch_shapes=[
            pltpu.SemaphoreType.DMA((copies,)),
            pltpu.SemaphoreType.DMA((copies,)),
            pltpu.SemaphoreType.DMA((8,)),
        ],
        compiler_params=pltpu.CompilerParams(
            collective_id=collective_id, has_side_effects=True, vmem_limit_bytes=60 * MIB
        ),
    )(*ins)


class Copier:
    def __init__(self, send_sem, recv_sem, local_sem):
        self.send_sem, self.recv_sem, self.local_sem = send_sem, recv_sem, local_sem
        self.remote, self.local = [], []

    def send(self, src, dst, axis, index):
        at = len(self.remote)
        copy = pltpu.make_async_remote_copy(
            src_ref=src,
            dst_ref=dst,
            send_sem=self.send_sem.at[at],
            recv_sem=self.recv_sem.at[at],
            device_id={axis: index},
            device_id_type=MESH,
        )
        copy.start()
        self.remote.append([copy, False])
        return at

    def keep(self, src, dst):
        copy = pltpu.make_async_copy(src, dst, self.local_sem.at[len(self.local)])
        copy.start()
        self.local.append([copy, False])
        return len(self.local) - 1

    def arrived(self, at):
        self.remote[at][0].wait_recv()
        self.remote[at][1] = True

    def kept(self, at):
        self.local[at][0].wait()
        self.local[at][1] = True

    def finish(self):
        for copy, seen in self.remote:
            if not seen:
                copy.wait_recv()
        for copy, _ in self.remote:
            copy.wait_send()
        for copy, seen in self.local:
            if not seen:
                copy.wait()


def meet(partners):
    barrier = pltpu.get_barrier_semaphore()
    for axis, index in partners:
        pl.semaphore_signal(barrier, inc=1, device_id={axis: index}, device_id_type=MESH)
    pl.semaphore_wait(barrier, len(partners))


def place():
    ctx = lax.axis_index("ctx")
    core = lax.rem(ctx, 2)
    return ctx, ctx // 2, core, ctx + 1 - 2 * core


def ring_of(me):
    half, spot = me // 4, lax.rem(me, 4)
    over = (1 - half) * 4
    turns = [lax.rem(spot + d, 4) for d in (0, 1, 3, 2)]
    return tuple([half * 4 + t for t in turns] + [over + t for t in turns])


def relay(copier, own, slot, rows, ring, reach, landed=lambda partner: None):
    me, right, left, far, over, over_right, over_left, over_far = ring
    half = rows // 2
    low, high = pl.ds(0, half), pl.ds(half, half)

    def send(block, to, part, partner):
        return copier.send(block.at[part], slot(to).at[part], *reach(partner))

    def on(of, part, partner):
        return send(slot(of), of, part, partner)

    over_low = send(own, me, low, over)
    over_high = send(own, me, high, over)
    yield
    right_low = send(own, me, low, right)
    left_high = send(own, me, high, left)
    right_high = send(own, me, high, right)
    left_low = send(own, me, low, left)
    yield
    copier.arrived(right_low)
    far_right = on(left, low, right)
    copier.arrived(left_high)
    far_left = on(right, high, left)
    yield
    copier.arrived(over_low)
    next_right_low = on(over, low, right)
    next_left_low = on(over, low, left)
    copier.arrived(over_high)
    next_left_high = on(over, high, left)
    next_right_high = on(over, high, right)
    landed(over)
    yield
    copier.arrived(right_high)
    landed(left)
    copier.arrived(left_low)
    landed(right)
    yield
    copier.arrived(far_right)
    copier.arrived(far_left)
    landed(far)
    yield
    copier.arrived(next_right_low)
    far_right = on(over_left, low, right)
    copier.arrived(next_left_high)
    far_left = on(over_right, high, left)
    copier.arrived(next_right_high)
    landed(over_left)
    copier.arrived(next_left_low)
    landed(over_right)
    yield
    copier.arrived(far_right)
    copier.arrived(far_left)
    landed(over_far)


def side_by_side(*relays):
    for _ in zip(*relays):
        pass
    for one in relays:
        for _ in one:
            pass


def lanes(index):
    return pl.ds(pl.multiple_of(index * 128, 128), 128)


def attend(q, kv, key_pos, places, cotangent, w_out, tokens, gains, routes_t, logits_t):
    def body(
        q_ref, kv_ref, kp_ref, p_ref, cot_ref, w_ref, t_ref, g_ref, r_ref, l_ref,
        a_ref, ot_ref, lt_ref, res_ref, o_ref, mo_ref, co_ref,
        keys, values, key_at, done, w_v, ffn, m_v, out_sem, in_sem, send_sem, recv_sem, local_sem,
    ):
        _, chip, core, _ = place()
        ring = ring_of(lax.axis_index("exp"))
        me = ring[0]
        twins = [lax.rem(chip + d, CHIPS) for d in FAR_FIRST]
        to_chip = lambda p: ("ctx", 2 * p + core)
        to_exp = lambda p: ("exp", p)
        copier = Copier(send_sem, recv_sem, local_sem)
        load = copier.keep(w_ref, w_v)
        meet([to_chip(p) for p in twins] + [to_exp(p) for p in ring[1:]])
        extra = relay(copier, cot_ref, lambda s: co_ref.at[s], ROWS, ring, to_exp)
        next(extra)
        next(extra)
        copier.keep(cot_ref, co_ref.at[me])

        logits = l_ref[...]
        raised = jnp.exp(logits - jnp.max(logits, axis=0, keepdims=True))
        gates = raised / jnp.sum(raised, axis=0, keepdims=True)
        experts = lax.broadcasted_iota(jnp.int32, (32, ROWS), 0)
        member = jnp.zeros((32, ROWS), F32)
        weight = jnp.zeros((32, ROWS), F32)
        for c in range(8):
            hit = r_ref[c : c + 1, :] == experts
            member = member + jnp.where(hit, 1.0, 0.0)
            weight = weight + jnp.where(hit, gates[c : c + 1, :], 0.0)
        before = lax.broadcasted_iota(jnp.int32, (ROWS, ROWS), 0) < lax.broadcasted_iota(
            jnp.int32, (ROWS, ROWS), 1
        )
        rank = dot(member.astype(BF16), jnp.where(before, 1.0, 0.0).astype(BF16))
        spot = jnp.where(member > 0.5, rank, -1.0)
        for e in range(EXP):
            m_v[e, 0:4, :] = spot[e * 4 : e * 4 + 4, :]
            m_v[e, 4:8, :] = weight[e * 4 : e * 4 + 4, :]
        for p in ring[1:]:
            copier.send(m_v.at[p], mo_ref.at[me], *to_exp(p))
        copier.keep(m_v.at[me], mo_ref.at[me])

        low = key_lanes()

        def place_keys(p, _):
            rows = pl.ds(pl.multiple_of(p * CHUNK, CHUNK), CHUNK)
            both = kv_ref[rows, :].astype(F32)
            keys[rows, :] = jnp.where(low, both, 0.0).astype(BF16)
            values[:, rows] = jnp.where(low, pltpu.roll(both, 64, 1), 0.0).T.astype(BF16)
            key_at[rows, :] = key_columns(kp_ref[p])
            return 0

        lax.fori_loop(0, CHIPS, place_keys, 0)

        def homeward(target, source):
            return pltpu.make_async_remote_copy(
                src_ref=done.at[target],
                dst_ref=a_ref.at[:, lanes(source)],
                send_sem=out_sem.at[target],
                recv_sem=in_sem.at[source],
                device_id={"ctx": 2 * target + core},
                device_id_type=MESH,
            )

        def block(k, _):
            i = CHIPS - 1 - k
            wide = q_ref[i].astype(F32)
            stacked = jnp.concatenate([wide, pltpu.roll(wide, 64, 1)], axis=0).astype(BF16)
            at_row, start_row = pair_rows(p_ref[i])

            def step(diagonal, p, carry):
                top, total, acc = carry
                rows = pl.ds(pl.multiple_of(p * CHUNK, CHUNK), CHUNK)
                scores = dot(keys[rows, :], stacked, NT)
                at_key = jnp.concatenate([key_at[rows, :]] * (CHUNK // 128), axis=1)
                seen = at_key >= start_row
                if diagonal:
                    seen = seen & (at_key <= at_row)
                scores = jnp.where(seen, scores, MASKED)
                new_top = jnp.maximum(top, jnp.max(scores, axis=0, keepdims=True))
                probs = jnp.exp(scores - new_top)
                scale = jnp.exp(top - new_top)
                total = total * scale + jnp.sum(probs, axis=0, keepdims=True)
                acc = acc * scale + dot(values[:, rows], probs.astype(BF16))
                return new_top, total, acc

            none = jnp.zeros((1, 2 * ROWS), F32)
            carry = (none + MASKED, none, jnp.zeros((128, 2 * ROWS), F32))
            carry = lax.fori_loop(first_chunk(i, core), i, lambda p, c: step(False, p, c), carry)
            top, total, acc = step(True, i, carry)
            turned = acc[0:64, :] / total
            ot_ref[i] = turned
            lt_ref[i] = top + jnp.log(total)
            out = jnp.concatenate([turned, turned], axis=0).T
            done[i] = jnp.where(low, out[:ROWS], out[ROWS:]).astype(BF16)

            @pl.when(i != chip)
            def _():
                homeward(i, chip).start()

            return 0

        for first, last in ((0, 1), (1, 2), (2, 3), (3, 4)):
            lax.fori_loop(first, last, block, 0)
            next(extra)
        lax.fori_loop(4, CHIPS, block, 0)
        next(extra)
        a_ref[:, lanes(chip)] = done[chip]
        copier.kept(load)
        for p in twins:
            homeward(chip, p).wait_recv()
        branch = dot(a_ref[...], w_v[...]).astype(BF16).astype(F32)
        resid = t_ref[...].astype(F32) + branch
        res_ref[...] = resid
        scale = row_scale(jnp.sum(resid * resid, axis=1, keepdims=True), WIDTH)
        for e in range(EXP):
            at = slice(e * 128, (e + 1) * 128)
            ffn[:, at] = (resid[:, at] * scale * g_ref[e, 3:4, :]).astype(BF16)
        rows_out = relay(copier, ffn, lambda s: o_ref.at[s], ROWS, ring, to_exp)
        next(rows_out)
        next(rows_out)
        copier.keep(ffn, o_ref.at[me])
        side_by_side(extra)
        side_by_side(rows_out)
        for p in twins:
            homeward(p, chip).wait_send()
        copier.finish()

    vmem = pl.BlockSpec(memory_space=pltpu.VMEM)
    return pl.pallas_call(
        body,
        name="attend",
        out_shape=[
            jax.ShapeDtypeStruct((ROWS, WIDTH), BF16),
            jax.ShapeDtypeStruct((CHIPS, 64, 2 * ROWS), F32),
            jax.ShapeDtypeStruct((CHIPS, 1, 2 * ROWS), F32),
            jax.ShapeDtypeStruct((ROWS, WIDTH), F32),
            jax.ShapeDtypeStruct((EXP, ROWS, WIDTH), BF16),
            jax.ShapeDtypeStruct((EXP, 8, ROWS), F32),
            jax.ShapeDtypeStruct((EXP, ROWS, WIDTH), BF16),
        ],
        in_specs=[vmem] * 5 + [ANY_SPEC] + [vmem] * 4,
        out_specs=[vmem] * 4 + [ANY_SPEC] * 3,
        scratch_shapes=[
            pltpu.VMEM((KEYS, 128), BF16),
            pltpu.VMEM((128, KEYS), BF16),
            pltpu.VMEM((KEYS, 128), F32),
            pltpu.VMEM((CHIPS, ROWS, 128), BF16),
            pltpu.VMEM((WIDTH, WIDTH), BF16),
            pltpu.VMEM((ROWS, WIDTH), BF16),
            pltpu.VMEM((EXP, 8, ROWS), F32),
            pltpu.SemaphoreType.DMA((CHIPS,)),
            pltpu.SemaphoreType.DMA((CHIPS,)),
            pltpu.SemaphoreType.DMA((36,)),
            pltpu.SemaphoreType.DMA((36,)),
            pltpu.SemaphoreType.DMA((8,)),
        ],
        compiler_params=pltpu.CompilerParams(
            collective_id=2, has_side_effects=True, vmem_limit_bytes=60 * MIB
        ),
    )(q, kv, key_pos, places, cotangent, w_out, tokens, gains, routes_t, logits_t)


def settle_experts(
    rows, d_rows, act, d_gate, d_up, d_parts, layer_parts, resid, cotangent, gains, w_out
):
    def body(
        x_ref, r_ref, a_ref, g_ref, u_ref, p_ref, l_ref, res_ref, cot_ref, gain_ref, w_ref,
        gate_out, up_out, down_a_out, down_b_out, dr_out, db_out, gg_out, do_out, keep_out, give_out, dx_out, d_att,
        x_v, r_v, a_v, g_v, u_v, gate, up, down, gate_o, up_o, down_o, gate_a, down_a, up_b, down_b,
        to_z, from_z, d_own, d_right, d_left, d_low, d_high, d_from, l_own, l_right, l_left, l_low, l_high, l_from, send_sem, recv_sem, local_sem,
    ):
        _, chip, core, sibling = place()
        me = lax.axis_index("exp")
        zl, x = me // 4, lax.rem(me, 4)
        zh, y = chip // 4, lax.rem(chip, 4)
        at_ctx = lambda z, yy: ("ctx", z * 8 + yy * 2 + core)
        over = at_ctx(1 - zh, y)
        columns = [lax.rem(y + d, 4) for d in (1, 3, 2)]
        twins = [lax.rem(chip + d, CHIPS) for d in FAR_FIRST]
        right, left, far = [lax.rem(x + d, 4) for d in (1, 3, 2)]
        at_exp = lambda p: ("exp", zl * 4 + p)
        low, high = pl.ds(0, ROWS // 2), pl.ds(ROWS // 2, ROWS // 2)
        copier = Copier(send_sem, recv_sem, local_sem)
        loads = []
        for e in range(LOCAL):
            pairs = ((x_ref, x_v), (r_ref, r_v), (a_ref, a_v), (g_ref, g_v), (u_ref, u_v))
            loads.append([copier.keep(src.at[e], dst.at[e]) for src, dst in pairs])
        parts = (p_ref, d_own, d_right, d_left, d_low, d_high, d_from)
        layers = (l_ref, l_own, l_right, l_left, l_low, l_high, l_from)

        def fetch(src, own, to_right, to_left, *_):
            return [
                copier.keep(src.at[:, x], own),
                copier.keep(src.at[:, right, low], to_right),
                copier.keep(src.at[:, left, high], to_left),
            ]

        part_loads, layer_loads = fetch(*parts), fetch(*layers)
        meet(
            [("ctx", sibling)]
            + [("ctx", 2 * p + core) for p in twins]
            + [at_exp(right), at_exp(left)]
            + [("exp", (1 - zl) * 4 + x)]
        )

        def set_out(src, own, to_right, to_left, in_low, in_high, arrived):
            return [
                copier.send(src.at[:, far, low], in_low, *at_exp(right)),
                copier.send(src.at[:, far, high], in_high, *at_exp(left)),
                copier.send(src.at[:, right, high], arrived.at[0, :, high], *at_exp(right)),
                copier.send(src.at[:, left, low], arrived.at[1, :, low], *at_exp(left)),
            ]

        def pass_on(stage, loads_of, src, own, to_right, to_left, in_low, in_high, arrived):
            for at in loads_of:
                copier.kept(at)
            for at in stage[:2]:
                copier.arrived(at)

            def add(r, _):
                at = pl.ds(pl.multiple_of(r * 48, 16), 48)
                for z in range(2):
                    for mine, other in ((to_right, in_low), (to_left, in_high)):
                        mine[z, at, :] = (mine[z, at, :].astype(F32) + other[z, at, :].astype(F32)).astype(BF16)
                return 0

            lax.fori_loop(0, 2, add, 0)
            return stage[2:] + [
                copier.send(to_right, arrived.at[0, :, low], *at_exp(right)),
                copier.send(to_left, arrived.at[1, :, high], *at_exp(left)),
            ]

        part_stage = set_out(*parts)

        def work(e):
            for at in loads[e]:
                copier.kept(at)

            def wide(r, _):
                rows_r = x_v[e, :, pl.ds(pl.multiple_of(r * 256, 256), 256)]
                for d_v, o_v in ((g_v, gate), (u_v, up)):
                    grad = dot(rows_r, d_v[e], TN).astype(BF16)
                    for k in range(4):
                        o_v[k % 2, r // 2, 2 * lax.rem(r, 2) + k // 2, e] = grad[k * 64 : (k + 1) * 64]
                return 0

            lax.fori_loop(0, 4, wide, 0)

            def tall(r, _):
                act_r = a_v[e, :, pl.ds(pl.multiple_of(r * 256, 256), 256)]
                grad = dot(act_r, r_v[e], TN).astype(BF16)
                for k in range(8):
                    down[k % 2, r, k // 2, e] = grad[k * 32 : (k + 1) * 32]
                return 0

            lax.fori_loop(0, 2, tall, 0)
            return [
                copier.send(full.at[1 - core, :, :, e], other.at[:, :, e], "ctx", sibling)
                for full, other in ((gate, gate_o), (up, up_o), (down, down_o))
            ]

        first_a, first_b = [], []

        def join(e, swaps):
            for at in swaps:
                copier.arrived(at)

            def add(c, _):
                z, yy = c // 4, lax.rem(c, 4)
                for full, other in ((gate, gate_o), (up, up_o), (down, down_o)):
                    both = full[core, z, yy, e].astype(F32) + other[z, yy, e].astype(F32)
                    full[core, z, yy, e] = both.astype(BF16)
                return 0

            lax.fori_loop(0, CHIPS, add, 0)
            first_a.append(copier.send(gate.at[core, 1 - zh, :, e], gate_a.at[:, e], *over))
            if e < 2:
                first_a.append(copier.send(down.at[core, 1 - zh, :, e], down_a.at[:, e], *over))
            for c in columns:
                to = at_ctx(zh, c)
                first_b.append(copier.send(up.at[core, :, c, e], up_b.at[y, :, e], *to))
                if e >= 2:
                    first_b.append(copier.send(down.at[core, :, c, e], down_b.at[y, :, e - 2], *to))

        swaps = work(0)
        later = work(1)
        join(0, swaps)
        part_stage = pass_on(part_stage, part_loads, *parts)
        layer_stage = set_out(*layers)
        swaps = later
        later = work(2)
        join(1, swaps)
        swaps = later
        later = work(3)
        w_loads = [copier.keep(w_ref.at[pl.ds(k * FF, FF)], r_v.at[k, pl.ds(0, FF)]) for k in range(2)]
        join(2, swaps)
        join(3, later)

        def sum_up(stage, own, arrived, keep_ref, give_ref):
            for at in stage:
                copier.arrived(at)

            def add(r, _):
                at = pl.ds(pl.multiple_of(r * 48, 16), 48)
                keep, give = [
                    own[z, at, :].astype(F32) + arrived[0, z, at, :].astype(F32) + arrived[1, z, at, :].astype(F32)
                    for z in (zl, 1 - zl)
                ]
                keep_ref[at, :] = keep
                give_ref[at, :] = give.astype(BF16)
                return 0

            lax.fori_loop(0, 4, add, 0)

        sum_up(part_stage, d_own, d_from, dx_out, to_z)
        z_stage = copier.send(to_z, from_z, "exp", (1 - zl) * 4 + x)
        layer_stage = pass_on(layer_stage, layer_loads, *layers)

        copier.arrived(z_stage)
        incoming = dx_out[...] + from_z[...].astype(F32)
        resid_v = res_ref[...]
        scale = row_scale(jnp.sum(resid_v * resid_v, axis=1, keepdims=True), WIDTH)
        inner = jnp.zeros((ROWS, 1), F32)
        for e in range(EXP):
            at = slice(e * 128, (e + 1) * 128)
            product = incoming[:, at] * resid_v[:, at]
            gg_out[:, at] = jnp.sum(product * scale, axis=0, keepdims=True)
            inner = inner + jnp.sum(product * gain_ref[e, 3:4, :], axis=1, keepdims=True)
        cut = scale * scale * scale * inner * (1.0 / WIDTH)
        for e in range(EXP):
            at = slice(e * 128, (e + 1) * 128)
            d_norm = scale * (incoming[:, at] * gain_ref[e, 3:4, :]) - resid_v[:, at] * cut
            d_resid = cot_ref[:, at].astype(F32) + d_norm
            dr_out[:, at] = d_resid
            db_out[:, at] = d_resid.astype(BF16)
        for at in w_loads:
            copier.kept(at)
        for k in range(2):
            d_att[:, k * FF : (k + 1) * FF] = dot(db_out[...], r_v[k, 0:FF, :], NT).astype(BF16)
        for p in twins:
            copier.send(d_att.at[:, lanes(p)], do_out.at[chip], "ctx", 2 * p + core)
        copier.keep(d_att.at[:, lanes(chip)], do_out.at[chip])
        for at in first_a:
            copier.arrived(at)

        def sum_a(c, _):
            for e in range(LOCAL):
                both = gate[core, zh, c, e].astype(F32) + gate_a[c, e].astype(F32)
                gate_out[c, e] = both.astype(BF16)
            for e in range(2):
                both = down[core, zh, c, e].astype(F32) + down_a[c, e].astype(F32)
                down_a_out[c, e] = both.astype(BF16)
            return 0

        lax.fori_loop(0, 4, sum_a, 0)

        for at in first_b:
            copier.arrived(at)
        others = [lax.rem(y + d, 4) for d in (1, 2, 3)]

        def sum_b(e, _):
            for z in range(2):
                total = up[core, z, y, e].astype(F32)
                for c in others:
                    total = total + up_b[c, z, e].astype(F32)
                up_out[z, e] = total.astype(BF16)
            return 0

        lax.fori_loop(0, LOCAL, sum_b, 0)

        def sum_b_down(e, _):
            for z in range(2):
                total = down[core, z, y, e + 2].astype(F32)
                for c in others:
                    total = total + down_b[c, z, e].astype(F32)
                down_b_out[z, e] = total.astype(BF16)
            return 0

        lax.fori_loop(0, 2, sum_b_down, 0)
        sum_up(layer_stage, l_own, l_from, keep_out, give_out)
        copier.finish()

    vmem = pl.BlockSpec(memory_space=pltpu.VMEM)
    buf = lambda *shape: pltpu.VMEM(shape, BF16)
    wide, tall = (64, FF), (32, WIDTH)
    return pl.pallas_call(
        body,
        name="settle_experts",
        out_shape=[
            jax.ShapeDtypeStruct((4, LOCAL) + wide, BF16),
            jax.ShapeDtypeStruct((2, LOCAL) + wide, BF16),
            jax.ShapeDtypeStruct((4, 2) + tall, BF16),
            jax.ShapeDtypeStruct((2, 2) + tall, BF16),
            jax.ShapeDtypeStruct((ROWS, WIDTH), F32),
            jax.ShapeDtypeStruct((ROWS, WIDTH), BF16),
            jax.ShapeDtypeStruct((1, WIDTH), F32),
            jax.ShapeDtypeStruct((CHIPS, ROWS, 128), BF16),
            jax.ShapeDtypeStruct((ROWS, WIDTH), F32),
            jax.ShapeDtypeStruct((ROWS, WIDTH), BF16),
        ],
        in_specs=[ANY_SPEC] * 7 + [vmem] * 3 + [ANY_SPEC],
        out_specs=[vmem] * 7 + [ANY_SPEC] + [vmem] * 2,
        scratch_shapes=[
            pltpu.VMEM((ROWS, WIDTH), F32),
            buf(ROWS, WIDTH),
            buf(LOCAL, SLOTS, WIDTH),
            buf(LOCAL, SLOTS, WIDTH),
            buf(LOCAL, SLOTS, FF),
            buf(LOCAL, SLOTS, FF),
            buf(LOCAL, SLOTS, FF),
            buf(2, 2, 4, LOCAL, *wide),
            buf(2, 2, 4, LOCAL, *wide),
            buf(2, 2, 4, LOCAL, *tall),
            buf(2, 4, LOCAL, *wide),
            buf(2, 4, LOCAL, *wide),
            buf(2, 4, LOCAL, *tall),
            buf(4, LOCAL, *wide),
            buf(4, 2, *tall),
            buf(4, 2, LOCAL, *wide),
            buf(4, 2, 2, *tall),
            buf(ROWS, WIDTH),
            buf(ROWS, WIDTH),
        ]
        + [
            buf(2, ROWS, WIDTH),
            buf(2, ROWS // 2, WIDTH),
            buf(2, ROWS // 2, WIDTH),
            buf(2, ROWS // 2, WIDTH),
            buf(2, ROWS // 2, WIDTH),
            buf(2, 2, ROWS, WIDTH),
        ]
        * 2
        + [
            pltpu.SemaphoreType.DMA((56,)),
            pltpu.SemaphoreType.DMA((56,)),
            pltpu.SemaphoreType.DMA((32,)),
        ],
        compiler_params=pltpu.CompilerParams(
            collective_id=8, has_side_effects=True, vmem_limit_bytes=63 * MIB
        ),
    )(rows, d_rows, act, d_gate, d_up, d_parts, layer_parts, resid, cotangent, gains, w_out)


def compute_call(body, name, outs, ins, vmem=60, **kw):
    return pl.pallas_call(
        body,
        name=name,
        out_shape=outs,
        compiler_params=pltpu.CompilerParams(vmem_limit_bytes=vmem * MIB),
        **kw,
    )(*ins)


def row_scale(total, width):
    return lax.rsqrt(total * (1.0 / width) + EPSILON)


def key_lanes():
    return lax.broadcasted_iota(jnp.int32, (1, 128), 1) < 64


def turn(values, cosine, sine):
    first = lax.rem(lax.broadcasted_iota(jnp.int32, (1, 128), 1), 64) < 32
    return values * cosine + jnp.where(first, -pltpu.roll(values, 96, 1), pltpu.roll(values, 32, 1)) * sine


def across(select, values):
    return lax.dot_general(
        select, values, (NT, ((), ())), precision=lax.Precision.HIGHEST, preferred_element_type=F32
    )


def both_totals(left, right):
    row_id = lax.broadcasted_iota(jnp.int32, (8, 128), 0)
    ones = jnp.where(row_id == 0, 1.0, 0.0)
    keys = jnp.where((row_id == 1) & key_lanes(), 1.0, 0.0)
    return (across(ones, left) + across(keys, right))[0:2, :]


def down_rows(values, row, width=128):
    chosen = lax.broadcasted_iota(jnp.int32, (2, width), 0) == row
    return lax.dot_general(
        values,
        jnp.where(chosen, 1.0, 0.0),
        (TN, ((), ())),
        precision=lax.Precision.HIGHEST,
        preferred_element_type=F32,
    )


def own_chip():
    return lax.axis_index("ctx") // 2


def key_columns(row):
    upper = jnp.floor(row * (1.0 / 64.0))
    parts = jnp.concatenate([upper, row - 64.0 * upper], axis=0).astype(BF16)
    scale = jnp.where(lax.broadcasted_iota(jnp.int32, (2, 128), 0) == 0, 64.0, 1.0).astype(BF16)
    return dot(parts, scale, TN)


def first_chunk(i, core):
    return jnp.maximum((2 * i + core) * ROWS - (LONGEST - 1), 0) // CHUNK


def pair_rows(places_i):
    return [jnp.concatenate([places_i[k : k + 1, :]] * 2, axis=1) for k in range(2)]


def experts(rows, grads, meta, w_gate, w_up, w_down):
    half = SLOTS // 2
    main, rest = 64, CAP - 64

    def body(
        x_ref, g_ref, m_ref, wg_ref, wu_ref, wd_ref,
        xin_ref, dr_ref, act_ref, dg_ref, du_ref, out_ref, dx_ref,
        x, g, wg, wu, wd, xin, dr, act, dg, du, out, dx, made, back, made_rest, back_rest, weight, sems,
    ):
        def pair_in(p):
            at = pl.ds(2 * p, 2)
            return [pltpu.make_async_copy(a.at[at], b.at[at], sems.at[0, p]) for a, b in ((x_ref, x), (g_ref, g))]

        def weights_in(e):
            pairs = ((wg_ref, wg), (wu_ref, wu), (wd_ref, wd))
            return [pltpu.make_async_copy(a.at[e], b.at[e], sems.at[1, e]) for a, b in pairs]

        def rows_out(e):
            return [pltpu.make_async_copy(a.at[e], b.at[e], sems.at[2, e]) for a, b in ((xin, xin_ref), (dr, dr_ref))]

        def acts_out(e):
            pairs = ((act, act_ref), (dg, dg_ref), (du, du_ref))
            return [pltpu.make_async_copy(a.at[e], b.at[e], sems.at[3, e]) for a, b in pairs]

        def pair_out(p):
            at = pl.ds(2 * p, 2)
            return [pltpu.make_async_copy(a.at[at], b.at[at], sems.at[4, p]) for a, b in ((dx, dx_ref), (out, out_ref))]

        def start(copies):
            for copy in copies:
                copy.start()

        def wait(copies):
            for copy in copies:
                copy.wait()

        for p in range(PAIRS):
            start(pair_in(p))
        start(weights_in(0))

        row_id = lax.broadcasted_iota(jnp.int32, (LOCAL * CAP, ROWS), 0).astype(F32)

        def pick_source(s):
            meta_s = m_ref[s]
            chosen = jnp.zeros((LOCAL * CAP, ROWS), F32)
            gates = jnp.zeros((LOCAL * CAP, ROWS), F32)
            for k in range(LOCAL):
                slot = meta_s[k : k + 1, :]
                spot = jnp.where(slot < main, slot + k * main, slot + (LOCAL * main + k * rest - main))
                hit = row_id == jnp.where(slot < 0.0, -1.0, spot)
                chosen = jnp.where(hit, 1.0, chosen)
                gates = jnp.where(hit, meta_s[4 + k : 5 + k, :], gates)
            return chosen.astype(BF16), jnp.sum(gates, axis=1, keepdims=True)

        def pick(p, _):
            wait(pair_in(p))
            found = []
            for b in range(2):
                chosen, gates = pick_source(2 * p + b)
                found.append((dot(chosen, x[2 * p + b]), dot(chosen, g[2 * p + b]) * gates, gates))
            at_rest = pl.ds(pl.multiple_of(p * PAIR_CAP + 2 * main, 16), 2 * rest)
            for k in range(LOCAL):
                last = slice(LOCAL * main + k * rest, LOCAL * main + (k + 1) * rest)
                for b in range(2):
                    at = pl.ds(pl.multiple_of(p * PAIR_CAP + b * main, 16), main)
                    piece = slice(k * main, (k + 1) * main)
                    xin[k, at, :] = found[b][0][piece].astype(BF16)
                    dr[k, at, :] = found[b][1][piece].astype(BF16)
                    weight[k, at, :] = found[b][2][piece]
                both = [jnp.concatenate([found[0][n][last], found[1][n][last]], axis=0) for n in range(3)]
                xin[k, at_rest, :] = both[0].astype(BF16)
                dr[k, at_rest, :] = both[1].astype(BF16)
                weight[k, at_rest, :] = both[2]
            return 0

        lax.fori_loop(0, PAIRS, pick, 0)
        start(weights_in(1))

        def expert(e, _):
            wait(weights_in(e))

            @pl.when(e < LOCAL - 2)
            def _():
                start(weights_in(e + 2))

            start(rows_out(e))

            def work(h, _):
                at = pl.ds(pl.multiple_of(h * half, half), half)
                x_h, dr_h = xin[e, at, :], dr[e, at, :]
                gate = dot(x_h, wg[e])
                up = dot(x_h, wu[e])
                sig = jax.nn.sigmoid(gate)
                silu = gate * sig
                act_h = (silu * up).astype(BF16)
                act[e, at, :] = act_h
                d_act = dot(dr_h, wd[e], NT)
                d_gate = (d_act * up * sig * (1.0 + gate * (1.0 - sig))).astype(BF16)
                d_up = (d_act * silu).astype(BF16)
                dg[e, at, :] = d_gate
                du[e, at, :] = d_up
                y = (dot(act_h, wd[e]) * weight[e, at, :]).astype(BF16)
                dch = (dot(d_gate, wg[e], NT) + dot(d_up, wu[e], NT)).astype(BF16)
                at_main = pl.ds(pl.multiple_of(e * main, main), main)
                at_rest = pl.ds(pl.multiple_of(e * 2 * rest, 2 * rest), 2 * rest)
                for k in range(2):
                    for rows_k, whole, last in ((y, made, made_rest), (dch, back, back_rest)):
                        piece = rows_k[k * PAIR_CAP : (k + 1) * PAIR_CAP]
                        for b in range(2):
                            whole[4 * h + 2 * k + b, at_main, :] = piece[b * main : (b + 1) * main]
                        last[2 * h + k, at_rest, :] = piece[2 * main :]
                return 0

            lax.fori_loop(0, 2, work, 0)
            start(acts_out(e))
            return 0

        lax.fori_loop(0, LOCAL, expert, 0)
        lane_main = lax.broadcasted_iota(jnp.int32, (PAIR_ROWS, LOCAL * main), 1).astype(F32)
        lane_rest = lax.broadcasted_iota(jnp.int32, (PAIR_ROWS, LOCAL * 2 * rest), 1).astype(F32)
        second = lax.broadcasted_iota(jnp.int32, (PAIR_ROWS, 1), 0) >= ROWS

        def give(p, _):
            both = jnp.concatenate([m_ref[2 * p], m_ref[2 * p + 1]], axis=1)
            turned = jnp.concatenate([both, jnp.zeros((120, PAIR_ROWS), F32)], axis=0).T
            in_main = jnp.zeros((PAIR_ROWS, LOCAL * main), F32)
            in_rest = jnp.zeros((PAIR_ROWS, LOCAL * 2 * rest), F32)
            for k in range(LOCAL):
                slot = turned[:, k : k + 1]
                here = jnp.where((slot >= 0.0) & (slot < main), slot + k * main, -1.0)
                in_main = jnp.where(lane_main == here, 1.0, in_main)
                there = slot + (k * 2 * rest - main) + jnp.where(second, float(rest), 0.0)
                in_rest = jnp.where(lane_rest == jnp.where(slot < main, -1.0, there), 1.0, in_rest)
            in_main, in_rest = in_main.astype(BF16), in_rest.astype(BF16)
            for whole, last, to in ((back, back_rest, dx), (made, made_rest, out)):
                more = dot(in_rest, last[p])
                for b in range(2):
                    at = slice(b * ROWS, (b + 1) * ROWS)
                    to[2 * p + b] = (dot(in_main[at], whole[2 * p + b]) + more[at]).astype(BF16)
            start(pair_out(p))
            return 0

        lax.fori_loop(0, PAIRS, give, 0)
        for e in range(LOCAL):
            wait(rows_out(e))
            wait(acts_out(e))
        for p in range(PAIRS):
            wait(pair_out(p))

    vmem = pl.BlockSpec(memory_space=pltpu.VMEM)
    buf = lambda *shape: pltpu.VMEM(shape, BF16)
    wide, narrow, source = (LOCAL, SLOTS, WIDTH), (LOCAL, SLOTS, FF), (EXP, ROWS, WIDTH)
    return compute_call(
        body,
        "experts",
        [jax.ShapeDtypeStruct(shape, BF16) for shape in (wide, wide, narrow, narrow, narrow, source, source)],
        [rows, grads, meta, w_gate, w_up, w_down],
        vmem=63,
        in_specs=[ANY_SPEC, ANY_SPEC, vmem] + [ANY_SPEC] * 3,
        out_specs=[ANY_SPEC] * 7,
        scratch_shapes=[
            buf(*source),
            buf(*source),
            buf(LOCAL, WIDTH, FF),
            buf(LOCAL, WIDTH, FF),
            buf(LOCAL, FF, WIDTH),
            buf(*wide),
            buf(*wide),
            buf(*narrow),
            buf(*narrow),
            buf(*narrow),
            buf(*source),
            buf(*source),
            buf(EXP, LOCAL * main, WIDTH),
            buf(EXP, LOCAL * main, WIDTH),
            buf(PAIRS, LOCAL * 2 * rest, WIDTH),
            buf(PAIRS, LOCAL * 2 * rest, WIDTH),
            pltpu.VMEM((LOCAL, SLOTS, 1), F32),
            pltpu.SemaphoreType.DMA((5, 4)),
        ],
    )


def norm_back(values, total_squares, width, weighted, mask=None):
    scale = row_scale(total_squares, width)
    inner = jnp.sum(weighted * values, axis=1, keepdims=True) * (1.0 / width)
    return scale * weighted - values * (scale * scale * scale) * inner, scale


def deliver(resid, layer_keep, layer_got, dense, out_grad, gain_sums, input_grad, expert_sums):
    def body(
        r_ref, k_ref, g_ref, d_ref, o_ref, s_ref, i_ref, eg_ref, eu_ref, ed_ref,
        lo, wq, wk, wv, wo, ga, gq, gk, gf, di, eg, eu, ed,
    ):
        lo[...] = (r_ref[...] + k_ref[...] + g_ref[...].astype(F32)).astype(BF16)
        wq[...] = d_ref[0].astype(F32)
        for c in range(4):
            k, v = apart([d_ref[1, :, (2 * c + j) * 128 : (2 * c + j + 1) * 128].astype(F32) for j in range(2)])
            wk[:, c * 128 : (c + 1) * 128] = k
            wv[:, c * 128 : (c + 1) * 128] = v
        wo[...] = o_ref[...].astype(F32)
        ga[...] = s_ref[0:1, :]
        gq[...] = s_ref[1:2, :]
        gk[...] = s_ref[2:3, 0:64]
        gf[...] = s_ref[3:4, :]
        di[...] = i_ref[...]
        eg[...] = eg_ref[...]
        eu[...] = eu_ref[...]
        ed[...] = ed_ref[...]

    def rows(count, width):
        return pl.BlockSpec((count // LOCAL, width), lambda i: (i, 0))

    def expert(*shape):
        return pl.BlockSpec((1,) + shape, lambda i: (i, 0, 0))

    return compute_call(
        body,
        "deliver",
        [
            jax.ShapeDtypeStruct((ROWS, WIDTH), BF16),
            jax.ShapeDtypeStruct((128, WIDTH), F32),
            jax.ShapeDtypeStruct((128, 512), F32),
            jax.ShapeDtypeStruct((128, 512), F32),
            jax.ShapeDtypeStruct((128, WIDTH), F32),
            jax.ShapeDtypeStruct((1, 128), F32),
            jax.ShapeDtypeStruct((1, 128), F32),
            jax.ShapeDtypeStruct((1, 64), F32),
            jax.ShapeDtypeStruct((1, 128), F32),
            jax.ShapeDtypeStruct((ROWS, WIDTH), F32),
        ]
        + [jax.ShapeDtypeStruct(a.shape, F32) for a in expert_sums],
        [resid, layer_keep, layer_got, dense, out_grad, gain_sums, input_grad, *expert_sums],
        grid=(LOCAL,),
        in_specs=[rows(ROWS, WIDTH)] * 3
        + [
            pl.BlockSpec((2, 128 // LOCAL, WIDTH), lambda i: (0, i, 0)),
            rows(128, WIDTH),
            pl.BlockSpec((8, 128), lambda i: (0, 0)),
            rows(ROWS, WIDTH),
        ]
        + [expert(64, FF), expert(64, FF), expert(32, WIDTH)],
        out_specs=[rows(ROWS, WIDTH), rows(128, WIDTH), rows(128, 512), rows(128, 512), rows(128, WIDTH)]
        + [pl.BlockSpec((1, n), lambda i: (0, 0)) for n in (128, 128, 64, 128)]
        + [rows(ROWS, WIDTH), expert(64, FF), expert(64, FF), expert(32, WIDTH)],
    )


def cosine_of_turns(turns):
    part = turns - jnp.floor(turns + 0.5)
    square = part * part * 39.47841760435743
    total = jnp.full_like(square, -1.0 / 6402373705728000.0)
    for n in (20922789888000.0, -87178291200.0, 479001600.0, -3628800.0, 40320.0, -720.0, 24.0, -2.0, 1.0):
        total = total * square + 1.0 / n
    return total


def front(tokens, dense, norms, perm, lengths):
    half = 64

    def body(
        t_ref, wq_ref, wk_ref, wv_ref, wd_ref, na_ref, nq_ref, nk_ref, nf_ref, perm_ref, len_ref,
        wo_ref, go_ref, n_ref, ql_ref, kl_ref, s_ref, c_ref, sn_ref, p_ref, kp_ref, q_ref, kv_ref,
        g_ref, w_mine, rows, normed, gains_v, w_own, totals, totals_all, kv_half, send_sem, recv_sem, local_sem,
    ):
        _, chip, core, sibling = place()
        me = lax.axis_index("exp")
        chips, exps = ring_of(chip), ring_of(me)
        twins = [lax.rem(chip + d, CHIPS) for d in (2, 6, 4, 1, 3, 5, 7)]
        to_chip = lambda p: ("ctx", 2 * p + core)
        to_exp = lambda p: ("exp", p)
        copier = Copier(send_sem, recv_sem, local_sem)
        keys = key_lanes()
        odd = lax.rem(chip, 2) == 1
        wk, wv = wk_ref[:, lanes(chip // 2)].astype(F32), wv_ref[:, lanes(chip // 2)].astype(F32)
        wk = jnp.where(odd, pltpu.roll(wk, 64, 1), wk)
        wv = jnp.where(odd, wv, pltpu.roll(wv, 64, 1))
        w_mine[:, 0:128] = wq_ref[:, lanes(chip)]
        w_mine[:, 128:256] = jnp.where(keys, wk, wv).astype(BF16)
        g_ref[...] = jnp.ones((8, 128), F32)
        g_ref[0:1, :] = na_ref[...].astype(F32)
        g_ref[1:2, :] = nq_ref[...].astype(F32)
        g_ref[2:3, 0:64] = nk_ref[...].astype(F32)
        g_ref[3:4, :] = nf_ref[...].astype(F32)
        meet([to_chip(p) for p in twins] + [to_exp(p) for p in exps[1:]] + [("ctx", sibling)])
        gain_sends = [copier.send(g_ref, gains_v.at[me], *to_exp(p)) for p in exps[1:]]
        part = pl.ds(pl.multiple_of(core * half, half), half)
        slot = lambda s: wo_ref.at[s, part]
        handed = []

        def norm(block, s):
            x = block.astype(F32)
            scale = row_scale(jnp.sum(x * x, axis=1, keepdims=True), WIDTH)
            for e in range(EXP):
                at = slice(e * 128, (e + 1) * 128)
                normed[s, :, at] = (x[:, at] * scale * gains_v[e, 0:1, :]).astype(BF16)

        projected = []

        def project(s):
            both = dot(normed[s], w_own[...].reshape(WIDTH, 256))
            q, kv = both[:, 0:128], both[:, 128:256]
            ql_ref[s] = q
            kl_ref[s] = kv
            totals[s] = both_totals(q * q, kv * kv)

        def landed(s):
            norm(rows[s], s)
            projected.append(s)

        main = relay(copier, t_ref, lambda s: rows.at[s], ROWS, chips, to_chip, landed)
        dense = relay(
            copier,
            wd_ref.at[part],
            slot,
            half,
            exps,
            to_exp,
            lambda s: handed.append(copier.send(slot(s), slot(s), "ctx", sibling)),
        )
        next(main)
        next(main)
        next(dense)
        next(dense)
        copier.keep(wd_ref, wo_ref.at[me])
        w_own[me] = w_mine[...]
        gains_v[me] = g_ref[...]

        row = lax.broadcasted_iota(jnp.int32, (CTX, ROWS), 1)
        piece = jnp.where(row // 12 == lax.broadcasted_iota(jnp.int32, (CTX, ROWS), 0), 1.0, 0.0)
        dealt = dot(perm_ref[...].astype(F32).astype(BF16), piece.astype(BF16))
        source = lax.broadcasted_iota(jnp.int32, (CTX, ROWS), 0)
        position = (source * CTX).astype(F32) + dealt
        position = position * 12.0 + lax.rem(row, 12).astype(F32)
        begin = jnp.zeros((CTX, ROWS), F32)
        ends = jnp.zeros((1, 1), F32)
        for k in range(3):
            ends = ends + len_ref[0:1, k : k + 1].astype(F32)
            begin = jnp.where(position >= ends, ends, begin)
        for i in range(CHIPS):
            mine = [jnp.where(core == 0, v[2 * i : 2 * i + 1], v[2 * i + 1 : 2 * i + 2]) for v in (position, begin)]
            p_ref[i] = jnp.concatenate(mine, axis=0)
            kp_ref[i] = jnp.concatenate([position[2 * i : 2 * i + 1], position[2 * i + 1 : 2 * i + 2]], axis=1)

        def angles(i, _):
            keys = key_lanes()
            lane = lax.broadcasted_iota(jnp.int32, (1, 128), 1)
            freq = jnp.exp(lax.rem(lane, 32).astype(F32) * (-2.0 / 64 * 9.210340371976184))
            place_i = p_ref[i]
            offset = down_rows(place_i, 0) - down_rows(place_i, 1)
            mixed = cosine_of_turns(offset * (freq * 0.15915494309189535) - jnp.where(keys, 0.0, 0.25))
            other = pltpu.roll(mixed, 64, 1)
            c_ref[i] = jnp.where(keys, mixed, other)
            sn_ref[i] = jnp.where(keys, other, mixed)
            return 0

        lax.fori_loop(0, CHIPS, angles, 0)
        for at in gain_sends:
            copier.arrived(at)
        go_ref[...] = gains_v[...]
        norm(t_ref[...], chip)
        projected.append(chip)
        next(main)
        next(dense)
        next(main)
        own_sends = [copier.send(w_mine, w_own.at[me], *to_exp(p)) for p in exps[1:]]
        next(dense)
        next(main)
        next(main)
        next(dense)
        for at in own_sends:
            copier.arrived(at)
        for s in projected:
            project(s)
        projected.clear()
        next(main)
        next(dense)
        for s in projected:
            project(s)
        projected.clear()
        side_by_side(main)
        for s in projected:
            project(s)
        shares = [copier.send(totals, totals_all.at[chip], *to_chip(p)) for p in twins]
        totals_all[chip] = totals[...]
        side_by_side(dense)
        copier.keep(normed, n_ref)
        for at in shares:
            copier.arrived(at)

        def turn_one(i, _):
            squares = totals_all[0, i]
            for c in range(1, CHIPS):
                squares = squares + totals_all[c, i]
            s_ref[i] = squares
            cos, sin = c_ref[i], sn_ref[i]
            gain = gains_v[chip]
            q = ql_ref[i] * row_scale(down_rows(squares, 0), WIDTH) * gain[1:2, :]
            q = turn(q, cos, sin).astype(BF16).astype(F32)
            q_ref[i] = (q * 0.125).astype(BF16)
            scale = jnp.where(keys, row_scale(down_rows(squares, 1), WIDTH // 2), 1.0)
            kv = kl_ref[i] * scale * gain[2:3, :]
            kv_half[i] = turn(kv, jnp.where(keys, cos, 1.0), jnp.where(keys, sin, 0.0)).astype(BF16)
            return 0

        lax.fori_loop(0, CHIPS, turn_one, 0)
        copier.send(kv_half, kv_ref.at[:, core], "ctx", sibling)
        copier.keep(kv_half, kv_ref.at[:, core])
        copier.finish()

    vmem = pl.BlockSpec(memory_space=pltpu.VMEM)
    wide = jax.ShapeDtypeStruct((CHIPS, ROWS, 128), F32)
    return pl.pallas_call(
        body,
        name="front",
        out_shape=[
            jax.ShapeDtypeStruct((EXP, 128, WIDTH), BF16),
            jax.ShapeDtypeStruct((EXP, 8, 128), F32),
            jax.ShapeDtypeStruct((CHIPS, ROWS, WIDTH), BF16),
            wide,
            wide,
            jax.ShapeDtypeStruct((CHIPS, 2, ROWS), F32),
            wide,
            wide,
            jax.ShapeDtypeStruct((CHIPS, 2, ROWS), F32),
            jax.ShapeDtypeStruct((CHIPS, 1, CHUNK), F32),
            jax.ShapeDtypeStruct((CHIPS, ROWS, 128), BF16),
            jax.ShapeDtypeStruct((CHIPS, 2, ROWS, 128), BF16),
        ],
        in_specs=[vmem] * 11,
        out_specs=[ANY_SPEC, vmem, ANY_SPEC] + [vmem] * 8 + [ANY_SPEC],
        scratch_shapes=[
            pltpu.VMEM((8, 128), F32),
            pltpu.VMEM((128, 256), BF16),
            pltpu.VMEM((CHIPS, ROWS, WIDTH), BF16),
            pltpu.VMEM((CHIPS, ROWS, WIDTH), BF16),
            pltpu.VMEM((EXP, 8, 128), F32),
            pltpu.VMEM((EXP, 128, 256), BF16),
            pltpu.VMEM((CHIPS, 2, ROWS), F32),
            pltpu.VMEM((CHIPS, CHIPS, 2, ROWS), F32),
            pltpu.VMEM((CHIPS, ROWS, 128), BF16),
            pltpu.SemaphoreType.DMA((57,)),
            pltpu.SemaphoreType.DMA((57,)),
            pltpu.SemaphoreType.DMA((8,)),
        ],
        compiler_params=pltpu.CompilerParams(
            collective_id=1, has_side_effects=True, vmem_limit_bytes=60 * MIB
        ),
    )(tokens, *dense, *norms, perm, lengths)


def apart(pieces):
    first, second = pieces
    keys = key_lanes()
    return (
        jnp.where(keys, first, pltpu.roll(second, 64, 1)),
        jnp.where(keys, pltpu.roll(first, 64, 1), second),
    )


def tail(
    q, kv, d_out, out_turned, log_total, key_pos, places, q_lin, kv_lin, cosine, sine, squares, gains, normed, attended, d_branch, layer_part,
    w_query, w_key, w_value, tokens, d_resid, ffn_gain, gate_part, up_part, down_a, down_b,
):
    def body(
        q_ref, kv_ref, do_ref, ot_ref, l_ref, kp_ref, p_ref, ql_ref, kl_ref, c_ref, sn_ref, s_ref, g_ref, n_ref, at_ref, br_ref, lp_ref,
        wq_ref, wk_ref, wv_ref, t_ref, r_ref, fg_ref, gp_ref, up_ref, da_ref, db_ref,
        eg_ref, eu_ref, ed_ref, di_ref, dense_ref, og_ref, lo_ref, gs_ref,
        keys_v, values, acc, key_at, keys_t, other_v, w_mine, ql_v, kl_v, c_v, sn_v, n_v, w_v, t_v, r_v,
        got, e_q, e_kv, totals, totals_all, d_lin, home, w_give, w_keep, w_got, joint, traded, done,
        o_both, o_keep, o_got, o_traded, o_pair, o_half, o_full, a_got, a_done, packet, packets, mine, shared, gate_c, down_c, up_d, down_d, out_sem, in_sem, send_sem, recv_sem, local_sem,
    ):
        ctx, chip, core, sibling = place()
        me = lax.axis_index("exp")
        twins = [lax.rem(chip + d, CHIPS) for d in (2, 6, 4, 1, 3, 5, 7)]
        exps = [lax.rem(me + d, EXP) for d in range(1, EXP)]
        others = [lax.rem(ctx + d, CTX) for d in range(1, CTX)]
        to_chip = lambda p: ("ctx", 2 * p + core)
        copier = Copier(send_sem, recv_sem, local_sem)
        heads = [
            copier.keep(src, dst)
            for src, dst in ((c_ref, c_v), (sn_ref, sn_v), (ql_ref, ql_v), (kl_ref, kl_v))
        ]
        late = [
            copier.keep(src, dst)
            for src, dst in ((n_ref, n_v),  (t_ref, t_v), (r_ref, r_v))
        ]
        w_mine[:, 0:1024] = wq_ref[...]
        w_mine[:, 1024:1536] = wk_ref[...]
        w_mine[:, 1536:2048] = wv_ref[...]
        w_v[me] = w_mine[...]
        w_part = pl.ds(pl.multiple_of(core * 64, 64), 64)
        w_slot = lambda s: w_v.at[s, w_part]
        handed = []
        weights = relay(
            copier,
            w_mine.at[w_part],
            w_slot,
            64,
            ring_of(me),
            lambda p: ("exp", p),
            lambda s: handed.append(copier.send(w_slot(s), w_slot(s), "ctx", sibling)),
        )
        meet([("ctx", p) for p in others] + [("exp", p) for p in exps])
        next(weights)
        next(weights)
        copier.send(lp_ref, lo_ref, "exp", lax.rem(me + 4, EXP))
        zh, y = chip // 4, lax.rem(chip, 4)
        second = []
        for d in (1, 3, 2):
            c = lax.rem(y + d, 4)
            second.append(copier.send(gp_ref.at[c], gate_c.at[y], *to_chip(zh * 4 + c)))
            second.append(copier.send(da_ref.at[c], down_c.at[y], *to_chip(zh * 4 + c)))
        second.append(copier.send(up_ref.at[1 - zh], up_d, *to_chip((1 - zh) * 4 + y)))
        second.append(copier.send(db_ref.at[1 - zh], down_d, *to_chip((1 - zh) * 4 + y)))

        def out_grad(r, _):
            grad = dot(at_ref[:, pl.ds(pl.multiple_of(r * 256, 256), 256)], br_ref[...], TN).astype(BF16)
            for k in range(2):
                for c in range(2):
                    o_both[c, 2 * r + k] = grad[(2 * k + c) * 64 : (2 * k + c + 1) * 64]
            return 0

        lax.fori_loop(0, 4, out_grad, 0)
        o_swap = copier.send(o_both.at[1 - core], o_got, "ctx", sibling)
        low = key_lanes()

        def place_keys(p, _):
            rows = pl.ds(pl.multiple_of(p * CHUNK, CHUNK), CHUNK)
            both = kv_ref[rows, :].astype(F32)
            own_keys = jnp.where(low, both, 0.0)
            keys_v[rows, :] = own_keys.astype(BF16)
            keys_t[:, rows] = own_keys.T.astype(BF16)
            values[rows, :] = jnp.where(low, pltpu.roll(both, 64, 1), 0.0).astype(BF16)
            key_at[rows, :] = key_columns(kp_ref[p])
            acc[rows, :] = jnp.zeros((CHUNK, 128), F32)
            return 0

        lax.fori_loop(0, CHIPS, place_keys, 0)

        def swap(i):
            return pltpu.make_async_remote_copy(
                src_ref=other_v.at[i],
                dst_ref=got.at[i],
                send_sem=out_sem.at[i],
                recv_sem=in_sem.at[i],
                device_id={"ctx": sibling},
                device_id_type=MESH,
            )

        def attend_block(k, _):
            i = CHIPS - 1 - k
            q_wide, do_wide = q_ref[i].astype(F32), do_ref[i].astype(F32)
            q_turned, do_turned = pltpu.roll(q_wide, 64, 1), pltpu.roll(do_wide, 64, 1)
            q_rows = jnp.concatenate([q_wide, q_turned], axis=0)
            do_rows = jnp.concatenate([do_wide, do_turned], axis=0)
            do_high = jnp.concatenate([do_turned, do_wide], axis=0)
            right = [jnp.where(low, q_rows, 0.0), jnp.where(low, 0.0, do_high)]
            right = jnp.concatenate(right, axis=0).astype(BF16)
            q_rows = q_rows.astype(BF16)
            delta = jnp.sum(do_rows.T[0:64, :] * ot_ref[i], axis=0, keepdims=True)
            do_rows = do_rows.astype(BF16)
            total = l_ref[i]
            at_row, start_row = pair_rows(p_ref[i])

            def step(diagonal, p, dq):
                rows = pl.ds(pl.multiple_of(p * CHUNK, CHUNK), CHUNK)
                scores = dot(keys_v[rows, :], q_rows, NT)
                at_key = jnp.concatenate([key_at[rows, :]] * (CHUNK // 128), axis=1)
                seen = at_key >= start_row
                if diagonal:
                    seen = seen & (at_key <= at_row)
                probs = jnp.exp(jnp.where(seen, scores, MASKED) - total)
                d_scores = (probs * (dot(values[rows, :], do_rows, NT) - delta)).astype(BF16)
                acc[rows, :] += dot(jnp.concatenate([d_scores, probs.astype(BF16)], axis=1), right)
                return dq + dot(keys_t[:, rows], d_scores)

            dq = jnp.zeros((128, 2 * ROWS), F32)
            dq = lax.fori_loop(first_chunk(i, core), i, lambda p, dq: step(False, p, dq), dq)
            dq = step(True, i, dq).T * 0.125
            dq = jnp.where(low, dq[:ROWS], pltpu.roll(dq[ROWS:], 64, 1))
            e_q[i] = turn(dq, c_v[i], -sn_v[i])
            other = pl.ds(pl.multiple_of((2 * i + 1 - core) * ROWS, ROWS), ROWS)
            other_v[i] = acc[other, :].astype(BF16)
            swap(i).start()
            return 0

        for at in heads:
            copier.kept(at)

        lax.fori_loop(0, 1, attend_block, 0)
        next(weights)
        next(weights)
        copier.arrived(o_swap)

        def add_cores(e, _):
            o_keep[e] = (o_both[core, e].astype(F32) + o_got[e].astype(F32)).astype(BF16)
            return 0

        lax.fori_loop(0, EXP, add_cores, 0)
        zl, x = me // 4, lax.rem(me, 4)
        o_trades = []
        for d in (2, 1, 3):
            p = lax.rem(x + d, 4)
            for z in range(2):
                o_trades.append(copier.send(o_keep.at[z * 4 + p], o_traded.at[x, z], "exp", zl * 4 + p))
        lax.fori_loop(1, 2, attend_block, 0)
        next(weights)
        next(weights)
        lax.fori_loop(2, 3, attend_block, 0)
        next(weights)
        for at in o_trades:
            copier.arrived(at)
        keep, give = o_keep[zl * 4 + x].astype(F32), o_keep[(1 - zl) * 4 + x].astype(F32)
        for d in (1, 2, 3):
            p = lax.rem(x + d, 4)
            keep = keep + o_traded[p, zl].astype(F32)
            give = give + o_traded[p, 1 - zl].astype(F32)
        o_half[...] = give.astype(BF16)
        o_full[...] = keep.astype(BF16)
        o_pairs = copier.send(o_half, o_pair, "exp", (1 - zl) * 4 + x)
        lax.fori_loop(3, CHIPS, attend_block, 0)

        side_by_side(weights)

        copier.arrived(o_pairs)
        o_full[...] = (o_full[...].astype(F32) + o_pair[...].astype(F32)).astype(BF16)
        spread = [copier.send(o_full.at[:, lanes(p)], a_got.at[chip], *to_chip(p)) for p in twins]
        a_got[chip] = o_full[:, lanes(chip)]
        keys = key_lanes()
        gain = g_ref[chip]

        def unturn_kv(k, carry):
            q_sum, kv_sum = carry
            i = CHIPS - 1 - k
            swap(i).wait_recv()
            cos, sin = jnp.where(keys, c_v[i], 1.0), jnp.where(keys, -sn_v[i], 0.0)
            mine_rows = pl.ds(pl.multiple_of((2 * i + core) * ROWS, ROWS), ROWS)
            e = turn(acc[mine_rows, :] + got[i].astype(F32), cos, sin)
            e_kv[i] = e
            q_part, kv_part = e_q[i] * ql_v[i], e * kl_v[i]
            totals[i] = both_totals(q_part * gain[1:2, :], kv_part * gain[2:3, :])
            q_scale = row_scale(down_rows(s_ref[i], 0), WIDTH)
            k_scale = row_scale(down_rows(s_ref[i], 1), WIDTH // 2)
            q_sum = q_sum + jnp.sum(q_part * q_scale, axis=0, keepdims=True)
            kv_sum = kv_sum + jnp.sum(kv_part * jnp.where(keys, k_scale, 1.0), axis=0, keepdims=True)
            return q_sum, kv_sum

        none = jnp.zeros((1, 128), F32)
        q_sum, kv_sum = lax.fori_loop(0, CHIPS, unturn_kv, (none, none))
        shares = [copier.send(totals, totals_all.at[chip], *to_chip(p)) for p in twins]
        totals_all[chip] = totals[...]
        for at in spread:
            copier.arrived(at)
        total = a_got[0].astype(F32)
        for c in range(1, CHIPS):
            total = total + a_got[c].astype(F32)
        a_done[...] = total.astype(BF16)
        half = pl.ds(pl.multiple_of(core * 64, 64), 64)
        a_shares = [copier.send(a_done, og_ref.at[half, lanes(chip)], *to_chip(p)) for p in twins]
        copier.send(a_done, og_ref.at[half, lanes(chip)], "ctx", sibling)
        copier.keep(a_done, og_ref.at[half, lanes(chip)])
        for at in shares:
            copier.arrived(at)

        def gradient(i):
            inner = totals_all[0, i]
            for c in range(1, CHIPS):
                inner = inner + totals_all[c, i]
            squares_i = s_ref[i]
            q_scale = row_scale(down_rows(squares_i, 0), WIDTH)
            k_scale = row_scale(down_rows(squares_i, 1), WIDTH // 2)
            q_cut = q_scale * q_scale * q_scale * down_rows(inner, 0) * (1.0 / WIDTH)
            k_cut = k_scale * k_scale * k_scale * down_rows(inner, 1) * (2.0 / WIDTH)
            d_lin[0, i] = (q_scale * (e_q[i] * gain[1:2, :]) - ql_v[i] * q_cut).astype(BF16)
            kv_scale = jnp.where(keys, k_scale, 1.0)
            k_cut = jnp.where(keys, k_cut, 0.0)
            d_lin[1, i] = (kv_scale * (e_kv[i] * gain[2:3, :]) - kl_v[i] * k_cut).astype(BF16)

        homeward = []
        for p in twins:
            gradient(p)
            for k in range(2):
                homeward.append(copier.send(d_lin.at[k, p], home.at[k, :, lanes(chip)], *to_chip(p)))
        gradient(chip)
        for k in range(2):
            home[k, :, lanes(chip)] = d_lin[k, chip]
        for at in late:
            copier.kept(at)

        def columns_grad(half, out):
            d = d_lin[half].reshape(CHIPS * ROWS, 128)

            def part(r, _):
                n = n_v[:, :, pl.ds(pl.multiple_of(r * 256, 256), 256)].reshape(CHIPS * ROWS, 256)
                out[pl.ds(pl.multiple_of(r * 256, 256), 256), :] = dot(n, d, TN).astype(BF16)
                return 0

            lax.fori_loop(0, 4, part, 0)

        columns_grad(1 - core, w_give)
        w_swap = copier.send(w_give, w_got, "ctx", sibling)
        columns_grad(core, w_keep)
        copier.arrived(w_swap)
        both = w_keep[...].astype(F32) + w_got[...].astype(F32)
        joint[...] = both.astype(BF16).reshape(EXP, 128, 128)
        trades = [copier.send(joint.at[p], traded.at[me], "exp", p) for p in exps]
        traded[me] = joint[me]

        for at in homeward + handed:
            copier.arrived(at)
        k_parts, v_parts = [], []
        for c in range(4):
            k, v = apart([home[1, :, (2 * c + j) * 128 : (2 * c + j + 1) * 128].astype(F32) for j in range(2)])
            k_parts.append(k.astype(BF16))
            v_parts.append(v.astype(BF16))
        left = jnp.concatenate([home[0]] + k_parts + v_parts, axis=1)
        x = t_v[...].astype(F32)
        scale = row_scale(jnp.sum(x * x, axis=1, keepdims=True), WIDTH)
        inner = jnp.zeros((ROWS, 1), F32)
        pieces = []
        for e in range(EXP):
            at = slice(e * 128, (e + 1) * 128)
            d_normed = dot(left, w_v[e], NT).astype(BF16).astype(F32)
            packet[e] = jnp.zeros((8, 128), F32)
            packet[e, 0:1, :] = jnp.sum(d_normed * x[:, at] * scale, axis=0, keepdims=True)
            packet[e, 3:4, :] = fg_ref[:, at]
            weighted = d_normed * g_ref[e, 0:1, :]
            inner = inner + jnp.sum(weighted * x[:, at], axis=1, keepdims=True)
            pieces.append(weighted)
        packet[chip, 1:2, :] = q_sum
        packet[chip, 2:3, :] = kv_sum
        gain_trades = [copier.send(packet.at[p], packets.at[me], "exp", p) for p in exps]
        packets[me] = packet[me]

        for at in trades:
            copier.arrived(at)
        total = traded[0].astype(F32)
        for e in range(1, EXP):
            total = total + traded[e].astype(F32)
        done[...] = total.astype(BF16)
        spot = dense_ref.at[core, :, lanes(chip)]
        w_shares = [copier.send(done, spot, *to_chip(p)) for p in twins]
        copier.send(done, spot, "ctx", sibling)
        copier.keep(done, spot)

        for at in gain_trades:
            copier.arrived(at)
        total = packets[0]
        for e in range(1, EXP):
            total = total + packets[e]
        mine[...] = total
        gain_shares = [copier.send(mine, shared.at[ctx], "ctx", p) for p in others]
        shared[ctx] = total

        inner = inner * (1.0 / WIDTH)
        cut = scale * scale * scale * inner
        for e in range(EXP):
            at = slice(e * 128, (e + 1) * 128)
            di_ref[:, at] = r_v[:, at] + scale * pieces[e] - x[:, at] * cut
        for at in second:
            copier.arrived(at)
        columns = [lax.rem(y + d, 4) for d in (1, 2, 3)]

        def add_experts(e, _):
            total = gp_ref[y, e].astype(F32)
            for c in columns:
                total = total + gate_c[c, e].astype(F32)
            eg_ref[e] = total
            eu_ref[e] = up_ref[zh, e].astype(F32) + up_d[e].astype(F32)
            return 0

        lax.fori_loop(0, LOCAL, add_experts, 0)
        for e in range(2):
            total = da_ref[y, e].astype(F32)
            for c in columns:
                total = total + down_c[c, e].astype(F32)
            ed_ref[e] = total
            ed_ref[e + 2] = db_ref[zh, e].astype(F32) + down_d[e].astype(F32)
        for d, at in zip((2, 6, 4, 1, 3, 5, 7), w_shares):
            copier.arrived(at)
            got_at = dense_ref.at[core, :, lanes(lax.rem(chip + CHIPS - d, CHIPS))]
            copier.send(got_at, got_at, "ctx", sibling)
        for d, at in zip((2, 6, 4, 1, 3, 5, 7), a_shares):
            copier.arrived(at)
            got_at = og_ref.at[half, lanes(lax.rem(chip + CHIPS - d, CHIPS))]
            copier.send(got_at, got_at, "ctx", sibling)
        for at in gain_shares:
            copier.arrived(at)
        total = shared[0]
        for c in range(1, CTX):
            total = total + shared[c]
        gs_ref[...] = total
        for i in range(CHIPS):
            swap(i).wait_send()
        copier.finish()

    vmem = pl.BlockSpec(memory_space=pltpu.VMEM)
    block = (CHIPS, ROWS, 128)
    tile = pltpu.VMEM((128, 128), BF16)
    return pl.pallas_call(
        body,
        name="tail",
        out_shape=[
            jax.ShapeDtypeStruct((LOCAL, 64, FF), F32),
            jax.ShapeDtypeStruct((LOCAL, 64, FF), F32),
            jax.ShapeDtypeStruct((LOCAL, 32, WIDTH), F32),
            jax.ShapeDtypeStruct((ROWS, WIDTH), F32),
            jax.ShapeDtypeStruct((2, 128, WIDTH), BF16),
            jax.ShapeDtypeStruct((128, WIDTH), BF16),
            jax.ShapeDtypeStruct((ROWS, WIDTH), BF16),
            jax.ShapeDtypeStruct((8, 128), F32),
        ],
        in_specs=[vmem] * 7 + [ANY_SPEC] * 4 + [vmem] * 2 + [ANY_SPEC] + [vmem] * 2 + [ANY_SPEC] + [vmem] * 3 + [ANY_SPEC] * 2 + [vmem] * 5,
        out_specs=[vmem] * 4 + [ANY_SPEC] * 3 + [vmem],
        scratch_shapes=[
            pltpu.VMEM((KEYS, 128), BF16),
            pltpu.VMEM((KEYS, 128), BF16),
            pltpu.VMEM((KEYS, 128), F32),
            pltpu.VMEM((KEYS, 128), F32),
            pltpu.VMEM((128, KEYS), BF16),
            pltpu.VMEM(block, BF16),
            pltpu.VMEM((128, 2 * WIDTH), BF16),
            pltpu.VMEM(block, F32),
            pltpu.VMEM(block, F32),
            pltpu.VMEM(block, F32),
            pltpu.VMEM(block, F32),
            pltpu.VMEM((CHIPS, ROWS, WIDTH), BF16),
            pltpu.VMEM((EXP, 128, 2 * WIDTH), BF16),
            pltpu.VMEM((ROWS, WIDTH), BF16),
            pltpu.VMEM((ROWS, WIDTH), F32),
            pltpu.VMEM(block, BF16),
            pltpu.VMEM(block, F32),
            pltpu.VMEM(block, F32),
            pltpu.VMEM((CHIPS, 2, ROWS), F32),
            pltpu.VMEM((CHIPS, CHIPS, 2, ROWS), F32),
            pltpu.VMEM((2,) + block, BF16),
            pltpu.VMEM((2, ROWS, WIDTH), BF16),
            pltpu.VMEM((WIDTH, 128), BF16),
            pltpu.VMEM((WIDTH, 128), BF16),
            pltpu.VMEM((WIDTH, 128), BF16),
            pltpu.VMEM((EXP, 128, 128), BF16),
            pltpu.VMEM((EXP, 128, 128), BF16),
            tile,
            pltpu.VMEM((2, EXP, 64, WIDTH), BF16),
            pltpu.VMEM((EXP, 64, WIDTH), BF16),
            pltpu.VMEM((EXP, 64, WIDTH), BF16),
            pltpu.VMEM((4, 2, 64, WIDTH), BF16),
            pltpu.VMEM((64, WIDTH), BF16),
            pltpu.VMEM((64, WIDTH), BF16),
            pltpu.VMEM((64, WIDTH), BF16),
            pltpu.VMEM((CHIPS, 64, 128), BF16),
            pltpu.VMEM((64, 128), BF16),
            pltpu.VMEM((EXP, 8, 128), F32),
            pltpu.VMEM((EXP, 8, 128), F32),
            pltpu.VMEM((8, 128), F32),
            pltpu.VMEM((CTX, 8, 128), F32),
            pltpu.VMEM((4, LOCAL, 64, FF), BF16),
            pltpu.VMEM((4, 2, 32, WIDTH), BF16),
            pltpu.VMEM((LOCAL, 64, FF), BF16),
            pltpu.VMEM((2, 32, WIDTH), BF16),
            pltpu.SemaphoreType.DMA((CHIPS,)),
            pltpu.SemaphoreType.DMA((CHIPS,)),
            pltpu.SemaphoreType.DMA((126,)),
            pltpu.SemaphoreType.DMA((126,)),
            pltpu.SemaphoreType.DMA((15,)),
        ],
        compiler_params=pltpu.CompilerParams(
            collective_id=6, has_side_effects=True, vmem_limit_bytes=60 * MIB
        ),
    )(
        q, kv, d_out, out_turned, log_total, key_pos, places, q_lin, kv_lin, cosine, sine, squares, gains, normed, attended, d_branch, layer_part,
        w_query, w_key, w_value, tokens, d_resid, ffn_gain, gate_part, up_part, down_a, down_b,
    )


def sum_blocks(blocks):
    return jnp.sum(blocks.astype(F32), axis=0)


def per_device(
    tokens,
    cotangent,
    lengths,
    deal_perm,
    routes,
    gate_logits,
    norm_attn,
    norm_query,
    norm_key,
    norm_ffn,
    w_query,
    w_key,
    w_value,
    w_out,
    w_gate,
    w_up,
    w_down,
):
    tokens, cotangent = tokens[0], cotangent[0]

    row = lambda v: v.reshape(1, -1)
    (
        w_o, gain_all, normed, q_lin, kv_lin, squares, cosine, sine, places, key_pos, q_all, kv_all,
    ) = front(
        tokens,
        (w_query, w_key, w_value, w_out),
        (row(norm_attn), row(norm_query), row(norm_key), row(norm_ffn)),
        deal_perm[0],
        lengths,
    )

    w_o = w_o.reshape(WIDTH, WIDTH)
    kv_all = kv_all.reshape(KEYS, 128)
    attended, out_turned, log_total, resid, rows_all, meta_all, grads_all = attend(
        q_all, kv_all, key_pos, places, cotangent, w_o, tokens, gain_all, routes[0].T, gate_logits[0].T
    )
    rows_in, d_rows, act, d_gate, d_up, out_parts, d_parts = experts(
        rows_all, grads_all, meta_all, w_gate, w_up, w_down
    )
    (
        gate_part, up_part, down_a, down_b, d_resid, d_branch, ffn_gain_grad, d_out, layer_keep, layer_give,
    ) = settle_experts(
        rows_in,
        d_rows,
        act,
        d_gate,
        d_up,
        d_parts.reshape(2, 4, ROWS, WIDTH),
        out_parts.reshape(2, 4, ROWS, WIDTH),
        resid,
        cotangent,
        gain_all,
        w_o,
    )
    gate_grad, up_grad, down_grad, input_grad, dense, out_grad, layer_got, gain_sums = tail(
        q_all,
        kv_all,
        d_out,
        out_turned,
        log_total,
        key_pos,
        places,
        q_lin,
        kv_lin,
        cosine,
        sine,
        squares,
        gain_all,
        normed,
        attended,
        d_branch,
        layer_give,
        w_query,
        w_key,
        w_value,
        tokens,
        d_resid,
        ffn_gain_grad,
        gate_part,
        up_part,
        down_a,
        down_b,
    )
    outs = deliver(
        resid,
        layer_keep,
        layer_got,
        dense,
        out_grad,
        gain_sums,
        input_grad,
        (gate_grad, up_grad, down_grad),
    )
    return (
        outs[0][None],
        outs[9][None],
        *outs[1:5],
        *[g.reshape(-1) for g in outs[5:9]],
        *outs[10:],
    )


def solution(mesh):
    in_specs = (
        P("exp", "ctx", None),
        P("exp", "ctx", None),
        P("exp", None),
        P("exp", None, None),
        P("exp", "ctx", None),
        P("exp", "ctx", None),
        P("exp"),
        P("exp"),
        P("exp"),
        P("exp"),
        P("exp", None),
        P("exp", None),
        P("exp", None),
        P("exp", None),
        P("exp", None, None),
        P("exp", None, None),
        P("exp", None, None),
    )
    out_specs = (
        P("exp", "ctx", None),
        P("exp", "ctx", None),
        P("exp", None),
        P("exp", None),
        P("exp", None),
        P("exp", None),
        P("exp"),
        P("exp"),
        P("exp"),
        P("exp"),
        P("exp", "ctx", None),
        P("exp", "ctx", None),
        P("exp", "ctx", None),
    )
    return jax.shard_map(
        per_device, mesh=mesh, in_specs=in_specs, out_specs=out_specs, check_vma=False
    )
```

```python
import jax
import jax.numpy as jnp
from jax import lax
from jax.experimental import pallas as pl
from jax.experimental.pallas import tpu as pltpu
from jax.sharding import PartitionSpec as P

HEADS = 16
KV_HEADS = 8
EPSILON = 1e-05
ROPE_BASE = 10000.0
MASKED = -1e30

MESH = pl.DeviceIdType.MESH
CTX = 16
EXP = 8
CHIPS = 8
ROWS = 192
WIDTH = 1024
FF = 512
LOCAL = 4
CAP = 72
PAIRS = EXP // 2
LONGEST = 2048
DOWN_A = 1
DOWN_B = LOCAL - DOWN_A
PAIR_ROWS = 2 * ROWS
PAIR_CAP = 2 * CAP
SLOTS = EXP * CAP
PAIR_SLOTS = LOCAL * PAIR_CAP
KEYS = CTX * ROWS
CHUNK = 2 * ROWS
MIB = 1 << 20
FAR_FIRST = (6, 2, 5, 7, 4, 1, 3)

ANY_SPEC = pl.BlockSpec(memory_space=pl.ANY)
F32 = jnp.float32
BF16 = jnp.bfloat16


def dot(a, b, dims=((1,), (0,))):
    return lax.dot_general(a, b, (dims, ((), ())), preferred_element_type=F32)


NT = ((1,), (1,))
TN = ((0,), (0,))


def comm_call(body, name, collective_id, outs, ins, copies, in_specs=None):
    return pl.pallas_call(
        body,
        name=name,
        out_shape=outs,
        in_specs=in_specs or [ANY_SPEC] * len(ins),
        out_specs=[ANY_SPEC] * len(outs),
        scratch_shapes=[
            pltpu.SemaphoreType.DMA((copies,)),
            pltpu.SemaphoreType.DMA((copies,)),
            pltpu.SemaphoreType.DMA((8,)),
        ],
        compiler_params=pltpu.CompilerParams(
            collective_id=collective_id, has_side_effects=True, vmem_limit_bytes=60 * MIB
        ),
    )(*ins)


class Copier:
    def __init__(self, send_sem, recv_sem, local_sem):
        self.send_sem, self.recv_sem, self.local_sem = send_sem, recv_sem, local_sem
        self.remote, self.local = [], []

    def send(self, src, dst, axis, index):
        at = len(self.remote)
        copy = pltpu.make_async_remote_copy(
            src_ref=src,
            dst_ref=dst,
            send_sem=self.send_sem.at[at],
            recv_sem=self.recv_sem.at[at],
            device_id={axis: index},
            device_id_type=MESH,
        )
        copy.start()
        self.remote.append([copy, False])
        return at

    def keep(self, src, dst):
        copy = pltpu.make_async_copy(src, dst, self.local_sem.at[len(self.local)])
        copy.start()
        self.local.append([copy, False])
        return len(self.local) - 1

    def arrived(self, at):
        self.remote[at][0].wait_recv()
        self.remote[at][1] = True

    def kept(self, at):
        self.local[at][0].wait()
        self.local[at][1] = True

    def finish(self):
        for copy, seen in self.remote:
            if not seen:
                copy.wait_recv()
        for copy, _ in self.remote:
            copy.wait_send()
        for copy, seen in self.local:
            if not seen:
                copy.wait()


def meet(partners):
    barrier = pltpu.get_barrier_semaphore()
    for axis, index in partners:
        pl.semaphore_signal(barrier, inc=1, device_id={axis: index}, device_id_type=MESH)
    pl.semaphore_wait(barrier, len(partners))


def place():
    ctx = lax.axis_index("ctx")
    core = lax.rem(ctx, 2)
    return ctx, ctx // 2, core, ctx + 1 - 2 * core


def ring_of(me):
    half, spot = me // 4, lax.rem(me, 4)
    over = (1 - half) * 4
    turns = [lax.rem(spot + d, 4) for d in (0, 1, 3, 2)]
    return tuple([half * 4 + t for t in turns] + [over + t for t in turns])


def relay(copier, own, slot, rows, ring, reach, landed=lambda partner: None):
    me, right, left, far, over, over_right, over_left, over_far = ring
    half = rows // 2
    low, high = pl.ds(0, half), pl.ds(half, half)

    def send(block, to, part, partner):
        return copier.send(block.at[part], slot(to).at[part], *reach(partner))

    def on(of, part, partner):
        return send(slot(of), of, part, partner)

    over_low = send(own, me, low, over)
    over_high = send(own, me, high, over)
    yield
    right_low = send(own, me, low, right)
    left_high = send(own, me, high, left)
    right_high = send(own, me, high, right)
    left_low = send(own, me, low, left)
    yield
    copier.arrived(right_low)
    far_right = on(left, low, right)
    copier.arrived(left_high)
    far_left = on(right, high, left)
    yield
    copier.arrived(over_low)
    next_right_low = on(over, low, right)
    next_left_low = on(over, low, left)
    copier.arrived(over_high)
    next_left_high = on(over, high, left)
    next_right_high = on(over, high, right)
    landed(over)
    yield
    copier.arrived(right_high)
    landed(left)
    copier.arrived(left_low)
    landed(right)
    yield
    copier.arrived(far_right)
    copier.arrived(far_left)
    landed(far)
    yield
    copier.arrived(next_right_low)
    far_right = on(over_left, low, right)
    copier.arrived(next_left_high)
    far_left = on(over_right, high, left)
    copier.arrived(next_right_high)
    landed(over_left)
    copier.arrived(next_left_low)
    landed(over_right)
    yield
    copier.arrived(far_right)
    copier.arrived(far_left)
    landed(over_far)


def side_by_side(*relays):
    for _ in zip(*relays):
        pass
    for one in relays:
        for _ in one:
            pass


def lanes(index):
    return pl.ds(pl.multiple_of(index * 128, 128), 128)


def attend(q, kv, key_pos, places, cotangent, w_out, tokens, gains, routes_t, logits_t):
    def body(
        q_ref, kv_ref, kp_ref, p_ref, cot_ref, w_ref, t_ref, g_ref, r_ref, l_ref,
        a_ref, ot_ref, lt_ref, res_ref, o_ref, mo_ref, co_ref,
        keys, values, key_at, done, w_v, ffn, m_v, out_sem, in_sem, send_sem, recv_sem, local_sem,
    ):
        _, chip, core, _ = place()
        ring = ring_of(lax.axis_index("exp"))
        me = ring[0]
        twins = [lax.rem(chip + d, CHIPS) for d in FAR_FIRST]
        to_chip = lambda p: ("ctx", 2 * p + core)
        to_exp = lambda p: ("exp", p)
        copier = Copier(send_sem, recv_sem, local_sem)
        load = copier.keep(w_ref, w_v)
        meet([to_chip(p) for p in twins] + [to_exp(p) for p in ring[1:]])
        extra = relay(copier, cot_ref, lambda s: co_ref.at[s], ROWS, ring, to_exp)
        next(extra)
        next(extra)
        copier.keep(cot_ref, co_ref.at[me])

        logits = l_ref[...]
        raised = jnp.exp(logits - jnp.max(logits, axis=0, keepdims=True))
        gates = raised / jnp.sum(raised, axis=0, keepdims=True)
        experts = lax.broadcasted_iota(jnp.int32, (32, ROWS), 0)
        member = jnp.zeros((32, ROWS), F32)
        weight = jnp.zeros((32, ROWS), F32)
        for c in range(8):
            hit = r_ref[c : c + 1, :] == experts
            member = member + jnp.where(hit, 1.0, 0.0)
            weight = weight + jnp.where(hit, gates[c : c + 1, :], 0.0)
        before = lax.broadcasted_iota(jnp.int32, (ROWS, ROWS), 0) < lax.broadcasted_iota(
            jnp.int32, (ROWS, ROWS), 1
        )
        rank = dot(member.astype(BF16), jnp.where(before, 1.0, 0.0).astype(BF16))
        spot = jnp.where(member > 0.5, rank, -1.0)
        for e in range(EXP):
            m_v[e, 0:4, :] = spot[e * 4 : e * 4 + 4, :]
            m_v[e, 4:8, :] = weight[e * 4 : e * 4 + 4, :]
        for p in ring[1:]:
            copier.send(m_v.at[p], mo_ref.at[me], *to_exp(p))
        copier.keep(m_v.at[me], mo_ref.at[me])

        low = key_lanes()

        def place_keys(p, _):
            rows = pl.ds(pl.multiple_of(p * CHUNK, CHUNK), CHUNK)
            both = kv_ref[rows, :].astype(F32)
            keys[rows, :] = jnp.where(low, both, 0.0).astype(BF16)
            values[:, rows] = jnp.where(low, pltpu.roll(both, 64, 1), 0.0).T.astype(BF16)
            key_at[rows, :] = key_columns(kp_ref[p])
            return 0

        lax.fori_loop(0, CHIPS, place_keys, 0)

        def homeward(target, source):
            return pltpu.make_async_remote_copy(
                src_ref=done.at[target],
                dst_ref=a_ref.at[:, lanes(source)],
                send_sem=out_sem.at[target],
                recv_sem=in_sem.at[source],
                device_id={"ctx": 2 * target + core},
                device_id_type=MESH,
            )

        def block(k, _):
            i = CHIPS - 1 - k
            wide = q_ref[i].astype(F32)
            stacked = jnp.concatenate([wide, pltpu.roll(wide, 64, 1)], axis=0).astype(BF16)
            at_row, start_row = pair_rows(p_ref[i])

            def step(diagonal, p, carry):
                top, total, acc = carry
                rows = pl.ds(pl.multiple_of(p * CHUNK, CHUNK), CHUNK)
                scores = dot(keys[rows, :], stacked, NT)
                at_key = jnp.concatenate([key_at[rows, :]] * (CHUNK // 128), axis=1)
                seen = at_key >= start_row
                if diagonal:
                    seen = seen & (at_key <= at_row)
                scores = jnp.where(seen, scores, MASKED)
                new_top = jnp.maximum(top, jnp.max(scores, axis=0, keepdims=True))
                probs = jnp.exp(scores - new_top)
                scale = jnp.exp(top - new_top)
                total = total * scale + jnp.sum(probs, axis=0, keepdims=True)
                acc = acc * scale + dot(values[:, rows], probs.astype(BF16))
                return new_top, total, acc

            none = jnp.zeros((1, 2 * ROWS), F32)
            carry = (none + MASKED, none, jnp.zeros((128, 2 * ROWS), F32))
            carry = lax.fori_loop(first_chunk(i, core), i, lambda p, c: step(False, p, c), carry)
            top, total, acc = step(True, i, carry)
            turned = acc[0:64, :] / total
            ot_ref[i] = turned
            lt_ref[i] = top + jnp.log(total)
            out = jnp.concatenate([turned, turned], axis=0).T
            done[i] = jnp.where(low, out[:ROWS], out[ROWS:]).astype(BF16)

            @pl.when(i != chip)
            def _():
                homeward(i, chip).start()

            return 0

        for first, last in ((0, 1), (1, 2), (2, 3), (3, 4)):
            lax.fori_loop(first, last, block, 0)
            next(extra)
        lax.fori_loop(4, CHIPS, block, 0)
        next(extra)
        a_ref[:, lanes(chip)] = done[chip]
        copier.kept(load)
        for p in twins:
            homeward(chip, p).wait_recv()
        branch = dot(a_ref[...], w_v[...]).astype(BF16).astype(F32)
        resid = t_ref[...].astype(F32) + branch
        res_ref[...] = resid
        scale = row_scale(jnp.sum(resid * resid, axis=1, keepdims=True), WIDTH)
        for e in range(EXP):
            at = slice(e * 128, (e + 1) * 128)
            ffn[:, at] = (resid[:, at] * scale * g_ref[e, 3:4, :]).astype(BF16)
        rows_out = relay(copier, ffn, lambda s: o_ref.at[s], ROWS, ring, to_exp)
        next(rows_out)
        next(rows_out)
        copier.keep(ffn, o_ref.at[me])
        side_by_side(extra)
        side_by_side(rows_out)
        for p in twins:
            homeward(p, chip).wait_send()
        copier.finish()

    vmem = pl.BlockSpec(memory_space=pltpu.VMEM)
    return pl.pallas_call(
        body,
        name="attend",
        out_shape=[
            jax.ShapeDtypeStruct((ROWS, WIDTH), BF16),
            jax.ShapeDtypeStruct((CHIPS, 64, 2 * ROWS), F32),
            jax.ShapeDtypeStruct((CHIPS, 1, 2 * ROWS), F32),
            jax.ShapeDtypeStruct((ROWS, WIDTH), F32),
            jax.ShapeDtypeStruct((EXP, ROWS, WIDTH), BF16),
            jax.ShapeDtypeStruct((EXP, 8, ROWS), F32),
            jax.ShapeDtypeStruct((EXP, ROWS, WIDTH), BF16),
        ],
        in_specs=[vmem] * 5 + [ANY_SPEC] + [vmem] * 4,
        out_specs=[vmem] * 4 + [ANY_SPEC] * 3,
        scratch_shapes=[
            pltpu.VMEM((KEYS, 128), BF16),
            pltpu.VMEM((128, KEYS), BF16),
            pltpu.VMEM((KEYS, 128), F32),
            pltpu.VMEM((CHIPS, ROWS, 128), BF16),
            pltpu.VMEM((WIDTH, WIDTH), BF16),
            pltpu.VMEM((ROWS, WIDTH), BF16),
            pltpu.VMEM((EXP, 8, ROWS), F32),
            pltpu.SemaphoreType.DMA((CHIPS,)),
            pltpu.SemaphoreType.DMA((CHIPS,)),
            pltpu.SemaphoreType.DMA((36,)),
            pltpu.SemaphoreType.DMA((36,)),
            pltpu.SemaphoreType.DMA((8,)),
        ],
        compiler_params=pltpu.CompilerParams(
            collective_id=2, has_side_effects=True, vmem_limit_bytes=60 * MIB
        ),
    )(q, kv, key_pos, places, cotangent, w_out, tokens, gains, routes_t, logits_t)


def settle_experts(
    rows, d_rows, act, d_gate, d_up, d_parts, layer_parts, resid, cotangent, gains, w_out
):
    def body(
        x_ref, r_ref, a_ref, g_ref, u_ref, p_ref, l_ref, res_ref, cot_ref, gain_ref, w_ref,
        gate_out, up_out, down_a_out, down_b_out, dr_out, db_out, gg_out, do_out, keep_out, give_out, dx_out, d_att,
        x_v, r_v, a_v, g_v, u_v, gate, up, down, gate_o, up_o, down_o, gate_a, down_a, up_b, down_b,
        to_z, from_z, d_own, d_right, d_left, d_low, d_high, d_from, l_own, l_right, l_left, l_low, l_high, l_from, send_sem, recv_sem, local_sem,
    ):
        _, chip, core, sibling = place()
        me = lax.axis_index("exp")
        zl, x = me // 4, lax.rem(me, 4)
        zh, y = chip // 4, lax.rem(chip, 4)
        at_ctx = lambda z, yy: ("ctx", z * 8 + yy * 2 + core)
        over = at_ctx(1 - zh, y)
        columns = [lax.rem(y + d, 4) for d in (1, 3, 2)]
        twins = [lax.rem(chip + d, CHIPS) for d in FAR_FIRST]
        right, left, far = [lax.rem(x + d, 4) for d in (1, 3, 2)]
        at_exp = lambda p: ("exp", zl * 4 + p)
        low, high = pl.ds(0, ROWS // 2), pl.ds(ROWS // 2, ROWS // 2)
        copier = Copier(send_sem, recv_sem, local_sem)
        loads = []
        for e in range(LOCAL):
            pairs = ((x_ref, x_v), (r_ref, r_v), (a_ref, a_v), (g_ref, g_v), (u_ref, u_v))
            loads.append([copier.keep(src.at[e], dst.at[e]) for src, dst in pairs])
        parts = (p_ref, d_own, d_right, d_left, d_low, d_high, d_from)
        layers = (l_ref, l_own, l_right, l_left, l_low, l_high, l_from)

        def fetch(src, own, to_right, to_left, *_):
            return [
                copier.keep(src.at[:, x], own),
                copier.keep(src.at[:, right, low], to_right),
                copier.keep(src.at[:, left, high], to_left),
            ]

        part_loads, layer_loads = fetch(*parts), fetch(*layers)
        meet(
            [("ctx", sibling)]
            + [("ctx", 2 * p + core) for p in twins]
            + [at_exp(right), at_exp(left)]
            + [("exp", (1 - zl) * 4 + x)]
        )

        def set_out(src, own, to_right, to_left, in_low, in_high, arrived):
            return [
                copier.send(src.at[:, far, low], in_low, *at_exp(right)),
                copier.send(src.at[:, far, high], in_high, *at_exp(left)),
                copier.send(src.at[:, right, high], arrived.at[0, :, high], *at_exp(right)),
                copier.send(src.at[:, left, low], arrived.at[1, :, low], *at_exp(left)),
            ]

        def pass_on(stage, loads_of, src, own, to_right, to_left, in_low, in_high, arrived):
            for at in loads_of:
                copier.kept(at)
            for at in stage[:2]:
                copier.arrived(at)

            def add(r, _):
                at = pl.ds(pl.multiple_of(r * 48, 16), 48)
                for z in range(2):
                    for mine, other in ((to_right, in_low), (to_left, in_high)):
                        mine[z, at, :] = (mine[z, at, :].astype(F32) + other[z, at, :].astype(F32)).astype(BF16)
                return 0

            lax.fori_loop(0, 2, add, 0)
            return stage[2:] + [
                copier.send(to_right, arrived.at[0, :, low], *at_exp(right)),
                copier.send(to_left, arrived.at[1, :, high], *at_exp(left)),
            ]

        part_stage = set_out(*parts)

        def work(e):
            for at in loads[e]:
                copier.kept(at)

            def wide(r, _):
                rows_r = x_v[e, :, pl.ds(pl.multiple_of(r * 256, 256), 256)]
                for d_v, o_v in ((g_v, gate), (u_v, up)):
                    grad = dot(rows_r, d_v[e], TN).astype(BF16)
                    for k in range(4):
                        o_v[k % 2, r // 2, 2 * lax.rem(r, 2) + k // 2, e] = grad[k * 64 : (k + 1) * 64]
                return 0

            lax.fori_loop(0, 4, wide, 0)

            def tall(r, _):
                act_r = a_v[e, :, pl.ds(pl.multiple_of(r * 256, 256), 256)]
                grad = dot(act_r, r_v[e], TN).astype(BF16)
                for k in range(8):
                    down[k % 2, r, k // 2, e] = grad[k * 32 : (k + 1) * 32]
                return 0

            lax.fori_loop(0, 2, tall, 0)
            return [
                copier.send(full.at[1 - core, :, :, e], other.at[:, :, e], "ctx", sibling)
                for full, other in ((gate, gate_o), (up, up_o), (down, down_o))
            ]

        first_a, first_b = [], []

        def join(e, swaps):
            for at in swaps:
                copier.arrived(at)

            def add(c, _):
                z, yy = c // 4, lax.rem(c, 4)
                for full, other in ((gate, gate_o), (up, up_o), (down, down_o)):
                    both = full[core, z, yy, e].astype(F32) + other[z, yy, e].astype(F32)
                    full[core, z, yy, e] = both.astype(BF16)
                return 0

            lax.fori_loop(0, CHIPS, add, 0)
            first_a.append(copier.send(gate.at[core, 1 - zh, :, e], gate_a.at[:, e], *over))
            if e < DOWN_A:
                first_a.append(copier.send(down.at[core, 1 - zh, :, e], down_a.at[:, e], *over))
            for c in columns:
                to = at_ctx(zh, c)
                first_b.append(copier.send(up.at[core, :, c, e], up_b.at[y, :, e], *to))
                if e >= DOWN_A:
                    first_b.append(copier.send(down.at[core, :, c, e], down_b.at[y, :, e - DOWN_A], *to))

        swaps = work(0)
        later = work(1)
        join(0, swaps)
        part_stage = pass_on(part_stage, part_loads, *parts)
        layer_stage = set_out(*layers)
        swaps = later
        later = work(2)
        join(1, swaps)
        swaps = later
        later = work(3)
        w_loads = [copier.keep(w_ref.at[pl.ds(k * FF, FF)], r_v.at[k, pl.ds(0, FF)]) for k in range(2)]
        join(2, swaps)
        join(3, later)

        def sum_up(stage, own, arrived, keep_ref, give_ref):
            for at in stage:
                copier.arrived(at)

            def add(r, _):
                at = pl.ds(pl.multiple_of(r * 48, 16), 48)
                keep, give = [
                    own[z, at, :].astype(F32) + arrived[0, z, at, :].astype(F32) + arrived[1, z, at, :].astype(F32)
                    for z in (zl, 1 - zl)
                ]
                keep_ref[at, :] = keep
                give_ref[at, :] = give.astype(BF16)
                return 0

            lax.fori_loop(0, 4, add, 0)

        sum_up(part_stage, d_own, d_from, dx_out, to_z)
        z_stage = copier.send(to_z, from_z, "exp", (1 - zl) * 4 + x)
        layer_stage = pass_on(layer_stage, layer_loads, *layers)

        copier.arrived(z_stage)
        incoming = dx_out[...] + from_z[...].astype(F32)
        resid_v = res_ref[...]
        scale = row_scale(jnp.sum(resid_v * resid_v, axis=1, keepdims=True), WIDTH)
        inner = jnp.zeros((ROWS, 1), F32)
        for e in range(EXP):
            at = slice(e * 128, (e + 1) * 128)
            product = incoming[:, at] * resid_v[:, at]
            gg_out[:, at] = jnp.sum(product * scale, axis=0, keepdims=True)
            inner = inner + jnp.sum(product * gain_ref[e, 3:4, :], axis=1, keepdims=True)
        cut = scale * scale * scale * inner * (1.0 / WIDTH)
        for e in range(EXP):
            at = slice(e * 128, (e + 1) * 128)
            d_norm = scale * (incoming[:, at] * gain_ref[e, 3:4, :]) - resid_v[:, at] * cut
            d_resid = cot_ref[:, at].astype(F32) + d_norm
            dr_out[:, at] = d_resid
            db_out[:, at] = d_resid.astype(BF16)
        for at in w_loads:
            copier.kept(at)
        for k in range(2):
            d_att[:, k * FF : (k + 1) * FF] = dot(db_out[...], r_v[k, 0:FF, :], NT).astype(BF16)
        for p in twins:
            copier.send(d_att.at[:, lanes(p)], do_out.at[chip], "ctx", 2 * p + core)
        copier.keep(d_att.at[:, lanes(chip)], do_out.at[chip])
        for at in first_a:
            copier.arrived(at)

        def sum_a(c, _):
            for e in range(LOCAL):
                both = gate[core, zh, c, e].astype(F32) + gate_a[c, e].astype(F32)
                gate_out[c, e] = both.astype(BF16)
            for e in range(DOWN_A):
                both = down[core, zh, c, e].astype(F32) + down_a[c, e].astype(F32)
                down_a_out[c, e] = both.astype(BF16)
            return 0

        lax.fori_loop(0, 4, sum_a, 0)

        for at in first_b:
            copier.arrived(at)
        others = [lax.rem(y + d, 4) for d in (1, 2, 3)]

        def sum_b(e, _):
            for z in range(2):
                total = up[core, z, y, e].astype(F32)
                for c in others:
                    total = total + up_b[c, z, e].astype(F32)
                up_out[z, e] = total.astype(BF16)
            return 0

        lax.fori_loop(0, LOCAL, sum_b, 0)

        def sum_b_down(e, _):
            for z in range(2):
                total = down[core, z, y, e + DOWN_A].astype(F32)
                for c in others:
                    total = total + down_b[c, z, e].astype(F32)
                down_b_out[z, e] = total.astype(BF16)
            return 0

        lax.fori_loop(0, DOWN_B, sum_b_down, 0)
        sum_up(layer_stage, l_own, l_from, keep_out, give_out)
        copier.finish()

    vmem = pl.BlockSpec(memory_space=pltpu.VMEM)
    buf = lambda *shape: pltpu.VMEM(shape, BF16)
    wide, tall = (64, FF), (32, WIDTH)
    return pl.pallas_call(
        body,
        name="settle_experts",
        out_shape=[
            jax.ShapeDtypeStruct((4, LOCAL) + wide, BF16),
            jax.ShapeDtypeStruct((2, LOCAL) + wide, BF16),
            jax.ShapeDtypeStruct((4, DOWN_A) + tall, BF16),
            jax.ShapeDtypeStruct((2, DOWN_B) + tall, BF16),
            jax.ShapeDtypeStruct((ROWS, WIDTH), F32),
            jax.ShapeDtypeStruct((ROWS, WIDTH), BF16),
            jax.ShapeDtypeStruct((1, WIDTH), F32),
            jax.ShapeDtypeStruct((CHIPS, ROWS, 128), BF16),
            jax.ShapeDtypeStruct((ROWS, WIDTH), F32),
            jax.ShapeDtypeStruct((ROWS, WIDTH), BF16),
        ],
        in_specs=[ANY_SPEC] * 7 + [vmem] * 3 + [ANY_SPEC],
        out_specs=[vmem] * 7 + [ANY_SPEC] + [vmem] * 2,
        scratch_shapes=[
            pltpu.VMEM((ROWS, WIDTH), F32),
            buf(ROWS, WIDTH),
            buf(LOCAL, SLOTS, WIDTH),
            buf(LOCAL, SLOTS, WIDTH),
            buf(LOCAL, SLOTS, FF),
            buf(LOCAL, SLOTS, FF),
            buf(LOCAL, SLOTS, FF),
            buf(2, 2, 4, LOCAL, *wide),
            buf(2, 2, 4, LOCAL, *wide),
            buf(2, 2, 4, LOCAL, *tall),
            buf(2, 4, LOCAL, *wide),
            buf(2, 4, LOCAL, *wide),
            buf(2, 4, LOCAL, *tall),
            buf(4, LOCAL, *wide),
            buf(4, DOWN_A, *tall),
            buf(4, 2, LOCAL, *wide),
            buf(4, 2, DOWN_B, *tall),
            buf(ROWS, WIDTH),
            buf(ROWS, WIDTH),
        ]
        + [
            buf(2, ROWS, WIDTH),
            buf(2, ROWS // 2, WIDTH),
            buf(2, ROWS // 2, WIDTH),
            buf(2, ROWS // 2, WIDTH),
            buf(2, ROWS // 2, WIDTH),
            buf(2, 2, ROWS, WIDTH),
        ]
        * 2
        + [
            pltpu.SemaphoreType.DMA((58,)),
            pltpu.SemaphoreType.DMA((58,)),
            pltpu.SemaphoreType.DMA((32,)),
        ],
        compiler_params=pltpu.CompilerParams(
            collective_id=8, has_side_effects=True, vmem_limit_bytes=63 * MIB
        ),
    )(rows, d_rows, act, d_gate, d_up, d_parts, layer_parts, resid, cotangent, gains, w_out)


def compute_call(body, name, outs, ins, vmem=60, **kw):
    return pl.pallas_call(
        body,
        name=name,
        out_shape=outs,
        compiler_params=pltpu.CompilerParams(vmem_limit_bytes=vmem * MIB),
        **kw,
    )(*ins)


def row_scale(total, width):
    return lax.rsqrt(total * (1.0 / width) + EPSILON)


def key_lanes():
    return lax.broadcasted_iota(jnp.int32, (1, 128), 1) < 64


def turn(values, cosine, sine):
    first = lax.rem(lax.broadcasted_iota(jnp.int32, (1, 128), 1), 64) < 32
    return values * cosine + jnp.where(first, -pltpu.roll(values, 96, 1), pltpu.roll(values, 32, 1)) * sine


def across(select, values):
    return lax.dot_general(
        select, values, (NT, ((), ())), precision=lax.Precision.HIGHEST, preferred_element_type=F32
    )


def both_totals(left, right):
    row_id = lax.broadcasted_iota(jnp.int32, (8, 128), 0)
    ones = jnp.where(row_id == 0, 1.0, 0.0)
    keys = jnp.where((row_id == 1) & key_lanes(), 1.0, 0.0)
    return (across(ones, left) + across(keys, right))[0:2, :]


def down_rows(values, row, width=128):
    chosen = lax.broadcasted_iota(jnp.int32, (2, width), 0) == row
    return lax.dot_general(
        values,
        jnp.where(chosen, 1.0, 0.0),
        (TN, ((), ())),
        precision=lax.Precision.HIGHEST,
        preferred_element_type=F32,
    )


def own_chip():
    return lax.axis_index("ctx") // 2


def key_columns(row):
    upper = jnp.floor(row * (1.0 / 64.0))
    parts = jnp.concatenate([upper, row - 64.0 * upper], axis=0).astype(BF16)
    scale = jnp.where(lax.broadcasted_iota(jnp.int32, (2, 128), 0) == 0, 64.0, 1.0).astype(BF16)
    return dot(parts, scale, TN)


def first_chunk(i, core):
    return jnp.maximum((2 * i + core) * ROWS - (LONGEST - 1), 0) // CHUNK


def pair_rows(places_i):
    return [jnp.concatenate([places_i[k : k + 1, :]] * 2, axis=1) for k in range(2)]


def experts(rows, grads, meta, w_gate, w_up, w_down):
    half = SLOTS // 2
    main, rest = 64, CAP - 64

    def body(
        x_ref, g_ref, m_ref, wg_ref, wu_ref, wd_ref,
        xin_ref, dr_ref, act_ref, dg_ref, du_ref, out_ref, dx_ref,
        x, g, wg, wu, wd, xin, dr, act, dg, du, out, dx, made, back, made_rest, back_rest, weight, sems,
    ):
        def pair_in(p):
            at = pl.ds(2 * p, 2)
            return [pltpu.make_async_copy(a.at[at], b.at[at], sems.at[0, p]) for a, b in ((x_ref, x), (g_ref, g))]

        def weights_in(e):
            pairs = ((wg_ref, wg), (wu_ref, wu), (wd_ref, wd))
            return [pltpu.make_async_copy(a.at[e], b.at[e], sems.at[1, e]) for a, b in pairs]

        def rows_out(e):
            return [pltpu.make_async_copy(a.at[e], b.at[e], sems.at[2, e]) for a, b in ((xin, xin_ref), (dr, dr_ref))]

        def acts_out(e):
            pairs = ((act, act_ref), (dg, dg_ref), (du, du_ref))
            return [pltpu.make_async_copy(a.at[e], b.at[e], sems.at[3, e]) for a, b in pairs]

        def pair_out(p):
            at = pl.ds(2 * p, 2)
            return [pltpu.make_async_copy(a.at[at], b.at[at], sems.at[4, p]) for a, b in ((dx, dx_ref), (out, out_ref))]

        def start(copies):
            for copy in copies:
                copy.start()

        def wait(copies):
            for copy in copies:
                copy.wait()

        for p in range(PAIRS):
            start(pair_in(p))
        start(weights_in(0))

        row_id = lax.broadcasted_iota(jnp.int32, (LOCAL * CAP, ROWS), 0).astype(F32)

        def pick_source(s):
            meta_s = m_ref[s]
            chosen = jnp.zeros((LOCAL * CAP, ROWS), F32)
            gates = jnp.zeros((LOCAL * CAP, ROWS), F32)
            for k in range(LOCAL):
                slot = meta_s[k : k + 1, :]
                spot = jnp.where(slot < main, slot + k * main, slot + (LOCAL * main + k * rest - main))
                hit = row_id == jnp.where(slot < 0.0, -1.0, spot)
                chosen = jnp.where(hit, 1.0, chosen)
                gates = jnp.where(hit, meta_s[4 + k : 5 + k, :], gates)
            return chosen.astype(BF16), jnp.sum(gates, axis=1, keepdims=True)

        def pick(p, _):
            wait(pair_in(p))
            found = []
            for b in range(2):
                chosen, gates = pick_source(2 * p + b)
                found.append((dot(chosen, x[2 * p + b]), dot(chosen, g[2 * p + b]) * gates, gates))
            at_rest = pl.ds(pl.multiple_of(p * PAIR_CAP + 2 * main, 16), 2 * rest)
            for k in range(LOCAL):
                last = slice(LOCAL * main + k * rest, LOCAL * main + (k + 1) * rest)
                for b in range(2):
                    at = pl.ds(pl.multiple_of(p * PAIR_CAP + b * main, 16), main)
                    piece = slice(k * main, (k + 1) * main)
                    xin[k, at, :] = found[b][0][piece].astype(BF16)
                    dr[k, at, :] = found[b][1][piece].astype(BF16)
                    weight[k, at, :] = found[b][2][piece]
                both = [jnp.concatenate([found[0][n][last], found[1][n][last]], axis=0) for n in range(3)]
                xin[k, at_rest, :] = both[0].astype(BF16)
                dr[k, at_rest, :] = both[1].astype(BF16)
                weight[k, at_rest, :] = both[2]
            return 0

        lax.fori_loop(0, PAIRS, pick, 0)
        start(weights_in(1))

        def expert(e, _):
            wait(weights_in(e))

            @pl.when(e < LOCAL - 2)
            def _():
                start(weights_in(e + 2))

            start(rows_out(e))

            def work(h, _):
                at = pl.ds(pl.multiple_of(h * half, half), half)
                x_h, dr_h = xin[e, at, :], dr[e, at, :]
                gate = dot(x_h, wg[e])
                up = dot(x_h, wu[e])
                sig = jax.nn.sigmoid(gate)
                silu = gate * sig
                act_h = (silu * up).astype(BF16)
                act[e, at, :] = act_h
                d_act = dot(dr_h, wd[e], NT)
                d_gate = (d_act * up * sig * (1.0 + gate * (1.0 - sig))).astype(BF16)
                d_up = (d_act * silu).astype(BF16)
                dg[e, at, :] = d_gate
                du[e, at, :] = d_up
                y = (dot(act_h, wd[e]) * weight[e, at, :]).astype(BF16)
                dch = (dot(d_gate, wg[e], NT) + dot(d_up, wu[e], NT)).astype(BF16)
                at_main = pl.ds(pl.multiple_of(e * main, main), main)
                at_rest = pl.ds(pl.multiple_of(e * 2 * rest, 2 * rest), 2 * rest)
                for k in range(2):
                    for rows_k, whole, last in ((y, made, made_rest), (dch, back, back_rest)):
                        piece = rows_k[k * PAIR_CAP : (k + 1) * PAIR_CAP]
                        for b in range(2):
                            whole[4 * h + 2 * k + b, at_main, :] = piece[b * main : (b + 1) * main]
                        last[2 * h + k, at_rest, :] = piece[2 * main :]
                return 0

            lax.fori_loop(0, 2, work, 0)
            start(acts_out(e))
            return 0

        lax.fori_loop(0, LOCAL, expert, 0)
        lane_main = lax.broadcasted_iota(jnp.int32, (PAIR_ROWS, LOCAL * main), 1).astype(F32)
        lane_rest = lax.broadcasted_iota(jnp.int32, (PAIR_ROWS, LOCAL * 2 * rest), 1).astype(F32)
        second = lax.broadcasted_iota(jnp.int32, (PAIR_ROWS, 1), 0) >= ROWS

        def give(p, _):
            both = jnp.concatenate([m_ref[2 * p], m_ref[2 * p + 1]], axis=1)
            turned = jnp.concatenate([both, jnp.zeros((120, PAIR_ROWS), F32)], axis=0).T
            in_main = jnp.zeros((PAIR_ROWS, LOCAL * main), F32)
            in_rest = jnp.zeros((PAIR_ROWS, LOCAL * 2 * rest), F32)
            for k in range(LOCAL):
                slot = turned[:, k : k + 1]
                here = jnp.where((slot >= 0.0) & (slot < main), slot + k * main, -1.0)
                in_main = jnp.where(lane_main == here, 1.0, in_main)
                there = slot + (k * 2 * rest - main) + jnp.where(second, float(rest), 0.0)
                in_rest = jnp.where(lane_rest == jnp.where(slot < main, -1.0, there), 1.0, in_rest)
            in_main, in_rest = in_main.astype(BF16), in_rest.astype(BF16)
            for whole, last, to in ((back, back_rest, dx), (made, made_rest, out)):
                more = dot(in_rest, last[p])
                for b in range(2):
                    at = slice(b * ROWS, (b + 1) * ROWS)
                    to[2 * p + b] = (dot(in_main[at], whole[2 * p + b]) + more[at]).astype(BF16)
            start(pair_out(p))
            return 0

        lax.fori_loop(0, PAIRS, give, 0)
        for e in range(LOCAL):
            wait(rows_out(e))
            wait(acts_out(e))
        for p in range(PAIRS):
            wait(pair_out(p))

    vmem = pl.BlockSpec(memory_space=pltpu.VMEM)
    buf = lambda *shape: pltpu.VMEM(shape, BF16)
    wide, narrow, source = (LOCAL, SLOTS, WIDTH), (LOCAL, SLOTS, FF), (EXP, ROWS, WIDTH)
    return compute_call(
        body,
        "experts",
        [jax.ShapeDtypeStruct(shape, BF16) for shape in (wide, wide, narrow, narrow, narrow, source, source)],
        [rows, grads, meta, w_gate, w_up, w_down],
        vmem=63,
        in_specs=[ANY_SPEC, ANY_SPEC, vmem] + [ANY_SPEC] * 3,
        out_specs=[ANY_SPEC] * 7,
        scratch_shapes=[
            buf(*source),
            buf(*source),
            buf(LOCAL, WIDTH, FF),
            buf(LOCAL, WIDTH, FF),
            buf(LOCAL, FF, WIDTH),
            buf(*wide),
            buf(*wide),
            buf(*narrow),
            buf(*narrow),
            buf(*narrow),
            buf(*source),
            buf(*source),
            buf(EXP, LOCAL * main, WIDTH),
            buf(EXP, LOCAL * main, WIDTH),
            buf(PAIRS, LOCAL * 2 * rest, WIDTH),
            buf(PAIRS, LOCAL * 2 * rest, WIDTH),
            pltpu.VMEM((LOCAL, SLOTS, 1), F32),
            pltpu.SemaphoreType.DMA((5, 4)),
        ],
    )


def norm_back(values, total_squares, width, weighted, mask=None):
    scale = row_scale(total_squares, width)
    inner = jnp.sum(weighted * values, axis=1, keepdims=True) * (1.0 / width)
    return scale * weighted - values * (scale * scale * scale) * inner, scale


def deliver(resid, layer_keep, layer_got, dense, out_grad, gain_sums, input_grad, expert_sums):
    def body(
        r_ref, k_ref, g_ref, d_ref, o_ref, s_ref, i_ref, eg_ref, eu_ref, ed_ref,
        lo, wq, wk, wv, wo, ga, gq, gk, gf, di, eg, eu, ed,
    ):
        lo[...] = (r_ref[...] + k_ref[...] + g_ref[...].astype(F32)).astype(BF16)
        wq[...] = d_ref[0].astype(F32)
        for c in range(4):
            k, v = apart([d_ref[1, :, (2 * c + j) * 128 : (2 * c + j + 1) * 128].astype(F32) for j in range(2)])
            wk[:, c * 128 : (c + 1) * 128] = k
            wv[:, c * 128 : (c + 1) * 128] = v
        wo[...] = o_ref[...].astype(F32)
        ga[...] = s_ref[0:1, :]
        gq[...] = s_ref[1:2, :]
        gk[...] = s_ref[2:3, 0:64]
        gf[...] = s_ref[3:4, :]
        di[...] = i_ref[...]
        eg[...] = eg_ref[...]
        eu[...] = eu_ref[...]
        ed[...] = ed_ref[...]

    def rows(count, width):
        return pl.BlockSpec((count // LOCAL, width), lambda i: (i, 0))

    def expert(*shape):
        return pl.BlockSpec((1,) + shape, lambda i: (i, 0, 0))

    return compute_call(
        body,
        "deliver",
        [
            jax.ShapeDtypeStruct((ROWS, WIDTH), BF16),
            jax.ShapeDtypeStruct((128, WIDTH), F32),
            jax.ShapeDtypeStruct((128, 512), F32),
            jax.ShapeDtypeStruct((128, 512), F32),
            jax.ShapeDtypeStruct((128, WIDTH), F32),
            jax.ShapeDtypeStruct((1, 128), F32),
            jax.ShapeDtypeStruct((1, 128), F32),
            jax.ShapeDtypeStruct((1, 64), F32),
            jax.ShapeDtypeStruct((1, 128), F32),
            jax.ShapeDtypeStruct((ROWS, WIDTH), F32),
        ]
        + [jax.ShapeDtypeStruct(a.shape, F32) for a in expert_sums],
        [resid, layer_keep, layer_got, dense, out_grad, gain_sums, input_grad, *expert_sums],
        grid=(LOCAL,),
        in_specs=[rows(ROWS, WIDTH)] * 3
        + [
            pl.BlockSpec((2, 128 // LOCAL, WIDTH), lambda i: (0, i, 0)),
            rows(128, WIDTH),
            pl.BlockSpec((8, 128), lambda i: (0, 0)),
            rows(ROWS, WIDTH),
        ]
        + [expert(64, FF), expert(64, FF), expert(32, WIDTH)],
        out_specs=[rows(ROWS, WIDTH), rows(128, WIDTH), rows(128, 512), rows(128, 512), rows(128, WIDTH)]
        + [pl.BlockSpec((1, n), lambda i: (0, 0)) for n in (128, 128, 64, 128)]
        + [rows(ROWS, WIDTH), expert(64, FF), expert(64, FF), expert(32, WIDTH)],
    )


def cosine_of_turns(turns):
    part = turns - jnp.floor(turns + 0.5)
    square = part * part * 39.47841760435743
    total = jnp.full_like(square, -1.0 / 6402373705728000.0)
    for n in (20922789888000.0, -87178291200.0, 479001600.0, -3628800.0, 40320.0, -720.0, 24.0, -2.0, 1.0):
        total = total * square + 1.0 / n
    return total


def front(tokens, dense, norms, perm, lengths):
    half = 64

    def body(
        t_ref, wq_ref, wk_ref, wv_ref, wd_ref, na_ref, nq_ref, nk_ref, nf_ref, perm_ref, len_ref,
        wo_ref, go_ref, n_ref, ql_ref, kl_ref, s_ref, c_ref, sn_ref, p_ref, kp_ref, q_ref, kv_ref,
        g_ref, w_mine, rows, normed, gains_v, w_own, totals, totals_all, kv_half, send_sem, recv_sem, local_sem,
    ):
        _, chip, core, sibling = place()
        me = lax.axis_index("exp")
        chips, exps = ring_of(chip), ring_of(me)
        twins = [lax.rem(chip + d, CHIPS) for d in (2, 6, 4, 1, 3, 5, 7)]
        to_chip = lambda p: ("ctx", 2 * p + core)
        to_exp = lambda p: ("exp", p)
        copier = Copier(send_sem, recv_sem, local_sem)
        keys = key_lanes()
        odd = lax.rem(chip, 2) == 1
        wk, wv = wk_ref[:, lanes(chip // 2)].astype(F32), wv_ref[:, lanes(chip // 2)].astype(F32)
        wk = jnp.where(odd, pltpu.roll(wk, 64, 1), wk)
        wv = jnp.where(odd, wv, pltpu.roll(wv, 64, 1))
        w_mine[:, 0:128] = wq_ref[:, lanes(chip)]
        w_mine[:, 128:256] = jnp.where(keys, wk, wv).astype(BF16)
        g_ref[...] = jnp.ones((8, 128), F32)
        g_ref[0:1, :] = na_ref[...].astype(F32)
        g_ref[1:2, :] = nq_ref[...].astype(F32)
        g_ref[2:3, 0:64] = nk_ref[...].astype(F32)
        g_ref[3:4, :] = nf_ref[...].astype(F32)
        meet([to_chip(p) for p in twins] + [to_exp(p) for p in exps[1:]] + [("ctx", sibling)])
        gain_sends = [copier.send(g_ref, gains_v.at[me], *to_exp(p)) for p in exps[1:]]
        part = pl.ds(pl.multiple_of(core * half, half), half)
        slot = lambda s: wo_ref.at[s, part]
        handed = []

        def norm(block, s):
            x = block.astype(F32)
            scale = row_scale(jnp.sum(x * x, axis=1, keepdims=True), WIDTH)
            for e in range(EXP):
                at = slice(e * 128, (e + 1) * 128)
                normed[s, :, at] = (x[:, at] * scale * gains_v[e, 0:1, :]).astype(BF16)

        projected = []

        def project(s):
            both = dot(normed[s], w_own[...].reshape(WIDTH, 256))
            q, kv = both[:, 0:128], both[:, 128:256]
            ql_ref[s] = q
            kl_ref[s] = kv
            totals[s] = both_totals(q * q, kv * kv)

        def landed(s):
            norm(rows[s], s)
            projected.append(s)

        main = relay(copier, t_ref, lambda s: rows.at[s], ROWS, chips, to_chip, landed)
        dense = relay(
            copier,
            wd_ref.at[part],
            slot,
            half,
            exps,
            to_exp,
            lambda s: handed.append(copier.send(slot(s), slot(s), "ctx", sibling)),
        )
        next(main)
        next(main)
        next(dense)
        next(dense)
        copier.keep(wd_ref, wo_ref.at[me])
        w_own[me] = w_mine[...]
        gains_v[me] = g_ref[...]

        row = lax.broadcasted_iota(jnp.int32, (CTX, ROWS), 1)
        piece = jnp.where(row // 12 == lax.broadcasted_iota(jnp.int32, (CTX, ROWS), 0), 1.0, 0.0)
        dealt = dot(perm_ref[...].astype(F32).astype(BF16), piece.astype(BF16))
        source = lax.broadcasted_iota(jnp.int32, (CTX, ROWS), 0)
        position = (source * CTX).astype(F32) + dealt
        position = position * 12.0 + lax.rem(row, 12).astype(F32)
        begin = jnp.zeros((CTX, ROWS), F32)
        ends = jnp.zeros((1, 1), F32)
        for k in range(3):
            ends = ends + len_ref[0:1, k : k + 1].astype(F32)
            begin = jnp.where(position >= ends, ends, begin)
        for i in range(CHIPS):
            mine = [jnp.where(core == 0, v[2 * i : 2 * i + 1], v[2 * i + 1 : 2 * i + 2]) for v in (position, begin)]
            p_ref[i] = jnp.concatenate(mine, axis=0)
            kp_ref[i] = jnp.concatenate([position[2 * i : 2 * i + 1], position[2 * i + 1 : 2 * i + 2]], axis=1)

        def angles(i, _):
            keys = key_lanes()
            lane = lax.broadcasted_iota(jnp.int32, (1, 128), 1)
            freq = jnp.exp(lax.rem(lane, 32).astype(F32) * (-2.0 / 64 * 9.210340371976184))
            place_i = p_ref[i]
            offset = down_rows(place_i, 0) - down_rows(place_i, 1)
            mixed = cosine_of_turns(offset * (freq * 0.15915494309189535) - jnp.where(keys, 0.0, 0.25))
            other = pltpu.roll(mixed, 64, 1)
            c_ref[i] = jnp.where(keys, mixed, other)
            sn_ref[i] = jnp.where(keys, other, mixed)
            return 0

        lax.fori_loop(0, CHIPS, angles, 0)
        for at in gain_sends:
            copier.arrived(at)
        go_ref[...] = gains_v[...]
        norm(t_ref[...], chip)
        projected.append(chip)
        next(main)
        next(dense)
        next(main)
        own_sends = [copier.send(w_mine, w_own.at[me], *to_exp(p)) for p in exps[1:]]
        next(dense)
        next(main)
        next(main)
        next(dense)
        for at in own_sends:
            copier.arrived(at)
        for s in projected:
            project(s)
        projected.clear()
        next(main)
        next(dense)
        for s in projected:
            project(s)
        projected.clear()
        side_by_side(main)
        for s in projected:
            project(s)
        shares = [copier.send(totals, totals_all.at[chip], *to_chip(p)) for p in twins]
        totals_all[chip] = totals[...]
        side_by_side(dense)
        copier.keep(normed, n_ref)
        for at in shares:
            copier.arrived(at)

        def turn_one(i, _):
            squares = totals_all[0, i]
            for c in range(1, CHIPS):
                squares = squares + totals_all[c, i]
            s_ref[i] = squares
            cos, sin = c_ref[i], sn_ref[i]
            gain = gains_v[chip]
            q = ql_ref[i] * row_scale(down_rows(squares, 0), WIDTH) * gain[1:2, :]
            q = turn(q, cos, sin).astype(BF16).astype(F32)
            q_ref[i] = (q * 0.125).astype(BF16)
            scale = jnp.where(keys, row_scale(down_rows(squares, 1), WIDTH // 2), 1.0)
            kv = kl_ref[i] * scale * gain[2:3, :]
            kv_half[i] = turn(kv, jnp.where(keys, cos, 1.0), jnp.where(keys, sin, 0.0)).astype(BF16)
            return 0

        lax.fori_loop(0, CHIPS, turn_one, 0)
        copier.send(kv_half, kv_ref.at[:, core], "ctx", sibling)
        copier.keep(kv_half, kv_ref.at[:, core])
        copier.finish()

    vmem = pl.BlockSpec(memory_space=pltpu.VMEM)
    wide = jax.ShapeDtypeStruct((CHIPS, ROWS, 128), F32)
    return pl.pallas_call(
        body,
        name="front",
        out_shape=[
            jax.ShapeDtypeStruct((EXP, 128, WIDTH), BF16),
            jax.ShapeDtypeStruct((EXP, 8, 128), F32),
            jax.ShapeDtypeStruct((CHIPS, ROWS, WIDTH), BF16),
            wide,
            wide,
            jax.ShapeDtypeStruct((CHIPS, 2, ROWS), F32),
            wide,
            wide,
            jax.ShapeDtypeStruct((CHIPS, 2, ROWS), F32),
            jax.ShapeDtypeStruct((CHIPS, 1, CHUNK), F32),
            jax.ShapeDtypeStruct((CHIPS, ROWS, 128), BF16),
            jax.ShapeDtypeStruct((CHIPS, 2, ROWS, 128), BF16),
        ],
        in_specs=[vmem] * 11,
        out_specs=[ANY_SPEC, vmem, ANY_SPEC] + [vmem] * 8 + [ANY_SPEC],
        scratch_shapes=[
            pltpu.VMEM((8, 128), F32),
            pltpu.VMEM((128, 256), BF16),
            pltpu.VMEM((CHIPS, ROWS, WIDTH), BF16),
            pltpu.VMEM((CHIPS, ROWS, WIDTH), BF16),
            pltpu.VMEM((EXP, 8, 128), F32),
            pltpu.VMEM((EXP, 128, 256), BF16),
            pltpu.VMEM((CHIPS, 2, ROWS), F32),
            pltpu.VMEM((CHIPS, CHIPS, 2, ROWS), F32),
            pltpu.VMEM((CHIPS, ROWS, 128), BF16),
            pltpu.SemaphoreType.DMA((57,)),
            pltpu.SemaphoreType.DMA((57,)),
            pltpu.SemaphoreType.DMA((8,)),
        ],
        compiler_params=pltpu.CompilerParams(
            collective_id=1, has_side_effects=True, vmem_limit_bytes=60 * MIB
        ),
    )(tokens, *dense, *norms, perm, lengths)


def apart(pieces):
    first, second = pieces
    keys = key_lanes()
    return (
        jnp.where(keys, first, pltpu.roll(second, 64, 1)),
        jnp.where(keys, pltpu.roll(first, 64, 1), second),
    )


def tail(
    q, kv, d_out, out_turned, log_total, key_pos, places, q_lin, kv_lin, cosine, sine, squares, gains, normed, attended, d_branch, layer_part,
    w_query, w_key, w_value, tokens, d_resid, ffn_gain, gate_part, up_part, down_a, down_b,
):
    def body(
        q_ref, kv_ref, do_ref, ot_ref, l_ref, kp_ref, p_ref, ql_ref, kl_ref, c_ref, sn_ref, s_ref, g_ref, n_ref, at_ref, br_ref, lp_ref,
        wq_ref, wk_ref, wv_ref, t_ref, r_ref, fg_ref, gp_ref, up_ref, da_ref, db_ref,
        eg_ref, eu_ref, ed_ref, di_ref, dense_ref, og_ref, lo_ref, gs_ref,
        keys_v, values, acc, key_at, keys_t, other_v, w_mine, ql_v, kl_v, c_v, sn_v, n_v, w_v, t_v, r_v,
        got, e_q, e_kv, totals, totals_all, d_lin, home, w_give, w_keep, w_got, joint, traded, done,
        o_both, o_keep, o_got, o_traded, o_pair, o_half, o_full, a_got, a_done, packet, packets, mine, shared, gate_c, down_c, up_d, down_d, out_sem, in_sem, send_sem, recv_sem, local_sem,
    ):
        ctx, chip, core, sibling = place()
        me = lax.axis_index("exp")
        twins = [lax.rem(chip + d, CHIPS) for d in (2, 6, 4, 1, 3, 5, 7)]
        exps = [lax.rem(me + d, EXP) for d in range(1, EXP)]
        others = [lax.rem(ctx + d, CTX) for d in range(1, CTX)]
        to_chip = lambda p: ("ctx", 2 * p + core)
        copier = Copier(send_sem, recv_sem, local_sem)
        heads = [
            copier.keep(src, dst)
            for src, dst in ((c_ref, c_v), (sn_ref, sn_v), (ql_ref, ql_v), (kl_ref, kl_v))
        ]
        late = [
            copier.keep(src, dst)
            for src, dst in ((n_ref, n_v),  (t_ref, t_v), (r_ref, r_v))
        ]
        w_mine[:, 0:1024] = wq_ref[...]
        w_mine[:, 1024:1536] = wk_ref[...]
        w_mine[:, 1536:2048] = wv_ref[...]
        w_v[me] = w_mine[...]
        w_part = pl.ds(pl.multiple_of(core * 64, 64), 64)
        w_slot = lambda s: w_v.at[s, w_part]
        handed = []
        weights = relay(
            copier,
            w_mine.at[w_part],
            w_slot,
            64,
            ring_of(me),
            lambda p: ("exp", p),
            lambda s: handed.append(copier.send(w_slot(s), w_slot(s), "ctx", sibling)),
        )
        meet([("ctx", p) for p in others] + [("exp", p) for p in exps])
        next(weights)
        next(weights)
        copier.send(lp_ref, lo_ref, "exp", lax.rem(me + 4, EXP))
        zh, y = chip // 4, lax.rem(chip, 4)
        second = []
        for d in (1, 3, 2):
            c = lax.rem(y + d, 4)
            second.append(copier.send(gp_ref.at[c], gate_c.at[y], *to_chip(zh * 4 + c)))
            second.append(copier.send(da_ref.at[c], down_c.at[y], *to_chip(zh * 4 + c)))
        second.append(copier.send(up_ref.at[1 - zh], up_d, *to_chip((1 - zh) * 4 + y)))
        second.append(copier.send(db_ref.at[1 - zh], down_d, *to_chip((1 - zh) * 4 + y)))

        def out_grad(r, _):
            grad = dot(at_ref[:, pl.ds(pl.multiple_of(r * 256, 256), 256)], br_ref[...], TN).astype(BF16)
            for k in range(2):
                for c in range(2):
                    o_both[c, 2 * r + k] = grad[(2 * k + c) * 64 : (2 * k + c + 1) * 64]
            return 0

        lax.fori_loop(0, 4, out_grad, 0)
        o_swap = copier.send(o_both.at[1 - core], o_got, "ctx", sibling)
        low = key_lanes()

        def place_keys(p, _):
            rows = pl.ds(pl.multiple_of(p * CHUNK, CHUNK), CHUNK)
            both = kv_ref[rows, :].astype(F32)
            own_keys = jnp.where(low, both, 0.0)
            keys_v[rows, :] = own_keys.astype(BF16)
            keys_t[:, rows] = own_keys.T.astype(BF16)
            values[rows, :] = jnp.where(low, pltpu.roll(both, 64, 1), 0.0).astype(BF16)
            key_at[rows, :] = key_columns(kp_ref[p])
            acc[rows, :] = jnp.zeros((CHUNK, 128), F32)
            return 0

        lax.fori_loop(0, CHIPS, place_keys, 0)

        def swap(i):
            return pltpu.make_async_remote_copy(
                src_ref=other_v.at[i],
                dst_ref=got.at[i],
                send_sem=out_sem.at[i],
                recv_sem=in_sem.at[i],
                device_id={"ctx": sibling},
                device_id_type=MESH,
            )

        def attend_block(k, _):
            i = CHIPS - 1 - k
            q_wide, do_wide = q_ref[i].astype(F32), do_ref[i].astype(F32)
            q_turned, do_turned = pltpu.roll(q_wide, 64, 1), pltpu.roll(do_wide, 64, 1)
            q_rows = jnp.concatenate([q_wide, q_turned], axis=0)
            do_rows = jnp.concatenate([do_wide, do_turned], axis=0)
            do_high = jnp.concatenate([do_turned, do_wide], axis=0)
            right = [jnp.where(low, q_rows, 0.0), jnp.where(low, 0.0, do_high)]
            right = jnp.concatenate(right, axis=0).astype(BF16)
            q_rows = q_rows.astype(BF16)
            delta = jnp.sum(do_rows.T[0:64, :] * ot_ref[i], axis=0, keepdims=True)
            do_rows = do_rows.astype(BF16)
            total = l_ref[i]
            at_row, start_row = pair_rows(p_ref[i])

            def step(diagonal, p, dq):
                rows = pl.ds(pl.multiple_of(p * CHUNK, CHUNK), CHUNK)
                scores = dot(keys_v[rows, :], q_rows, NT)
                at_key = jnp.concatenate([key_at[rows, :]] * (CHUNK // 128), axis=1)
                seen = at_key >= start_row
                if diagonal:
                    seen = seen & (at_key <= at_row)
                probs = jnp.exp(jnp.where(seen, scores, MASKED) - total)
                d_scores = (probs * (dot(values[rows, :], do_rows, NT) - delta)).astype(BF16)
                acc[rows, :] += dot(jnp.concatenate([d_scores, probs.astype(BF16)], axis=1), right)
                return dq + dot(keys_t[:, rows], d_scores)

            dq = jnp.zeros((128, 2 * ROWS), F32)
            dq = lax.fori_loop(first_chunk(i, core), i, lambda p, dq: step(False, p, dq), dq)
            dq = step(True, i, dq).T * 0.125
            dq = jnp.where(low, dq[:ROWS], pltpu.roll(dq[ROWS:], 64, 1))
            e_q[i] = turn(dq, c_v[i], -sn_v[i])
            other = pl.ds(pl.multiple_of((2 * i + 1 - core) * ROWS, ROWS), ROWS)
            other_v[i] = acc[other, :].astype(BF16)
            swap(i).start()
            return 0

        for at in heads:
            copier.kept(at)

        lax.fori_loop(0, 1, attend_block, 0)
        next(weights)
        next(weights)
        copier.arrived(o_swap)

        def add_cores(e, _):
            o_keep[e] = (o_both[core, e].astype(F32) + o_got[e].astype(F32)).astype(BF16)
            return 0

        lax.fori_loop(0, EXP, add_cores, 0)
        zl, x = me // 4, lax.rem(me, 4)
        o_trades = []
        for d in (2, 1, 3):
            p = lax.rem(x + d, 4)
            for z in range(2):
                o_trades.append(copier.send(o_keep.at[z * 4 + p], o_traded.at[x, z], "exp", zl * 4 + p))
        lax.fori_loop(1, 2, attend_block, 0)
        next(weights)
        next(weights)
        lax.fori_loop(2, 3, attend_block, 0)
        next(weights)
        lax.fori_loop(3, CHIPS, attend_block, 0)

        side_by_side(weights)

        for at in o_trades:
            copier.arrived(at)
        keep, give = o_keep[zl * 4 + x].astype(F32), o_keep[(1 - zl) * 4 + x].astype(F32)
        for d in (1, 2, 3):
            p = lax.rem(x + d, 4)
            keep = keep + o_traded[p, zl].astype(F32)
            give = give + o_traded[p, 1 - zl].astype(F32)
        o_half[...] = give.astype(BF16)
        o_full[...] = keep.astype(BF16)
        o_pairs = copier.send(o_half, o_pair, "exp", (1 - zl) * 4 + x)
        keys = key_lanes()
        gain = g_ref[chip]

        def unturn_kv(k, carry):
            q_sum, kv_sum = carry
            i = CHIPS - 1 - k
            swap(i).wait_recv()
            cos, sin = jnp.where(keys, c_v[i], 1.0), jnp.where(keys, -sn_v[i], 0.0)
            mine_rows = pl.ds(pl.multiple_of((2 * i + core) * ROWS, ROWS), ROWS)
            e = turn(acc[mine_rows, :] + got[i].astype(F32), cos, sin)
            e_kv[i] = e
            q_part, kv_part = e_q[i] * ql_v[i], e * kl_v[i]
            totals[i] = both_totals(q_part * gain[1:2, :], kv_part * gain[2:3, :])
            q_scale = row_scale(down_rows(s_ref[i], 0), WIDTH)
            k_scale = row_scale(down_rows(s_ref[i], 1), WIDTH // 2)
            q_sum = q_sum + jnp.sum(q_part * q_scale, axis=0, keepdims=True)
            kv_sum = kv_sum + jnp.sum(kv_part * jnp.where(keys, k_scale, 1.0), axis=0, keepdims=True)
            return q_sum, kv_sum

        none = jnp.zeros((1, 128), F32)
        q_sum, kv_sum = lax.fori_loop(0, CHIPS, unturn_kv, (none, none))
        shares = [copier.send(totals, totals_all.at[chip], *to_chip(p)) for p in twins]
        totals_all[chip] = totals[...]
        copier.arrived(o_pairs)
        o_full[...] = (o_full[...].astype(F32) + o_pair[...].astype(F32)).astype(BF16)
        spread = [copier.send(o_full.at[:, lanes(p)], a_got.at[chip], *to_chip(p)) for p in twins]
        a_got[chip] = o_full[:, lanes(chip)]
        for at in shares:
            copier.arrived(at)

        def gradient(i):
            inner = totals_all[0, i]
            for c in range(1, CHIPS):
                inner = inner + totals_all[c, i]
            squares_i = s_ref[i]
            q_scale = row_scale(down_rows(squares_i, 0), WIDTH)
            k_scale = row_scale(down_rows(squares_i, 1), WIDTH // 2)
            q_cut = q_scale * q_scale * q_scale * down_rows(inner, 0) * (1.0 / WIDTH)
            k_cut = k_scale * k_scale * k_scale * down_rows(inner, 1) * (2.0 / WIDTH)
            d_lin[0, i] = (q_scale * (e_q[i] * gain[1:2, :]) - ql_v[i] * q_cut).astype(BF16)
            kv_scale = jnp.where(keys, k_scale, 1.0)
            k_cut = jnp.where(keys, k_cut, 0.0)
            d_lin[1, i] = (kv_scale * (e_kv[i] * gain[2:3, :]) - kl_v[i] * k_cut).astype(BF16)

        homeward = []
        for p in twins:
            gradient(p)
            for k in range(2):
                homeward.append(copier.send(d_lin.at[k, p], home.at[k, :, lanes(chip)], *to_chip(p)))
        gradient(chip)
        for k in range(2):
            home[k, :, lanes(chip)] = d_lin[k, chip]
        for at in late:
            copier.kept(at)

        def columns_grad(half, out):
            d = d_lin[half].reshape(CHIPS * ROWS, 128)

            def part(r, _):
                n = n_v[:, :, pl.ds(pl.multiple_of(r * 256, 256), 256)].reshape(CHIPS * ROWS, 256)
                out[pl.ds(pl.multiple_of(r * 256, 256), 256), :] = dot(n, d, TN).astype(BF16)
                return 0

            lax.fori_loop(0, 4, part, 0)

        columns_grad(1 - core, w_give)
        w_swap = copier.send(w_give, w_got, "ctx", sibling)
        columns_grad(core, w_keep)
        for at in spread:
            copier.arrived(at)
        total = a_got[0].astype(F32)
        for c in range(1, CHIPS):
            total = total + a_got[c].astype(F32)
        a_done[...] = total.astype(BF16)
        half = pl.ds(pl.multiple_of(core * 64, 64), 64)
        a_shares = [copier.send(a_done, og_ref.at[half, lanes(chip)], *to_chip(p)) for p in twins]
        copier.send(a_done, og_ref.at[half, lanes(chip)], "ctx", sibling)
        copier.keep(a_done, og_ref.at[half, lanes(chip)])
        copier.arrived(w_swap)
        both = w_keep[...].astype(F32) + w_got[...].astype(F32)
        joint[...] = both.astype(BF16).reshape(EXP, 128, 128)
        trades = [copier.send(joint.at[p], traded.at[me], "exp", p) for p in exps]
        traded[me] = joint[me]

        for at in homeward + handed:
            copier.arrived(at)
        k_parts, v_parts = [], []
        for c in range(4):
            k, v = apart([home[1, :, (2 * c + j) * 128 : (2 * c + j + 1) * 128].astype(F32) for j in range(2)])
            k_parts.append(k.astype(BF16))
            v_parts.append(v.astype(BF16))
        left = jnp.concatenate([home[0]] + k_parts + v_parts, axis=1)
        x = t_v[...].astype(F32)
        scale = row_scale(jnp.sum(x * x, axis=1, keepdims=True), WIDTH)
        inner = jnp.zeros((ROWS, 1), F32)
        pieces = []
        for e in range(EXP):
            at = slice(e * 128, (e + 1) * 128)
            d_normed = dot(left, w_v[e], NT).astype(BF16).astype(F32)
            packet[e] = jnp.zeros((8, 128), F32)
            packet[e, 0:1, :] = jnp.sum(d_normed * x[:, at] * scale, axis=0, keepdims=True)
            packet[e, 3:4, :] = fg_ref[:, at]
            weighted = d_normed * g_ref[e, 0:1, :]
            inner = inner + jnp.sum(weighted * x[:, at], axis=1, keepdims=True)
            pieces.append(weighted)
        packet[chip, 1:2, :] = q_sum
        packet[chip, 2:3, :] = kv_sum
        gain_trades = [copier.send(packet.at[p], packets.at[me], "exp", p) for p in exps]
        packets[me] = packet[me]

        for at in trades:
            copier.arrived(at)
        total = traded[0].astype(F32)
        for e in range(1, EXP):
            total = total + traded[e].astype(F32)
        done[...] = total.astype(BF16)
        spot = dense_ref.at[core, :, lanes(chip)]
        w_shares = [copier.send(done, spot, *to_chip(p)) for p in twins]
        copier.send(done, spot, "ctx", sibling)
        copier.keep(done, spot)

        for at in gain_trades:
            copier.arrived(at)
        total = packets[0]
        for e in range(1, EXP):
            total = total + packets[e]
        mine[...] = total
        gain_shares = [copier.send(mine, shared.at[ctx], "ctx", p) for p in others]
        shared[ctx] = total

        inner = inner * (1.0 / WIDTH)
        cut = scale * scale * scale * inner
        for e in range(EXP):
            at = slice(e * 128, (e + 1) * 128)
            di_ref[:, at] = r_v[:, at] + scale * pieces[e] - x[:, at] * cut
        for at in second:
            copier.arrived(at)
        columns = [lax.rem(y + d, 4) for d in (1, 2, 3)]

        def add_experts(e, _):
            total = gp_ref[y, e].astype(F32)
            for c in columns:
                total = total + gate_c[c, e].astype(F32)
            eg_ref[e] = total
            eu_ref[e] = up_ref[zh, e].astype(F32) + up_d[e].astype(F32)
            return 0

        lax.fori_loop(0, LOCAL, add_experts, 0)
        for e in range(DOWN_A):
            total = da_ref[y, e].astype(F32)
            for c in columns:
                total = total + down_c[c, e].astype(F32)
            ed_ref[e] = total
        for e in range(DOWN_B):
            ed_ref[e + DOWN_A] = db_ref[zh, e].astype(F32) + down_d[e].astype(F32)
        for d, at in zip((2, 6, 4, 1, 3, 5, 7), w_shares):
            copier.arrived(at)
            got_at = dense_ref.at[core, :, lanes(lax.rem(chip + CHIPS - d, CHIPS))]
            copier.send(got_at, got_at, "ctx", sibling)
        for d, at in zip((2, 6, 4, 1, 3, 5, 7), a_shares):
            copier.arrived(at)
            got_at = og_ref.at[half, lanes(lax.rem(chip + CHIPS - d, CHIPS))]
            copier.send(got_at, got_at, "ctx", sibling)
        for at in gain_shares:
            copier.arrived(at)
        total = shared[0]
        for c in range(1, CTX):
            total = total + shared[c]
        gs_ref[...] = total
        for i in range(CHIPS):
            swap(i).wait_send()
        copier.finish()

    vmem = pl.BlockSpec(memory_space=pltpu.VMEM)
    block = (CHIPS, ROWS, 128)
    tile = pltpu.VMEM((128, 128), BF16)
    return pl.pallas_call(
        body,
        name="tail",
        out_shape=[
            jax.ShapeDtypeStruct((LOCAL, 64, FF), F32),
            jax.ShapeDtypeStruct((LOCAL, 64, FF), F32),
            jax.ShapeDtypeStruct((LOCAL, 32, WIDTH), F32),
            jax.ShapeDtypeStruct((ROWS, WIDTH), F32),
            jax.ShapeDtypeStruct((2, 128, WIDTH), BF16),
            jax.ShapeDtypeStruct((128, WIDTH), BF16),
            jax.ShapeDtypeStruct((ROWS, WIDTH), BF16),
            jax.ShapeDtypeStruct((8, 128), F32),
        ],
        in_specs=[vmem] * 7 + [ANY_SPEC] * 4 + [vmem] * 2 + [ANY_SPEC] + [vmem] * 2 + [ANY_SPEC] + [vmem] * 3 + [ANY_SPEC] * 2 + [vmem] * 5,
        out_specs=[vmem] * 4 + [ANY_SPEC] * 3 + [vmem],
        scratch_shapes=[
            pltpu.VMEM((KEYS, 128), BF16),
            pltpu.VMEM((KEYS, 128), BF16),
            pltpu.VMEM((KEYS, 128), F32),
            pltpu.VMEM((KEYS, 128), F32),
            pltpu.VMEM((128, KEYS), BF16),
            pltpu.VMEM(block, BF16),
            pltpu.VMEM((128, 2 * WIDTH), BF16),
            pltpu.VMEM(block, F32),
            pltpu.VMEM(block, F32),
            pltpu.VMEM(block, F32),
            pltpu.VMEM(block, F32),
            pltpu.VMEM((CHIPS, ROWS, WIDTH), BF16),
            pltpu.VMEM((EXP, 128, 2 * WIDTH), BF16),
            pltpu.VMEM((ROWS, WIDTH), BF16),
            pltpu.VMEM((ROWS, WIDTH), F32),
            pltpu.VMEM(block, BF16),
            pltpu.VMEM(block, F32),
            pltpu.VMEM(block, F32),
            pltpu.VMEM((CHIPS, 2, ROWS), F32),
            pltpu.VMEM((CHIPS, CHIPS, 2, ROWS), F32),
            pltpu.VMEM((2,) + block, BF16),
            pltpu.VMEM((2, ROWS, WIDTH), BF16),
            pltpu.VMEM((WIDTH, 128), BF16),
            pltpu.VMEM((WIDTH, 128), BF16),
            pltpu.VMEM((WIDTH, 128), BF16),
            pltpu.VMEM((EXP, 128, 128), BF16),
            pltpu.VMEM((EXP, 128, 128), BF16),
            tile,
            pltpu.VMEM((2, EXP, 64, WIDTH), BF16),
            pltpu.VMEM((EXP, 64, WIDTH), BF16),
            pltpu.VMEM((EXP, 64, WIDTH), BF16),
            pltpu.VMEM((4, 2, 64, WIDTH), BF16),
            pltpu.VMEM((64, WIDTH), BF16),
            pltpu.VMEM((64, WIDTH), BF16),
            pltpu.VMEM((64, WIDTH), BF16),
            pltpu.VMEM((CHIPS, 64, 128), BF16),
            pltpu.VMEM((64, 128), BF16),
            pltpu.VMEM((EXP, 8, 128), F32),
            pltpu.VMEM((EXP, 8, 128), F32),
            pltpu.VMEM((8, 128), F32),
            pltpu.VMEM((CTX, 8, 128), F32),
            pltpu.VMEM((4, LOCAL, 64, FF), BF16),
            pltpu.VMEM((4, DOWN_A, 32, WIDTH), BF16),
            pltpu.VMEM((LOCAL, 64, FF), BF16),
            pltpu.VMEM((DOWN_B, 32, WIDTH), BF16),
            pltpu.SemaphoreType.DMA((CHIPS,)),
            pltpu.SemaphoreType.DMA((CHIPS,)),
            pltpu.SemaphoreType.DMA((126,)),
            pltpu.SemaphoreType.DMA((126,)),
            pltpu.SemaphoreType.DMA((15,)),
        ],
        compiler_params=pltpu.CompilerParams(
            collective_id=6, has_side_effects=True, vmem_limit_bytes=60 * MIB
        ),
    )(
        q, kv, d_out, out_turned, log_total, key_pos, places, q_lin, kv_lin, cosine, sine, squares, gains, normed, attended, d_branch, layer_part,
        w_query, w_key, w_value, tokens, d_resid, ffn_gain, gate_part, up_part, down_a, down_b,
    )


def sum_blocks(blocks):
    return jnp.sum(blocks.astype(F32), axis=0)


def per_device(
    tokens,
    cotangent,
    lengths,
    deal_perm,
    routes,
    gate_logits,
    norm_attn,
    norm_query,
    norm_key,
    norm_ffn,
    w_query,
    w_key,
    w_value,
    w_out,
    w_gate,
    w_up,
    w_down,
):
    tokens, cotangent = tokens[0], cotangent[0]

    row = lambda v: v.reshape(1, -1)
    (
        w_o, gain_all, normed, q_lin, kv_lin, squares, cosine, sine, places, key_pos, q_all, kv_all,
    ) = front(
        tokens,
        (w_query, w_key, w_value, w_out),
        (row(norm_attn), row(norm_query), row(norm_key), row(norm_ffn)),
        deal_perm[0],
        lengths,
    )

    w_o = w_o.reshape(WIDTH, WIDTH)
    kv_all = kv_all.reshape(KEYS, 128)
    attended, out_turned, log_total, resid, rows_all, meta_all, grads_all = attend(
        q_all, kv_all, key_pos, places, cotangent, w_o, tokens, gain_all, routes[0].T, gate_logits[0].T
    )
    rows_in, d_rows, act, d_gate, d_up, out_parts, d_parts = experts(
        rows_all, grads_all, meta_all, w_gate, w_up, w_down
    )
    (
        gate_part, up_part, down_a, down_b, d_resid, d_branch, ffn_gain_grad, d_out, layer_keep, layer_give,
    ) = settle_experts(
        rows_in,
        d_rows,
        act,
        d_gate,
        d_up,
        d_parts.reshape(2, 4, ROWS, WIDTH),
        out_parts.reshape(2, 4, ROWS, WIDTH),
        resid,
        cotangent,
        gain_all,
        w_o,
    )
    gate_grad, up_grad, down_grad, input_grad, dense, out_grad, layer_got, gain_sums = tail(
        q_all,
        kv_all,
        d_out,
        out_turned,
        log_total,
        key_pos,
        places,
        q_lin,
        kv_lin,
        cosine,
        sine,
        squares,
        gain_all,
        normed,
        attended,
        d_branch,
        layer_give,
        w_query,
        w_key,
        w_value,
        tokens,
        d_resid,
        ffn_gain_grad,
        gate_part,
        up_part,
        down_a,
        down_b,
    )
    outs = deliver(
        resid,
        layer_keep,
        layer_got,
        dense,
        out_grad,
        gain_sums,
        input_grad,
        (gate_grad, up_grad, down_grad),
    )
    return (
        outs[0][None],
        outs[9][None],
        *outs[1:5],
        *[g.reshape(-1) for g in outs[5:9]],
        *outs[10:],
    )


def solution(mesh):
    in_specs = (
        P("exp", "ctx", None),
        P("exp", "ctx", None),
        P("exp", None),
        P("exp", None, None),
        P("exp", "ctx", None),
        P("exp", "ctx", None),
        P("exp"),
        P("exp"),
        P("exp"),
        P("exp"),
        P("exp", None),
        P("exp", None),
        P("exp", None),
        P("exp", None),
        P("exp", None, None),
        P("exp", None, None),
        P("exp", None, None),
    )
    out_specs = (
        P("exp", "ctx", None),
        P("exp", "ctx", None),
        P("exp", None),
        P("exp", None),
        P("exp", None),
        P("exp", None),
        P("exp"),
        P("exp"),
        P("exp"),
        P("exp"),
        P("exp", "ctx", None),
        P("exp", "ctx", None),
        P("exp", "ctx", None),
    )
    return jax.shard_map(
        per_device, mesh=mesh, in_specs=in_specs, out_specs=out_specs, check_vma=False
    )
```
